32 devices in a mesh: dp: 8 (over y, x, core), mp: 4 (over z).
Axes of the slice: x: 2, y: 2, z: 4, core: 2. Of those that a mesh axis runs over, the one named last changes fastest.
Arguments:
- block_input: bfloat16 [16512, 1152], P('dp'), may hold values from -6 to 6
- skip_input: bfloat16 [16512, 1152], P('dp'), may hold values from -6 to 6
- timesteps: int32 [64], P('dp'), may hold values from 0 to 999
- class_labels: int32 [64], P('dp'), may hold values from 0 to 999
- loss_weights: float32 [64], P('dp'), may hold values from 0.5 to 2
- grad_output: bfloat16 [16512, 1152], P('dp'), may hold values from -6 to 6
- skip_weight: float32 [2, 1152, 1152], P(None, 'mp'), may hold values from -0.125 to 0.125
- qkv_weight: float32 [3, 1152, 1152], P(None, None, 'mp'), may hold values from -0.1875 to 0.1875
- proj_weight: float32 [1152, 1152], P('mp'), may hold values from -0.75 to 0.75
- fc1_weight: float32 [1152, 4608], P(None, 'mp'), may hold values from -0.1875 to 0.1875
- fc2_weight: float32 [4608, 1152], P('mp'), may hold values from -0.09375 to 0.09375
- vectors: float32 [7, 1152], replicated, may hold values from -1.2 to 1.75, as said below
- hidden_bias: float32 [4608], P('mp'), may hold values from -1.5 to 1.5
- skip_rows: float32 [2, 1152], replicated, may hold values from 1651.2 to 280704
- skip_cols: float32 [2, 1152], replicated, may hold values from 16512 to 66048
- qkv_rows: float32 [3, 1152], replicated, may hold values from 516 to 2064
- qkv_cols: float32 [3, 1152], replicated, may hold values from 51.6 to 8772
- proj_rows: float32 [1152], replicated, may hold values from 51.6 to 8772
- proj_cols: float32 [1152], replicated, may hold values from 516 to 2064
- fc1_rows: float32 [1152], replicated, may hold values from 2064 to 8256
- fc1_cols: float32 [4608], replicated, may hold values from 206.4 to 35088
- fc2_rows: float32 [4608], replicated, may hold values from 412.8 to 70176
- fc2_cols: float32 [1152], replicated, may hold values from 4128 to 16512
- vector_moments: float32 [7, 1152], replicated, may hold values from 16512 to 66048
- hidden_moments: float32 [4608], P('mp'), may hold values from 206.4 to 35088
Outputs:
- block_output: bfloat16 [16512, 1152], P('dp')
- input_grad: float32 [16512, 1152], P('dp', 'mp')
- skip_input_grad: float32 [16512, 1152], P('dp', 'mp')
- skip_weight_grad: float32 [2, 1152, 1152], P(None, 'mp', 'dp')
- qkv_weight_grad: float32 [3, 1152, 1152], P(None, 'dp', 'mp')
- proj_weight_grad: float32 [1152, 1152], P('mp', 'dp')
- fc1_weight_grad: float32 [1152, 4608], P('dp', 'mp')
- fc2_weight_grad: float32 [4608, 1152], P('mp', 'dp')
- vector_grads: float32 [7, 1152], P(None, 'dp')
- hidden_bias_grad: float32 [4608], P('mp')
- skip_rows_new: float32 [2, 1152], replicated
- skip_cols_new: float32 [2, 1152], replicated
- qkv_rows_new: float32 [3, 1152], replicated
- qkv_cols_new: float32 [3, 1152], replicated
- proj_rows_new: float32 [1152], replicated
- proj_cols_new: float32 [1152], replicated
- fc1_rows_new: float32 [1152], replicated
- fc1_cols_new: float32 [4608], replicated
- fc2_rows_new: float32 [4608], replicated
- fc2_cols_new: float32 [1152], replicated
- vector_moments_new: float32 [7, 1152], replicated
- hidden_moments_new: float32 [4608], P('mp')
- skip_weight_new: float32 [2, 1152, 1152], P(None, 'mp')
- qkv_weight_new: float32 [3, 1152, 1152], P(None, None, 'mp')
- proj_weight_new: float32 [1152, 1152], P('mp')
- fc1_weight_new: float32 [1152, 4608], P(None, 'mp')
- fc2_weight_new: float32 [4608, 1152], P('mp')
- vectors_new: float32 [7, 1152], replicated
- hidden_bias_new: float32 [4608], P('mp')
- skip_weight_low: bfloat16 [2, 1152, 1152], P(None, 'mp')
- qkv_weight_low: bfloat16 [3, 1152, 1152], P(None, None, 'mp')
- proj_weight_low: bfloat16 [1152, 1152], P('mp')
- fc1_weight_low: bfloat16 [1152, 4608], P(None, 'mp')
- fc2_weight_low: bfloat16 [4608, 1152], P('mp')
- update_rms: float32 [], replicated
The draws below stay inside these ranges and needn't reach their ends.
Inputs may be any that keep to these rules, and one draw needn't show every extreme that they name: `vectors`: norm gains lie near one, biases are of both signs.
All inputs are finite; a program needn't handle non-finite values.
Results may differ from the reference program's by a relative error of at most 0.0095.
Values sent between devices are 32-bit elements; how exact they have to be, the bound alone decides.
No kernel may reach another device: no remote copies, remote signals or barrier semaphores. Data moves between devices by JAX's collectives and lax.ppermute only.
A program may use at most 256 MiB of HBM per device.

```python
import math
import jax
import jax.numpy as jnp
import numpy as np
from jax import lax

D = 1152
HEADS = 16
HEAD_DIM = 72
FF = 4608
CLASSES = 1000
SEQ = 258
IMAGES = 64
TOKENS = 16512


def draw_vectors(key, part):
    key = jax.random.fold_in(key, 11)
    gain_key, bias_key = jax.random.split(key)
    gains = jnp.clip(1.0 + 0.25 * jax.random.normal(gain_key, (7, D), jnp.float32), 0.25, 1.75)
    biases = jnp.clip(0.3 * jax.random.normal(bias_key, (7, D), jnp.float32), -1.2, 1.2)
    row_ids = jnp.arange(7)[:, None]
    return jnp.where((row_ids == 0) | (row_ids == 2), gains, biases)


def moment_ramp(key, shape, base_level, first_level, last_level):
    length = shape[-1]
    position = jnp.arange(length, dtype=jnp.float32) / max(length - 1, 1)
    ramp = jnp.exp(math.log(first_level) + (math.log(last_level) - math.log(first_level)) * position)
    factor = jnp.exp(jax.random.uniform(key, shape, jnp.float32, math.log(0.7), math.log(1.4)))
    return base_level * ramp * factor


def draw_skip_rows(key, part):
    key = jax.random.fold_in(key, 21)
    return moment_ramp(key, (2, D), float(TOKENS), 8.0, 0.25)


def draw_qkv_cols(key, part):
    key = jax.random.fold_in(key, 22)
    return moment_ramp(key, (3, D), float(TOKENS // 32), 8.0, 0.25)


def draw_proj_rows(key, part):
    key = jax.random.fold_in(key, 23)
    return moment_ramp(key, (D,), float(TOKENS // 32), 8.0, 0.25)


def draw_fc1_cols(key, part):
    key = jax.random.fold_in(key, 24)
    return moment_ramp(key, (FF,), float(TOKENS // 8), 8.0, 0.25)


def draw_fc2_rows(key, part):
    key = jax.random.fold_in(key, 25)
    return moment_ramp(key, (FF,), float(TOKENS // 4), 8.0, 0.25)


def draw_hidden_moments(key, part):
    key = jax.random.fold_in(key, 26)
    return moment_ramp(key, (FF,), float(TOKENS // 8), 8.0, 0.25)


def with_ends(array, key, low, top_value):
    longest = array.shape.index(max(array.shape))
    spots = []
    for shift in (0, 1):
        where = [jax.random.randint(jax.random.fold_in(key, axis), (), 0, length) for axis, length in enumerate(array.shape)]
        where[longest] = (where[longest] + shift) % array.shape[longest]
        spots.append(tuple(where))
    return array.at[spots[0]].set(low).at[spots[1]].set(top_value)


def level_of(stream_key, extent, cuts, least, largest):
    factor_of = 1.0
    for dim, parts in cuts:
        heights = jax.random.uniform(jax.random.fold_in(jax.random.fold_in(stream_key, 6), dim), (parts,), jnp.float32, least / len(cuts), largest / len(cuts))
        factor_of = factor_of * jnp.repeat(jnp.exp(heights), extent[dim] // parts).reshape((-1,) + (1,) * (len(extent) - 1 - dim))
    return factor_of


def rank_table(amount, slope):
    weights = [(1 << 20) // math.isqrt(rank ** slope) + 1 for rank in range(1, amount + 1)]
    spread = 1 + sum(weights) // (1 << 30)
    return np.cumsum(np.array([max(1, weight // spread) for weight in weights]))


def skewed_ids(stream_key, dims, number_of, skew):
    table = rank_table(number_of, skew)
    pick = jax.random.randint(jax.random.fold_in(stream_key, 1), dims, 0, int(table[number_of - 1]))
    rank = jnp.searchsorted(jnp.asarray(table, jnp.int32), pick, side="right")
    return jax.random.permutation(jax.random.fold_in(stream_key, 2), number_of)[rank].astype(jnp.int32)


def normal_values(stream_key, extent, deviation, reach, shards=(), held_as=jnp.bfloat16):
    result = deviation * jax.random.normal(stream_key, extent, jnp.float32)
    if shards:
        result = result * level_of(stream_key, extent, shards, -0.22, 0.18)
    return jnp.clip(result, -reach, reach).astype(held_as)


def setup_inputs(seed: int = 0) -> dict:
    splits = jax.random.split(jax.random.key(seed), 26)
    return {
        "block_input": normal_values(splits[0], (TOKENS, D), 1.0, 6.0, ((0, 8),)),
        "skip_input": normal_values(splits[1], (TOKENS, D), 1.0, 6.0, ((0, 8),)),
        "timesteps": with_ends(jax.random.randint(splits[2], (IMAGES,), 0, 1000), jax.random.fold_in(splits[2], 1), 0, 999).astype(jnp.int32),
        "class_labels": with_ends(skewed_ids(splits[3], (IMAGES,), CLASSES, 2), jax.random.fold_in(splits[3], 3), 0, CLASSES - 1).astype(jnp.int32),
        "loss_weights": jnp.clip(0.5 + 1.5 * jax.random.uniform(splits[4], (IMAGES,), jnp.float32) ** level_of(splits[4], (IMAGES,), ((0, 8),), -0.2, 0.2), 0.5, 2.0),
        "grad_output": normal_values(splits[5], (TOKENS, D), 1.0, 6.0, ((0, 8),)),
        "skip_weight": normal_values(splits[6], (2, D, D), (2 * D) ** -0.5, 0.125, ((1, 4),), jnp.float32),
        "qkv_weight": normal_values(splits[7], (3, D, D), D ** -0.5, 0.1875, ((2, 4),), jnp.float32),
        "proj_weight": normal_values(splits[8], (D, D), HEAD_DIM ** -0.5, 0.75, ((0, 4),), jnp.float32),
        "fc1_weight": normal_values(splits[9], (D, FF), D ** -0.5, 0.1875, ((1, 4),), jnp.float32),
        "fc2_weight": normal_values(splits[10], (FF, D), FF ** -0.5, 0.09375, ((0, 4),), jnp.float32),
        "vectors": draw_vectors(jax.random.fold_in(splits[25], 71), 0),
        "hidden_bias": normal_values(splits[12], (FF,), 0.3, 1.5, ((0, 4),), jnp.float32),
        "skip_rows": draw_skip_rows(jax.random.fold_in(splits[25], 71), 0),
        "skip_cols": jnp.clip(jnp.exp(jax.random.uniform(splits[14], (2, D), jnp.float32, math.log(16512.0), math.log(66048.0))), 16512.0, 66048.0),
        "qkv_rows": jnp.clip(jnp.exp(jax.random.uniform(splits[15], (3, D), jnp.float32, math.log(516.0), math.log(2064.0))), 516.0, 2064.0),
        "qkv_cols": draw_qkv_cols(jax.random.fold_in(splits[25], 71), 0),
        "proj_rows": draw_proj_rows(jax.random.fold_in(splits[25], 71), 0),
        "proj_cols": jnp.clip(jnp.exp(jax.random.uniform(splits[18], (D,), jnp.float32, math.log(516.0), math.log(2064.0))), 516.0, 2064.0),
        "fc1_rows": jnp.clip(jnp.exp(jax.random.uniform(splits[19], (D,), jnp.float32, math.log(2064.0), math.log(8256.0))), 2064.0, 8256.0),
        "fc1_cols": draw_fc1_cols(jax.random.fold_in(splits[25], 71), 0),
        "fc2_rows": draw_fc2_rows(jax.random.fold_in(splits[25], 71), 0),
        "fc2_cols": jnp.clip(jnp.exp(jax.random.uniform(splits[22], (D,), jnp.float32, math.log(4128.0), math.log(16512.0))), 4128.0, 16512.0),
        "vector_moments": jnp.clip(jnp.exp(jax.random.uniform(splits[23], (7, D), jnp.float32, math.log(16512.0), math.log(66048.0))), 16512.0, 66048.0),
        "hidden_moments": draw_hidden_moments(jax.random.fold_in(splits[25], 71), 0),
    }


@jax.custom_vjp
def low(v):
    return lax.optimization_barrier(v.astype(jnp.bfloat16)).astype(jnp.float32)

@jax.custom_vjp
def low_back(v):
    return v

def low_keep(v):
    return (low(v), None)

def low_pass(kept, grad):
    return (grad,)

def back_keep(v):
    return (v, None)

def back_low(kept, grad):
    return (low(grad),)
low.defvjp(low_keep, low_pass)
low_back.defvjp(back_keep, back_low)
highest = lax.Precision.HIGHEST
ln_eps = 1e-05
moment_eps = 1e-30
clip_level = 0.25
step_rate = 2.0
total_steps = 1000.0

def product(left_side, right_side):
    return jnp.dot(left_side, right_side, precision=highest, preferred_element_type=jnp.float32)

def layer_norm(inputs, norm_gain, norm_bias):
    centre = lax.optimization_barrier(jnp.mean(inputs, -1, keepdims=True))
    centred = inputs - centre
    variance = lax.optimization_barrier(jnp.mean(centred * centred, -1, keepdims=True))
    return centred * lax.rsqrt(variance + ln_eps) * norm_gain + norm_bias

def gelu_exact(inputs):
    return 0.5 * inputs * (1.0 + lax.erf(inputs * (1.0 / math.sqrt(2.0))))

def attend_image(triple):
    query_img, key_img, value_img = triple
    scores = low_back(jnp.einsum('qhe,khe->hqk', query_img, key_img, precision=highest) * HEAD_DIM ** (-0.5))
    score_top = lax.optimization_barrier(jnp.max(scores, -1, keepdims=True))
    expo_scores = jnp.exp(scores - score_top)
    weights_prob = expo_scores / lax.optimization_barrier(jnp.sum(expo_scores, -1, keepdims=True))
    return jnp.einsum('hqk,khe->qhe', low(weights_prob), value_img, precision=highest)

def forward(block_in, skip_in, skip_weight, qkv_weight, proj_weight, fc1_weight, fc2_weight, vectors, hidden_bias):
    skip_low = low(skip_weight)
    joined = low_back(product(block_in, skip_low[0]) + product(skip_in, skip_low[1])) + vectors[4]
    normed = low(layer_norm(joined, vectors[0], vectors[1]))
    qkv_all = jnp.einsum('td,sde->ste', normed, low(qkv_weight), precision=highest)
    qkv_all = low_back(low(qkv_all))
    shaped = qkv_all.reshape(3, IMAGES, SEQ, HEADS, HEAD_DIM)
    attended = lax.map(jax.checkpoint(attend_image), (shaped[0], shaped[1], shaped[2]))
    attended = low_back(low(attended.reshape(IMAGES * SEQ, D)))
    residual = joined + low_back(product(attended, low(proj_weight))) + vectors[5]
    normed_two = low(layer_norm(residual, vectors[2], vectors[3]))
    pre_act = low_back(product(normed_two, low(fc1_weight))) + hidden_bias
    activated = low(gelu_exact(pre_act))
    return residual + low_back(product(activated, low(fc2_weight))) + vectors[6]

def factored_step(grad_now, rows_old, cols_old):
    squares = grad_now * grad_now + moment_eps
    rows_new = 0.5 * rows_old + 0.5 * lax.optimization_barrier(jnp.mean(squares, -1))
    cols_new = 0.5 * cols_old + 0.5 * lax.optimization_barrier(jnp.mean(squares, -2))
    denom = rows_new[..., :, None] * cols_new[..., None, :] / lax.optimization_barrier(jnp.mean(rows_new, -1))[..., None, None]
    return (grad_now * lax.rsqrt(denom), rows_new, cols_new)

def reference(block_input, skip_input, timesteps, class_labels, loss_weights, grad_output, skip_weight, qkv_weight, proj_weight, fc1_weight, fc2_weight, vectors, hidden_bias, skip_rows, skip_cols, qkv_rows, qkv_cols, proj_rows, proj_cols, fc1_rows, fc1_cols, fc2_rows, fc2_cols, vector_moments, hidden_moments):
    angles = (timesteps.astype(jnp.float32) + 0.5) * (0.5 * math.pi / total_steps)
    alpha_sq = jnp.square(jnp.cos(angles))
    sigma_sq = jnp.square(jnp.sin(angles))
    snr_weight = 5.0 * sigma_sq / jnp.maximum(alpha_sq, 5.0 * sigma_sq)
    base_weight = loss_weights * snr_weight
    one_hot = (class_labels[:, None] == jnp.arange(CLASSES, dtype=jnp.int32)[None, :]).astype(jnp.float32)
    class_counts = lax.optimization_barrier(jnp.sum(one_hot, 0))
    own_count = jnp.dot(one_hot, class_counts, precision=highest)
    item_weight = base_weight * (IMAGES / jnp.sum(base_weight)) * lax.rsqrt(own_count)
    upstream = grad_output.astype(jnp.float32) * jnp.repeat(item_weight, SEQ)[:, None]
    output_full, pullback = jax.vjp(forward, block_input.astype(jnp.float32), skip_input.astype(jnp.float32), skip_weight, qkv_weight, proj_weight, fc1_weight, fc2_weight, vectors, hidden_bias)
    grads = pullback(upstream)
    input_grad, skip_input_grad, skip_grad, qkv_grad, proj_grad, fc1_grad, fc2_grad, vector_grad, hidden_grad = grads
    skip_step, skip_rows_new, skip_cols_new = factored_step(skip_grad, skip_rows, skip_cols)
    qkv_step, qkv_rows_new, qkv_cols_new = factored_step(qkv_grad, qkv_rows, qkv_cols)
    proj_step, proj_rows_new, proj_cols_new = factored_step(proj_grad, proj_rows, proj_cols)
    fc1_step, fc1_rows_new, fc1_cols_new = factored_step(fc1_grad, fc1_rows, fc1_cols)
    fc2_step, fc2_rows_new, fc2_cols_new = factored_step(fc2_grad, fc2_rows, fc2_cols)
    vector_moments_new = 0.5 * vector_moments + 0.5 * (vector_grad * vector_grad + moment_eps)
    vector_step = vector_grad * lax.rsqrt(vector_moments_new)
    hidden_moments_new = 0.5 * hidden_moments + 0.5 * (hidden_grad * hidden_grad + moment_eps)
    hidden_step = hidden_grad * lax.rsqrt(hidden_moments_new)
    step_sq = jnp.sum(skip_step * skip_step) + jnp.sum(qkv_step * qkv_step) + jnp.sum(proj_step * proj_step)
    step_sq = step_sq + jnp.sum(fc1_step * fc1_step) + jnp.sum(fc2_step * fc2_step)
    step_sq = step_sq + jnp.sum(vector_step * vector_step) + jnp.sum(hidden_step * hidden_step)
    param_count = 6.0 * D * D + 2.0 * D * FF + 7.0 * D + FF
    update_rms = jnp.sqrt(step_sq / param_count)
    divisor = jnp.maximum(1.0, update_rms / clip_level)

    def renew_weight(weight_now, step_now):
        return weight_now - step_rate * jnp.maximum(0.001, jnp.sqrt(jnp.mean(weight_now * weight_now))) * step_now / divisor
    skip_new = renew_weight(skip_weight, skip_step)
    qkv_new = renew_weight(qkv_weight, qkv_step)
    proj_new = renew_weight(proj_weight, proj_step)
    fc1_new = renew_weight(fc1_weight, fc1_step)
    fc2_new = renew_weight(fc2_weight, fc2_step)
    hidden_new = renew_weight(hidden_bias, hidden_step)
    vector_rms = jnp.sqrt(lax.optimization_barrier(jnp.mean(vectors * vectors, 1, keepdims=True)))
    vectors_new = vectors - step_rate * jnp.maximum(0.001, vector_rms) * vector_step / divisor
    return (output_full.astype(jnp.bfloat16), input_grad, skip_input_grad, skip_grad, qkv_grad, proj_grad, fc1_grad, fc2_grad, vector_grad, hidden_grad, skip_rows_new, skip_cols_new, qkv_rows_new, qkv_cols_new, proj_rows_new, proj_cols_new, fc1_rows_new, fc1_cols_new, fc2_rows_new, fc2_cols_new, vector_moments_new, hidden_moments_new, skip_new, qkv_new, proj_new, fc1_new, fc2_new, vectors_new, hidden_new, skip_new.astype(jnp.bfloat16), qkv_new.astype(jnp.bfloat16), proj_new.astype(jnp.bfloat16), fc1_new.astype(jnp.bfloat16), fc2_new.astype(jnp.bfloat16), update_rms)
```

```python
import math

import jax
import jax.numpy as jnp
from jax import lax
from jax.experimental import pallas as pl
from jax.experimental.pallas import tpu as pltpu
from jax.sharding import PartitionSpec as P

D = 1152
HEAD_DIM = 72
FF = 4608
CLASSES = 1000
SEQ = 258


ln_eps = 1e-05
moment_eps = 1e-30
clip_level = 0.25
step_rate = 2.0
total_steps = 1000.0


def gelu_exact(inputs):
    return 0.5 * inputs * (1.0 + lax.erf(inputs * (1.0 / math.sqrt(2.0))))


def matmul(left_side, right_side):
    return jnp.dot(left_side, right_side, preferred_element_type=jnp.float32)


def norm_forward(inputs, norm_gain, norm_bias):
    centre = jnp.mean(inputs, -1, keepdims=True)
    centred = inputs - centre
    inverse = lax.rsqrt(jnp.mean(centred * centred, -1, keepdims=True) + ln_eps)
    normal = centred * inverse
    return (normal * norm_gain + norm_bias, normal, inverse)


def norm_backward(incoming, normal, inverse, norm_gain):
    scaled = incoming * norm_gain
    inner_mean = jnp.mean(scaled, -1, keepdims=True)
    proj_mean = jnp.mean(scaled * normal, -1, keepdims=True)
    return (
        inverse * (scaled - inner_mean - normal * proj_mean),
        jnp.sum(incoming * normal, 0),
        jnp.sum(incoming, 0),
    )


def adafactor(
    grad_pieces,
    weight_pieces,
    starts,
    row_states,
    col_states,
    vector_piece,
    vector_weight,
    vector_state,
    hidden_piece,
    hidden_weight,
    hidden_state,
    first_mask,
    reduce_moments,
    reduce_norm,
):
    full_shapes = ((D, D), (D, D), (D, D), (D, FF), (FF, D))
    tensor_sizes = (2.0 * D * D, 3.0 * D * D, 1.0 * D * D, 1.0 * D * FF, 1.0 * FF * D)
    zero_start = jnp.zeros((), jnp.int32)
    row_parts = []
    col_parts = []
    weight_sq = []
    for position in range(5):
        grad_piece = grad_pieces[position]
        leading = grad_piece.shape[0]
        squares = grad_piece * grad_piece + moment_eps
        row_zero = jnp.zeros((leading, full_shapes[position][0]), jnp.float32)
        col_zero = jnp.zeros((leading, full_shapes[position][1]), jnp.float32)
        row_parts.append(
            lax.dynamic_update_slice(
                row_zero, jnp.sum(squares, 2), (zero_start, starts[position][0])
            ).reshape(-1)
        )
        col_parts.append(
            lax.dynamic_update_slice(
                col_zero, jnp.sum(squares, 1), (zero_start, starts[position][1])
            ).reshape(-1)
        )
        weight_sq.append(jnp.sum(weight_pieces[position] * weight_pieces[position])[None])
    weight_sq.append(jnp.sum(vector_weight * vector_weight, 1) * first_mask)
    weight_sq.append(jnp.sum(hidden_weight * hidden_weight)[None])
    row_total, col_total, weight_total = reduce_moments(
        jnp.concatenate(row_parts), jnp.concatenate(col_parts), jnp.concatenate(weight_sq)
    )
    row_news = []
    col_news = []
    updates = []
    step_sq = jnp.zeros((), jnp.float32)
    row_offset = 0
    col_offset = 0
    for position in range(5):
        grad_piece = grad_pieces[position]
        leading = grad_piece.shape[0]
        rows_full, cols_full = full_shapes[position]
        row_sum = row_total[row_offset : row_offset + leading * rows_full].reshape(
            leading, rows_full
        )
        col_sum = col_total[col_offset : col_offset + leading * cols_full].reshape(
            leading, cols_full
        )
        row_offset = row_offset + leading * rows_full
        col_offset = col_offset + leading * cols_full
        row_new = 0.5 * row_states[position] + 0.5 * (row_sum / cols_full)
        col_new = 0.5 * col_states[position] + 0.5 * (col_sum / rows_full)
        row_piece = lax.dynamic_slice(
            row_new, (zero_start, starts[position][0]), (leading, grad_piece.shape[1])
        )
        col_piece = lax.dynamic_slice(
            col_new, (zero_start, starts[position][1]), (leading, grad_piece.shape[2])
        )
        row_mean = jnp.mean(row_new, 1)
        update = grad_piece * lax.rsqrt(
            row_piece[:, :, None] * col_piece[:, None, :] / row_mean[:, None, None]
        )
        step_sq = step_sq + jnp.sum(update * update)
        row_news.append(row_new)
        col_news.append(col_new)
        updates.append(update)
    vector_new = 0.5 * vector_state + 0.5 * (vector_piece * vector_piece + moment_eps)
    vector_update = vector_piece * lax.rsqrt(vector_new)
    hidden_new = 0.5 * hidden_state + 0.5 * (hidden_piece * hidden_piece + moment_eps)
    hidden_update = hidden_piece * lax.rsqrt(hidden_new)
    step_sq = (
        step_sq
        + jnp.sum(vector_update * vector_update) * first_mask
        + jnp.sum(hidden_update * hidden_update)
    )
    step_total = reduce_norm(step_sq)
    param_count = 6.0 * D * D + 2.0 * D * FF + 7.0 * D + FF
    update_rms = jnp.sqrt(step_total / param_count)
    divisor = jnp.maximum(1.0, update_rms / clip_level)
    new_weights = []
    for position in range(5):
        weight_rms = jnp.sqrt(weight_total[position] / tensor_sizes[position])
        new_weights.append(
            weight_pieces[position]
            - step_rate * jnp.maximum(0.001, weight_rms) * updates[position] / divisor
        )
    vector_rms = jnp.sqrt(weight_total[5:12] / D)[:, None]
    vector_weight_new = (
        vector_weight - step_rate * jnp.maximum(0.001, vector_rms) * vector_update / divisor
    )
    hidden_rms = jnp.sqrt(weight_total[12] / FF)
    hidden_weight_new = (
        hidden_weight - step_rate * jnp.maximum(0.001, hidden_rms) * hidden_update / divisor
    )
    return (
        new_weights,
        row_news,
        col_news,
        vector_new,
        vector_weight_new,
        hidden_new,
        hidden_weight_new,
        update_rms,
    )


def body_tensor(
    block_input,
    skip_input,
    timesteps,
    class_labels,
    loss_weights,
    grad_output,
    skip_weight,
    qkv_weight,
    proj_weight,
    fc1_weight,
    fc2_weight,
    vectors,
    hidden_bias,
    skip_rows,
    skip_cols,
    qkv_rows,
    qkv_cols,
    proj_rows,
    proj_cols,
    fc1_rows,
    fc1_cols,
    fc2_rows,
    fc2_cols,
    vector_moments,
    hidden_moments,
):
    image_count = timesteps.shape[0]
    width_local = qkv_weight.shape[2]
    heads_local = width_local // HEAD_DIM
    hidden_local = fc1_weight.shape[1]
    mp_index = lax.axis_index("mp")
    dp_index = lax.axis_index("dp")
    dp_count = lax.axis_size("dp")
    first_mask = (mp_index == 0).astype(jnp.float32)
    feature_start = mp_index * skip_weight.shape[1]
    block_local = lax.dynamic_slice_in_dim(block_input, feature_start, skip_weight.shape[1], 1)
    skip_local = lax.dynamic_slice_in_dim(skip_input, feature_start, skip_weight.shape[1], 1)
    angles = (timesteps.astype(jnp.float32) + 0.5) * (0.5 * math.pi / total_steps)
    alpha_sq = jnp.square(jnp.cos(angles))
    sigma_sq = jnp.square(jnp.sin(angles))
    snr_weight = 5.0 * sigma_sq / jnp.maximum(alpha_sq, 5.0 * sigma_sq)
    base_weight = loss_weights * snr_weight
    one_hot = (class_labels[:, None] == jnp.arange(CLASSES, dtype=jnp.int32)[None, :]).astype(
        jnp.float32
    )
    class_counts, weight_total = lax.psum((jnp.sum(one_hot, 0), jnp.sum(base_weight)), "dp")
    own_count = jnp.dot(one_hot, class_counts, precision=lax.Precision.HIGHEST)
    item_weight = base_weight * (image_count * dp_count / weight_total) * lax.rsqrt(own_count)
    upstream = (
        grad_output.astype(jnp.float32).reshape(image_count, SEQ, D) * item_weight[:, None, None]
    ).reshape(-1, D)
    skip_low = skip_weight.astype(jnp.bfloat16)
    qkv_low = qkv_weight.astype(jnp.bfloat16)
    proj_low = proj_weight.astype(jnp.bfloat16)
    fc1_low = fc1_weight.astype(jnp.bfloat16)
    fc2_low = fc2_weight.astype(jnp.bfloat16)
    joined = (
        lax.psum(matmul(block_local, skip_low[0]) + matmul(skip_local, skip_low[1]), "mp")
        + vectors[4]
    )
    normed, normal_one, inverse_one = norm_forward(joined, vectors[0], vectors[1])
    normed_low = normed.astype(jnp.bfloat16)
    qkv_all = jnp.einsum(
        "td,sde->ste", normed_low, qkv_low, preferred_element_type=jnp.float32
    ).astype(jnp.bfloat16)
    heads_view = qkv_all.reshape(3, image_count, SEQ, heads_local, HEAD_DIM)
    query_low = heads_view[0]
    key_low = heads_view[1]
    value_low = heads_view[2]
    score_scale = HEAD_DIM ** (-0.5)

    def score_block():
        return (
            jnp.einsum("iqhe,ikhe->ihqk", query_low, key_low, preferred_element_type=jnp.float32)
            * score_scale
        )

    scores = score_block()
    score_top = jnp.max(scores, -1, keepdims=True)
    expo_scores = jnp.exp(scores - score_top)
    expo_total = jnp.sum(expo_scores, -1, keepdims=True)
    weights_low = (expo_scores / expo_total).astype(jnp.bfloat16)
    log_total = score_top + jnp.log(expo_total)
    attended = (
        jnp.einsum("ihqk,ikhe->iqhe", weights_low, value_low, preferred_element_type=jnp.float32)
        .astype(jnp.bfloat16)
        .reshape(-1, width_local)
    )
    residual = joined + lax.psum(matmul(attended, proj_low), "mp") + vectors[5]
    normed_two, normal_two, inverse_two = norm_forward(residual, vectors[2], vectors[3])
    normed_two_low = normed_two.astype(jnp.bfloat16)
    pre_act = matmul(normed_two_low, fc1_low) + hidden_bias
    activated, gelu_pull = jax.vjp(gelu_exact, pre_act)
    activated_low = activated.astype(jnp.bfloat16)
    block_output = (residual + lax.psum(matmul(activated_low, fc2_low), "mp") + vectors[6]).astype(
        jnp.bfloat16
    )
    upstream_low = upstream.astype(jnp.bfloat16)
    fc2_grad = jnp.einsum(
        "tf,td->fd", activated_low, upstream_low, preferred_element_type=jnp.float32
    )
    fc2_bias_grad = jnp.sum(upstream, 0)
    act_grad = jnp.einsum("td,fd->tf", upstream_low, fc2_low, preferred_element_type=jnp.float32)
    pre_grad = gelu_pull(act_grad)[0]
    pre_low = pre_grad.astype(jnp.bfloat16)
    fc1_grad = jnp.einsum("td,tf->df", normed_two_low, pre_low, preferred_element_type=jnp.float32)
    hidden_grad = jnp.sum(pre_grad, 0)
    norm_two_in = lax.psum(
        jnp.einsum("tf,df->td", pre_low, fc1_low, preferred_element_type=jnp.float32), "mp"
    )
    back_two, gain_two_grad, bias_two_grad = norm_backward(
        norm_two_in, normal_two, inverse_two, vectors[2]
    )
    residual_grad = upstream + back_two
    proj_bias_grad = jnp.sum(residual_grad, 0)
    residual_low = residual_grad.astype(jnp.bfloat16)
    proj_grad = jnp.einsum("te,td->ed", attended, residual_low, preferred_element_type=jnp.float32)
    attended_grad = jnp.einsum(
        "td,ed->te", residual_low, proj_low, preferred_element_type=jnp.float32
    ).astype(jnp.bfloat16)
    attended_grad = attended_grad.reshape(image_count, SEQ, heads_local, HEAD_DIM)
    scores = score_block()
    probs_exact = jnp.exp(scores - log_total)
    prob_grad = jnp.einsum(
        "iqhe,ikhe->ihqk", attended_grad, value_low, preferred_element_type=jnp.float32
    )
    score_grad = (
        probs_exact * (prob_grad - jnp.sum(probs_exact * prob_grad, -1, keepdims=True))
    ).astype(jnp.bfloat16)
    query_grad = (
        jnp.einsum("ihqk,ikhe->iqhe", score_grad, key_low, preferred_element_type=jnp.float32)
        * score_scale
    )
    key_grad = (
        jnp.einsum("ihqk,iqhe->ikhe", score_grad, query_low, preferred_element_type=jnp.float32)
        * score_scale
    )
    value_grad = jnp.einsum(
        "ihqk,iqhe->ikhe", weights_low, attended_grad, preferred_element_type=jnp.float32
    )
    qkv_grad_low = (
        jnp.stack([query_grad, key_grad, value_grad])
        .astype(jnp.bfloat16)
        .reshape(3, -1, width_local)
    )
    qkv_grad = jnp.einsum(
        "td,ste->sde", normed_low, qkv_grad_low, preferred_element_type=jnp.float32
    )
    norm_one_in = lax.psum(
        jnp.einsum("ste,sde->td", qkv_grad_low, qkv_low, preferred_element_type=jnp.float32), "mp"
    )
    back_one, gain_one_grad, bias_one_grad = norm_backward(
        norm_one_in, normal_one, inverse_one, vectors[0]
    )
    joined_grad = residual_grad + back_one
    skip_bias_grad = jnp.sum(joined_grad, 0)
    joined_low = joined_grad.astype(jnp.bfloat16)
    skip_grad = jnp.stack(
        [
            jnp.einsum("tc,td->cd", block_local, joined_low, preferred_element_type=jnp.float32),
            jnp.einsum("tc,td->cd", skip_local, joined_low, preferred_element_type=jnp.float32),
        ]
    )
    input_grad = jnp.einsum(
        "td,cd->tc", joined_low, skip_low[0], preferred_element_type=jnp.float32
    )
    skip_input_grad = jnp.einsum(
        "td,cd->tc", joined_low, skip_low[1], preferred_element_type=jnp.float32
    )
    vector_grad = jnp.stack(
        [
            gain_one_grad,
            bias_one_grad,
            gain_two_grad,
            bias_two_grad,
            skip_bias_grad,
            proj_bias_grad,
            fc2_bias_grad,
        ]
    )
    row_states = [skip_rows, qkv_rows, proj_rows[None], fc1_rows[None], fc2_rows[None]]
    col_states = [skip_cols, qkv_cols, proj_cols[None], fc1_cols[None], fc2_cols[None]]
    piece_width = D // dp_count
    dp_start = dp_index * piece_width
    zero_start = jnp.zeros((), jnp.int32)
    summed = lax.psum(
        (skip_grad, qkv_grad, proj_grad, fc1_grad, fc2_grad, vector_grad, hidden_grad), "dp"
    )

    def moments_mp(row_all, col_all, squares_all):
        return lax.psum((row_all, col_all, squares_all), "mp")

    def norm_mp(step_sq):
        return lax.psum(step_sq, "mp")

    grad_pieces = [summed[0], summed[1], summed[2][None], summed[3][None], summed[4][None]]
    weight_pieces = [skip_weight, qkv_weight, proj_weight[None], fc1_weight[None], fc2_weight[None]]
    starts = [
        (mp_index * width_local, zero_start),
        (zero_start, mp_index * width_local),
        (mp_index * width_local, zero_start),
        (zero_start, mp_index * hidden_local),
        (mp_index * hidden_local, zero_start),
    ]
    results = adafactor(
        grad_pieces,
        weight_pieces,
        starts,
        row_states,
        col_states,
        summed[5],
        vectors,
        vector_moments,
        summed[6],
        hidden_bias,
        hidden_moments,
        first_mask,
        moments_mp,
        norm_mp,
    )
    (
        new_weights,
        row_news,
        col_news,
        vector_state_new,
        vectors_new,
        hidden_state_new,
        hidden_new,
        update_rms,
    ) = results
    skip_new = new_weights[0]
    qkv_new = new_weights[1]
    proj_new = new_weights[2][0]
    fc1_new = new_weights[3][0]
    fc2_new = new_weights[4][0]
    skip_grad_out = lax.dynamic_slice_in_dim(summed[0], dp_start, piece_width, 2)
    qkv_grad_out = lax.dynamic_slice_in_dim(summed[1], dp_start, piece_width, 1)
    proj_grad_out = lax.dynamic_slice_in_dim(summed[2], dp_start, piece_width, 1)
    fc1_grad_out = lax.dynamic_slice_in_dim(summed[3], dp_start, piece_width, 0)
    fc2_grad_out = lax.dynamic_slice_in_dim(summed[4], dp_start, piece_width, 1)
    vector_grad_out = lax.dynamic_slice_in_dim(summed[5], dp_start, piece_width, 1)
    hidden_grad_out = summed[6]
    return (
        block_output,
        input_grad,
        skip_input_grad,
        skip_grad_out,
        qkv_grad_out,
        proj_grad_out,
        fc1_grad_out,
        fc2_grad_out,
        vector_grad_out,
        hidden_grad_out,
        row_news[0],
        col_news[0],
        row_news[1],
        col_news[1],
        row_news[2][0],
        col_news[2][0],
        row_news[3][0],
        col_news[3][0],
        row_news[4][0],
        col_news[4][0],
        vector_state_new,
        hidden_state_new,
        skip_new,
        qkv_new,
        proj_new,
        fc1_new,
        fc2_new,
        vectors_new,
        hidden_new,
        skip_new.astype(jnp.bfloat16),
        qkv_new.astype(jnp.bfloat16),
        proj_new.astype(jnp.bfloat16),
        fc1_new.astype(jnp.bfloat16),
        fc2_new.astype(jnp.bfloat16),
        update_rms,
    )


def body(*operands):
    images = operands[2].shape[0]
    if images % lax.axis_size("mp") == 0 and lax.axis_size("dp") == 8:
        return body_data(*operands)
    return body_tensor(*operands)


def to_core(array):
    return lax.ppermute(array, "dp", [(i, i ^ 1) for i in range(8)])


def to_x(array):
    return lax.ppermute(array, "dp", [(i, i ^ 2) for i in range(8)])


def to_y(array):
    return lax.ppermute(array, "dp", [(i, i ^ 4) for i in range(8)])


def turn_mp(array, shift):
    count = lax.axis_size("mp")
    return lax.ppermute(array, "mp", [(i, (i + shift) % count) for i in range(count)])


def pick(array, index, axis):
    return lax.dynamic_index_in_dim(array, index, axis, keepdims=False)


def assemble(steps, targets, core, rows, blocks, split):
    arrays = []
    for step in steps:
        for array, _ in step:
            if not any(array is other for other in arrays):
                arrays.append(array)
    place = [
        [(next(n for n, other in enumerate(arrays) if other is array), k) for array, k in step]
        for step in steps
    ]
    table = jnp.stack([jnp.asarray(v, jnp.int32) for v in [*targets, core]])
    depth = 4
    outs = 2 if split < blocks else 1

    def kernel(table_ref, *refs):
        sources = refs[: len(arrays)]
        wholes = refs[len(arrays) : len(arrays) + outs]
        wide, narrow, in_sem, out_sem = refs[len(arrays) + outs :]
        half = rows // 2
        first = pl.multiple_of(table_ref[len(steps)] * half, half)
        second = pl.multiple_of(half - first, half)

        def fetch(step):
            slot = step % depth
            if len(place[step]) == 1:
                ((n, k),) = place[step]
                return [pltpu.make_async_copy(sources[n].at[k], wide.at[slot], in_sem.at[slot, 0])]
            copies = []
            for part, ((n, k), start) in enumerate(zip(place[step], (first, second))):
                spot = wide.at[slot, pl.ds(start, half)]
                copies.append(pltpu.make_async_copy(sources[n].at[k], spot, in_sem.at[slot, part]))
            return copies

        def leave(step, whole, spot):
            slot = step % depth
            return pltpu.make_async_copy(narrow.at[slot], whole.at[spot], out_sem.at[slot])

        for step in range(len(steps) + depth - 1):
            if step < len(steps):
                for copy in fetch(step):
                    copy.start()
            step = step - (depth - 1)
            if step < 0:
                continue
            slot = step % depth
            for copy in fetch(step):
                copy.wait()
            if step >= depth:
                leave(step - depth, wholes[0], 0).wait()
            narrow[slot] = wide[slot].astype(jnp.bfloat16)
            spot = table_ref[step]
            if outs == 1:
                leave(step, wholes[0], spot).start()
            else:

                @pl.when(spot < split)
                def _():
                    leave(step, wholes[0], spot).start()

                @pl.when(spot >= split)
                def _():
                    leave(step, wholes[1], spot - split).start()

        for step in range(max(0, len(steps) - depth), len(steps)):
            leave(step, wholes[0], 0).wait()

    shapes = [jax.ShapeDtypeStruct((split, rows, D), jnp.bfloat16)]
    if outs == 2:
        shapes.append(jax.ShapeDtypeStruct((blocks - split, rows, D), jnp.bfloat16))
    anywhere = pl.BlockSpec(memory_space=pl.ANY)
    return pl.pallas_call(
        kernel,
        in_specs=[pl.BlockSpec(memory_space=pltpu.SMEM)] + [anywhere] * len(arrays),
        out_specs=[anywhere] * outs,
        out_shape=shapes,
        scratch_shapes=[
            pltpu.VMEM((depth, rows, D), jnp.float32),
            pltpu.VMEM((depth, rows, D), jnp.bfloat16),
            pltpu.SemaphoreType.DMA((depth, 2)),
            pltpu.SemaphoreType.DMA((depth,)),
        ],
        compiler_params=pltpu.CompilerParams(vmem_limit_bytes=32 * 1024 * 1024),
        cost_estimate=pl.CostEstimate(flops=0, bytes_accessed=blocks * rows * D * 6, transcendentals=0),
    )(table, *arrays)


class Order:
    def __init__(self):
        self.token = None

    def after(self, *arrays):
        if self.token is not None:
            arrays = lax.optimization_barrier((*arrays, self.token))[:-1]
        return arrays if len(arrays) > 1 else arrays[0]

    def mark(self, *arrays):
        arrays = self.after(*arrays)
        self.token = arrays[0] if isinstance(arrays, tuple) else arrays
        return arrays


def swap_plane(order, for_x, for_y):
    for_x, for_y = order.after(for_x, for_y)
    return to_x(for_x), to_y(for_y)


def in_turn(arrays):
    count = len(arrays)
    twice = jnp.stack(list(arrays[::-1]) * 2)
    return lax.dynamic_slice_in_dim(twice, count - 1 - lax.axis_index("mp"), count, 0)


def gather_deep(array):
    return in_turn([array] + [turn_mp(array, shift) for shift in range(1, lax.axis_size("mp"))])


def sum_flat(array):
    for swap in (to_core, to_x, to_y):
        array = array + swap(array)
    return array


def bring(order, shard, quarter, core):
    count = lax.axis_size("mp")
    part = pick(pick(shard.reshape(4, 2, -1, D), quarter, 0), core, 0)
    return lax.all_gather(order.after(part), "mp")


def others(whole):
    count = lax.axis_size("mp")
    twice = jnp.concatenate([whole, whole], 0)
    return lax.dynamic_slice_in_dim(twice, lax.axis_index("mp") + 1, count - 1, 0)


def assemble_weight(shard, parts, swapped, core, shard_major, split):
    count = lax.axis_size("mp")
    rows = shard.shape[0] // 8

    def spot(shard_index, quarter):
        shard_index = lax.rem(lax.axis_index("mp") + shard_index, count)
        return shard_index * 4 + quarter if shard_major else quarter * count + shard_index

    if swapped is None:
        mine = pick(shard.reshape(4, 2, rows, D), core, 1)
    else:
        mine = shard.reshape(4, 2 * rows, D)
    steps = [((mine, n),) for n in range(4)]
    targets = [spot(0, n) for n in range(4)]
    for n, (array, quarter, first) in enumerate(parts):
        for k in range(array.shape[0]):
            steps.append(((array, k),) if swapped is None else ((array, k), (swapped[n], k)))
            targets.append(spot(first + k, quarter))
    rows = mine.shape[1]
    whole = assemble(steps, targets, core, rows, count * 4, split or count * 4)
    return [array.reshape(-1, D) for array in whole]


def cut_corner(grad, quarter):
    corner = pick(grad, quarter ^ 3, 0)
    half = corner.shape[0] // 2
    return corner[:half], corner[half:]


def cut_sides(grad, quarter, add_y, add_x):
    half = add_y.shape[0]
    for_y = pick(grad, quarter ^ 2, 0)
    for_x = pick(grad, quarter ^ 1, 0)
    for_y = jnp.concatenate([for_y[:half] + add_y, for_y[half:]], 0)
    for_x = jnp.concatenate([for_x[:half], for_x[half:] + add_x], 0)
    return for_x, for_y


def sum_deep(order, grad, quarter, from_x, from_y):
    own = pick(grad, quarter, 0) + from_x + from_y
    return lax.psum_scatter(order.after(own), "mp", scatter_dimension=0, tiled=False)


def hold(parts, quarter):
    own, from_x, from_y, corner_one, corner_two = parts
    held = jnp.zeros((4,) + own.shape, jnp.float32)
    corner = jnp.concatenate([corner_one, corner_two], 0)
    for turn, array in enumerate((own, from_x, from_y, corner)):
        held = lax.dynamic_update_slice(held, array[None], (quarter ^ turn, jnp.int32(0), jnp.int32(0)))
    return held


def interleave(held, other, core):
    low_core = jnp.where(core == 0, held, other)
    high_core = jnp.where(core == 0, other, held)
    return jnp.stack([low_core, high_core], 1).reshape(-1, D)


class Tensor:
    def __init__(self, grad, weight, row_state, col_state, axis):
        self.grad, self.weight, self.axis = grad, weight, axis
        self.row_state, self.col_state = row_state, col_state
        self.leading = grad.shape[0]
        self.rows_full = row_state.shape[1]
        self.cols_full = col_state.shape[1]
        squares = grad * grad + moment_eps
        row_sum, col_sum = jnp.sum(squares, 2), jnp.sum(squares, 1)
        start = lax.axis_index("mp") * grad.shape[axis]
        if axis == 1:
            state = lax.dynamic_slice_in_dim(row_state, start, grad.shape[1], 1)
            self.near = 0.5 * state + 0.5 * (row_sum / self.cols_full)
            self.partial = col_sum
        else:
            state = lax.dynamic_slice_in_dim(col_state, start, grad.shape[2], 1)
            self.near = 0.5 * state + 0.5 * (col_sum / self.rows_full)
            self.partial = row_sum

    def sent(self):
        return [self.near.reshape(-1), self.partial.reshape(-1)]

    def received(self, near, partial):
        near = near.reshape(near.shape[0], self.leading, -1).transpose(1, 0, 2)
        near = near.reshape(self.leading, -1)
        total = jnp.sum(partial, 0).reshape(self.leading, -1)
        if self.axis == 1:
            self.row_new = near
            self.col_new = 0.5 * self.col_state + 0.5 * (total / self.rows_full)
            row_piece, col_piece = self.near, self.col_new
        else:
            self.col_new = near
            self.row_new = 0.5 * self.row_state + 0.5 * (total / self.cols_full)
            row_piece, col_piece = self.row_new, self.near
        row_mean = jnp.mean(self.row_new, 1)
        self.row_scale = lax.rsqrt(row_piece / row_mean[:, None])
        self.col_scale = lax.rsqrt(col_piece)
        update = self.update()
        self.step_sq = jnp.sum(update * update)

    def update(self):
        return self.grad * self.row_scale[:, :, None] * self.col_scale[:, None, :]


def exchange(tensors, extra):
    pieces = [part for tensor in tensors for part in tensor.sent()]
    whole = gather_deep(jnp.concatenate(pieces + [extra]))
    offset = 0
    for tensor in tensors:
        parts = []
        for part in tensor.sent():
            parts.append(whole[:, offset : offset + part.shape[0]])
            offset = offset + part.shape[0]
        tensor.received(*parts)
    return whole[:, offset:]


def head_windows():
    spans = []
    for head in range(D // HEAD_DIM):
        first = head * HEAD_DIM
        start = first // 128 * 128
        stop = -(-(first + HEAD_DIM) // 128) * 128
        spans.append((first, start, stop - start))
    return spans


def head_mask(first, start, width):
    lanes = start + lax.broadcasted_iota(jnp.int32, (SEQ, width), 1)
    return (lanes >= first) & (lanes < first + HEAD_DIM)


def dot_nt(left_side, right_side):
    return lax.dot_general(
        left_side, right_side, (((1,), (1,)), ((), ())), preferred_element_type=jnp.float32
    )


def attend_kernel(qkv_ref, out_ref, total):
    total[...] = jnp.zeros_like(total)
    for first, start, width in head_windows():
        keep = head_mask(first, start, width)
        query = qkv_ref[0, :, start : start + width]
        key = jnp.where(keep, qkv_ref[0, :, D + start : D + start + width], 0)
        value = jnp.where(keep, qkv_ref[0, :, 2 * D + start : 2 * D + start + width], 0)
        scores = dot_nt(query, key) * HEAD_DIM ** (-0.5)
        expo = jnp.exp(scores - jnp.max(scores, 1, keepdims=True))
        probs = (expo / jnp.sum(expo, 1, keepdims=True)).astype(jnp.bfloat16)
        total[:, start : start + width] += matmul(probs, value)
    out_ref[0] = total[...].astype(jnp.bfloat16)


def attend(qkv):
    images = qkv.shape[0]
    return pl.pallas_call(
        attend_kernel,
        grid=(images,),
        in_specs=[pl.BlockSpec((1, SEQ, 3 * D), lambda i: (i, 0, 0))],
        out_specs=pl.BlockSpec((1, SEQ, D), lambda i: (i, 0, 0)),
        out_shape=jax.ShapeDtypeStruct((images, SEQ, D), jnp.bfloat16),
        scratch_shapes=[pltpu.VMEM((SEQ, D), jnp.float32)],
        compiler_params=pltpu.CompilerParams(vmem_limit_bytes=40 * 1024 * 1024),
        cost_estimate=pl.CostEstimate(
            flops=images * 4 * SEQ * SEQ * 256 * 16,
            bytes_accessed=images * SEQ * D * 8,
            transcendentals=images * 16 * SEQ * SEQ,
        ),
    )(qkv)


def attend_back_kernel(qkv_ref, grad_ref, out_ref, query_sum, key_sum, value_sum):
    scale = HEAD_DIM ** (-0.5)
    for ref in (query_sum, key_sum, value_sum):
        ref[...] = jnp.zeros_like(ref)
    for first, start, width in head_windows():
        span = slice(start, start + width)
        keep = head_mask(first, start, width)
        query = jnp.where(keep, qkv_ref[0, :, span], 0)
        key = jnp.where(keep, qkv_ref[0, :, D + start : D + start + width], 0)
        value = jnp.where(keep, qkv_ref[0, :, 2 * D + start : 2 * D + start + width], 0)
        above = jnp.where(keep, grad_ref[0, :, span], 0)
        scores = dot_nt(key, query) * scale
        expo = jnp.exp(scores - jnp.max(scores, 0, keepdims=True))
        probs = expo / jnp.sum(expo, 0, keepdims=True)
        prob_grad = dot_nt(value, above)
        inner = jnp.sum(probs * prob_grad, 0, keepdims=True)
        score_grad = (probs * (prob_grad - inner)).astype(jnp.bfloat16)
        value_sum[:, span] += matmul(probs.astype(jnp.bfloat16), above)
        key_sum[:, span] += matmul(score_grad, query) * scale
        query_sum[:, span] += (
            lax.dot_general(
                score_grad, key, (((0,), (0,)), ((), ())), preferred_element_type=jnp.float32
            )
            * scale
        )
    out_ref[0, :, :D] = query_sum[...].astype(jnp.bfloat16)
    out_ref[0, :, D : 2 * D] = key_sum[...].astype(jnp.bfloat16)
    out_ref[0, :, 2 * D :] = value_sum[...].astype(jnp.bfloat16)


def attend_back(qkv, grad):
    images = qkv.shape[0]
    return pl.pallas_call(
        attend_back_kernel,
        grid=(images,),
        in_specs=[
            pl.BlockSpec((1, SEQ, 3 * D), lambda i: (i, 0, 0)),
            pl.BlockSpec((1, SEQ, D), lambda i: (i, 0, 0)),
        ],
        out_specs=pl.BlockSpec((1, SEQ, 3 * D), lambda i: (i, 0, 0)),
        out_shape=jax.ShapeDtypeStruct((images, SEQ, 3 * D), jnp.bfloat16),
        scratch_shapes=[pltpu.VMEM((SEQ, D), jnp.float32)] * 3,
        compiler_params=pltpu.CompilerParams(vmem_limit_bytes=40 * 1024 * 1024),
        cost_estimate=pl.CostEstimate(
            flops=images * 10 * SEQ * SEQ * 256 * 16,
            bytes_accessed=images * SEQ * D * 14,
            transcendentals=images * 16 * SEQ * SEQ,
        ),
    )(qkv, grad)


def body_data(
    block_input,
    skip_input,
    timesteps,
    class_labels,
    loss_weights,
    grad_output,
    skip_weight,
    qkv_weight,
    proj_weight,
    fc1_weight,
    fc2_weight,
    vectors,
    hidden_bias,
    skip_rows,
    skip_cols,
    qkv_rows,
    qkv_cols,
    proj_rows,
    proj_cols,
    fc1_rows,
    fc1_cols,
    fc2_rows,
    fc2_cols,
    vector_moments,
    hidden_moments,
):
    image_count = timesteps.shape[0]
    mp_count = lax.axis_size("mp")
    dp_count = lax.axis_size("dp")
    mp_index = lax.axis_index("mp")
    dp_index = lax.axis_index("dp")
    core = lax.rem(dp_index, 2)
    quarter = lax.div(dp_index, 2)
    images = image_count // mp_count
    tokens = images * SEQ
    width_local = qkv_weight.shape[2]
    hidden_local = fc1_weight.shape[1]
    hidden_slice = hidden_local // dp_count
    order = Order()

    skip_shard = skip_weight.reshape(-1, D)
    skip_whole = bring(order, skip_shard, quarter, core)
    hidden_all = gather_deep(hidden_bias)

    angles = (timesteps.astype(jnp.float32) + 0.5) * (0.5 * math.pi / total_steps)
    alpha_sq = jnp.square(jnp.cos(angles))
    sigma_sq = jnp.square(jnp.sin(angles))
    snr_weight = 5.0 * sigma_sq / jnp.maximum(alpha_sq, 5.0 * sigma_sq)
    base_weight = loss_weights * snr_weight
    one_hot = (class_labels[:, None] == jnp.arange(CLASSES, dtype=jnp.int32)[None, :]).astype(
        jnp.float32
    )
    batch = jnp.concatenate([jnp.sum(one_hot, 0), jnp.sum(base_weight)[None]])

    attn_shard = jnp.concatenate(
        [qkv_weight.transpose(0, 2, 1).reshape(3 * width_local, D), proj_weight], 0
    )
    attn_shard = order.mark(attn_shard)
    attn_whole = bring(order, attn_shard, quarter, core)
    batch = order.mark(batch + to_core(batch))
    batch_x = to_x(batch)
    fc1_shard = order.mark(fc1_weight.T)
    fc2_shard = fc2_weight
    batch = order.mark(batch + batch_x)
    batch_y = to_y(batch)
    start = mp_index * tokens
    block_local = lax.dynamic_slice_in_dim(block_input, start, tokens, 0)
    skip_local = lax.dynamic_slice_in_dim(skip_input, start, tokens, 0)
    both_inputs = jnp.stack(
        [
            block_local.reshape(tokens, mp_count, width_local),
            skip_local.reshape(tokens, mp_count, width_local),
        ],
        2,
    ).reshape(tokens, -1)
    both_inputs = order.mark(both_inputs)
    batch = order.mark(batch + batch_y)

    skip_own = others(order.mark(skip_whole))
    skip_x, skip_y = swap_plane(order, skip_own, skip_own)
    skip_swapped = [to_core(skip_own)]
    fc1_whole = bring(order, fc1_shard, quarter, core)
    hidden_own = pick(hidden_all.reshape(mp_count, 4, 2, hidden_slice), core, 2)
    hidden_own = hidden_own.transpose(1, 0, 2).reshape(-1)
    own_count = jnp.dot(one_hot, batch[:CLASSES], precision=lax.Precision.HIGHEST)
    item_weight = base_weight * lax.rsqrt(own_count)
    hidden_own, item_weight = order.mark(hidden_own, item_weight)
    batch_scale = image_count * dp_count / batch[CLASSES]
    grad_local = lax.dynamic_slice_in_dim(grad_output, start, tokens, 0)
    item_local = lax.dynamic_slice_in_dim(item_weight, mp_index * images, images, 0)
    upstream = (
        grad_local.astype(jnp.float32).reshape(images, SEQ, D) * item_local[:, None, None]
    ).reshape(-1, D)
    upstream = order.mark(upstream)

    skip_x, skip_y = order.mark(skip_x, skip_y)
    skip_one, skip_two = swap_plane(order, skip_y[:2], skip_x[2:])
    skip_swapped = skip_swapped + [to_core(skip_x), to_core(skip_y)]
    skip_one, skip_two = order.mark(skip_one, skip_two)
    skip_swapped = skip_swapped + [to_core(skip_one), to_core(skip_two)]
    attn_own = others(order.mark(attn_whole))
    attn_x, attn_y = swap_plane(order, attn_own, attn_own)
    fc2_whole = bring(order, fc2_shard, quarter, core)
    skip_swapped = order.mark(*skip_swapped)
    attn_swapped = [to_core(order.after(attn_own))]
    skip_parts = [
        (skip_own, quarter, 1),
        (skip_x, quarter ^ 1, 1),
        (skip_y, quarter ^ 2, 1),
        (skip_one, quarter ^ 3, 1),
        (skip_two, quarter ^ 3, 3),
    ]
    (skip_low,) = assemble_weight(skip_shard, skip_parts, skip_swapped, core, True, 0)
    joined = matmul(both_inputs, skip_low) + vectors[4]
    normed, normal_one, inverse_one = norm_forward(joined, vectors[0], vectors[1])
    normed_low = normed.astype(jnp.bfloat16)
    joined, normed_low, normal_one = order.mark(joined, normed_low, normal_one)
    upstream_other = to_core(order.after(upstream))

    attn_x, attn_y = order.mark(attn_x, attn_y)
    attn_one, attn_two = swap_plane(order, attn_y[:1], attn_x[1:])
    attn_swapped = attn_swapped + [to_core(attn_x), to_core(attn_y)]
    upstream_other = order.mark(upstream_other) * batch_scale
    upstream = upstream * batch_scale
    upstream_low = jnp.concatenate([upstream, upstream_other], 0).astype(jnp.bfloat16)
    upstream_low = order.mark(upstream_low)
    fc1_own = others(order.mark(fc1_whole))
    fc1_x, fc1_y = swap_plane(order, fc1_own, fc1_own)
    attn_one, attn_two = order.mark(attn_one, attn_two)
    attn_swapped = attn_swapped + [to_core(attn_one), to_core(attn_two)]
    attn_parts = [
        (attn_own, quarter, 1),
        (attn_x, quarter ^ 1, 1),
        (attn_y, quarter ^ 2, 1),
        (attn_one, quarter ^ 3, 1),
        (attn_two, quarter ^ 3, 2),
    ]
    attn_swapped = order.mark(*attn_swapped)
    qkv_low, proj_low = assemble_weight(
        attn_shard, attn_parts, attn_swapped, core, False, 3 * mp_count
    )
    qkv_all = jnp.einsum(
        "itd,ed->ite",
        normed_low.reshape(images, SEQ, D),
        qkv_low,
        preferred_element_type=jnp.float32,
    ).astype(jnp.bfloat16)
    qkv_all = order.mark(qkv_all)
    fc2_own = others(order.mark(fc2_whole))
    fc1_x, fc1_y = order.mark(fc1_x, fc1_y)
    fc1_one, fc1_two = swap_plane(order, fc1_y[:2], fc1_x[2:])
    fc2_x, fc2_y = swap_plane(order, fc2_own, fc2_own)
    attended = attend(order.after(qkv_all)).reshape(tokens, D)
    residual = joined + matmul(attended, proj_low) + vectors[5]
    normed_two, normal_two, inverse_two = norm_forward(residual, vectors[2], vectors[3])
    residual, normed_two, normal_two = order.mark(residual, normed_two, normal_two)
    normed_two_other = to_core(normal_two)
    fc1_one, fc1_two = order.mark(fc1_one, fc1_two)
    fc1_parts = [
        (fc1_own, quarter, 1),
        (fc1_x, quarter ^ 1, 1),
        (fc1_y, quarter ^ 2, 1),
        (fc1_one, quarter ^ 3, 1),
        (fc1_two, quarter ^ 3, 3),
    ]
    (fc1_low,) = assemble_weight(fc1_shard, fc1_parts, None, core, False, 0)
    fc1_low = order.mark(fc1_low)
    normed_two_other = order.mark(normed_two_other) * vectors[2] + vectors[3]
    normed_two_low = jnp.concatenate([normed_two, normed_two_other], 0).astype(jnp.bfloat16)
    normed_two_low = order.mark(normed_two_low)
    fc2_x, fc2_y = order.mark(fc2_x, fc2_y)
    fc2_one, fc2_two = swap_plane(order, fc2_y[:1], fc2_x[1:])
    pre_act = (
        jnp.einsum("td,fd->tf", normed_two_low, fc1_low, preferred_element_type=jnp.float32)
        + hidden_own
    )
    activated, gelu_pull = jax.vjp(gelu_exact, pre_act)
    activated_low = activated.astype(jnp.bfloat16)
    fc2_grad = jnp.einsum(
        "tf,td->fd", activated_low, upstream_low, preferred_element_type=jnp.float32
    ).reshape(4, mp_count, hidden_slice, D)
    fc2_grad = order.mark(fc2_grad)
    fc2_add = swap_plane(order, *cut_corner(fc2_grad, quarter))

    fc2_one, fc2_two = order.mark(fc2_one, fc2_two)
    fc2_parts = [
        (fc2_own, quarter, 1),
        (fc2_x, quarter ^ 1, 1),
        (fc2_y, quarter ^ 2, 1),
        (fc2_one, quarter ^ 3, 1),
        (fc2_two, quarter ^ 3, 2),
    ]
    (fc2_low,) = assemble_weight(fc2_shard, fc2_parts, None, core, False, 0)
    fc2_low = order.mark(fc2_low)
    act_grad = jnp.einsum("td,fd->tf", upstream_low, fc2_low, preferred_element_type=jnp.float32)
    pre_grad = gelu_pull(act_grad)[0]
    hidden_grad = jnp.sum(pre_grad, 0)
    pre_low, hidden_grad = order.mark(pre_grad.astype(jnp.bfloat16), hidden_grad)
    back_part = order.mark(matmul(pre_low, fc1_low))
    back_other = to_core(back_part[tokens:])
    fc2_add = order.mark(*fc2_add)
    fc2_sides = swap_plane(order, *cut_sides(fc2_grad, quarter, *fc2_add))
    fc1_grad = jnp.einsum(
        "tf,td->fd",
        order.after(pre_low),
        normed_two_low,
        preferred_element_type=jnp.float32,
    ).reshape(4, mp_count, hidden_slice, D)
    fc1_grad = order.mark(fc1_grad)
    fc1_add = swap_plane(order, *cut_corner(fc1_grad, quarter))
    norm_two_in = back_part[:tokens] + order.mark(back_other)
    back_two, gain_two_grad, bias_two_grad = norm_backward(
        norm_two_in, normal_two, inverse_two, vectors[2]
    )
    residual_grad = upstream + back_two
    residual_low = residual_grad.astype(jnp.bfloat16)
    residual_grad, residual_low = order.mark(residual_grad, residual_low)
    forward_part = order.mark(matmul(order.after(activated_low), fc2_low))
    forward_other = to_core(forward_part[tokens:])
    attended_grad = jnp.einsum(
        "td,ed->te", residual_low, proj_low, preferred_element_type=jnp.float32
    ).astype(jnp.bfloat16)
    attended_grad = order.mark(attended_grad)
    block_own = residual + forward_part[:tokens] + order.mark(forward_other)
    block_all = lax.all_gather(order.mark(block_own), "mp")
    qkv_grad_low = attend_back(
        qkv_all, order.after(attended_grad).reshape(images, SEQ, D)
    ).reshape(tokens, 3 * D)
    qkv_grad_low = order.mark(qkv_grad_low)
    fc1_add = order.mark(*fc1_add)
    fc1_sides = swap_plane(order, *cut_sides(fc1_grad, quarter, *fc1_add))
    fc2_sides = order.mark(*fc2_sides)
    fc2_piece = sum_deep(order, fc2_grad, quarter, *fc2_sides)

    def by_core(array, leading):
        return array.reshape(tokens, leading, mp_count, 2, -1)

    def attn_half(which):
        left = pick(by_core(qkv_grad_low, 3), which, 3).reshape(tokens, -1)
        first = jnp.einsum("te,td->ed", left, normed_low, preferred_element_type=jnp.float32)
        left = pick(by_core(attended, 1), which, 3).reshape(tokens, -1)
        second = jnp.einsum("te,td->ed", left, residual_low, preferred_element_type=jnp.float32)
        return first, second

    attn_given = order.mark(*attn_half(1 - core))
    attn_given = [to_core(array) for array in attn_given]
    norm_one_in = matmul(order.after(qkv_grad_low), qkv_low)
    back_one, gain_one_grad, bias_one_grad = norm_backward(
        norm_one_in, normal_one, inverse_one, vectors[0]
    )
    joined_grad = residual_grad + back_one
    joined_low = joined_grad.astype(jnp.bfloat16)
    joined_grad, joined_low = order.mark(joined_grad, joined_low)
    attn_kept = order.mark(*attn_half(core))

    inputs_view = both_inputs.reshape(tokens, mp_count, 4, 2, -1).transpose(0, 2, 1, 3, 4)

    def skip_half(which):
        left = pick(inputs_view, which, 3).reshape(tokens, -1)
        return jnp.einsum("te,td->ed", left, joined_low, preferred_element_type=jnp.float32)

    skip_given = order.mark(skip_half(1 - core))
    skip_given = to_core(skip_given)
    attn_given = order.mark(*attn_given)
    attn_grad = jnp.concatenate(
        [kept + given for kept, given in zip(attn_kept, attn_given)], 0
    ).reshape(4, mp_count, hidden_slice, D)
    attn_grad = order.mark(attn_grad)
    attn_add = swap_plane(order, *cut_corner(attn_grad, quarter))
    skip_shards = skip_low.reshape(mp_count, 2 * width_local, D)
    both_grads = []
    for shift in (1, 2, 3, 0):
        shard_low = pick(skip_shards, lax.rem(mp_index + shift, mp_count), 0)
        both = jnp.einsum("td,cd->tc", joined_low, shard_low, preferred_element_type=jnp.float32)
        both = order.mark(both)
        both_grads.append(turn_mp(both, shift) if shift == 1 else both)
    skip_kept = order.mark(skip_half(core))
    skip_grad = order.mark((skip_kept + order.mark(skip_given)).reshape(4, mp_count, -1, D))

    fc1_sides = order.mark(*fc1_sides)
    fc1_piece = sum_deep(order, fc1_grad, quarter, *fc1_sides)
    attn_add = order.mark(*attn_add)
    attn_sides = swap_plane(order, *cut_sides(attn_grad, quarter, *attn_add))
    skip_add = swap_plane(order, *cut_corner(skip_grad, quarter))
    both_grads[0] = order.mark(both_grads[0])
    both_grads[1] = turn_mp(order.after(both_grads[1]), 2)
    vector_grad = jnp.stack(
        [
            gain_one_grad,
            bias_one_grad,
            gain_two_grad,
            bias_two_grad,
            jnp.sum(joined_grad, 0),
            jnp.sum(residual_grad, 0),
            jnp.sum(upstream, 0),
        ]
    )
    hidden_grad = hidden_grad.reshape(4, mp_count, 1, hidden_slice).transpose(1, 0, 2, 3)
    hidden_grad = jnp.where(jnp.arange(2)[None, None, :, None] == core, hidden_grad, 0.0)
    small = order.mark(jnp.concatenate([vector_grad.reshape(-1), hidden_grad.reshape(-1)]))
    skip_add = order.mark(*skip_add)
    skip_sides = swap_plane(order, *cut_sides(skip_grad, quarter, *skip_add))
    attn_sides = order.mark(*attn_sides)
    attn_piece = sum_deep(order, attn_grad, quarter, *attn_sides)
    small = order.mark(small + to_core(small))
    both_grads[1] = order.mark(both_grads[1])
    both_grads[2] = turn_mp(order.after(both_grads[2]), 3)
    block_all = order.mark(block_all)
    block_output = (block_all.reshape(-1, D) + vectors[6]).astype(jnp.bfloat16)
    block_output = order.mark(block_output)
    half = hidden_slice // 2

    def spread(piece):
        return swap_plane(order, piece, piece)

    def spread_far(near):
        half = near[0].shape[0] // 2
        return swap_plane(order, near[1][:half], near[0][half:])

    fc2_piece = order.mark(fc2_piece)
    fc2_near = spread(fc2_piece)
    small_x = to_x(order.after(small))
    skip_sides = order.mark(*skip_sides)
    skip_piece = sum_deep(order, skip_grad, quarter, *skip_sides)
    fc2_near = order.mark(*fc2_near)
    fc2_far = spread_far(fc2_near)
    small = order.mark(small + small_x)
    small_y = to_y(small)
    fc1_piece = order.mark(fc1_piece)
    fc1_near = spread(fc1_piece)
    fc2_far = order.mark(*fc2_far)
    fc2_held = order.mark(hold((fc2_piece, *fc2_near, *fc2_far), quarter))
    fc2_other = to_core(fc2_held)
    small = order.mark(small + small_y)
    small = order.mark(jnp.sum(gather_deep(small), 0))
    fc1_near = order.mark(*fc1_near)
    fc1_far = spread_far(fc1_near)
    both_grads[2] = order.mark(both_grads[2])
    input_grads = in_turn([both_grads[3]] + both_grads[:3])
    input_grad = input_grads[:, :, :width_local].reshape(-1, width_local)
    skip_input_grad = input_grads[:, :, width_local:].reshape(-1, width_local)
    input_grad, skip_input_grad = order.mark(input_grad, skip_input_grad)
    fc2_sum = interleave(fc2_held, order.mark(fc2_other), core)
    fc2_part = Tensor(fc2_sum[None], fc2_weight[None], fc2_rows[None], fc2_cols[None], 1)
    fc1_far = order.mark(*fc1_far)
    fc1_held = order.mark(hold((fc1_piece, *fc1_near, *fc1_far), quarter))
    fc1_other = to_core(fc1_held)
    attn_piece = order.mark(attn_piece)
    attn_near = spread(attn_piece)
    fc1_sum = interleave(fc1_held, order.mark(fc1_other), core).T
    fc1_part = Tensor(fc1_sum[None], fc1_weight[None], fc1_rows[None], fc1_cols[None], 2)
    weight_sq = jnp.stack(
        [
            jnp.sum(array * array)
            for array in (skip_weight, qkv_weight, proj_weight, fc1_weight, fc2_weight, hidden_bias)
        ]
    )
    weight_sq = order.mark(weight_sq)
    weight_sq = jnp.sum(exchange([fc2_part, fc1_part], weight_sq), 0)
    fc2_part.step_sq, fc1_part.step_sq = order.mark(fc2_part.step_sq, fc1_part.step_sq)
    attn_near = order.mark(*attn_near)
    attn_far = spread_far(attn_near)
    skip_piece = order.mark(skip_piece)
    skip_near = spread(skip_piece)
    attn_far = order.mark(*attn_far)
    attn_held = order.mark(hold((attn_piece, *attn_near, *attn_far), quarter))
    attn_other = to_core(attn_held)
    skip_near = order.mark(*skip_near)
    skip_far = spread_far(skip_near)
    attn_sum = interleave(attn_held, order.mark(attn_other), core)
    qkv_sum = attn_sum[: 3 * width_local].reshape(3, width_local, D).transpose(0, 2, 1)
    proj_sum = attn_sum[3 * width_local :]
    qkv_sum, proj_sum = order.mark(qkv_sum, proj_sum)
    skip_far = order.mark(*skip_far)
    skip_held = order.mark(hold((skip_piece, *skip_near, *skip_far), quarter))
    skip_other = to_core(skip_held)
    qkv_part = Tensor(qkv_sum, qkv_weight, qkv_rows, qkv_cols, 2)
    proj_part = Tensor(proj_sum[None], proj_weight[None], proj_rows[None], proj_cols[None], 1)
    skip_sum = interleave(skip_held, order.mark(skip_other), core).reshape(2, width_local, D)
    skip_part = Tensor(skip_sum, skip_weight, skip_rows, skip_cols, 1)
    exchange([qkv_part, proj_part, skip_part], jnp.zeros((128,), jnp.float32))

    vector_sum = small[: 7 * D].reshape(7, D)
    hidden_sum = lax.dynamic_slice_in_dim(small[7 * D :], mp_index * hidden_local, hidden_local, 0)
    vector_new = 0.5 * vector_moments + 0.5 * (vector_sum * vector_sum + moment_eps)
    vector_update = vector_sum * lax.rsqrt(vector_new)
    hidden_new = 0.5 * hidden_moments + 0.5 * (hidden_sum * hidden_sum + moment_eps)
    hidden_update = hidden_sum * lax.rsqrt(hidden_new)
    parts = [skip_part, qkv_part, proj_part, fc1_part, fc2_part]
    step_sq = jnp.sum(hidden_update * hidden_update)
    for part in parts:
        step_sq = step_sq + part.step_sq
    step_total = jnp.sum(gather_deep(jnp.broadcast_to(step_sq, (128,)))[:, 0])
    step_total = step_total + jnp.sum(vector_update * vector_update)
    param_count = 6.0 * D * D + 2.0 * D * FF + 7.0 * D + FF
    update_rms = jnp.sqrt(step_total / param_count)
    divisor = jnp.maximum(1.0, update_rms / clip_level)
    tensor_sizes = (2.0 * D * D, 3.0 * D * D, 1.0 * D * D, 1.0 * D * FF, 1.0 * FF * D)
    new_weights = []
    for position, part in enumerate(parts):
        weight_rms = jnp.sqrt(weight_sq[position] / tensor_sizes[position])
        factor = step_rate * jnp.maximum(0.001, weight_rms) / divisor
        new_weights.append(part.weight - factor * part.update())
    vector_rms = jnp.sqrt(jnp.mean(vectors * vectors, 1, keepdims=True))
    vectors_new = vectors - step_rate * jnp.maximum(0.001, vector_rms) * vector_update / divisor
    hidden_rms = jnp.sqrt(weight_sq[5] / FF)
    hidden_bias_new = (
        hidden_bias - step_rate * jnp.maximum(0.001, hidden_rms) * hidden_update / divisor
    )
    skip_new, qkv_new = new_weights[0], new_weights[1]
    proj_new, fc1_new, fc2_new = (array[0] for array in new_weights[2:])
    piece_width = D // dp_count
    dp_start = dp_index * piece_width

    def own_piece(array, axis):
        return lax.dynamic_slice_in_dim(array, dp_start, piece_width, axis)

    return (
        block_output,
        input_grad,
        skip_input_grad,
        own_piece(skip_sum, 2),
        own_piece(qkv_sum, 1),
        own_piece(proj_sum, 1),
        own_piece(fc1_sum, 0),
        own_piece(fc2_sum, 1),
        own_piece(vector_sum, 1),
        hidden_sum,
        skip_part.row_new,
        skip_part.col_new,
        qkv_part.row_new,
        qkv_part.col_new,
        proj_part.row_new[0],
        proj_part.col_new[0],
        fc1_part.row_new[0],
        fc1_part.col_new[0],
        fc2_part.row_new[0],
        fc2_part.col_new[0],
        vector_new,
        hidden_new,
        skip_new,
        qkv_new,
        proj_new,
        fc1_new,
        fc2_new,
        vectors_new,
        hidden_bias_new,
        skip_new.astype(jnp.bfloat16),
        qkv_new.astype(jnp.bfloat16),
        proj_new.astype(jnp.bfloat16),
        fc1_new.astype(jnp.bfloat16),
        fc2_new.astype(jnp.bfloat16),
        update_rms,
    )


def solution(mesh):
    placed = (
        P("dp", None),
        P("dp", None),
        P("dp"),
        P("dp"),
        P("dp"),
        P("dp", None),
        P(None, "mp", None),
        P(None, None, "mp"),
        P("mp", None),
        P(None, "mp"),
        P("mp", None),
        P(),
        P("mp"),
        P(),
        P(),
        P(),
        P(),
        P(),
        P(),
        P(),
        P(),
        P(),
        P(),
        P(),
        P("mp"),
    )
    return jax.shard_map(
        body,
        mesh=mesh,
        in_specs=placed,
        out_specs=(
            P("dp", None),
            P("dp", "mp"),
            P("dp", "mp"),
            P(None, "mp", "dp"),
            P(None, "dp", "mp"),
            P("mp", "dp"),
            P("dp", "mp"),
            P("mp", "dp"),
            P(None, "dp"),
            P("mp"),
            P(),
            P(),
            P(),
            P(),
            P(),
            P(),
            P(),
            P(),
            P(),
            P(),
            P(),
            P("mp"),
            P(None, "mp", None),
            P(None, None, "mp"),
            P("mp", None),
            P(None, "mp"),
            P("mp", None),
            P(),
            P("mp"),
            P(None, "mp", None),
            P(None, None, "mp"),
            P("mp", None),
            P(None, "mp"),
            P("mp", None),
            P(),
        ),
        check_vma=False,
    )
```

```python
import functools
import math

import jax
import jax.numpy as jnp
from jax import lax
from jax.experimental import pallas as pl
from jax.experimental.pallas import tpu as pltpu
from jax.sharding import PartitionSpec as P

D = 1152
HEAD_DIM = 72
FF = 4608
CLASSES = 1000
SEQ = 258


ln_eps = 1e-05
moment_eps = 1e-30
clip_level = 0.25
step_rate = 2.0
total_steps = 1000.0


def gelu_exact(inputs):
    return 0.5 * inputs * (1.0 + lax.erf(inputs * (1.0 / math.sqrt(2.0))))


def matmul(left_side, right_side):
    return jnp.dot(left_side, right_side, preferred_element_type=jnp.float32)


def norm_forward(inputs, norm_gain, norm_bias):
    centre = jnp.mean(inputs, -1, keepdims=True)
    centred = inputs - centre
    inverse = lax.rsqrt(jnp.mean(centred * centred, -1, keepdims=True) + ln_eps)
    normal = centred * inverse
    return (normal * norm_gain + norm_bias, normal, inverse)


def norm_backward(incoming, normal, inverse, norm_gain):
    scaled = incoming * norm_gain
    inner_mean = jnp.mean(scaled, -1, keepdims=True)
    proj_mean = jnp.mean(scaled * normal, -1, keepdims=True)
    return (
        inverse * (scaled - inner_mean - normal * proj_mean),
        jnp.sum(incoming * normal, 0),
        jnp.sum(incoming, 0),
    )


def adafactor(
    grad_pieces,
    weight_pieces,
    starts,
    row_states,
    col_states,
    vector_piece,
    vector_weight,
    vector_state,
    hidden_piece,
    hidden_weight,
    hidden_state,
    first_mask,
    reduce_moments,
    reduce_norm,
):
    full_shapes = ((D, D), (D, D), (D, D), (D, FF), (FF, D))
    tensor_sizes = (2.0 * D * D, 3.0 * D * D, 1.0 * D * D, 1.0 * D * FF, 1.0 * FF * D)
    zero_start = jnp.zeros((), jnp.int32)
    row_parts = []
    col_parts = []
    weight_sq = []
    for position in range(5):
        grad_piece = grad_pieces[position]
        leading = grad_piece.shape[0]
        squares = grad_piece * grad_piece + moment_eps
        row_zero = jnp.zeros((leading, full_shapes[position][0]), jnp.float32)
        col_zero = jnp.zeros((leading, full_shapes[position][1]), jnp.float32)
        row_parts.append(
            lax.dynamic_update_slice(
                row_zero, jnp.sum(squares, 2), (zero_start, starts[position][0])
            ).reshape(-1)
        )
        col_parts.append(
            lax.dynamic_update_slice(
                col_zero, jnp.sum(squares, 1), (zero_start, starts[position][1])
            ).reshape(-1)
        )
        weight_sq.append(jnp.sum(weight_pieces[position] * weight_pieces[position])[None])
    weight_sq.append(jnp.sum(vector_weight * vector_weight, 1) * first_mask)
    weight_sq.append(jnp.sum(hidden_weight * hidden_weight)[None])
    row_total, col_total, weight_total = reduce_moments(
        jnp.concatenate(row_parts), jnp.concatenate(col_parts), jnp.concatenate(weight_sq)
    )
    row_news = []
    col_news = []
    updates = []
    step_sq = jnp.zeros((), jnp.float32)
    row_offset = 0
    col_offset = 0
    for position in range(5):
        grad_piece = grad_pieces[position]
        leading = grad_piece.shape[0]
        rows_full, cols_full = full_shapes[position]
        row_sum = row_total[row_offset : row_offset + leading * rows_full].reshape(
            leading, rows_full
        )
        col_sum = col_total[col_offset : col_offset + leading * cols_full].reshape(
            leading, cols_full
        )
        row_offset = row_offset + leading * rows_full
        col_offset = col_offset + leading * cols_full
        row_new = 0.5 * row_states[position] + 0.5 * (row_sum / cols_full)
        col_new = 0.5 * col_states[position] + 0.5 * (col_sum / rows_full)
        row_piece = lax.dynamic_slice(
            row_new, (zero_start, starts[position][0]), (leading, grad_piece.shape[1])
        )
        col_piece = lax.dynamic_slice(
            col_new, (zero_start, starts[position][1]), (leading, grad_piece.shape[2])
        )
        row_mean = jnp.mean(row_new, 1)
        update = grad_piece * lax.rsqrt(
            row_piece[:, :, None] * col_piece[:, None, :] / row_mean[:, None, None]
        )
        step_sq = step_sq + jnp.sum(update * update)
        row_news.append(row_new)
        col_news.append(col_new)
        updates.append(update)
    vector_new = 0.5 * vector_state + 0.5 * (vector_piece * vector_piece + moment_eps)
    vector_update = vector_piece * lax.rsqrt(vector_new)
    hidden_new = 0.5 * hidden_state + 0.5 * (hidden_piece * hidden_piece + moment_eps)
    hidden_update = hidden_piece * lax.rsqrt(hidden_new)
    step_sq = (
        step_sq
        + jnp.sum(vector_update * vector_update) * first_mask
        + jnp.sum(hidden_update * hidden_update)
    )
    step_total = reduce_norm(step_sq)
    param_count = 6.0 * D * D + 2.0 * D * FF + 7.0 * D + FF
    update_rms = jnp.sqrt(step_total / param_count)
    divisor = jnp.maximum(1.0, update_rms / clip_level)
    new_weights = []
    for position in range(5):
        weight_rms = jnp.sqrt(weight_total[position] / tensor_sizes[position])
        new_weights.append(
            weight_pieces[position]
            - step_rate * jnp.maximum(0.001, weight_rms) * updates[position] / divisor
        )
    vector_rms = jnp.sqrt(weight_total[5:12] / D)[:, None]
    vector_weight_new = (
        vector_weight - step_rate * jnp.maximum(0.001, vector_rms) * vector_update / divisor
    )
    hidden_rms = jnp.sqrt(weight_total[12] / FF)
    hidden_weight_new = (
        hidden_weight - step_rate * jnp.maximum(0.001, hidden_rms) * hidden_update / divisor
    )
    return (
        new_weights,
        row_news,
        col_news,
        vector_new,
        vector_weight_new,
        hidden_new,
        hidden_weight_new,
        update_rms,
    )


def body_tensor(
    block_input,
    skip_input,
    timesteps,
    class_labels,
    loss_weights,
    grad_output,
    skip_weight,
    qkv_weight,
    proj_weight,
    fc1_weight,
    fc2_weight,
    vectors,
    hidden_bias,
    skip_rows,
    skip_cols,
    qkv_rows,
    qkv_cols,
    proj_rows,
    proj_cols,
    fc1_rows,
    fc1_cols,
    fc2_rows,
    fc2_cols,
    vector_moments,
    hidden_moments,
):
    image_count = timesteps.shape[0]
    width_local = qkv_weight.shape[2]
    heads_local = width_local // HEAD_DIM
    hidden_local = fc1_weight.shape[1]
    mp_index = lax.axis_index("mp")
    dp_index = lax.axis_index("dp")
    dp_count = lax.axis_size("dp")
    first_mask = (mp_index == 0).astype(jnp.float32)
    feature_start = mp_index * skip_weight.shape[1]
    block_local = lax.dynamic_slice_in_dim(block_input, feature_start, skip_weight.shape[1], 1)
    skip_local = lax.dynamic_slice_in_dim(skip_input, feature_start, skip_weight.shape[1], 1)
    angles = (timesteps.astype(jnp.float32) + 0.5) * (0.5 * math.pi / total_steps)
    alpha_sq = jnp.square(jnp.cos(angles))
    sigma_sq = jnp.square(jnp.sin(angles))
    snr_weight = 5.0 * sigma_sq / jnp.maximum(alpha_sq, 5.0 * sigma_sq)
    base_weight = loss_weights * snr_weight
    one_hot = (class_labels[:, None] == jnp.arange(CLASSES, dtype=jnp.int32)[None, :]).astype(
        jnp.float32
    )
    class_counts, weight_total = lax.psum((jnp.sum(one_hot, 0), jnp.sum(base_weight)), "dp")
    own_count = jnp.dot(one_hot, class_counts, precision=lax.Precision.HIGHEST)
    item_weight = base_weight * (image_count * dp_count / weight_total) * lax.rsqrt(own_count)
    upstream = (
        grad_output.astype(jnp.float32).reshape(image_count, SEQ, D) * item_weight[:, None, None]
    ).reshape(-1, D)
    skip_low = skip_weight.astype(jnp.bfloat16)
    qkv_low = qkv_weight.astype(jnp.bfloat16)
    proj_low = proj_weight.astype(jnp.bfloat16)
    fc1_low = fc1_weight.astype(jnp.bfloat16)
    fc2_low = fc2_weight.astype(jnp.bfloat16)
    joined = (
        lax.psum(matmul(block_local, skip_low[0]) + matmul(skip_local, skip_low[1]), "mp")
        + vectors[4]
    )
    normed, normal_one, inverse_one = norm_forward(joined, vectors[0], vectors[1])
    normed_low = normed.astype(jnp.bfloat16)
    qkv_all = jnp.einsum(
        "td,sde->ste", normed_low, qkv_low, preferred_element_type=jnp.float32
    ).astype(jnp.bfloat16)
    heads_view = qkv_all.reshape(3, image_count, SEQ, heads_local, HEAD_DIM)
    query_low = heads_view[0]
    key_low = heads_view[1]
    value_low = heads_view[2]
    score_scale = HEAD_DIM ** (-0.5)

    def score_block():
        return (
            jnp.einsum("iqhe,ikhe->ihqk", query_low, key_low, preferred_element_type=jnp.float32)
            * score_scale
        )

    scores = score_block()
    score_top = jnp.max(scores, -1, keepdims=True)
    expo_scores = jnp.exp(scores - score_top)
    expo_total = jnp.sum(expo_scores, -1, keepdims=True)
    weights_low = (expo_scores / expo_total).astype(jnp.bfloat16)
    log_total = score_top + jnp.log(expo_total)
    attended = (
        jnp.einsum("ihqk,ikhe->iqhe", weights_low, value_low, preferred_element_type=jnp.float32)
        .astype(jnp.bfloat16)
        .reshape(-1, width_local)
    )
    residual = joined + lax.psum(matmul(attended, proj_low), "mp") + vectors[5]
    normed_two, normal_two, inverse_two = norm_forward(residual, vectors[2], vectors[3])
    normed_two_low = normed_two.astype(jnp.bfloat16)
    pre_act = matmul(normed_two_low, fc1_low) + hidden_bias
    activated, gelu_pull = jax.vjp(gelu_exact, pre_act)
    activated_low = activated.astype(jnp.bfloat16)
    block_output = (residual + lax.psum(matmul(activated_low, fc2_low), "mp") + vectors[6]).astype(
        jnp.bfloat16
    )
    upstream_low = upstream.astype(jnp.bfloat16)
    fc2_grad = jnp.einsum(
        "tf,td->fd", activated_low, upstream_low, preferred_element_type=jnp.float32
    )
    fc2_bias_grad = jnp.sum(upstream, 0)
    act_grad = jnp.einsum("td,fd->tf", upstream_low, fc2_low, preferred_element_type=jnp.float32)
    pre_grad = gelu_pull(act_grad)[0]
    pre_low = pre_grad.astype(jnp.bfloat16)
    fc1_grad = jnp.einsum("td,tf->df", normed_two_low, pre_low, preferred_element_type=jnp.float32)
    hidden_grad = jnp.sum(pre_grad, 0)
    norm_two_in = lax.psum(
        jnp.einsum("tf,df->td", pre_low, fc1_low, preferred_element_type=jnp.float32), "mp"
    )
    back_two, gain_two_grad, bias_two_grad = norm_backward(
        norm_two_in, normal_two, inverse_two, vectors[2]
    )
    residual_grad = upstream + back_two
    proj_bias_grad = jnp.sum(residual_grad, 0)
    residual_low = residual_grad.astype(jnp.bfloat16)
    proj_grad = jnp.einsum("te,td->ed", attended, residual_low, preferred_element_type=jnp.float32)
    attended_grad = jnp.einsum(
        "td,ed->te", residual_low, proj_low, preferred_element_type=jnp.float32
    ).astype(jnp.bfloat16)
    attended_grad = attended_grad.reshape(image_count, SEQ, heads_local, HEAD_DIM)
    scores = score_block()
    probs_exact = jnp.exp(scores - log_total)
    prob_grad = jnp.einsum(
        "iqhe,ikhe->ihqk", attended_grad, value_low, preferred_element_type=jnp.float32
    )
    score_grad = (
        probs_exact * (prob_grad - jnp.sum(probs_exact * prob_grad, -1, keepdims=True))
    ).astype(jnp.bfloat16)
    query_grad = (
        jnp.einsum("ihqk,ikhe->iqhe", score_grad, key_low, preferred_element_type=jnp.float32)
        * score_scale
    )
    key_grad = (
        jnp.einsum("ihqk,iqhe->ikhe", score_grad, query_low, preferred_element_type=jnp.float32)
        * score_scale
    )
    value_grad = jnp.einsum(
        "ihqk,iqhe->ikhe", weights_low, attended_grad, preferred_element_type=jnp.float32
    )
    qkv_grad_low = (
        jnp.stack([query_grad, key_grad, value_grad])
        .astype(jnp.bfloat16)
        .reshape(3, -1, width_local)
    )
    qkv_grad = jnp.einsum(
        "td,ste->sde", normed_low, qkv_grad_low, preferred_element_type=jnp.float32
    )
    norm_one_in = lax.psum(
        jnp.einsum("ste,sde->td", qkv_grad_low, qkv_low, preferred_element_type=jnp.float32), "mp"
    )
    back_one, gain_one_grad, bias_one_grad = norm_backward(
        norm_one_in, normal_one, inverse_one, vectors[0]
    )
    joined_grad = residual_grad + back_one
    skip_bias_grad = jnp.sum(joined_grad, 0)
    joined_low = joined_grad.astype(jnp.bfloat16)
    skip_grad = jnp.stack(
        [
            jnp.einsum("tc,td->cd", block_local, joined_low, preferred_element_type=jnp.float32),
            jnp.einsum("tc,td->cd", skip_local, joined_low, preferred_element_type=jnp.float32),
        ]
    )
    input_grad = jnp.einsum(
        "td,cd->tc", joined_low, skip_low[0], preferred_element_type=jnp.float32
    )
    skip_input_grad = jnp.einsum(
        "td,cd->tc", joined_low, skip_low[1], preferred_element_type=jnp.float32
    )
    vector_grad = jnp.stack(
        [
            gain_one_grad,
            bias_one_grad,
            gain_two_grad,
            bias_two_grad,
            skip_bias_grad,
            proj_bias_grad,
            fc2_bias_grad,
        ]
    )
    row_states = [skip_rows, qkv_rows, proj_rows[None], fc1_rows[None], fc2_rows[None]]
    col_states = [skip_cols, qkv_cols, proj_cols[None], fc1_cols[None], fc2_cols[None]]
    piece_width = D // dp_count
    dp_start = dp_index * piece_width
    zero_start = jnp.zeros((), jnp.int32)
    summed = lax.psum(
        (skip_grad, qkv_grad, proj_grad, fc1_grad, fc2_grad, vector_grad, hidden_grad), "dp"
    )

    def moments_mp(row_all, col_all, squares_all):
        return lax.psum((row_all, col_all, squares_all), "mp")

    def norm_mp(step_sq):
        return lax.psum(step_sq, "mp")

    grad_pieces = [summed[0], summed[1], summed[2][None], summed[3][None], summed[4][None]]
    weight_pieces = [skip_weight, qkv_weight, proj_weight[None], fc1_weight[None], fc2_weight[None]]
    starts = [
        (mp_index * width_local, zero_start),
        (zero_start, mp_index * width_local),
        (mp_index * width_local, zero_start),
        (zero_start, mp_index * hidden_local),
        (mp_index * hidden_local, zero_start),
    ]
    results = adafactor(
        grad_pieces,
        weight_pieces,
        starts,
        row_states,
        col_states,
        summed[5],
        vectors,
        vector_moments,
        summed[6],
        hidden_bias,
        hidden_moments,
        first_mask,
        moments_mp,
        norm_mp,
    )
    (
        new_weights,
        row_news,
        col_news,
        vector_state_new,
        vectors_new,
        hidden_state_new,
        hidden_new,
        update_rms,
    ) = results
    skip_new = new_weights[0]
    qkv_new = new_weights[1]
    proj_new = new_weights[2][0]
    fc1_new = new_weights[3][0]
    fc2_new = new_weights[4][0]
    skip_grad_out = lax.dynamic_slice_in_dim(summed[0], dp_start, piece_width, 2)
    qkv_grad_out = lax.dynamic_slice_in_dim(summed[1], dp_start, piece_width, 1)
    proj_grad_out = lax.dynamic_slice_in_dim(summed[2], dp_start, piece_width, 1)
    fc1_grad_out = lax.dynamic_slice_in_dim(summed[3], dp_start, piece_width, 0)
    fc2_grad_out = lax.dynamic_slice_in_dim(summed[4], dp_start, piece_width, 1)
    vector_grad_out = lax.dynamic_slice_in_dim(summed[5], dp_start, piece_width, 1)
    hidden_grad_out = summed[6]
    return (
        block_output,
        input_grad,
        skip_input_grad,
        skip_grad_out,
        qkv_grad_out,
        proj_grad_out,
        fc1_grad_out,
        fc2_grad_out,
        vector_grad_out,
        hidden_grad_out,
        row_news[0],
        col_news[0],
        row_news[1],
        col_news[1],
        row_news[2][0],
        col_news[2][0],
        row_news[3][0],
        col_news[3][0],
        row_news[4][0],
        col_news[4][0],
        vector_state_new,
        hidden_state_new,
        skip_new,
        qkv_new,
        proj_new,
        fc1_new,
        fc2_new,
        vectors_new,
        hidden_new,
        skip_new.astype(jnp.bfloat16),
        qkv_new.astype(jnp.bfloat16),
        proj_new.astype(jnp.bfloat16),
        fc1_new.astype(jnp.bfloat16),
        fc2_new.astype(jnp.bfloat16),
        update_rms,
    )


def body(*operands):
    images = operands[2].shape[0]
    if images % lax.axis_size("mp") == 0 and lax.axis_size("dp") == 8:
        return body_data(*operands)
    return body_tensor(*operands)


small_cost = pl.CostEstimate(flops=0, bytes_accessed=1024, transcendentals=0)


def to_core(array):
    return lax.ppermute(array, "dp", [(i, i ^ 1) for i in range(8)])


def to_x(array):
    return lax.ppermute(array, "dp", [(i, i ^ 2) for i in range(8)])


def to_y(array):
    return lax.ppermute(array, "dp", [(i, i ^ 4) for i in range(8)])


def turn_mp(array, shift):
    count = lax.axis_size("mp")
    return lax.ppermute(array, "mp", [(i, (i + shift) % count) for i in range(count)])


def pick(array, index, axis):
    return lax.dynamic_index_in_dim(array, index, axis, keepdims=False)


def assemble(steps, targets, core, rows, blocks, split):
    arrays = []
    for step in steps:
        for array, _ in step:
            if not any(array is other for other in arrays):
                arrays.append(array)
    place = [
        [(next(n for n, other in enumerate(arrays) if other is array), k) for array, k in step]
        for step in steps
    ]
    table = jnp.stack([jnp.asarray(v, jnp.int32) for v in [*targets, core]])
    depth = 4
    outs = 2 if split < blocks else 1

    def kernel(table_ref, *refs):
        sources = refs[: len(arrays)]
        wholes = refs[len(arrays) : len(arrays) + outs]
        wide, narrow, in_sem, out_sem = refs[len(arrays) + outs :]
        half = rows // 2
        first = pl.multiple_of(table_ref[len(steps)] * half, half)
        second = pl.multiple_of(half - first, half)

        def fetch(step):
            slot = step % depth
            if len(place[step]) == 1:
                ((n, k),) = place[step]
                return [pltpu.make_async_copy(sources[n].at[k], wide.at[slot], in_sem.at[slot, 0])]
            copies = []
            for part, ((n, k), start) in enumerate(zip(place[step], (first, second))):
                spot = wide.at[slot, pl.ds(start, half)]
                copies.append(pltpu.make_async_copy(sources[n].at[k], spot, in_sem.at[slot, part]))
            return copies

        def leave(step, whole, spot):
            slot = step % depth
            return pltpu.make_async_copy(narrow.at[slot], whole.at[spot], out_sem.at[slot])

        for step in range(len(steps) + depth - 1):
            if step < len(steps):
                for copy in fetch(step):
                    copy.start()
            step = step - (depth - 1)
            if step < 0:
                continue
            slot = step % depth
            for copy in fetch(step):
                copy.wait()
            if step >= depth:
                leave(step - depth, wholes[0], 0).wait()
            narrow[slot] = wide[slot].astype(jnp.bfloat16)
            spot = table_ref[step]
            if outs == 1:
                leave(step, wholes[0], spot).start()
            else:

                @pl.when(spot < split)
                def _():
                    leave(step, wholes[0], spot).start()

                @pl.when(spot >= split)
                def _():
                    leave(step, wholes[1], spot - split).start()

        for step in range(max(0, len(steps) - depth), len(steps)):
            leave(step, wholes[0], 0).wait()

    shapes = [jax.ShapeDtypeStruct((split, rows, D), jnp.bfloat16)]
    if outs == 2:
        shapes.append(jax.ShapeDtypeStruct((blocks - split, rows, D), jnp.bfloat16))
    anywhere = pl.BlockSpec(memory_space=pl.ANY)
    return pl.pallas_call(
        kernel,
        in_specs=[pl.BlockSpec(memory_space=pltpu.SMEM)] + [anywhere] * len(arrays),
        out_specs=[anywhere] * outs,
        out_shape=shapes,
        scratch_shapes=[
            pltpu.VMEM((depth, rows, D), jnp.float32),
            pltpu.VMEM((depth, rows, D), jnp.bfloat16),
            pltpu.SemaphoreType.DMA((depth, 2)),
            pltpu.SemaphoreType.DMA((depth,)),
        ],
        compiler_params=pltpu.CompilerParams(vmem_limit_bytes=32 * 1024 * 1024),
        cost_estimate=small_cost,
    )(table, *arrays)


class Order:
    def __init__(self):
        self.token = None

    def after(self, *arrays):
        if self.token is not None:
            arrays = lax.optimization_barrier((*arrays, self.token))[:-1]
        return arrays if len(arrays) > 1 else arrays[0]

    def mark(self, *arrays):
        arrays = self.after(*arrays)
        self.token = arrays[0] if isinstance(arrays, tuple) else arrays
        return arrays


def swap_plane(order, for_x, for_y):
    for_x, for_y = order.after(for_x, for_y)
    return to_x(for_x), to_y(for_y)


def in_turn(arrays):
    count = len(arrays)
    twice = jnp.stack(list(arrays[::-1]) * 2)
    return lax.dynamic_slice_in_dim(twice, count - 1 - lax.axis_index("mp"), count, 0)


def gather_deep(array):
    return in_turn([array] + [turn_mp(array, shift) for shift in range(1, lax.axis_size("mp"))])


def sum_flat(array):
    for swap in (to_core, to_x, to_y):
        array = array + swap(array)
    return array


def bring(order, shard, quarter, core):
    count = lax.axis_size("mp")
    part = pick(pick(shard.reshape(4, 2, -1, D), quarter, 0), core, 0)
    return lax.all_gather(order.after(part), "mp")


def others(whole):
    count = lax.axis_size("mp")
    twice = jnp.concatenate([whole, whole], 0)
    return lax.dynamic_slice_in_dim(twice, lax.axis_index("mp") + 1, count - 1, 0)


def assemble_weight(shard, parts, swapped, core, split):
    count = lax.axis_size("mp")
    rows = shard.shape[0] // 8

    def spot(shard_index, quarter):
        shard_index = lax.rem(lax.axis_index("mp") + shard_index, count)
        return quarter * count + shard_index

    if swapped is None:
        mine = pick(shard.reshape(4, 2, rows, D), core, 1)
    else:
        mine = shard.reshape(4, 2 * rows, D)
    steps = [((mine, n),) for n in range(4)]
    targets = [spot(0, n) for n in range(4)]
    for n, (array, quarter, first) in enumerate(parts):
        for k in range(array.shape[0]):
            steps.append(((array, k),) if swapped is None else ((array, k), (swapped[n], k)))
            targets.append(spot(first + k, quarter))
    rows = mine.shape[1]
    whole = assemble(steps, targets, core, rows, count * 4, split or count * 4)
    return [array.reshape(-1, D) for array in whole]


def cut_corner(grad, quarter):
    corner = pick(grad, quarter ^ 3, 0)
    half = corner.shape[0] // 2
    return corner[:half], corner[half:]


def cut_sides(grad, quarter, add_y, add_x):
    half = add_y.shape[0]
    for_y = pick(grad, quarter ^ 2, 0)
    for_x = pick(grad, quarter ^ 1, 0)
    for_y = jnp.concatenate([for_y[:half] + add_y, for_y[half:]], 0)
    for_x = jnp.concatenate([for_x[:half], for_x[half:] + add_x], 0)
    return for_x, for_y


def sum_deep(order, grad, quarter, from_x, from_y):
    own = order.mark(pick(grad, quarter, 0) + from_x + from_y)
    return lax.psum_scatter(own, "mp", scatter_dimension=0, tiled=False)


def place_rows(pieces, rows, near_state=None):
    arrays = []
    for array, *_ in pieces:
        if not any(array is other for other in arrays):
            arrays.append(array)
    steps = [
        (next(n for n, other in enumerate(arrays) if other is array), first, amount)
        for array, first, amount, _ in pieces
    ]
    table = jnp.stack([jnp.asarray(spot, jnp.int32) for *_, spot in pieces])

    def kernel(table_ref, *refs):
        sources = refs[: len(arrays)]
        sems = refs[-1]
        if near_state is None:
            out_ref = refs[len(arrays)]
        else:
            state_ref, out_ref, moment_ref = refs[len(arrays) : -1]
        copies = []
        for step, (n, first, amount) in enumerate(steps):
            spot = pl.multiple_of(table_ref[step], 8)
            source = sources[n].at[pl.ds(first, amount)]
            copies.append(
                pltpu.make_async_copy(source, out_ref.at[pl.ds(spot, amount)], sems.at[step])
            )
        for copy in copies:
            copy.start()
        for copy in copies:
            copy.wait()
        if near_state is None:
            return
        leading, length = near_state.shape
        chunk = length if length < 384 else 384
        for lead in range(leading):
            total = jnp.zeros((1, D), jnp.float32)
            for first in range(0, length, chunk):
                grad = out_ref[lead * length + first : lead * length + first + chunk]
                squares = grad * grad + moment_eps
                total = total + jnp.sum(squares, 0, keepdims=True)
                near = 0.5 * state_ref[lead, :1, first : first + chunk]
                near = near + 0.5 * (as_row(lanes_of(squares)) / D)
                moment_ref[lead, 1:2, first : first + chunk] = near
            moment_ref[lead, :1] = total
            if length < D:
                moment_ref[lead, 1:2, length:] = jnp.zeros((1, D - length), jnp.float32)

    vmem = pl.BlockSpec(memory_space=pltpu.VMEM)
    in_specs = [pl.BlockSpec(memory_space=pltpu.SMEM)]
    in_specs = in_specs + [pl.BlockSpec(memory_space=pl.ANY)] * len(arrays)
    out_specs, shapes = [vmem], [jax.ShapeDtypeStruct((rows, D), jnp.float32)]
    operands = [table, *arrays]
    if near_state is not None:
        leading, length = near_state.shape
        in_specs.append(vmem)
        operands.append(near_state.reshape(leading, 1, length))
        out_specs.append(vmem)
        shapes.append(jax.ShapeDtypeStruct((leading, 2, D), jnp.float32))
    result = pl.pallas_call(
        kernel,
        in_specs=in_specs,
        out_specs=out_specs,
        out_shape=shapes,
        scratch_shapes=[pltpu.SemaphoreType.DMA((len(steps),))],
        compiler_params=pltpu.CompilerParams(vmem_limit_bytes=40 * 1024 * 1024),
        cost_estimate=small_cost,
    )(*operands)
    return result[0] if near_state is None else result


def add_half(grads, given, core):
    rows = grads[0].shape[2]
    amounts = [array.shape[0] for array in grads]
    firsts = [sum(amounts[:n]) for n in range(len(amounts))]

    def kernel(core_ref, *refs):
        for n, (first, amount) in enumerate(zip(firsts, amounts)):

            @pl.when((pl.program_id(0) >= first) & (pl.program_id(0) < first + amount))
            def _():
                refs[-1][...] = refs[n][0] + refs[len(grads) + n][...]

    def at(first, amount):
        return lambda step: jnp.clip(step - first, 0, amount - 1)

    spots = [at(*pair) for pair in zip(firsts, amounts)]
    own_specs = [
        pl.BlockSpec((1, 1, rows, D), lambda step, core_ref, at=at: (at(step), core_ref[0], 0, 0))
        for at in spots
    ]
    given_specs = [
        pl.BlockSpec((1, rows, D), lambda step, core_ref, at=at: (at(step), 0, 0)) for at in spots
    ]
    total = sum(amounts)
    return pl.pallas_call(
        kernel,
        grid_spec=pltpu.PrefetchScalarGridSpec(
            num_scalar_prefetch=1,
            grid=(total,),
            in_specs=own_specs + given_specs,
            out_specs=pl.BlockSpec((1, rows, D), lambda step, core_ref: (step, 0, 0)),
        ),
        out_shape=jax.ShapeDtypeStruct((total, rows, D), jnp.float32),
        compiler_params=pltpu.CompilerParams(vmem_limit_bytes=40 * 1024 * 1024),
        cost_estimate=small_cost,
    )(core[None], *grads, *given)


def lanes_of(array):
    total = array[:, :128]
    for tile in range(1, array.shape[1] // 128):
        total = total + array[:, tile * 128 : (tile + 1) * 128]
    return total


def as_row(column):
    return jnp.sum(column.T, 0, keepdims=True)


def as_column(row):
    return jnp.broadcast_to(row, (128, row.shape[1])).T


def scale_kernel(count, by_rows, place_ref, grad_ref, state_ref, *refs):
    sources = refs[:count]
    far_ref, scale_ref, near_ref, step_ref = refs[count:]
    rows = grad_ref.shape[1]
    total = jnp.zeros((1, D), jnp.float32)
    near_sum = jnp.zeros((1, 1), jnp.float32)
    for index in range(count):
        part = jnp.zeros((2, D), jnp.float32)
        for shift in range(count):
            part = jnp.where(place_ref[0] == (index + shift) % count, sources[shift][0], part)
        total = total + part[:1]
        near_sum = near_sum + jnp.sum(part[1:], 1, keepdims=True)
    far = 0.5 * state_ref[0] + 0.5 * (total / (count * rows))
    far_ref[0] = far
    lead = pl.program_id(0)
    near_mean = near_sum / (count * rows)
    far_mean = jnp.sum(far, 1, keepdims=True) / D
    if all(by_rows):
        mean = near_mean
    elif not any(by_rows):
        mean = far_mean
    else:
        split = by_rows.index(True)
        mean = jnp.where(lead >= split, near_mean, far_mean)
    far_scale = lax.rsqrt(far)
    near_scale = as_column(lax.rsqrt(sources[0][0][1:2, :rows] / mean))
    scale_ref[0] = far_scale
    near_ref[0] = near_scale
    step = grad_ref[0] * far_scale
    step = lanes_of(step * step) * near_scale * near_scale

    @pl.when(lead == 0)
    def _():
        step_ref[...] = jnp.zeros_like(step_ref)

    step_ref[...] += jnp.sum(step.reshape(rows // 8, 8, 128), 0)


def scales(grad, far_state, sources, mp_index, by_rows):
    leading, rows, _ = grad.shape
    count = len(sources)
    small = pl.BlockSpec((1, 2, D), lambda i: (i, 0, 0))
    line = pl.BlockSpec((1, 1, D), lambda i: (i, 0, 0))
    return pl.pallas_call(
        functools.partial(scale_kernel, count, by_rows),
        grid=(leading,),
        in_specs=[
            pl.BlockSpec(memory_space=pltpu.SMEM),
            pl.BlockSpec((1, rows, D), lambda i: (i, 0, 0)),
            line,
        ]
        + [small] * count,
        out_specs=[
            line,
            line,
            pl.BlockSpec((1, rows, 128), lambda i: (i, 0, 0)),
            pl.BlockSpec((8, 128), lambda i: (0, 0)),
        ],
        out_shape=[
            jax.ShapeDtypeStruct((leading, 1, D), jnp.float32),
            jax.ShapeDtypeStruct((leading, 1, D), jnp.float32),
            jax.ShapeDtypeStruct((leading, rows, 128), jnp.float32),
            jax.ShapeDtypeStruct((8, 128), jnp.float32),
        ],
        compiler_params=pltpu.CompilerParams(vmem_limit_bytes=40 * 1024 * 1024),
        cost_estimate=small_cost,
    )(mp_index[None], grad, far_state.reshape(leading, 1, D), *sources)


def renew_kernel(turned, factor_ref, weight_ref, grad_ref, far_ref, near_ref, new_ref, low_ref):
    step = grad_ref[0] * far_ref[0] * (near_ref[0][:, :1] * factor_ref[0])
    new = weight_ref[0] - (step.T if turned else step)
    new_ref[0] = new
    low_ref[0] = new.astype(jnp.bfloat16)


def renew(weight, grad, far_scale, near_scale, factor, turned, first=0):
    leading, rows = weight.shape[0], grad.shape[1]
    if turned:
        width = 384
        grid = (leading, D // width)
        weight_spec = pl.BlockSpec((1, width, rows), lambda i, j: (i, j, 0))
        grad_spec = pl.BlockSpec((1, rows, width), lambda i, j: (i + first, 0, j))
        far_spec = pl.BlockSpec((1, 1, width), lambda i, j: (i + first, 0, j))
        near_spec = pl.BlockSpec((1, rows, 128), lambda i, j: (i + first, 0, 0))
    else:
        height = min(rows, 288)
        grid = (leading, rows // height)
        weight_spec = pl.BlockSpec((1, height, D), lambda i, j: (i, j, 0))
        grad_spec = pl.BlockSpec((1, height, D), lambda i, j: (i + first, j, 0))
        far_spec = pl.BlockSpec((1, 1, D), lambda i, j: (i + first, 0, 0))
        near_spec = pl.BlockSpec((1, height, 128), lambda i, j: (i + first, j, 0))
    return pl.pallas_call(
        functools.partial(renew_kernel, turned),
        grid=grid,
        in_specs=[pl.BlockSpec(memory_space=pltpu.SMEM), weight_spec, grad_spec, far_spec, near_spec],
        out_specs=[weight_spec, weight_spec],
        out_shape=[
            jax.ShapeDtypeStruct(weight.shape, jnp.float32),
            jax.ShapeDtypeStruct(weight.shape, jnp.bfloat16),
        ],
        compiler_params=pltpu.CompilerParams(vmem_limit_bytes=40 * 1024 * 1024),
        cost_estimate=small_cost,
    )(factor[None], weight, grad, far_scale, near_scale)


def head_windows():
    spans = []
    for head in range(D // HEAD_DIM):
        first = head * HEAD_DIM
        start = first // 128 * 128
        stop = -(-(first + HEAD_DIM) // 128) * 128
        spans.append((first, start, stop - start))
    return spans


def head_mask(first, start, width):
    lanes = start + lax.broadcasted_iota(jnp.int32, (SEQ, width), 1)
    return (lanes >= first) & (lanes < first + HEAD_DIM)


def dot_nt(left_side, right_side):
    return lax.dot_general(
        left_side, right_side, (((1,), (1,)), ((), ())), preferred_element_type=jnp.float32
    )


def attend_kernel(qkv_ref, out_ref, total):
    total[...] = jnp.zeros_like(total)
    for first, start, width in head_windows():
        keep = head_mask(first, start, width)
        query = qkv_ref[0, :, start : start + width]
        key = jnp.where(keep, qkv_ref[0, :, D + start : D + start + width], 0)
        value = jnp.where(keep, qkv_ref[0, :, 2 * D + start : 2 * D + start + width], 0)
        scores = dot_nt(query, key) * HEAD_DIM ** (-0.5)
        expo = jnp.exp(scores - jnp.max(scores, 1, keepdims=True))
        probs = (expo / jnp.sum(expo, 1, keepdims=True)).astype(jnp.bfloat16)
        total[:, start : start + width] += matmul(probs, value)
    out_ref[0] = total[...].astype(jnp.bfloat16)


def attend(qkv):
    images = qkv.shape[0]
    return pl.pallas_call(
        attend_kernel,
        grid=(images,),
        in_specs=[pl.BlockSpec((1, SEQ, 3 * D), lambda i: (i, 0, 0))],
        out_specs=pl.BlockSpec((1, SEQ, D), lambda i: (i, 0, 0)),
        out_shape=jax.ShapeDtypeStruct((images, SEQ, D), jnp.bfloat16),
        scratch_shapes=[pltpu.VMEM((SEQ, D), jnp.float32)],
        compiler_params=pltpu.CompilerParams(vmem_limit_bytes=40 * 1024 * 1024),
        cost_estimate=small_cost,
    )(qkv)


def attend_back_kernel(qkv_ref, grad_ref, out_ref, query_sum, key_sum, value_sum):
    scale = HEAD_DIM ** (-0.5)
    for ref in (query_sum, key_sum, value_sum):
        ref[...] = jnp.zeros_like(ref)
    for first, start, width in head_windows():
        span = slice(start, start + width)
        keep = head_mask(first, start, width)
        query = jnp.where(keep, qkv_ref[0, :, span], 0)
        key = jnp.where(keep, qkv_ref[0, :, D + start : D + start + width], 0)
        value = jnp.where(keep, qkv_ref[0, :, 2 * D + start : 2 * D + start + width], 0)
        above = jnp.where(keep, grad_ref[0, :, span], 0)
        scores = dot_nt(key, query) * scale
        expo = jnp.exp(scores - jnp.max(scores, 0, keepdims=True))
        probs = expo / jnp.sum(expo, 0, keepdims=True)
        prob_grad = dot_nt(value, above)
        inner = jnp.sum(probs * prob_grad, 0, keepdims=True)
        score_grad = (probs * (prob_grad - inner)).astype(jnp.bfloat16)
        value_sum[:, span] += matmul(probs.astype(jnp.bfloat16), above)
        key_sum[:, span] += matmul(score_grad, query) * scale
        query_sum[:, span] += (
            lax.dot_general(
                score_grad, key, (((0,), (0,)), ((), ())), preferred_element_type=jnp.float32
            )
            * scale
        )
    out_ref[0, :, :D] = query_sum[...].astype(jnp.bfloat16)
    out_ref[0, :, D : 2 * D] = key_sum[...].astype(jnp.bfloat16)
    out_ref[0, :, 2 * D :] = value_sum[...].astype(jnp.bfloat16)


def attend_back(qkv, grad):
    images = qkv.shape[0]
    return pl.pallas_call(
        attend_back_kernel,
        grid=(images,),
        in_specs=[
            pl.BlockSpec((1, SEQ, 3 * D), lambda i: (i, 0, 0)),
            pl.BlockSpec((1, SEQ, D), lambda i: (i, 0, 0)),
        ],
        out_specs=pl.BlockSpec((1, SEQ, 3 * D), lambda i: (i, 0, 0)),
        out_shape=jax.ShapeDtypeStruct((images, SEQ, 3 * D), jnp.bfloat16),
        scratch_shapes=[pltpu.VMEM((SEQ, D), jnp.float32)] * 3,
        compiler_params=pltpu.CompilerParams(vmem_limit_bytes=40 * 1024 * 1024),
        cost_estimate=small_cost,
    )(qkv, grad)


def body_data(
    block_input,
    skip_input,
    timesteps,
    class_labels,
    loss_weights,
    grad_output,
    skip_weight,
    qkv_weight,
    proj_weight,
    fc1_weight,
    fc2_weight,
    vectors,
    hidden_bias,
    skip_rows,
    skip_cols,
    qkv_rows,
    qkv_cols,
    proj_rows,
    proj_cols,
    fc1_rows,
    fc1_cols,
    fc2_rows,
    fc2_cols,
    vector_moments,
    hidden_moments,
):
    image_count = timesteps.shape[0]
    mp_count = lax.axis_size("mp")
    dp_count = lax.axis_size("dp")
    mp_index = lax.axis_index("mp")
    dp_index = lax.axis_index("dp")
    core = lax.rem(dp_index, 2)
    quarter = lax.div(dp_index, 2)
    images = image_count // mp_count
    tokens = images * SEQ
    width_local = qkv_weight.shape[2]
    hidden_local = fc1_weight.shape[1]
    hidden_slice = hidden_local // dp_count
    order = Order()

    skip_shard = skip_weight.reshape(-1, D)
    skip_whole = bring(order, skip_shard, quarter, core)
    hidden_all = gather_deep(hidden_bias)

    angles = (timesteps.astype(jnp.float32) + 0.5) * (0.5 * math.pi / total_steps)
    alpha_sq = jnp.square(jnp.cos(angles))
    sigma_sq = jnp.square(jnp.sin(angles))
    snr_weight = 5.0 * sigma_sq / jnp.maximum(alpha_sq, 5.0 * sigma_sq)
    base_weight = loss_weights * snr_weight
    one_hot = (class_labels[:, None] == jnp.arange(CLASSES, dtype=jnp.int32)[None, :]).astype(
        jnp.float32
    )
    batch = jnp.concatenate([jnp.sum(one_hot, 0), jnp.sum(base_weight)[None]])

    attn_shard = jnp.concatenate(
        [qkv_weight.transpose(0, 2, 1).reshape(3 * width_local, D), proj_weight], 0
    )
    attn_shard = order.mark(attn_shard)
    attn_whole = bring(order, attn_shard, quarter, core)
    batch = order.mark(batch + to_core(batch))
    batch_x = to_x(batch)
    fc1_shard = order.mark(fc1_weight.T)
    fc2_shard = fc2_weight
    batch = order.mark(batch + batch_x)
    batch_y = to_y(batch)
    start = mp_index * tokens
    block_local = lax.dynamic_slice_in_dim(block_input, start, tokens, 0)
    skip_local = lax.dynamic_slice_in_dim(skip_input, start, tokens, 0)
    both_inputs = jnp.concatenate(
        [
            array.reshape(tokens, mp_count, 2, -1).transpose(0, 2, 1, 3).reshape(tokens, D)
            for array in (block_local, skip_local)
        ],
        1,
    )
    both_inputs = order.mark(both_inputs)
    batch = order.mark(batch + batch_y)

    skip_own = others(order.mark(skip_whole))
    skip_x, skip_y = swap_plane(order, skip_own, skip_own)
    skip_swapped = [to_core(skip_own)]
    fc1_whole = bring(order, fc1_shard, quarter, core)
    hidden_own = pick(hidden_all.reshape(mp_count, 4, 2, hidden_slice), core, 2)
    hidden_own = hidden_own.transpose(1, 0, 2).reshape(-1)
    own_count = jnp.dot(one_hot, batch[:CLASSES], precision=lax.Precision.HIGHEST)
    item_weight = base_weight * lax.rsqrt(own_count)
    hidden_own, item_weight = order.mark(hidden_own, item_weight)
    batch_scale = image_count * dp_count / batch[CLASSES]
    grad_local = lax.dynamic_slice_in_dim(grad_output, start, tokens, 0)
    item_local = lax.dynamic_slice_in_dim(item_weight, mp_index * images, images, 0)
    upstream = (
        grad_local.astype(jnp.float32).reshape(images, SEQ, D) * item_local[:, None, None]
    ).reshape(-1, D)
    upstream = order.mark(upstream)

    skip_x, skip_y = order.mark(skip_x, skip_y)
    skip_one, skip_two = swap_plane(order, skip_y[:2], skip_x[2:])
    skip_swapped = skip_swapped + [to_core(skip_x), to_core(skip_y)]
    skip_one, skip_two = order.mark(skip_one, skip_two)
    skip_swapped = skip_swapped + [to_core(skip_one), to_core(skip_two)]
    attn_own = others(order.mark(attn_whole))
    attn_x, attn_y = swap_plane(order, attn_own, attn_own)
    fc2_whole = bring(order, fc2_shard, quarter, core)
    fc2_across = bring(order, fc2_shard, quarter ^ 3, core)
    skip_swapped = order.mark(*skip_swapped)
    attn_swapped = [to_core(order.after(attn_own))]
    skip_parts = [
        (skip_own, quarter, 1),
        (skip_x, quarter ^ 1, 1),
        (skip_y, quarter ^ 2, 1),
        (skip_one, quarter ^ 3, 1),
        (skip_two, quarter ^ 3, 3),
    ]
    (skip_low,) = assemble_weight(skip_shard, skip_parts, skip_swapped, core, 0)
    joined = matmul(both_inputs, skip_low) + vectors[4]
    normed, normal_one, inverse_one = norm_forward(joined, vectors[0], vectors[1])
    normed_low = normed.astype(jnp.bfloat16)
    joined, normed_low, normal_one = order.mark(joined, normed_low, normal_one)
    upstream_other = to_core(order.after(upstream))

    attn_x, attn_y = order.mark(attn_x, attn_y)
    attn_one, attn_two = swap_plane(order, attn_y[:1], attn_x[1:])
    attn_swapped = attn_swapped + [to_core(attn_x), to_core(attn_y)]
    upstream_other = order.mark(upstream_other) * batch_scale
    upstream = upstream * batch_scale
    upstream_low = jnp.concatenate([upstream, upstream_other], 0).astype(jnp.bfloat16)
    upstream_low = order.mark(upstream_low)
    fc1_own = others(order.mark(fc1_whole))
    fc1_x, fc1_y = swap_plane(order, fc1_own, fc1_own)
    attn_one, attn_two = order.mark(attn_one, attn_two)
    attn_swapped = attn_swapped + [to_core(attn_one), to_core(attn_two)]
    attn_parts = [
        (attn_own, quarter, 1),
        (attn_x, quarter ^ 1, 1),
        (attn_y, quarter ^ 2, 1),
        (attn_one, quarter ^ 3, 1),
        (attn_two, quarter ^ 3, 2),
    ]
    attn_swapped = order.mark(*attn_swapped)
    qkv_low, proj_low = assemble_weight(
        attn_shard, attn_parts, attn_swapped, core, 3 * mp_count
    )
    qkv_all = jnp.einsum(
        "itd,ed->ite",
        normed_low.reshape(images, SEQ, D),
        qkv_low,
        preferred_element_type=jnp.float32,
    ).astype(jnp.bfloat16)
    qkv_all = order.mark(qkv_all)
    attended = attend(qkv_all).reshape(tokens, D)
    residual = joined + matmul(attended, proj_low) + vectors[5]
    residual = order.mark(residual)
    fc1_x, fc1_y = order.mark(fc1_x, fc1_y)
    fc1_cut = order.mark(fc1_y[:2], fc1_x[2:])
    fc1_one, fc1_two = swap_plane(order, *fc1_cut)
    fc2_own = others(order.mark(fc2_whole))
    fc2_x, fc2_y = swap_plane(order, fc2_own, fc2_own)
    normed_two, normal_two, inverse_two = norm_forward(
        order.after(residual), vectors[2], vectors[3]
    )
    normed_two, normal_two = order.mark(normed_two, normal_two)
    normed_two_other = to_core(normal_two)
    fc1_one, fc1_two = order.mark(fc1_one, fc1_two)
    fc1_parts = [
        (fc1_own, quarter, 1),
        (fc1_x, quarter ^ 1, 1),
        (fc1_y, quarter ^ 2, 1),
        (fc1_one, quarter ^ 3, 1),
        (fc1_two, quarter ^ 3, 3),
    ]
    (fc1_low,) = assemble_weight(fc1_shard, fc1_parts, None, core, 0)
    fc1_low = order.mark(fc1_low)
    normed_two_other = order.mark(normed_two_other) * vectors[2] + vectors[3]
    normed_two_low = jnp.concatenate([normed_two, normed_two_other], 0).astype(jnp.bfloat16)
    normed_two_low = order.mark(normed_two_low)
    pre_act = (
        jnp.einsum("td,fd->tf", normed_two_low, fc1_low, preferred_element_type=jnp.float32)
        + hidden_own
    )
    activated, gelu_pull = jax.vjp(gelu_exact, pre_act)
    activated_low = activated.astype(jnp.bfloat16)
    fc2_grad = jnp.einsum(
        "tf,td->fd", activated_low, upstream_low, preferred_element_type=jnp.float32
    ).reshape(4, mp_count, hidden_slice, D)
    fc2_grad = order.mark(fc2_grad)
    fc2_add = swap_plane(order, *order.mark(*cut_corner(fc2_grad, quarter)))

    fc2_x, fc2_y = order.mark(fc2_x, fc2_y)
    fc2_corner = others(order.mark(fc2_across))
    fc2_parts = [
        (fc2_own, quarter, 1),
        (fc2_x, quarter ^ 1, 1),
        (fc2_y, quarter ^ 2, 1),
        (fc2_corner, quarter ^ 3, 1),
    ]
    (fc2_low,) = assemble_weight(fc2_shard, fc2_parts, None, core, 0)
    fc2_low = order.mark(fc2_low)
    forward_part = order.mark(matmul(activated_low, fc2_low))
    forward_other = to_core(forward_part[tokens:])
    act_grad = jnp.einsum(
        "td,fd->tf", order.after(upstream_low), fc2_low, preferred_element_type=jnp.float32
    )
    pre_grad = gelu_pull(act_grad)[0]
    hidden_grad = jnp.sum(pre_grad, 0)
    pre_low, hidden_grad = order.mark(pre_grad.astype(jnp.bfloat16), hidden_grad)
    block_own = residual + forward_part[:tokens] + order.mark(forward_other)
    block_own = order.mark(block_own.reshape(images, SEQ, D))
    block_all = lax.all_gather(block_own, "mp")
    fc2_add = order.mark(*fc2_add)
    fc2_sides = swap_plane(order, *order.mark(*cut_sides(fc2_grad, quarter, *fc2_add)))
    back_part = order.mark(matmul(order.after(pre_low), fc1_low))
    back_other = to_core(back_part[tokens:])
    fc1_grad = jnp.einsum(
        "tf,td->fd",
        order.after(pre_low),
        normed_two_low,
        preferred_element_type=jnp.float32,
    ).reshape(4, mp_count, hidden_slice, D)
    fc1_grad = order.mark(fc1_grad)
    fc1_add = swap_plane(order, *order.mark(*cut_corner(fc1_grad, quarter)))
    norm_two_in = back_part[:tokens] + order.mark(back_other)
    back_two, gain_two_grad, bias_two_grad = norm_backward(
        norm_two_in, normal_two, inverse_two, vectors[2]
    )
    residual_grad = upstream + back_two
    residual_low = residual_grad.astype(jnp.bfloat16)
    residual_grad, residual_low = order.mark(residual_grad, residual_low)
    attended_grad = jnp.einsum(
        "td,ed->te", residual_low, proj_low, preferred_element_type=jnp.float32
    ).astype(jnp.bfloat16)
    qkv_grad_low = attend_back(
        qkv_all, order.mark(attended_grad.reshape(images, SEQ, D))
    ).reshape(tokens, 3 * D)
    qkv_grad_low = order.mark(qkv_grad_low)
    fc2_sides = order.mark(*fc2_sides)
    fc2_piece = sum_deep(order, fc2_grad, quarter, *fc2_sides)
    qkv_grad = jnp.einsum(
        "te,td->ed", order.after(qkv_grad_low), normed_low, preferred_element_type=jnp.float32
    ).reshape(3 * mp_count, 2, hidden_slice, D)
    proj_grad = jnp.einsum(
        "te,td->ed", attended, order.after(residual_low), preferred_element_type=jnp.float32
    ).reshape(mp_count, 2, hidden_slice, D)
    attn_given = order.mark(pick(qkv_grad, 1 - core, 1), pick(proj_grad, 1 - core, 1))
    attn_given = [to_core(array) for array in attn_given]
    fc1_add = order.mark(*fc1_add)
    fc1_sides = swap_plane(order, *order.mark(*cut_sides(fc1_grad, quarter, *fc1_add)))
    norm_one_in = matmul(order.after(qkv_grad_low), qkv_low)
    back_one, gain_one_grad, bias_one_grad = norm_backward(
        norm_one_in, normal_one, inverse_one, vectors[0]
    )
    joined_grad = residual_grad + back_one
    joined_low = joined_grad.astype(jnp.bfloat16)
    joined_grad, joined_low = order.mark(joined_grad, joined_low)
    skip_grad = jnp.einsum(
        "tc,td->cd", both_inputs, joined_low, preferred_element_type=jnp.float32
    ).reshape(4 * mp_count, 2, -1, D)
    skip_given = order.mark(pick(skip_grad, 1 - core, 1))
    skip_given = to_core(skip_given)
    block_all = order.mark(block_all)
    attn_given = order.mark(*attn_given)
    attn_grad = add_half([qkv_grad, proj_grad], attn_given, core)
    attn_grad = order.mark(attn_grad.reshape(4, mp_count, hidden_slice, D))
    attn_add = swap_plane(order, *order.mark(*cut_corner(attn_grad, quarter)))
    fc1_sides = order.mark(*fc1_sides)
    fc1_piece = sum_deep(order, fc1_grad, quarter, *fc1_sides)
    skip_shards = skip_low.reshape(4, mp_count, -1, D)
    both_grads = []
    for shift in (1, 2, 3, 0):
        shard_low = pick(skip_shards, lax.rem(mp_index + shift, mp_count), 1).reshape(-1, D)
        both = jnp.einsum("td,cd->tc", joined_low, shard_low, preferred_element_type=jnp.float32)
        both = order.mark(both)
        both_grads.append(both)
    attn_add = order.mark(*attn_add)
    attn_sides = swap_plane(order, *order.mark(*cut_sides(attn_grad, quarter, *attn_add)))
    skip_given = order.mark(skip_given)
    skip_grad = add_half([skip_grad], [skip_given], core)
    skip_grad = order.mark(skip_grad.reshape(4, mp_count, -1, D))
    skip_add = swap_plane(order, *order.mark(*cut_corner(skip_grad, quarter)))
    fc2_piece = order.mark(fc2_piece)
    vector_grad = jnp.stack(
        [
            gain_one_grad,
            bias_one_grad,
            gain_two_grad,
            bias_two_grad,
            jnp.sum(joined_grad, 0),
            jnp.sum(residual_grad, 0),
            jnp.sum(upstream, 0),
        ]
    )
    hidden_grad = hidden_grad.reshape(4, mp_count, 1, hidden_slice).transpose(1, 0, 2, 3)
    hidden_grad = jnp.where(jnp.arange(2)[None, None, :, None] == core, hidden_grad, 0.0)
    small = order.mark(jnp.concatenate([vector_grad.reshape(-1), hidden_grad.reshape(-1)]))
    weight_sq = jnp.stack(
        [
            jnp.sum(array * array)
            for array in (skip_weight, qkv_weight, proj_weight, fc1_weight, fc2_weight, hidden_bias)
        ]
    )
    small_core = to_core(small)
    weight_sq = order.mark(weight_sq)
    fc1_piece = order.mark(fc1_piece)
    both_grads[0] = turn_mp(order.after(both_grads[0]), 1)
    attn_sides = order.mark(*attn_sides)
    attn_piece = sum_deep(order, attn_grad, quarter, *attn_sides)
    skip_add = order.mark(*skip_add)
    skip_sides = swap_plane(order, *order.mark(*cut_sides(skip_grad, quarter, *skip_add)))
    small = order.mark(small + order.mark(small_core))
    small_x = to_x(small)
    skip_sides = order.mark(*skip_sides)
    small = order.mark(small + order.mark(small_x))
    small_y = to_y(small)
    skip_piece = sum_deep(order, skip_grad, quarter, *skip_sides)

    def spread(piece):
        return swap_plane(order, piece, piece)

    def half_of(rows):
        return (rows // 2 + 7) // 8 * 8

    def spread_far(near):
        half = half_of(near[0].shape[0])
        return swap_plane(order, near[1][:half], near[0][half:])

    def hold(piece, near, far):
        rows, half = piece.shape[0], far[0].shape[0]
        return place_rows(
            [
                (piece, 0, rows, quarter * rows),
                (near[0], 0, rows, (quarter ^ 1) * rows),
                (near[1], 0, rows, (quarter ^ 2) * rows),
                (far[0], 0, half, (quarter ^ 3) * rows),
                (far[1], 0, rows - half, (quarter ^ 3) * rows + half),
            ],
            4 * rows,
        )

    def interleave(held, other, near_state):
        rows = held.shape[0] // 4
        pieces = []
        for n in range(4):
            pieces.append((held, n * rows, rows, (2 * n + core) * rows))
            pieces.append((other, n * rows, rows, (2 * n + 1 - core) * rows))
        whole, sent = place_rows(pieces, 8 * rows, near_state)
        return whole.reshape(near_state.shape + (D,)), sent

    def own_state(state):
        width = state.shape[-1] // mp_count
        return lax.dynamic_slice_in_dim(state, mp_index * width, width, state.ndim - 1)

    def everywhere(array):
        return [array] + [turn_mp(array, shift) for shift in range(1, mp_count)]

    fc2_near, fc1_near = spread(fc2_piece), spread(fc1_piece)
    attn_piece = order.mark(attn_piece)
    fc2_near = order.mark(*fc2_near)
    both_grads[0] = order.mark(both_grads[0])
    fc2_far = spread_far(fc2_near)
    small = order.mark(small + order.mark(small_y))
    fc1_near = order.mark(*fc1_near)
    fc1_far = spread_far(fc1_near)
    fc2_far = order.mark(*fc2_far)
    attn_near = spread(attn_piece)
    fc2_held = order.mark(hold(fc2_piece, fc2_near, fc2_far))
    skip_piece = order.mark(skip_piece)
    both_grads[1] = turn_mp(order.after(both_grads[1]), 2)
    fc1_far = order.mark(*fc1_far)
    skip_near = spread(skip_piece)
    fc1_held = order.mark(hold(fc1_piece, fc1_near, fc1_far))
    attn_near = order.mark(*attn_near)
    fc2_other = to_core(order.after(fc2_held))
    attn_far = spread_far(attn_near)
    skip_near = order.mark(*skip_near)
    skip_far = spread_far(skip_near)
    fc2_sum, fc2_moments = order.mark(
        *interleave(fc2_held, order.mark(fc2_other), own_state(fc2_rows)[None])
    )
    fc1_other = to_core(order.after(fc1_held))
    attn_far = order.mark(*attn_far)
    attn_held = order.mark(hold(attn_piece, attn_near, attn_far))
    attn_other = to_core(attn_held)
    skip_far = order.mark(*skip_far)
    skip_held = order.mark(hold(skip_piece, skip_near, skip_far))
    skip_other = to_core(skip_held)
    both_grads[1] = order.mark(both_grads[1])
    both_grads[2] = turn_mp(order.after(both_grads[2]), 3)
    fc1_sum, fc1_moments = order.mark(
        *interleave(fc1_held, order.mark(fc1_other), own_state(fc1_cols)[None])
    )
    hidden_sent = everywhere(order.mark(jnp.concatenate([fc2_moments, fc1_moments], 0)))
    attn_state = jnp.concatenate([own_state(qkv_cols), own_state(proj_rows)[None]], 0)
    attn_sum, attn_moments = order.mark(
        *interleave(attn_held, order.mark(attn_other), attn_state)
    )
    skip_sum, skip_moments = order.mark(
        *interleave(skip_held, order.mark(skip_other), own_state(skip_rows))
    )
    hidden_sent = order.mark(*hidden_sent)
    both_grads[2] = order.mark(both_grads[2])
    token_sent = everywhere(order.mark(jnp.concatenate([attn_moments, skip_moments], 0)))
    small_all = everywhere(order.after(small))
    fc2_sent = [array[:1] for array in hidden_sent]
    fc1_sent = [array[1:] for array in hidden_sent]
    fc2_far_new, *fc2_scales, fc2_step = order.mark(
        *scales(fc2_sum, fc2_cols[None], fc2_sent, mp_index, (True,))
    )
    fc1_far_new, *fc1_scales, fc1_step = order.mark(
        *scales(fc1_sum, fc1_rows[None], fc1_sent, mp_index, (False,))
    )
    token_sent = order.mark(*token_sent)
    small = jnp.sum(in_turn(order.mark(*small_all)), 0)
    attn_sent = [array[:4] for array in token_sent]
    skip_sent = [array[4:] for array in token_sent]
    attn_state = jnp.concatenate([qkv_rows, proj_cols[None]], 0)
    attn_far_new, *attn_scales, attn_step = order.mark(
        *scales(attn_sum, attn_state, attn_sent, mp_index, (False, False, False, True))
    )
    skip_far_new, *skip_scales, skip_step = order.mark(
        *scales(skip_sum, skip_cols, skip_sent, mp_index, (True, True))
    )

    vector_sum = small[: 7 * D].reshape(7, D)
    hidden_sum = lax.dynamic_slice_in_dim(small[7 * D :], mp_index * hidden_local, hidden_local, 0)
    vector_new = 0.5 * vector_moments + 0.5 * (vector_sum * vector_sum + moment_eps)
    vector_update = vector_sum * lax.rsqrt(vector_new)
    hidden_new = 0.5 * hidden_moments + 0.5 * (hidden_sum * hidden_sum + moment_eps)
    hidden_update = hidden_sum * lax.rsqrt(hidden_new)
    step_sq = jnp.sum(hidden_update * hidden_update)
    step_sq = step_sq + jnp.sum(skip_step + attn_step + fc1_step + fc2_step)
    sent = jnp.concatenate([step_sq[None], weight_sq, jnp.zeros((121,), jnp.float32)])
    sent = everywhere(order.mark(sent))
    input_grads = in_turn([both_grads[3]] + both_grads[:3])
    input_grad = input_grads[:, :, :width_local].reshape(-1, width_local)
    skip_input_grad = input_grads[:, :, width_local:].reshape(-1, width_local)
    input_grad, skip_input_grad = order.mark(input_grad, skip_input_grad)
    sent = jnp.sum(in_turn(order.mark(*sent)), 0)
    weight_sq = sent[1:]
    step_total = sent[0] + jnp.sum(vector_update * vector_update)
    param_count = 6.0 * D * D + 2.0 * D * FF + 7.0 * D + FF
    update_rms = jnp.sqrt(step_total / param_count)
    divisor = jnp.maximum(1.0, update_rms / clip_level)
    tensor_sizes = (2.0 * D * D, 3.0 * D * D, 1.0 * D * D, 1.0 * D * FF, 1.0 * FF * D, 1.0 * FF)

    def factor_of(position):
        weight_rms = jnp.sqrt(weight_sq[position] / tensor_sizes[position])
        return step_rate * jnp.maximum(0.001, weight_rms) / divisor

    skip_new, skip_new_low = renew(skip_weight, skip_sum, *skip_scales, factor_of(0), False)
    qkv_turned = qkv_weight.transpose(0, 2, 1)
    qkv_new, qkv_new_low = renew(qkv_turned, attn_sum, *attn_scales, factor_of(1), False)
    qkv_new, qkv_new_low = qkv_new.transpose(0, 2, 1), qkv_new_low.transpose(0, 2, 1)
    proj_new, proj_new_low = renew(
        proj_weight[None], attn_sum, *attn_scales, factor_of(2), False, first=3
    )
    fc1_new, fc1_new_low = renew(fc1_weight[None], fc1_sum, *fc1_scales, factor_of(3), True)
    fc2_new, fc2_new_low = renew(fc2_weight[None], fc2_sum, *fc2_scales, factor_of(4), False)
    block_output = (block_all + vectors[6]).astype(jnp.bfloat16).reshape(-1, D)
    vector_rms = jnp.sqrt(jnp.mean(vectors * vectors, 1, keepdims=True))
    vectors_new = vectors - step_rate * jnp.maximum(0.001, vector_rms) * vector_update / divisor
    hidden_bias_new = hidden_bias - factor_of(5) * hidden_update
    piece_width = D // dp_count
    dp_start = dp_index * piece_width

    def own_piece(array, axis):
        return lax.dynamic_slice_in_dim(array, dp_start, piece_width, axis)

    def near_whole(sent, width):
        near = in_turn([array[:, 1, :width] for array in sent])
        return near.transpose(1, 0, 2).reshape(near.shape[1], -1)

    skip_near_new = near_whole(skip_sent, width_local)
    attn_near_new = near_whole(attn_sent, width_local)
    fc1_near_new = near_whole(fc1_sent, hidden_local)
    fc2_near_new = near_whole(fc2_sent, hidden_local)
    return (
        block_output,
        input_grad,
        skip_input_grad,
        own_piece(skip_sum, 2),
        own_piece(attn_sum[:3], 2).transpose(0, 2, 1),
        own_piece(attn_sum[3], 1),
        own_piece(fc1_sum[0], 1).T,
        own_piece(fc2_sum[0], 1),
        own_piece(vector_sum, 1),
        hidden_sum,
        skip_near_new,
        skip_far_new[:, 0],
        attn_far_new[:3, 0],
        attn_near_new[:3],
        attn_near_new[3],
        attn_far_new[3, 0],
        fc1_far_new[0, 0],
        fc1_near_new[0],
        fc2_near_new[0],
        fc2_far_new[0, 0],
        vector_new,
        hidden_new,
        skip_new,
        qkv_new,
        proj_new[0],
        fc1_new[0],
        fc2_new[0],
        vectors_new,
        hidden_bias_new,
        skip_new_low,
        qkv_new_low,
        proj_new_low[0],
        fc1_new_low[0],
        fc2_new_low[0],
        update_rms,
    )


def solution(mesh):
    placed = (
        P("dp", None),
        P("dp", None),
        P("dp"),
        P("dp"),
        P("dp"),
        P("dp", None),
        P(None, "mp", None),
        P(None, None, "mp"),
        P("mp", None),
        P(None, "mp"),
        P("mp", None),
        P(),
        P("mp"),
        P(),
        P(),
        P(),
        P(),
        P(),
        P(),
        P(),
        P(),
        P(),
        P(),
        P(),
        P("mp"),
    )
    return jax.shard_map(
        body,
        mesh=mesh,
        in_specs=placed,
        out_specs=(
            P("dp", None),
            P("dp", "mp"),
            P("dp", "mp"),
            P(None, "mp", "dp"),
            P(None, "dp", "mp"),
            P("mp", "dp"),
            P("dp", "mp"),
            P("mp", "dp"),
            P(None, "dp"),
            P("mp"),
            P(),
            P(),
            P(),
            P(),
            P(),
            P(),
            P(),
            P(),
            P(),
            P(),
            P(),
            P("mp"),
            P(None, "mp", None),
            P(None, None, "mp"),
            P("mp", None),
            P(None, "mp"),
            P("mp", None),
            P(),
            P("mp"),
            P(None, "mp", None),
            P(None, None, "mp"),
            P("mp", None),
            P(None, "mp"),
            P("mp", None),
            P(),
        ),
        check_vma=False,
    )
```

```python
import functools
import math

import jax
import jax.numpy as jnp
from jax import lax
from jax.experimental import pallas as pl
from jax.experimental.pallas import tpu as pltpu
from jax.sharding import PartitionSpec as P

D = 1152
HEAD_DIM = 72
FF = 4608
CLASSES = 1000
SEQ = 258


ln_eps = 1e-05
moment_eps = 1e-30
clip_level = 0.25
step_rate = 2.0
total_steps = 1000.0


def gelu_exact(inputs):
    return 0.5 * inputs * (1.0 + lax.erf(inputs * (1.0 / math.sqrt(2.0))))


def matmul(left_side, right_side):
    return jnp.dot(left_side, right_side, preferred_element_type=jnp.float32)


def norm_forward(inputs, norm_gain, norm_bias):
    centre = jnp.mean(inputs, -1, keepdims=True)
    centred = inputs - centre
    inverse = lax.rsqrt(jnp.mean(centred * centred, -1, keepdims=True) + ln_eps)
    normal = centred * inverse
    return (normal * norm_gain + norm_bias, normal, inverse)


def norm_backward(incoming, normal, inverse, norm_gain):
    scaled = incoming * norm_gain
    inner_mean = jnp.mean(scaled, -1, keepdims=True)
    proj_mean = jnp.mean(scaled * normal, -1, keepdims=True)
    return (
        inverse * (scaled - inner_mean - normal * proj_mean),
        jnp.sum(incoming * normal, 0),
        jnp.sum(incoming, 0),
    )


def adafactor(
    grad_pieces,
    weight_pieces,
    starts,
    row_states,
    col_states,
    vector_piece,
    vector_weight,
    vector_state,
    hidden_piece,
    hidden_weight,
    hidden_state,
    first_mask,
    reduce_moments,
    reduce_norm,
):
    full_shapes = ((D, D), (D, D), (D, D), (D, FF), (FF, D))
    tensor_sizes = (2.0 * D * D, 3.0 * D * D, 1.0 * D * D, 1.0 * D * FF, 1.0 * FF * D)
    zero_start = jnp.zeros((), jnp.int32)
    row_parts = []
    col_parts = []
    weight_sq = []
    for position in range(5):
        grad_piece = grad_pieces[position]
        leading = grad_piece.shape[0]
        squares = grad_piece * grad_piece + moment_eps
        row_zero = jnp.zeros((leading, full_shapes[position][0]), jnp.float32)
        col_zero = jnp.zeros((leading, full_shapes[position][1]), jnp.float32)
        row_parts.append(
            lax.dynamic_update_slice(
                row_zero, jnp.sum(squares, 2), (zero_start, starts[position][0])
            ).reshape(-1)
        )
        col_parts.append(
            lax.dynamic_update_slice(
                col_zero, jnp.sum(squares, 1), (zero_start, starts[position][1])
            ).reshape(-1)
        )
        weight_sq.append(jnp.sum(weight_pieces[position] * weight_pieces[position])[None])
    weight_sq.append(jnp.sum(vector_weight * vector_weight, 1) * first_mask)
    weight_sq.append(jnp.sum(hidden_weight * hidden_weight)[None])
    row_total, col_total, weight_total = reduce_moments(
        jnp.concatenate(row_parts), jnp.concatenate(col_parts), jnp.concatenate(weight_sq)
    )
    row_news = []
    col_news = []
    updates = []
    step_sq = jnp.zeros((), jnp.float32)
    row_offset = 0
    col_offset = 0
    for position in range(5):
        grad_piece = grad_pieces[position]
        leading = grad_piece.shape[0]
        rows_full, cols_full = full_shapes[position]
        row_sum = row_total[row_offset : row_offset + leading * rows_full].reshape(
            leading, rows_full
        )
        col_sum = col_total[col_offset : col_offset + leading * cols_full].reshape(
            leading, cols_full
        )
        row_offset = row_offset + leading * rows_full
        col_offset = col_offset + leading * cols_full
        row_new = 0.5 * row_states[position] + 0.5 * (row_sum / cols_full)
        col_new = 0.5 * col_states[position] + 0.5 * (col_sum / rows_full)
        row_piece = lax.dynamic_slice(
            row_new, (zero_start, starts[position][0]), (leading, grad_piece.shape[1])
        )
        col_piece = lax.dynamic_slice(
            col_new, (zero_start, starts[position][1]), (leading, grad_piece.shape[2])
        )
        row_mean = jnp.mean(row_new, 1)
        update = grad_piece * lax.rsqrt(
            row_piece[:, :, None] * col_piece[:, None, :] / row_mean[:, None, None]
        )
        step_sq = step_sq + jnp.sum(update * update)
        row_news.append(row_new)
        col_news.append(col_new)
        updates.append(update)
    vector_new = 0.5 * vector_state + 0.5 * (vector_piece * vector_piece + moment_eps)
    vector_update = vector_piece * lax.rsqrt(vector_new)
    hidden_new = 0.5 * hidden_state + 0.5 * (hidden_piece * hidden_piece + moment_eps)
    hidden_update = hidden_piece * lax.rsqrt(hidden_new)
    step_sq = (
        step_sq
        + jnp.sum(vector_update * vector_update) * first_mask
        + jnp.sum(hidden_update * hidden_update)
    )
    step_total = reduce_norm(step_sq)
    param_count = 6.0 * D * D + 2.0 * D * FF + 7.0 * D + FF
    update_rms = jnp.sqrt(step_total / param_count)
    divisor = jnp.maximum(1.0, update_rms / clip_level)
    new_weights = []
    for position in range(5):
        weight_rms = jnp.sqrt(weight_total[position] / tensor_sizes[position])
        new_weights.append(
            weight_pieces[position]
            - step_rate * jnp.maximum(0.001, weight_rms) * updates[position] / divisor
        )
    vector_rms = jnp.sqrt(weight_total[5:12] / D)[:, None]
    vector_weight_new = (
        vector_weight - step_rate * jnp.maximum(0.001, vector_rms) * vector_update / divisor
    )
    hidden_rms = jnp.sqrt(weight_total[12] / FF)
    hidden_weight_new = (
        hidden_weight - step_rate * jnp.maximum(0.001, hidden_rms) * hidden_update / divisor
    )
    return (
        new_weights,
        row_news,
        col_news,
        vector_new,
        vector_weight_new,
        hidden_new,
        hidden_weight_new,
        update_rms,
    )


def body_tensor(
    block_input,
    skip_input,
    timesteps,
    class_labels,
    loss_weights,
    grad_output,
    skip_weight,
    qkv_weight,
    proj_weight,
    fc1_weight,
    fc2_weight,
    vectors,
    hidden_bias,
    skip_rows,
    skip_cols,
    qkv_rows,
    qkv_cols,
    proj_rows,
    proj_cols,
    fc1_rows,
    fc1_cols,
    fc2_rows,
    fc2_cols,
    vector_moments,
    hidden_moments,
):
    image_count = timesteps.shape[0]
    width_local = qkv_weight.shape[2]
    heads_local = width_local // HEAD_DIM
    hidden_local = fc1_weight.shape[1]
    mp_index = lax.axis_index("mp")
    dp_index = lax.axis_index("dp")
    dp_count = lax.axis_size("dp")
    first_mask = (mp_index == 0).astype(jnp.float32)
    feature_start = mp_index * skip_weight.shape[1]
    block_local = lax.dynamic_slice_in_dim(block_input, feature_start, skip_weight.shape[1], 1)
    skip_local = lax.dynamic_slice_in_dim(skip_input, feature_start, skip_weight.shape[1], 1)
    angles = (timesteps.astype(jnp.float32) + 0.5) * (0.5 * math.pi / total_steps)
    alpha_sq = jnp.square(jnp.cos(angles))
    sigma_sq = jnp.square(jnp.sin(angles))
    snr_weight = 5.0 * sigma_sq / jnp.maximum(alpha_sq, 5.0 * sigma_sq)
    base_weight = loss_weights * snr_weight
    one_hot = (class_labels[:, None] == jnp.arange(CLASSES, dtype=jnp.int32)[None, :]).astype(
        jnp.float32
    )
    class_counts, weight_total = lax.psum((jnp.sum(one_hot, 0), jnp.sum(base_weight)), "dp")
    own_count = jnp.dot(one_hot, class_counts, precision=lax.Precision.HIGHEST)
    item_weight = base_weight * (image_count * dp_count / weight_total) * lax.rsqrt(own_count)
    upstream = (
        grad_output.astype(jnp.float32).reshape(image_count, SEQ, D) * item_weight[:, None, None]
    ).reshape(-1, D)
    skip_low = skip_weight.astype(jnp.bfloat16)
    qkv_low = qkv_weight.astype(jnp.bfloat16)
    proj_low = proj_weight.astype(jnp.bfloat16)
    fc1_low = fc1_weight.astype(jnp.bfloat16)
    fc2_low = fc2_weight.astype(jnp.bfloat16)
    joined = (
        lax.psum(matmul(block_local, skip_low[0]) + matmul(skip_local, skip_low[1]), "mp")
        + vectors[4]
    )
    normed, normal_one, inverse_one = norm_forward(joined, vectors[0], vectors[1])
    normed_low = normed.astype(jnp.bfloat16)
    qkv_all = jnp.einsum(
        "td,sde->ste", normed_low, qkv_low, preferred_element_type=jnp.float32
    ).astype(jnp.bfloat16)
    heads_view = qkv_all.reshape(3, image_count, SEQ, heads_local, HEAD_DIM)
    query_low = heads_view[0]
    key_low = heads_view[1]
    value_low = heads_view[2]
    score_scale = HEAD_DIM ** (-0.5)

    def score_block():
        return (
            jnp.einsum("iqhe,ikhe->ihqk", query_low, key_low, preferred_element_type=jnp.float32)
            * score_scale
        )

    scores = score_block()
    score_top = jnp.max(scores, -1, keepdims=True)
    expo_scores = jnp.exp(scores - score_top)
    expo_total = jnp.sum(expo_scores, -1, keepdims=True)
    weights_low = (expo_scores / expo_total).astype(jnp.bfloat16)
    log_total = score_top + jnp.log(expo_total)
    attended = (
        jnp.einsum("ihqk,ikhe->iqhe", weights_low, value_low, preferred_element_type=jnp.float32)
        .astype(jnp.bfloat16)
        .reshape(-1, width_local)
    )
    residual = joined + lax.psum(matmul(attended, proj_low), "mp") + vectors[5]
    normed_two, normal_two, inverse_two = norm_forward(residual, vectors[2], vectors[3])
    normed_two_low = normed_two.astype(jnp.bfloat16)
    pre_act = matmul(normed_two_low, fc1_low) + hidden_bias
    activated, gelu_pull = jax.vjp(gelu_exact, pre_act)
    activated_low = activated.astype(jnp.bfloat16)
    block_output = (residual + lax.psum(matmul(activated_low, fc2_low), "mp") + vectors[6]).astype(
        jnp.bfloat16
    )
    upstream_low = upstream.astype(jnp.bfloat16)
    fc2_grad = jnp.einsum(
        "tf,td->fd", activated_low, upstream_low, preferred_element_type=jnp.float32
    )
    fc2_bias_grad = jnp.sum(upstream, 0)
    act_grad = jnp.einsum("td,fd->tf", upstream_low, fc2_low, preferred_element_type=jnp.float32)
    pre_grad = gelu_pull(act_grad)[0]
    pre_low = pre_grad.astype(jnp.bfloat16)
    fc1_grad = jnp.einsum("td,tf->df", normed_two_low, pre_low, preferred_element_type=jnp.float32)
    hidden_grad = jnp.sum(pre_grad, 0)
    norm_two_in = lax.psum(
        jnp.einsum("tf,df->td", pre_low, fc1_low, preferred_element_type=jnp.float32), "mp"
    )
    back_two, gain_two_grad, bias_two_grad = norm_backward(
        norm_two_in, normal_two, inverse_two, vectors[2]
    )
    residual_grad = upstream + back_two
    proj_bias_grad = jnp.sum(residual_grad, 0)
    residual_low = residual_grad.astype(jnp.bfloat16)
    proj_grad = jnp.einsum("te,td->ed", attended, residual_low, preferred_element_type=jnp.float32)
    attended_grad = jnp.einsum(
        "td,ed->te", residual_low, proj_low, preferred_element_type=jnp.float32
    ).astype(jnp.bfloat16)
    attended_grad = attended_grad.reshape(image_count, SEQ, heads_local, HEAD_DIM)
    scores = score_block()
    probs_exact = jnp.exp(scores - log_total)
    prob_grad = jnp.einsum(
        "iqhe,ikhe->ihqk", attended_grad, value_low, preferred_element_type=jnp.float32
    )
    score_grad = (
        probs_exact * (prob_grad - jnp.sum(probs_exact * prob_grad, -1, keepdims=True))
    ).astype(jnp.bfloat16)
    query_grad = (
        jnp.einsum("ihqk,ikhe->iqhe", score_grad, key_low, preferred_element_type=jnp.float32)
        * score_scale
    )
    key_grad = (
        jnp.einsum("ihqk,iqhe->ikhe", score_grad, query_low, preferred_element_type=jnp.float32)
        * score_scale
    )
    value_grad = jnp.einsum(
        "ihqk,iqhe->ikhe", weights_low, attended_grad, preferred_element_type=jnp.float32
    )
    qkv_grad_low = (
        jnp.stack([query_grad, key_grad, value_grad])
        .astype(jnp.bfloat16)
        .reshape(3, -1, width_local)
    )
    qkv_grad = jnp.einsum(
        "td,ste->sde", normed_low, qkv_grad_low, preferred_element_type=jnp.float32
    )
    norm_one_in = lax.psum(
        jnp.einsum("ste,sde->td", qkv_grad_low, qkv_low, preferred_element_type=jnp.float32), "mp"
    )
    back_one, gain_one_grad, bias_one_grad = norm_backward(
        norm_one_in, normal_one, inverse_one, vectors[0]
    )
    joined_grad = residual_grad + back_one
    skip_bias_grad = jnp.sum(joined_grad, 0)
    joined_low = joined_grad.astype(jnp.bfloat16)
    skip_grad = jnp.stack(
        [
            jnp.einsum("tc,td->cd", block_local, joined_low, preferred_element_type=jnp.float32),
            jnp.einsum("tc,td->cd", skip_local, joined_low, preferred_element_type=jnp.float32),
        ]
    )
    input_grad = jnp.einsum(
        "td,cd->tc", joined_low, skip_low[0], preferred_element_type=jnp.float32
    )
    skip_input_grad = jnp.einsum(
        "td,cd->tc", joined_low, skip_low[1], preferred_element_type=jnp.float32
    )
    vector_grad = jnp.stack(
        [
            gain_one_grad,
            bias_one_grad,
            gain_two_grad,
            bias_two_grad,
            skip_bias_grad,
            proj_bias_grad,
            fc2_bias_grad,
        ]
    )
    row_states = [skip_rows, qkv_rows, proj_rows[None], fc1_rows[None], fc2_rows[None]]
    col_states = [skip_cols, qkv_cols, proj_cols[None], fc1_cols[None], fc2_cols[None]]
    piece_width = D // dp_count
    dp_start = dp_index * piece_width
    zero_start = jnp.zeros((), jnp.int32)
    summed = lax.psum(
        (skip_grad, qkv_grad, proj_grad, fc1_grad, fc2_grad, vector_grad, hidden_grad), "dp"
    )

    def moments_mp(row_all, col_all, squares_all):
        return lax.psum((row_all, col_all, squares_all), "mp")

    def norm_mp(step_sq):
        return lax.psum(step_sq, "mp")

    grad_pieces = [summed[0], summed[1], summed[2][None], summed[3][None], summed[4][None]]
    weight_pieces = [skip_weight, qkv_weight, proj_weight[None], fc1_weight[None], fc2_weight[None]]
    starts = [
        (mp_index * width_local, zero_start),
        (zero_start, mp_index * width_local),
        (mp_index * width_local, zero_start),
        (zero_start, mp_index * hidden_local),
        (mp_index * hidden_local, zero_start),
    ]
    results = adafactor(
        grad_pieces,
        weight_pieces,
        starts,
        row_states,
        col_states,
        summed[5],
        vectors,
        vector_moments,
        summed[6],
        hidden_bias,
        hidden_moments,
        first_mask,
        moments_mp,
        norm_mp,
    )
    (
        new_weights,
        row_news,
        col_news,
        vector_state_new,
        vectors_new,
        hidden_state_new,
        hidden_new,
        update_rms,
    ) = results
    skip_new = new_weights[0]
    qkv_new = new_weights[1]
    proj_new = new_weights[2][0]
    fc1_new = new_weights[3][0]
    fc2_new = new_weights[4][0]
    skip_grad_out = lax.dynamic_slice_in_dim(summed[0], dp_start, piece_width, 2)
    qkv_grad_out = lax.dynamic_slice_in_dim(summed[1], dp_start, piece_width, 1)
    proj_grad_out = lax.dynamic_slice_in_dim(summed[2], dp_start, piece_width, 1)
    fc1_grad_out = lax.dynamic_slice_in_dim(summed[3], dp_start, piece_width, 0)
    fc2_grad_out = lax.dynamic_slice_in_dim(summed[4], dp_start, piece_width, 1)
    vector_grad_out = lax.dynamic_slice_in_dim(summed[5], dp_start, piece_width, 1)
    hidden_grad_out = summed[6]
    return (
        block_output,
        input_grad,
        skip_input_grad,
        skip_grad_out,
        qkv_grad_out,
        proj_grad_out,
        fc1_grad_out,
        fc2_grad_out,
        vector_grad_out,
        hidden_grad_out,
        row_news[0],
        col_news[0],
        row_news[1],
        col_news[1],
        row_news[2][0],
        col_news[2][0],
        row_news[3][0],
        col_news[3][0],
        row_news[4][0],
        col_news[4][0],
        vector_state_new,
        hidden_state_new,
        skip_new,
        qkv_new,
        proj_new,
        fc1_new,
        fc2_new,
        vectors_new,
        hidden_new,
        skip_new.astype(jnp.bfloat16),
        qkv_new.astype(jnp.bfloat16),
        proj_new.astype(jnp.bfloat16),
        fc1_new.astype(jnp.bfloat16),
        fc2_new.astype(jnp.bfloat16),
        update_rms,
    )


def body(*operands):
    images = operands[2].shape[0]
    if images % lax.axis_size("mp") == 0 and lax.axis_size("dp") == 8:
        return body_data(*operands)
    return body_tensor(*operands)


small_cost = pl.CostEstimate(flops=0, bytes_accessed=1024, transcendentals=0)


def to_core(array):
    return lax.ppermute(array, "dp", [(i, i ^ 1) for i in range(8)])


def to_x(array):
    return lax.ppermute(array, "dp", [(i, i ^ 2) for i in range(8)])


def to_y(array):
    return lax.ppermute(array, "dp", [(i, i ^ 4) for i in range(8)])


def turn_mp(array, shift):
    count = lax.axis_size("mp")
    return lax.ppermute(array, "mp", [(i, (i + shift) % count) for i in range(count)])


def pick(array, index, axis):
    return lax.dynamic_index_in_dim(array, index, axis, keepdims=False)


def assemble(steps, targets, core, rows, blocks, split):
    arrays = []
    for step in steps:
        for array, _ in step:
            if not any(array is other for other in arrays):
                arrays.append(array)
    place = [
        [(next(n for n, other in enumerate(arrays) if other is array), k) for array, k in step]
        for step in steps
    ]
    table = jnp.stack([jnp.asarray(v, jnp.int32) for v in [*targets, core]])
    depth = 4
    outs = 2 if split < blocks else 1

    def kernel(table_ref, *refs):
        sources = refs[: len(arrays)]
        wholes = refs[len(arrays) : len(arrays) + outs]
        wide, narrow, in_sem, out_sem = refs[len(arrays) + outs :]
        half = rows // 2
        first = pl.multiple_of(table_ref[len(steps)] * half, half)
        second = pl.multiple_of(half - first, half)

        def fetch(step):
            slot = step % depth
            if len(place[step]) == 1:
                ((n, k),) = place[step]
                return [pltpu.make_async_copy(sources[n].at[k], wide.at[slot], in_sem.at[slot, 0])]
            copies = []
            for part, ((n, k), start) in enumerate(zip(place[step], (first, second))):
                spot = wide.at[slot, pl.ds(start, half)]
                copies.append(pltpu.make_async_copy(sources[n].at[k], spot, in_sem.at[slot, part]))
            return copies

        def leave(step, whole, spot):
            slot = step % depth
            return pltpu.make_async_copy(narrow.at[slot], whole.at[spot], out_sem.at[slot])

        for step in range(len(steps) + depth - 1):
            if step < len(steps):
                for copy in fetch(step):
                    copy.start()
            step = step - (depth - 1)
            if step < 0:
                continue
            slot = step % depth
            for copy in fetch(step):
                copy.wait()
            if step >= depth:
                leave(step - depth, wholes[0], 0).wait()
            narrow[slot] = wide[slot].astype(jnp.bfloat16)
            spot = table_ref[step]
            if outs == 1:
                leave(step, wholes[0], spot).start()
            else:

                @pl.when(spot < split)
                def _():
                    leave(step, wholes[0], spot).start()

                @pl.when(spot >= split)
                def _():
                    leave(step, wholes[1], spot - split).start()

        for step in range(max(0, len(steps) - depth), len(steps)):
            leave(step, wholes[0], 0).wait()

    shapes = [jax.ShapeDtypeStruct((split, rows, D), jnp.bfloat16)]
    if outs == 2:
        shapes.append(jax.ShapeDtypeStruct((blocks - split, rows, D), jnp.bfloat16))
    anywhere = pl.BlockSpec(memory_space=pl.ANY)
    return pl.pallas_call(
        kernel,
        in_specs=[pl.BlockSpec(memory_space=pltpu.SMEM)] + [anywhere] * len(arrays),
        out_specs=[anywhere] * outs,
        out_shape=shapes,
        scratch_shapes=[
            pltpu.VMEM((depth, rows, D), jnp.float32),
            pltpu.VMEM((depth, rows, D), jnp.bfloat16),
            pltpu.SemaphoreType.DMA((depth, 2)),
            pltpu.SemaphoreType.DMA((depth,)),
        ],
        compiler_params=pltpu.CompilerParams(vmem_limit_bytes=32 * 1024 * 1024),
        cost_estimate=small_cost,
    )(table, *arrays)


class Order:
    def __init__(self):
        self.token = None

    def after(self, *arrays):
        if self.token is not None:
            arrays = lax.optimization_barrier((*arrays, self.token))[:-1]
        return arrays if len(arrays) > 1 else arrays[0]

    def mark(self, *arrays):
        arrays = self.after(*arrays)
        self.token = arrays[0] if isinstance(arrays, tuple) else arrays
        return arrays


def swap_plane(order, for_x, for_y):
    for_x, for_y = order.after(for_x, for_y)
    return to_x(for_x), to_y(for_y)


def in_turn(arrays):
    count = len(arrays)
    twice = jnp.stack(list(arrays[::-1]) * 2)
    return lax.dynamic_slice_in_dim(twice, count - 1 - lax.axis_index("mp"), count, 0)


def gather_deep(array):
    return in_turn([array] + [turn_mp(array, shift) for shift in range(1, lax.axis_size("mp"))])


def sum_flat(array):
    for swap in (to_core, to_x, to_y):
        array = array + swap(array)
    return array


def bring(order, shard, quarter, core):
    count = lax.axis_size("mp")
    part = pick(pick(shard.reshape(4, 2, -1, D), quarter, 0), core, 0)
    return lax.all_gather(order.after(part), "mp")


def others(whole):
    count = lax.axis_size("mp")
    twice = jnp.concatenate([whole, whole], 0)
    return lax.dynamic_slice_in_dim(twice, lax.axis_index("mp") + 1, count - 1, 0)


def assemble_weight(shard, parts, swapped, core, split):
    count = lax.axis_size("mp")
    rows = shard.shape[0] // 8

    def spot(shard_index, quarter):
        shard_index = lax.rem(lax.axis_index("mp") + shard_index, count)
        return quarter * count + shard_index

    if swapped is None:
        mine = pick(shard.reshape(4, 2, rows, D), core, 1)
    else:
        mine = shard.reshape(4, 2 * rows, D)
    steps = [((mine, n),) for n in range(4)]
    targets = [spot(0, n) for n in range(4)]
    for n, (array, quarter, first) in enumerate(parts):
        for k in range(array.shape[0]):
            steps.append(((array, k),) if swapped is None else ((array, k), (swapped[n], k)))
            targets.append(spot(first + k, quarter))
    rows = mine.shape[1]
    whole = assemble(steps, targets, core, rows, count * 4, split or count * 4)
    return [array.reshape(-1, D) for array in whole]


def cut_corner(grad, quarter):
    corner = pick(grad, quarter ^ 3, 0)
    half = corner.shape[0] // 2
    return corner[:half], corner[half:]


def cut_sides(grad, quarter, add_y, add_x):
    half = add_y.shape[0]
    for_y = pick(grad, quarter ^ 2, 0)
    for_x = pick(grad, quarter ^ 1, 0)
    for_y = jnp.concatenate([for_y[:half] + add_y, for_y[half:]], 0)
    for_x = jnp.concatenate([for_x[:half], for_x[half:] + add_x], 0)
    return for_x, for_y


def sum_deep(order, grad, quarter, from_x, from_y):
    own = order.mark(pick(grad, quarter, 0) + from_x + from_y)
    return lax.psum_scatter(own, "mp", scatter_dimension=0, tiled=False)


def place_rows(pieces, rows, near_state=None):
    arrays = []
    for array, *_ in pieces:
        if not any(array is other for other in arrays):
            arrays.append(array)
    steps = [
        (next(n for n, other in enumerate(arrays) if other is array), first, amount)
        for array, first, amount, _ in pieces
    ]
    table = jnp.stack([jnp.asarray(spot, jnp.int32) for *_, spot in pieces])

    def kernel(table_ref, *refs):
        sources = refs[: len(arrays)]
        sems = refs[-1]
        if near_state is None:
            out_ref = refs[len(arrays)]
        else:
            state_ref, out_ref, moment_ref = refs[len(arrays) : -1]
        copies = []
        for step, (n, first, amount) in enumerate(steps):
            spot = pl.multiple_of(table_ref[step], 8)
            source = sources[n].at[pl.ds(first, amount)]
            copies.append(
                pltpu.make_async_copy(source, out_ref.at[pl.ds(spot, amount)], sems.at[step])
            )
        for copy in copies:
            copy.start()
        for copy in copies:
            copy.wait()
        if near_state is None:
            return
        leading, length = near_state.shape
        chunk = length if length < 384 else 384
        for lead in range(leading):
            total = jnp.zeros((1, D), jnp.float32)
            for first in range(0, length, chunk):
                grad = out_ref[lead * length + first : lead * length + first + chunk]
                squares = grad * grad + moment_eps
                total = total + jnp.sum(squares, 0, keepdims=True)
                near = 0.5 * state_ref[lead, :1, first : first + chunk]
                near = near + 0.5 * (as_row(lanes_of(squares)) / D)
                moment_ref[lead, 1:2, first : first + chunk] = near
            moment_ref[lead, :1] = total
            if length < D:
                moment_ref[lead, 1:2, length:] = jnp.zeros((1, D - length), jnp.float32)

    vmem = pl.BlockSpec(memory_space=pltpu.VMEM)
    in_specs = [pl.BlockSpec(memory_space=pltpu.SMEM)]
    in_specs = in_specs + [pl.BlockSpec(memory_space=pl.ANY)] * len(arrays)
    out_specs, shapes = [vmem], [jax.ShapeDtypeStruct((rows, D), jnp.float32)]
    operands = [table, *arrays]
    if near_state is not None:
        leading, length = near_state.shape
        in_specs.append(vmem)
        operands.append(near_state.reshape(leading, 1, length))
        out_specs.append(vmem)
        shapes.append(jax.ShapeDtypeStruct((leading, 2, D), jnp.float32))
    result = pl.pallas_call(
        kernel,
        in_specs=in_specs,
        out_specs=out_specs,
        out_shape=shapes,
        scratch_shapes=[pltpu.SemaphoreType.DMA((len(steps),))],
        compiler_params=pltpu.CompilerParams(vmem_limit_bytes=40 * 1024 * 1024),
        cost_estimate=small_cost,
    )(*operands)
    return result[0] if near_state is None else result


def add_half(grads, given, core):
    rows = grads[0].shape[2]
    amounts = [array.shape[0] for array in grads]
    firsts = [sum(amounts[:n]) for n in range(len(amounts))]

    def kernel(core_ref, *refs):
        for n, (first, amount) in enumerate(zip(firsts, amounts)):

            @pl.when((pl.program_id(0) >= first) & (pl.program_id(0) < first + amount))
            def _():
                refs[-1][...] = refs[n][0] + refs[len(grads) + n][...]

    def at(first, amount):
        return lambda step: jnp.clip(step - first, 0, amount - 1)

    spots = [at(*pair) for pair in zip(firsts, amounts)]
    own_specs = [
        pl.BlockSpec((1, 1, rows, D), lambda step, core_ref, at=at: (at(step), core_ref[0], 0, 0))
        for at in spots
    ]
    given_specs = [
        pl.BlockSpec((1, rows, D), lambda step, core_ref, at=at: (at(step), 0, 0)) for at in spots
    ]
    total = sum(amounts)
    return pl.pallas_call(
        kernel,
        grid_spec=pltpu.PrefetchScalarGridSpec(
            num_scalar_prefetch=1,
            grid=(total,),
            in_specs=own_specs + given_specs,
            out_specs=pl.BlockSpec((1, rows, D), lambda step, core_ref: (step, 0, 0)),
        ),
        out_shape=jax.ShapeDtypeStruct((total, rows, D), jnp.float32),
        compiler_params=pltpu.CompilerParams(vmem_limit_bytes=40 * 1024 * 1024),
        cost_estimate=small_cost,
    )(core[None], *grads, *given)


def order_tokens(arrays, mp_index):
    count = len(arrays)
    tokens, width = arrays[0].shape[0], arrays[0].shape[1] // 2

    def kernel(place_ref, *refs):
        left_ref, right_ref, held, sems = refs[count:]

        def copy(n, index):
            return pltpu.make_async_copy(refs[n], held.at[index], sems.at[index])

        for index in range(count):
            for n in range(count):

                @pl.when(lax.rem(place_ref[0] + count - index, count) == n)
                def _():
                    copy(n, index).start()

        for index in range(count):
            copy(0, index).wait()
            rows = slice(index * tokens, (index + 1) * tokens)
            left_ref[rows] = held[index, :, :width]
            right_ref[rows] = held[index, :, width:]

    vmem = pl.BlockSpec(memory_space=pltpu.VMEM)
    shape = jax.ShapeDtypeStruct((count * tokens, width), jnp.float32)
    return pl.pallas_call(
        kernel,
        in_specs=[pl.BlockSpec(memory_space=pltpu.SMEM)]
        + [pl.BlockSpec(memory_space=pl.ANY)] * count,
        out_specs=[vmem, vmem],
        out_shape=[shape, shape],
        scratch_shapes=[
            pltpu.VMEM((count, tokens, 2 * width), jnp.float32),
            pltpu.SemaphoreType.DMA((count,)),
        ],
        compiler_params=pltpu.CompilerParams(vmem_limit_bytes=40 * 1024 * 1024),
        cost_estimate=small_cost,
    )(mp_index[None], *arrays)


def lanes_of(array):
    total = array[:, :128]
    for tile in range(1, array.shape[1] // 128):
        total = total + array[:, tile * 128 : (tile + 1) * 128]
    return total


def as_row(column):
    return jnp.sum(column.T, 0, keepdims=True)


def as_column(row):
    return jnp.broadcast_to(row, (128, row.shape[1])).T


def scale_kernel(count, by_rows, place_ref, grad_ref, state_ref, before_ref, *refs):
    sources = refs[:count]
    far_ref, scale_ref, near_ref, step_ref = refs[count:]
    rows = grad_ref.shape[1]
    total = jnp.zeros((1, D), jnp.float32)
    near_sum = jnp.zeros((1, 1), jnp.float32)
    for index in range(count):
        part = jnp.zeros((2, D), jnp.float32)
        for shift in range(count):
            part = jnp.where(place_ref[0] == (index + shift) % count, sources[shift][0], part)
        total = total + part[:1]
        near_sum = near_sum + jnp.sum(part[1:], 1, keepdims=True)
    far = 0.5 * state_ref[0] + 0.5 * (total / (count * rows))
    far_ref[0] = far
    lead = pl.program_id(0)
    near_mean = near_sum / (count * rows)
    far_mean = jnp.sum(far, 1, keepdims=True) / D
    if all(by_rows):
        mean = near_mean
    elif not any(by_rows):
        mean = far_mean
    else:
        split = by_rows.index(True)
        mean = jnp.where(lead >= split, near_mean, far_mean)
    far_scale = lax.rsqrt(far)
    near_scale = as_column(lax.rsqrt(sources[0][0][1:2, :rows] / mean))
    scale_ref[0] = far_scale
    near_ref[0] = near_scale
    step = grad_ref[0] * far_scale
    step = lanes_of(step * step) * near_scale * near_scale

    @pl.when(lead == 0)
    def _():
        step_ref[...] = before_ref[...]

    step_ref[...] += jnp.sum(step.reshape(rows // 8, 8, 128), 0)


def scales(grad, far_state, before, sources, first, mp_index, by_rows):
    leading, rows, _ = grad.shape
    count = len(sources)
    small = pl.BlockSpec((1, 2, D), lambda i: (i + first, 0, 0))
    line = pl.BlockSpec((1, 1, D), lambda i: (i, 0, 0))
    return pl.pallas_call(
        functools.partial(scale_kernel, count, by_rows),
        grid=(leading,),
        in_specs=[
            pl.BlockSpec(memory_space=pltpu.SMEM),
            pl.BlockSpec((1, rows, D), lambda i: (i, 0, 0)),
            line,
            pl.BlockSpec((8, 128), lambda i: (0, 0)),
        ]
        + [small] * count,
        out_specs=[
            line,
            line,
            pl.BlockSpec((1, rows, 128), lambda i: (i, 0, 0)),
            pl.BlockSpec((8, 128), lambda i: (0, 0)),
        ],
        out_shape=[
            jax.ShapeDtypeStruct((leading, 1, D), jnp.float32),
            jax.ShapeDtypeStruct((leading, 1, D), jnp.float32),
            jax.ShapeDtypeStruct((leading, rows, 128), jnp.float32),
            jax.ShapeDtypeStruct((8, 128), jnp.float32),
        ],
        compiler_params=pltpu.CompilerParams(vmem_limit_bytes=40 * 1024 * 1024),
        cost_estimate=small_cost,
    )(mp_index[None], grad, far_state.reshape(leading, 1, D), before, *sources)


param_count = 6.0 * D * D + 2.0 * D * FF + 7.0 * D + FF


def renew_kernel(turned, count, rate_ref, weight_ref, grad_ref, far_ref, near_ref, *refs):
    new_ref, low_ref = refs[count:]
    total = refs[0][...]
    for ref in refs[1:count]:
        total = total + ref[...]
    total = jnp.sum(jnp.sum(total, 0, keepdims=True), 1, keepdims=True) + rate_ref[1]
    divisor = jnp.maximum(1.0, jnp.sqrt(total / param_count) / clip_level)
    step = grad_ref[0] * far_ref[0] * (near_ref[0][:, :1] * (rate_ref[0] / divisor))
    new = weight_ref[0] - (step.T if turned else step)
    new_ref[0] = new
    low_ref[0] = new.astype(jnp.bfloat16)


def renew(weight, grad, far_scale, near_scale, rate, steps, turned, first=0):
    leading, rows = weight.shape[0], grad.shape[1]
    if turned:
        width = 384
        grid = (leading, D // width)
        weight_spec = pl.BlockSpec((1, width, rows), lambda i, j: (i, j, 0))
        grad_spec = pl.BlockSpec((1, rows, width), lambda i, j: (i + first, 0, j))
        far_spec = pl.BlockSpec((1, 1, width), lambda i, j: (i + first, 0, j))
        near_spec = pl.BlockSpec((1, rows, 128), lambda i, j: (i + first, 0, 0))
    else:
        height = min(rows, 288)
        grid = (leading, rows // height)
        weight_spec = pl.BlockSpec((1, height, D), lambda i, j: (i, j, 0))
        grad_spec = pl.BlockSpec((1, height, D), lambda i, j: (i + first, j, 0))
        far_spec = pl.BlockSpec((1, 1, D), lambda i, j: (i + first, 0, 0))
        near_spec = pl.BlockSpec((1, height, 128), lambda i, j: (i + first, j, 0))
    return pl.pallas_call(
        functools.partial(renew_kernel, turned, len(steps)),
        grid=grid,
        in_specs=[pl.BlockSpec(memory_space=pltpu.SMEM), weight_spec, grad_spec, far_spec, near_spec]
        + [pl.BlockSpec((8, 128), lambda i, j: (0, 0))] * len(steps),
        out_specs=[weight_spec, weight_spec],
        out_shape=[
            jax.ShapeDtypeStruct(weight.shape, jnp.float32),
            jax.ShapeDtypeStruct(weight.shape, jnp.bfloat16),
        ],
        compiler_params=pltpu.CompilerParams(vmem_limit_bytes=40 * 1024 * 1024),
        cost_estimate=small_cost,
    )(rate, weight, grad, far_scale, near_scale, *steps)


def head_windows():
    spans = []
    for head in range(D // HEAD_DIM):
        first = head * HEAD_DIM
        start = first // 128 * 128
        stop = -(-(first + HEAD_DIM) // 128) * 128
        spans.append((first, start, stop - start))
    return spans


def head_mask(first, start, width):
    lanes = start + lax.broadcasted_iota(jnp.int32, (SEQ, width), 1)
    return (lanes >= first) & (lanes < first + HEAD_DIM)


def dot_nt(left_side, right_side):
    return lax.dot_general(
        left_side, right_side, (((1,), (1,)), ((), ())), preferred_element_type=jnp.float32
    )


def attend_kernel(qkv_ref, out_ref, total):
    total[...] = jnp.zeros_like(total)
    for first, start, width in head_windows():
        keep = head_mask(first, start, width)
        query = qkv_ref[0, :, start : start + width]
        key = jnp.where(keep, qkv_ref[0, :, D + start : D + start + width], 0)
        value = jnp.where(keep, qkv_ref[0, :, 2 * D + start : 2 * D + start + width], 0)
        scores = dot_nt(query, key) * HEAD_DIM ** (-0.5)
        expo = jnp.exp(scores - jnp.max(scores, 1, keepdims=True))
        probs = (expo / jnp.sum(expo, 1, keepdims=True)).astype(jnp.bfloat16)
        total[:, start : start + width] += matmul(probs, value)
    out_ref[0] = total[...].astype(jnp.bfloat16)


def attend(qkv):
    images = qkv.shape[0]
    return pl.pallas_call(
        attend_kernel,
        grid=(images,),
        in_specs=[pl.BlockSpec((1, SEQ, 3 * D), lambda i: (i, 0, 0))],
        out_specs=pl.BlockSpec((1, SEQ, D), lambda i: (i, 0, 0)),
        out_shape=jax.ShapeDtypeStruct((images, SEQ, D), jnp.bfloat16),
        scratch_shapes=[pltpu.VMEM((SEQ, D), jnp.float32)],
        compiler_params=pltpu.CompilerParams(vmem_limit_bytes=40 * 1024 * 1024),
        cost_estimate=small_cost,
    )(qkv)


def attend_back_kernel(qkv_ref, grad_ref, out_ref, query_sum, key_sum, value_sum):
    scale = HEAD_DIM ** (-0.5)
    for ref in (query_sum, key_sum, value_sum):
        ref[...] = jnp.zeros_like(ref)
    for first, start, width in head_windows():
        span = slice(start, start + width)
        keep = head_mask(first, start, width)
        query = jnp.where(keep, qkv_ref[0, :, span], 0)
        key = jnp.where(keep, qkv_ref[0, :, D + start : D + start + width], 0)
        value = jnp.where(keep, qkv_ref[0, :, 2 * D + start : 2 * D + start + width], 0)
        above = jnp.where(keep, grad_ref[0, :, span], 0)
        scores = dot_nt(key, query) * scale
        expo = jnp.exp(scores - jnp.max(scores, 0, keepdims=True))
        probs = expo / jnp.sum(expo, 0, keepdims=True)
        prob_grad = dot_nt(value, above)
        inner = jnp.sum(probs * prob_grad, 0, keepdims=True)
        score_grad = (probs * (prob_grad - inner)).astype(jnp.bfloat16)
        value_sum[:, span] += matmul(probs.astype(jnp.bfloat16), above)
        key_sum[:, span] += matmul(score_grad, query) * scale
        query_sum[:, span] += (
            lax.dot_general(
                score_grad, key, (((0,), (0,)), ((), ())), preferred_element_type=jnp.float32
            )
            * scale
        )
    out_ref[0, :, :D] = query_sum[...].astype(jnp.bfloat16)
    out_ref[0, :, D : 2 * D] = key_sum[...].astype(jnp.bfloat16)
    out_ref[0, :, 2 * D :] = value_sum[...].astype(jnp.bfloat16)


def attend_back(qkv, grad):
    images = qkv.shape[0]
    return pl.pallas_call(
        attend_back_kernel,
        grid=(images,),
        in_specs=[
            pl.BlockSpec((1, SEQ, 3 * D), lambda i: (i, 0, 0)),
            pl.BlockSpec((1, SEQ, D), lambda i: (i, 0, 0)),
        ],
        out_specs=pl.BlockSpec((1, SEQ, 3 * D), lambda i: (i, 0, 0)),
        out_shape=jax.ShapeDtypeStruct((images, SEQ, 3 * D), jnp.bfloat16),
        scratch_shapes=[pltpu.VMEM((SEQ, D), jnp.float32)] * 3,
        compiler_params=pltpu.CompilerParams(vmem_limit_bytes=40 * 1024 * 1024),
        cost_estimate=small_cost,
    )(qkv, grad)


def body_data(
    block_input,
    skip_input,
    timesteps,
    class_labels,
    loss_weights,
    grad_output,
    skip_weight,
    qkv_weight,
    proj_weight,
    fc1_weight,
    fc2_weight,
    vectors,
    hidden_bias,
    skip_rows,
    skip_cols,
    qkv_rows,
    qkv_cols,
    proj_rows,
    proj_cols,
    fc1_rows,
    fc1_cols,
    fc2_rows,
    fc2_cols,
    vector_moments,
    hidden_moments,
):
    image_count = timesteps.shape[0]
    mp_count = lax.axis_size("mp")
    dp_count = lax.axis_size("dp")
    mp_index = lax.axis_index("mp")
    dp_index = lax.axis_index("dp")
    core = lax.rem(dp_index, 2)
    quarter = lax.div(dp_index, 2)
    images = image_count // mp_count
    tokens = images * SEQ
    width_local = qkv_weight.shape[2]
    hidden_local = fc1_weight.shape[1]
    hidden_slice = hidden_local // dp_count
    order = Order()

    skip_shard = skip_weight.reshape(-1, D)
    skip_whole = bring(order, skip_shard, quarter, core)
    hidden_all = gather_deep(hidden_bias)
    hidden_state = gather_deep(hidden_moments).reshape(-1)

    angles = (timesteps.astype(jnp.float32) + 0.5) * (0.5 * math.pi / total_steps)
    alpha_sq = jnp.square(jnp.cos(angles))
    sigma_sq = jnp.square(jnp.sin(angles))
    snr_weight = 5.0 * sigma_sq / jnp.maximum(alpha_sq, 5.0 * sigma_sq)
    base_weight = loss_weights * snr_weight
    one_hot = (class_labels[:, None] == jnp.arange(CLASSES, dtype=jnp.int32)[None, :]).astype(
        jnp.float32
    )
    batch = jnp.concatenate([jnp.sum(one_hot, 0), jnp.sum(base_weight)[None]])

    attn_shard = jnp.concatenate(
        [qkv_weight.transpose(0, 2, 1).reshape(3 * width_local, D), proj_weight], 0
    )
    attn_shard = order.mark(attn_shard)
    attn_whole = bring(order, attn_shard, quarter, core)
    batch = order.mark(batch + to_core(batch))
    batch_x = to_x(batch)
    fc1_shard = order.mark(fc1_weight.T)
    fc2_shard = fc2_weight
    batch = order.mark(batch + batch_x)
    batch_y = to_y(batch)
    start = mp_index * tokens
    block_local = lax.dynamic_slice_in_dim(block_input, start, tokens, 0)
    skip_local = lax.dynamic_slice_in_dim(skip_input, start, tokens, 0)
    both_inputs = jnp.concatenate(
        [
            array.reshape(tokens, mp_count, 2, -1).transpose(0, 2, 1, 3).reshape(tokens, D)
            for array in (block_local, skip_local)
        ],
        1,
    )
    both_inputs = order.mark(both_inputs)
    batch = order.mark(batch + batch_y)

    skip_own = others(order.mark(skip_whole))
    skip_x, skip_y = swap_plane(order, skip_own, skip_own)
    skip_swapped = [to_core(skip_own)]
    fc1_whole = bring(order, fc1_shard, quarter, core)
    hidden_own = pick(hidden_all.reshape(mp_count, 4, 2, hidden_slice), core, 2)
    hidden_own = hidden_own.transpose(1, 0, 2).reshape(-1)
    own_count = jnp.dot(one_hot, batch[:CLASSES], precision=lax.Precision.HIGHEST)
    item_weight = base_weight * lax.rsqrt(own_count)
    hidden_own, item_weight = order.mark(hidden_own, item_weight)
    batch_scale = image_count * dp_count / batch[CLASSES]
    grad_local = lax.dynamic_slice_in_dim(grad_output, start, tokens, 0)
    item_local = lax.dynamic_slice_in_dim(item_weight, mp_index * images, images, 0)
    upstream = (
        grad_local.astype(jnp.float32).reshape(images, SEQ, D) * item_local[:, None, None]
    ).reshape(-1, D)
    upstream = order.mark(upstream)

    skip_x, skip_y = order.mark(skip_x, skip_y)
    skip_one, skip_two = swap_plane(order, skip_y[:2], skip_x[2:])
    skip_swapped = skip_swapped + [to_core(skip_x), to_core(skip_y)]
    skip_one, skip_two = order.mark(skip_one, skip_two)
    skip_swapped = skip_swapped + [to_core(skip_one), to_core(skip_two)]
    attn_own = others(order.mark(attn_whole))
    attn_x, attn_y = swap_plane(order, attn_own, attn_own)
    fc2_whole = bring(order, fc2_shard, quarter, core)
    fc2_across = bring(order, fc2_shard, quarter ^ 3, core)
    skip_swapped = order.mark(*skip_swapped)
    attn_swapped = [to_core(order.after(attn_own))]
    skip_parts = [
        (skip_own, quarter, 1),
        (skip_x, quarter ^ 1, 1),
        (skip_y, quarter ^ 2, 1),
        (skip_one, quarter ^ 3, 1),
        (skip_two, quarter ^ 3, 3),
    ]
    (skip_low,) = assemble_weight(skip_shard, skip_parts, skip_swapped, core, 0)
    joined = matmul(both_inputs, skip_low) + vectors[4]
    normed, normal_one, inverse_one = norm_forward(joined, vectors[0], vectors[1])
    normed_low = normed.astype(jnp.bfloat16)
    joined, normed_low, normal_one = order.mark(joined, normed_low, normal_one)
    upstream_other = to_core(order.after(upstream))

    attn_x, attn_y = order.mark(attn_x, attn_y)
    attn_one, attn_two = swap_plane(order, attn_y[:1], attn_x[1:])
    attn_swapped = attn_swapped + [to_core(attn_x), to_core(attn_y)]
    upstream_other = order.mark(upstream_other) * batch_scale
    upstream = upstream * batch_scale
    upstream_low = jnp.concatenate([upstream, upstream_other], 0).astype(jnp.bfloat16)
    upstream_low = order.mark(upstream_low)
    weight_sq = jnp.stack(
        [
            jnp.sum(array * array)
            for array in (skip_weight, qkv_weight, proj_weight, fc1_weight, fc2_weight, hidden_bias)
        ]
    )
    weight_sq = order.mark(weight_sq)
    fc1_own = others(order.mark(fc1_whole))
    fc1_x, fc1_y = swap_plane(order, fc1_own, fc1_own)
    attn_one, attn_two = order.mark(attn_one, attn_two)
    attn_swapped = attn_swapped + [to_core(attn_one), to_core(attn_two)]
    attn_parts = [
        (attn_own, quarter, 1),
        (attn_x, quarter ^ 1, 1),
        (attn_y, quarter ^ 2, 1),
        (attn_one, quarter ^ 3, 1),
        (attn_two, quarter ^ 3, 2),
    ]
    attn_swapped = order.mark(*attn_swapped)
    qkv_low, proj_low = assemble_weight(
        attn_shard, attn_parts, attn_swapped, core, 3 * mp_count
    )
    qkv_all = jnp.einsum(
        "itd,ed->ite",
        normed_low.reshape(images, SEQ, D),
        qkv_low,
        preferred_element_type=jnp.float32,
    ).astype(jnp.bfloat16)
    qkv_all = order.mark(qkv_all)
    attended = attend(qkv_all).reshape(tokens, D)
    residual = joined + matmul(attended, proj_low) + vectors[5]
    residual = order.mark(residual)
    fc1_x, fc1_y = order.mark(fc1_x, fc1_y)
    fc1_cut = order.mark(fc1_y[:2], fc1_x[2:])
    fc1_one, fc1_two = swap_plane(order, *fc1_cut)
    fc2_own = others(order.mark(fc2_whole))
    fc2_x, fc2_y = swap_plane(order, fc2_own, fc2_own)
    normed_two, normal_two, inverse_two = norm_forward(
        order.after(residual), vectors[2], vectors[3]
    )
    normed_two, normal_two = order.mark(normed_two, normal_two)
    normed_two_other = to_core(normal_two)
    fc1_one, fc1_two = order.mark(fc1_one, fc1_two)
    fc1_parts = [
        (fc1_own, quarter, 1),
        (fc1_x, quarter ^ 1, 1),
        (fc1_y, quarter ^ 2, 1),
        (fc1_one, quarter ^ 3, 1),
        (fc1_two, quarter ^ 3, 3),
    ]
    (fc1_low,) = assemble_weight(fc1_shard, fc1_parts, None, core, 0)
    fc1_low = order.mark(fc1_low)
    normed_two_other = order.mark(normed_two_other) * vectors[2] + vectors[3]
    normed_two_low = jnp.concatenate([normed_two, normed_two_other], 0).astype(jnp.bfloat16)
    normed_two_low = order.mark(normed_two_low)
    pre_act = (
        jnp.einsum("td,fd->tf", normed_two_low, fc1_low, preferred_element_type=jnp.float32)
        + hidden_own
    )
    activated, gelu_pull = jax.vjp(gelu_exact, pre_act)
    activated_low = activated.astype(jnp.bfloat16)
    fc2_grad = jnp.einsum(
        "tf,td->fd", activated_low, upstream_low, preferred_element_type=jnp.float32
    ).reshape(4, mp_count, hidden_slice, D)
    fc2_grad = order.mark(fc2_grad)
    fc2_add = swap_plane(order, *order.mark(*cut_corner(fc2_grad, quarter)))

    fc2_x, fc2_y = order.mark(fc2_x, fc2_y)
    fc2_corner = others(order.mark(fc2_across))
    fc2_parts = [
        (fc2_own, quarter, 1),
        (fc2_x, quarter ^ 1, 1),
        (fc2_y, quarter ^ 2, 1),
        (fc2_corner, quarter ^ 3, 1),
    ]
    (fc2_low,) = assemble_weight(fc2_shard, fc2_parts, None, core, 0)
    fc2_low = order.mark(fc2_low)
    forward_part = order.mark(matmul(activated_low, fc2_low))
    forward_other = to_core(forward_part[tokens:])
    act_grad = jnp.einsum(
        "td,fd->tf", order.after(upstream_low), fc2_low, preferred_element_type=jnp.float32
    )
    pre_grad = gelu_pull(act_grad)[0]
    hidden_grad = jnp.sum(pre_grad, 0)
    pre_low, hidden_grad = order.mark(pre_grad.astype(jnp.bfloat16), hidden_grad)
    block_own = residual + forward_part[:tokens] + order.mark(forward_other)
    block_own = order.mark(block_own.reshape(images, SEQ, D))
    block_all = lax.all_gather(block_own, "mp")
    fc2_add = order.mark(*fc2_add)
    fc2_sides = swap_plane(order, *order.mark(*cut_sides(fc2_grad, quarter, *fc2_add)))
    back_part = order.mark(matmul(order.after(pre_low), fc1_low))
    back_other = to_core(back_part[tokens:])
    fc1_grad = jnp.einsum(
        "tf,td->fd",
        order.after(pre_low),
        normed_two_low,
        preferred_element_type=jnp.float32,
    ).reshape(4, mp_count, hidden_slice, D)
    fc1_grad = order.mark(fc1_grad)
    fc1_add = swap_plane(order, *order.mark(*cut_corner(fc1_grad, quarter)))
    norm_two_in = back_part[:tokens] + order.mark(back_other)
    back_two, gain_two_grad, bias_two_grad = norm_backward(
        norm_two_in, normal_two, inverse_two, vectors[2]
    )
    residual_grad = upstream + back_two
    residual_low = residual_grad.astype(jnp.bfloat16)
    residual_grad, residual_low = order.mark(residual_grad, residual_low)
    attended_grad = jnp.einsum(
        "td,ed->te", residual_low, proj_low, preferred_element_type=jnp.float32
    ).astype(jnp.bfloat16)
    qkv_grad_low = attend_back(
        qkv_all, order.mark(attended_grad.reshape(images, SEQ, D))
    ).reshape(tokens, 3 * D)
    qkv_grad_low = order.mark(qkv_grad_low)
    fc2_sides = order.mark(*fc2_sides)
    fc2_piece = sum_deep(order, fc2_grad, quarter, *fc2_sides)
    qkv_grad = jnp.einsum(
        "te,td->ed", order.after(qkv_grad_low), normed_low, preferred_element_type=jnp.float32
    ).reshape(3 * mp_count, 2, hidden_slice, D)
    qkv_grad = order.mark(qkv_grad)
    fc1_add = order.mark(*fc1_add)
    fc1_sides = swap_plane(order, *order.mark(*cut_sides(fc1_grad, quarter, *fc1_add)))
    proj_grad = jnp.einsum(
        "te,td->ed", attended, order.after(residual_low), preferred_element_type=jnp.float32
    ).reshape(mp_count, 2, hidden_slice, D)
    attn_given = order.mark(pick(qkv_grad, 1 - core, 1), pick(proj_grad, 1 - core, 1))
    attn_given = [to_core(array) for array in attn_given]
    norm_one_in = matmul(order.after(qkv_grad_low), qkv_low)
    back_one, gain_one_grad, bias_one_grad = norm_backward(
        norm_one_in, normal_one, inverse_one, vectors[0]
    )
    joined_grad = residual_grad + back_one
    joined_low = joined_grad.astype(jnp.bfloat16)
    joined_grad, joined_low = order.mark(joined_grad, joined_low)
    skip_grad = jnp.einsum(
        "tc,td->cd", both_inputs, joined_low, preferred_element_type=jnp.float32
    ).reshape(4 * mp_count, 2, -1, D)
    skip_given = order.mark(pick(skip_grad, 1 - core, 1))
    skip_given = to_core(skip_given)
    block_all = order.mark(block_all)
    attn_given = order.mark(*attn_given)
    attn_grad = add_half([qkv_grad, proj_grad], attn_given, core)
    attn_grad = order.mark(attn_grad.reshape(4, mp_count, hidden_slice, D))
    attn_add = swap_plane(order, *order.mark(*cut_corner(attn_grad, quarter)))
    fc1_sides = order.mark(*fc1_sides)
    fc1_piece = sum_deep(order, fc1_grad, quarter, *fc1_sides)
    skip_shards = skip_low.reshape(4, mp_count, -1, D)

    def input_product(shift):
        shard_low = pick(skip_shards, lax.rem(mp_index + shift, mp_count), 1).reshape(-1, D)
        return order.mark(
            jnp.einsum("td,cd->tc", joined_low, shard_low, preferred_element_type=jnp.float32)
        )

    turn_two = turn_mp(input_product(2), 2)
    turn_one, stay, turn_three = input_product(1), input_product(0), input_product(3)
    attn_add = order.mark(*attn_add)
    attn_sides = swap_plane(order, *order.mark(*cut_sides(attn_grad, quarter, *attn_add)))
    skip_given = order.mark(skip_given)
    skip_grad = add_half([skip_grad], [skip_given], core)
    skip_grad = order.mark(skip_grad.reshape(4, mp_count, -1, D))
    skip_add = swap_plane(order, *order.mark(*cut_corner(skip_grad, quarter)))
    fc2_piece = order.mark(fc2_piece)
    vector_grad = jnp.stack(
        [
            gain_one_grad,
            bias_one_grad,
            gain_two_grad,
            bias_two_grad,
            jnp.sum(joined_grad, 0),
            jnp.sum(residual_grad, 0),
            jnp.sum(upstream, 0),
        ]
    )
    hidden_grad = hidden_grad.reshape(4, mp_count, 1, hidden_slice).transpose(1, 0, 2, 3)
    hidden_grad = jnp.where(jnp.arange(2)[None, None, :, None] == core, hidden_grad, 0.0)
    small = order.mark(jnp.concatenate([vector_grad.reshape(-1), hidden_grad.reshape(-1)]))
    small_core = to_core(small)
    fc1_piece = order.mark(fc1_piece)
    turn_two = order.mark(turn_two)
    attn_sides = order.mark(*attn_sides)
    attn_piece = sum_deep(order, attn_grad, quarter, *attn_sides)
    skip_add = order.mark(*skip_add)
    skip_sides = swap_plane(order, *order.mark(*cut_sides(skip_grad, quarter, *skip_add)))
    small = order.mark(small + order.mark(small_core))
    small_x = to_x(small)
    skip_sides = order.mark(*skip_sides)
    small = order.mark(small + order.mark(small_x))
    small_y = to_y(small)
    skip_piece = sum_deep(order, skip_grad, quarter, *skip_sides)

    def spread(piece):
        return swap_plane(order, piece, piece)

    def half_of(rows):
        return (rows // 2 + 7) // 8 * 8

    def spread_far(near):
        half = half_of(near[0].shape[0])
        return swap_plane(order, near[1][:half], near[0][half:])

    def hold(piece, near, far):
        rows, half = piece.shape[0], far[0].shape[0]
        return place_rows(
            [
                (piece, 0, rows, quarter * rows),
                (near[0], 0, rows, (quarter ^ 1) * rows),
                (near[1], 0, rows, (quarter ^ 2) * rows),
                (far[0], 0, half, (quarter ^ 3) * rows),
                (far[1], 0, rows - half, (quarter ^ 3) * rows + half),
            ],
            4 * rows,
        )

    def interleave(held, other, near_state):
        rows = held.shape[0] // 4
        pieces = []
        for n in range(4):
            pieces.append((held, n * rows, rows, (2 * n + core) * rows))
            pieces.append((other, n * rows, rows, (2 * n + 1 - core) * rows))
        whole, sent = place_rows(pieces, 8 * rows, near_state)
        return whole.reshape(near_state.shape + (D,)), sent

    def own_state(state):
        width = state.shape[-1] // mp_count
        return lax.dynamic_slice_in_dim(state, mp_index * width, width, state.ndim - 1)

    def everywhere(array):
        return [array] + [turn_mp(array, shift) for shift in range(1, mp_count)]

    fc2_near, fc1_near = spread(fc2_piece), spread(fc1_piece)
    block_output = (block_all + vectors[6]).astype(jnp.bfloat16).reshape(-1, D)
    block_output = order.mark(block_output)
    fc2_near = order.mark(*fc2_near)
    fc2_far = spread_far(fc2_near)
    small = order.mark(small + order.mark(small_y))
    fc1_near = order.mark(*fc1_near)
    fc1_far = spread_far(fc1_near)
    fc2_far = order.mark(*fc2_far)
    attn_piece = order.mark(attn_piece)
    attn_near = spread(attn_piece)
    fc2_held = order.mark(hold(fc2_piece, fc2_near, fc2_far))
    fc2_other = to_core(fc2_held)
    fc1_far = order.mark(*fc1_far)
    skip_piece = order.mark(skip_piece)
    skip_near = spread(skip_piece)
    turn_one = turn_mp(order.after(turn_one), 1)
    fc1_held = order.mark(hold(fc1_piece, fc1_near, fc1_far))
    attn_near = order.mark(*attn_near)
    attn_far = spread_far(attn_near)
    fc1_other = to_core(order.after(fc1_held))
    skip_near = order.mark(*skip_near)
    skip_far = spread_far(skip_near)
    small = jnp.concatenate(
        [small, weight_sq, jnp.zeros((D - 6,), jnp.float32)], 0
    ).reshape(6, 2, D)
    fc2_sum, fc2_moments = order.mark(
        *interleave(fc2_held, order.mark(fc2_other), own_state(fc2_rows)[None])
    )
    attn_far = order.mark(*attn_far)
    attn_held = order.mark(hold(attn_piece, attn_near, attn_far))
    attn_other = to_core(attn_held)
    turn_one = order.mark(turn_one)
    turn_three = turn_mp(order.after(turn_three), 3)
    skip_far = order.mark(*skip_far)
    skip_held = order.mark(hold(skip_piece, skip_near, skip_far))
    skip_other = to_core(skip_held)
    fc1_sum, fc1_moments = order.mark(
        *interleave(fc1_held, order.mark(fc1_other), own_state(fc1_cols)[None])
    )
    hidden_sent = jnp.concatenate([fc2_moments, fc1_moments, small], 0)
    turn_three = order.mark(turn_three)
    hidden_sent = everywhere(order.mark(hidden_sent))
    attn_state = jnp.concatenate([own_state(qkv_cols), own_state(proj_rows)[None]], 0)
    attn_sum, attn_moments = order.mark(
        *interleave(attn_held, order.mark(attn_other), attn_state)
    )
    skip_sum, skip_moments = order.mark(
        *interleave(skip_held, order.mark(skip_other), own_state(skip_rows))
    )
    hidden_sent = order.mark(*hidden_sent)
    token_sent = everywhere(order.mark(jnp.concatenate([attn_moments, skip_moments], 0)))
    input_grad, skip_input_grad = order.mark(
        *order_tokens([stay, turn_one, turn_two, turn_three], mp_index)
    )
    step = jnp.zeros((8, 128), jnp.float32)
    fc2_far_new, *fc2_scales, step = order.mark(
        *scales(fc2_sum, fc2_cols[None], step, hidden_sent, 0, mp_index, (True,))
    )
    fc1_far_new, *fc1_scales, step = order.mark(
        *scales(fc1_sum, fc1_rows[None], step, hidden_sent, 1, mp_index, (False,))
    )
    token_sent = order.mark(*token_sent)
    attn_state = jnp.concatenate([qkv_rows, proj_cols[None]], 0)
    attn_far_new, *attn_scales, step = order.mark(
        *scales(attn_sum, attn_state, step, token_sent, 0, mp_index, (False, False, False, True))
    )
    skip_far_new, *skip_scales, step = order.mark(
        *scales(skip_sum, skip_cols, step, token_sent, 4, mp_index, (True, True))
    )
    steps = everywhere(step)
    small = jnp.sum(in_turn([array[2:] for array in hidden_sent]), 0).reshape(-1)
    vector_sum = small[: 7 * D].reshape(7, D)
    hidden_whole = small[7 * D : 7 * D + mp_count * hidden_local]
    weight_sq = small[11 * D : 11 * D + 6]
    vector_new = 0.5 * vector_moments + 0.5 * (vector_sum * vector_sum + moment_eps)
    vector_update = vector_sum * lax.rsqrt(vector_new)
    hidden_new = 0.5 * hidden_state + 0.5 * (hidden_whole * hidden_whole + moment_eps)
    hidden_update = hidden_whole * lax.rsqrt(hidden_new)
    vector_step = jnp.sum(vector_update * vector_update) + jnp.sum(hidden_update * hidden_update)

    def own_hidden(array):
        return lax.dynamic_slice_in_dim(array, mp_index * hidden_local, hidden_local, 0)

    hidden_sum, hidden_new = own_hidden(hidden_whole), own_hidden(hidden_new)
    hidden_update = own_hidden(hidden_update)
    tensor_sizes = (2.0 * D * D, 3.0 * D * D, 1.0 * D * D, 1.0 * D * FF, 1.0 * FF * D, 1.0 * FF)
    weight_rms = jnp.sqrt(weight_sq / jnp.array(tensor_sizes, jnp.float32))
    rates = step_rate * jnp.maximum(0.001, weight_rms)
    pairs = jnp.stack([rates, jnp.broadcast_to(vector_step, (6,))], 1)
    pairs = order.mark(pairs)
    steps = order.mark(*steps)

    qkv_turned = qkv_weight.transpose(0, 2, 1)
    skip_new, skip_new_low = renew(skip_weight, skip_sum, *skip_scales, pairs[0], steps, False)
    qkv_new, qkv_new_low = renew(qkv_turned, attn_sum, *attn_scales, pairs[1], steps, False)
    qkv_new, qkv_new_low = qkv_new.transpose(0, 2, 1), qkv_new_low.transpose(0, 2, 1)
    proj_new, proj_new_low = renew(
        proj_weight[None], attn_sum, *attn_scales, pairs[2], steps, False, first=3
    )
    fc1_new, fc1_new_low = renew(fc1_weight[None], fc1_sum, *fc1_scales, pairs[3], steps, True)
    fc2_new, fc2_new_low = renew(fc2_weight[None], fc2_sum, *fc2_scales, pairs[4], steps, False)
    step_total = jnp.sum(jnp.sum(in_turn(steps), 0)) + vector_step
    update_rms = jnp.sqrt(step_total / param_count)
    divisor = jnp.maximum(1.0, update_rms / clip_level)
    vector_rms = jnp.sqrt(jnp.mean(vectors * vectors, 1, keepdims=True))
    vectors_new = vectors - step_rate * jnp.maximum(0.001, vector_rms) * vector_update / divisor
    hidden_bias_new = hidden_bias - rates[5] / divisor * hidden_update
    piece_width = D // dp_count
    dp_start = dp_index * piece_width

    def own_piece(array, axis):
        return lax.dynamic_slice_in_dim(array, dp_start, piece_width, axis)

    def near_whole(sent, first, amount, width):
        near = in_turn([array[first : first + amount, 1, :width] for array in sent])
        return near.transpose(1, 0, 2).reshape(near.shape[1], -1)

    skip_near_new = near_whole(token_sent, 4, 2, width_local)
    attn_near_new = near_whole(token_sent, 0, 4, width_local)
    fc1_near_new = near_whole(hidden_sent, 1, 1, hidden_local)
    fc2_near_new = near_whole(hidden_sent, 0, 1, hidden_local)
    return (
        block_output,
        input_grad,
        skip_input_grad,
        own_piece(skip_sum, 2),
        own_piece(attn_sum[:3], 2).transpose(0, 2, 1),
        own_piece(attn_sum[3], 1),
        own_piece(fc1_sum[0], 1).T,
        own_piece(fc2_sum[0], 1),
        own_piece(vector_sum, 1),
        hidden_sum,
        skip_near_new,
        skip_far_new[:, 0],
        attn_far_new[:3, 0],
        attn_near_new[:3],
        attn_near_new[3],
        attn_far_new[3, 0],
        fc1_far_new[0, 0],
        fc1_near_new[0],
        fc2_near_new[0],
        fc2_far_new[0, 0],
        vector_new,
        hidden_new,
        skip_new,
        qkv_new,
        proj_new[0],
        fc1_new[0],
        fc2_new[0],
        vectors_new,
        hidden_bias_new,
        skip_new_low,
        qkv_new_low,
        proj_new_low[0],
        fc1_new_low[0],
        fc2_new_low[0],
        update_rms,
    )


def solution(mesh):
    placed = (
        P("dp", None),
        P("dp", None),
        P("dp"),
        P("dp"),
        P("dp"),
        P("dp", None),
        P(None, "mp", None),
        P(None, None, "mp"),
        P("mp", None),
        P(None, "mp"),
        P("mp", None),
        P(),
        P("mp"),
        P(),
        P(),
        P(),
        P(),
        P(),
        P(),
        P(),
        P(),
        P(),
        P(),
        P(),
        P("mp"),
    )
    return jax.shard_map(
        body,
        mesh=mesh,
        in_specs=placed,
        out_specs=(
            P("dp", None),
            P("dp", "mp"),
            P("dp", "mp"),
            P(None, "mp", "dp"),
            P(None, "dp", "mp"),
            P("mp", "dp"),
            P("dp", "mp"),
            P("mp", "dp"),
            P(None, "dp"),
            P("mp"),
            P(),
            P(),
            P(),
            P(),
            P(),
            P(),
            P(),
            P(),
            P(),
            P(),
            P(),
            P("mp"),
            P(None, "mp", None),
            P(None, None, "mp"),
            P("mp", None),
            P(None, "mp"),
            P("mp", None),
            P(),
            P("mp"),
            P(None, "mp", None),
            P(None, None, "mp"),
            P("mp", None),
            P(None, "mp"),
            P("mp", None),
            P(),
        ),
        check_vma=False,
    )
```

```python
import functools
import math

import jax
import jax.numpy as jnp
from jax import lax
from jax.experimental import pallas as pl
from jax.experimental.pallas import tpu as pltpu
from jax.sharding import PartitionSpec as P

D = 1152
HEAD_DIM = 72
FF = 4608
CLASSES = 1000
SEQ = 258


ln_eps = 1e-05
moment_eps = 1e-30
clip_level = 0.25
step_rate = 2.0
total_steps = 1000.0


def gelu_exact(inputs):
    return 0.5 * inputs * (1.0 + lax.erf(inputs * (1.0 / math.sqrt(2.0))))


def matmul(left_side, right_side):
    return jnp.dot(left_side, right_side, preferred_element_type=jnp.float32)


def norm_forward(inputs, norm_gain, norm_bias):
    centre = jnp.mean(inputs, -1, keepdims=True)
    centred = inputs - centre
    inverse = lax.rsqrt(jnp.mean(centred * centred, -1, keepdims=True) + ln_eps)
    normal = centred * inverse
    return (normal * norm_gain + norm_bias, normal, inverse)


def norm_backward(incoming, normal, inverse, norm_gain):
    scaled = incoming * norm_gain
    inner_mean = jnp.mean(scaled, -1, keepdims=True)
    proj_mean = jnp.mean(scaled * normal, -1, keepdims=True)
    return (
        inverse * (scaled - inner_mean - normal * proj_mean),
        jnp.sum(incoming * normal, 0),
        jnp.sum(incoming, 0),
    )


def adafactor(
    grad_pieces,
    weight_pieces,
    starts,
    row_states,
    col_states,
    vector_piece,
    vector_weight,
    vector_state,
    hidden_piece,
    hidden_weight,
    hidden_state,
    first_mask,
    reduce_moments,
    reduce_norm,
):
    full_shapes = ((D, D), (D, D), (D, D), (D, FF), (FF, D))
    tensor_sizes = (2.0 * D * D, 3.0 * D * D, 1.0 * D * D, 1.0 * D * FF, 1.0 * FF * D)
    zero_start = jnp.zeros((), jnp.int32)
    row_parts = []
    col_parts = []
    weight_sq = []
    for position in range(5):
        grad_piece = grad_pieces[position]
        leading = grad_piece.shape[0]
        squares = grad_piece * grad_piece + moment_eps
        row_zero = jnp.zeros((leading, full_shapes[position][0]), jnp.float32)
        col_zero = jnp.zeros((leading, full_shapes[position][1]), jnp.float32)
        row_parts.append(
            lax.dynamic_update_slice(
                row_zero, jnp.sum(squares, 2), (zero_start, starts[position][0])
            ).reshape(-1)
        )
        col_parts.append(
            lax.dynamic_update_slice(
                col_zero, jnp.sum(squares, 1), (zero_start, starts[position][1])
            ).reshape(-1)
        )
        weight_sq.append(jnp.sum(weight_pieces[position] * weight_pieces[position])[None])
    weight_sq.append(jnp.sum(vector_weight * vector_weight, 1) * first_mask)
    weight_sq.append(jnp.sum(hidden_weight * hidden_weight)[None])
    row_total, col_total, weight_total = reduce_moments(
        jnp.concatenate(row_parts), jnp.concatenate(col_parts), jnp.concatenate(weight_sq)
    )
    row_news = []
    col_news = []
    updates = []
    step_sq = jnp.zeros((), jnp.float32)
    row_offset = 0
    col_offset = 0
    for position in range(5):
        grad_piece = grad_pieces[position]
        leading = grad_piece.shape[0]
        rows_full, cols_full = full_shapes[position]
        row_sum = row_total[row_offset : row_offset + leading * rows_full].reshape(
            leading, rows_full
        )
        col_sum = col_total[col_offset : col_offset + leading * cols_full].reshape(
            leading, cols_full
        )
        row_offset = row_offset + leading * rows_full
        col_offset = col_offset + leading * cols_full
        row_new = 0.5 * row_states[position] + 0.5 * (row_sum / cols_full)
        col_new = 0.5 * col_states[position] + 0.5 * (col_sum / rows_full)
        row_piece = lax.dynamic_slice(
            row_new, (zero_start, starts[position][0]), (leading, grad_piece.shape[1])
        )
        col_piece = lax.dynamic_slice(
            col_new, (zero_start, starts[position][1]), (leading, grad_piece.shape[2])
        )
        row_mean = jnp.mean(row_new, 1)
        update = grad_piece * lax.rsqrt(
            row_piece[:, :, None] * col_piece[:, None, :] / row_mean[:, None, None]
        )
        step_sq = step_sq + jnp.sum(update * update)
        row_news.append(row_new)
        col_news.append(col_new)
        updates.append(update)
    vector_new = 0.5 * vector_state + 0.5 * (vector_piece * vector_piece + moment_eps)
    vector_update = vector_piece * lax.rsqrt(vector_new)
    hidden_new = 0.5 * hidden_state + 0.5 * (hidden_piece * hidden_piece + moment_eps)
    hidden_update = hidden_piece * lax.rsqrt(hidden_new)
    step_sq = (
        step_sq
        + jnp.sum(vector_update * vector_update) * first_mask
        + jnp.sum(hidden_update * hidden_update)
    )
    step_total = reduce_norm(step_sq)
    param_count = 6.0 * D * D + 2.0 * D * FF + 7.0 * D + FF
    update_rms = jnp.sqrt(step_total / param_count)
    divisor = jnp.maximum(1.0, update_rms / clip_level)
    new_weights = []
    for position in range(5):
        weight_rms = jnp.sqrt(weight_total[position] / tensor_sizes[position])
        new_weights.append(
            weight_pieces[position]
            - step_rate * jnp.maximum(0.001, weight_rms) * updates[position] / divisor
        )
    vector_rms = jnp.sqrt(weight_total[5:12] / D)[:, None]
    vector_weight_new = (
        vector_weight - step_rate * jnp.maximum(0.001, vector_rms) * vector_update / divisor
    )
    hidden_rms = jnp.sqrt(weight_total[12] / FF)
    hidden_weight_new = (
        hidden_weight - step_rate * jnp.maximum(0.001, hidden_rms) * hidden_update / divisor
    )
    return (
        new_weights,
        row_news,
        col_news,
        vector_new,
        vector_weight_new,
        hidden_new,
        hidden_weight_new,
        update_rms,
    )


def body_tensor(
    block_input,
    skip_input,
    timesteps,
    class_labels,
    loss_weights,
    grad_output,
    skip_weight,
    qkv_weight,
    proj_weight,
    fc1_weight,
    fc2_weight,
    vectors,
    hidden_bias,
    skip_rows,
    skip_cols,
    qkv_rows,
    qkv_cols,
    proj_rows,
    proj_cols,
    fc1_rows,
    fc1_cols,
    fc2_rows,
    fc2_cols,
    vector_moments,
    hidden_moments,
):
    image_count = timesteps.shape[0]
    width_local = qkv_weight.shape[2]
    heads_local = width_local // HEAD_DIM
    hidden_local = fc1_weight.shape[1]
    mp_index = lax.axis_index("mp")
    dp_index = lax.axis_index("dp")
    dp_count = lax.axis_size("dp")
    first_mask = (mp_index == 0).astype(jnp.float32)
    feature_start = mp_index * skip_weight.shape[1]
    block_local = lax.dynamic_slice_in_dim(block_input, feature_start, skip_weight.shape[1], 1)
    skip_local = lax.dynamic_slice_in_dim(skip_input, feature_start, skip_weight.shape[1], 1)
    angles = (timesteps.astype(jnp.float32) + 0.5) * (0.5 * math.pi / total_steps)
    alpha_sq = jnp.square(jnp.cos(angles))
    sigma_sq = jnp.square(jnp.sin(angles))
    snr_weight = 5.0 * sigma_sq / jnp.maximum(alpha_sq, 5.0 * sigma_sq)
    base_weight = loss_weights * snr_weight
    one_hot = (class_labels[:, None] == jnp.arange(CLASSES, dtype=jnp.int32)[None, :]).astype(
        jnp.float32
    )
    class_counts, weight_total = lax.psum((jnp.sum(one_hot, 0), jnp.sum(base_weight)), "dp")
    own_count = jnp.dot(one_hot, class_counts, precision=lax.Precision.HIGHEST)
    item_weight = base_weight * (image_count * dp_count / weight_total) * lax.rsqrt(own_count)
    upstream = (
        grad_output.astype(jnp.float32).reshape(image_count, SEQ, D) * item_weight[:, None, None]
    ).reshape(-1, D)
    skip_low = skip_weight.astype(jnp.bfloat16)
    qkv_low = qkv_weight.astype(jnp.bfloat16)
    proj_low = proj_weight.astype(jnp.bfloat16)
    fc1_low = fc1_weight.astype(jnp.bfloat16)
    fc2_low = fc2_weight.astype(jnp.bfloat16)
    joined = (
        lax.psum(matmul(block_local, skip_low[0]) + matmul(skip_local, skip_low[1]), "mp")
        + vectors[4]
    )
    normed, normal_one, inverse_one = norm_forward(joined, vectors[0], vectors[1])
    normed_low = normed.astype(jnp.bfloat16)
    qkv_all = jnp.einsum(
        "td,sde->ste", normed_low, qkv_low, preferred_element_type=jnp.float32
    ).astype(jnp.bfloat16)
    heads_view = qkv_all.reshape(3, image_count, SEQ, heads_local, HEAD_DIM)
    query_low = heads_view[0]
    key_low = heads_view[1]
    value_low = heads_view[2]
    score_scale = HEAD_DIM ** (-0.5)

    def score_block():
        return (
            jnp.einsum("iqhe,ikhe->ihqk", query_low, key_low, preferred_element_type=jnp.float32)
            * score_scale
        )

    scores = score_block()
    score_top = jnp.max(scores, -1, keepdims=True)
    expo_scores = jnp.exp(scores - score_top)
    expo_total = jnp.sum(expo_scores, -1, keepdims=True)
    weights_low = (expo_scores / expo_total).astype(jnp.bfloat16)
    log_total = score_top + jnp.log(expo_total)
    attended = (
        jnp.einsum("ihqk,ikhe->iqhe", weights_low, value_low, preferred_element_type=jnp.float32)
        .astype(jnp.bfloat16)
        .reshape(-1, width_local)
    )
    residual = joined + lax.psum(matmul(attended, proj_low), "mp") + vectors[5]
    normed_two, normal_two, inverse_two = norm_forward(residual, vectors[2], vectors[3])
    normed_two_low = normed_two.astype(jnp.bfloat16)
    pre_act = matmul(normed_two_low, fc1_low) + hidden_bias
    activated, gelu_pull = jax.vjp(gelu_exact, pre_act)
    activated_low = activated.astype(jnp.bfloat16)
    block_output = (residual + lax.psum(matmul(activated_low, fc2_low), "mp") + vectors[6]).astype(
        jnp.bfloat16
    )
    upstream_low = upstream.astype(jnp.bfloat16)
    fc2_grad = jnp.einsum(
        "tf,td->fd", activated_low, upstream_low, preferred_element_type=jnp.float32
    )
    fc2_bias_grad = jnp.sum(upstream, 0)
    act_grad = jnp.einsum("td,fd->tf", upstream_low, fc2_low, preferred_element_type=jnp.float32)
    pre_grad = gelu_pull(act_grad)[0]
    pre_low = pre_grad.astype(jnp.bfloat16)
    fc1_grad = jnp.einsum("td,tf->df", normed_two_low, pre_low, preferred_element_type=jnp.float32)
    hidden_grad = jnp.sum(pre_grad, 0)
    norm_two_in = lax.psum(
        jnp.einsum("tf,df->td", pre_low, fc1_low, preferred_element_type=jnp.float32), "mp"
    )
    back_two, gain_two_grad, bias_two_grad = norm_backward(
        norm_two_in, normal_two, inverse_two, vectors[2]
    )
    residual_grad = upstream + back_two
    proj_bias_grad = jnp.sum(residual_grad, 0)
    residual_low = residual_grad.astype(jnp.bfloat16)
    proj_grad = jnp.einsum("te,td->ed", attended, residual_low, preferred_element_type=jnp.float32)
    attended_grad = jnp.einsum(
        "td,ed->te", residual_low, proj_low, preferred_element_type=jnp.float32
    ).astype(jnp.bfloat16)
    attended_grad = attended_grad.reshape(image_count, SEQ, heads_local, HEAD_DIM)
    scores = score_block()
    probs_exact = jnp.exp(scores - log_total)
    prob_grad = jnp.einsum(
        "iqhe,ikhe->ihqk", attended_grad, value_low, preferred_element_type=jnp.float32
    )
    score_grad = (
        probs_exact * (prob_grad - jnp.sum(probs_exact * prob_grad, -1, keepdims=True))
    ).astype(jnp.bfloat16)
    query_grad = (
        jnp.einsum("ihqk,ikhe->iqhe", score_grad, key_low, preferred_element_type=jnp.float32)
        * score_scale
    )
    key_grad = (
        jnp.einsum("ihqk,iqhe->ikhe", score_grad, query_low, preferred_element_type=jnp.float32)
        * score_scale
    )
    value_grad = jnp.einsum(
        "ihqk,iqhe->ikhe", weights_low, attended_grad, preferred_element_type=jnp.float32
    )
    qkv_grad_low = (
        jnp.stack([query_grad, key_grad, value_grad])
        .astype(jnp.bfloat16)
        .reshape(3, -1, width_local)
    )
    qkv_grad = jnp.einsum(
        "td,ste->sde", normed_low, qkv_grad_low, preferred_element_type=jnp.float32
    )
    norm_one_in = lax.psum(
        jnp.einsum("ste,sde->td", qkv_grad_low, qkv_low, preferred_element_type=jnp.float32), "mp"
    )
    back_one, gain_one_grad, bias_one_grad = norm_backward(
        norm_one_in, normal_one, inverse_one, vectors[0]
    )
    joined_grad = residual_grad + back_one
    skip_bias_grad = jnp.sum(joined_grad, 0)
    joined_low = joined_grad.astype(jnp.bfloat16)
    skip_grad = jnp.stack(
        [
            jnp.einsum("tc,td->cd", block_local, joined_low, preferred_element_type=jnp.float32),
            jnp.einsum("tc,td->cd", skip_local, joined_low, preferred_element_type=jnp.float32),
        ]
    )
    input_grad = jnp.einsum(
        "td,cd->tc", joined_low, skip_low[0], preferred_element_type=jnp.float32
    )
    skip_input_grad = jnp.einsum(
        "td,cd->tc", joined_low, skip_low[1], preferred_element_type=jnp.float32
    )
    vector_grad = jnp.stack(
        [
            gain_one_grad,
            bias_one_grad,
            gain_two_grad,
            bias_two_grad,
            skip_bias_grad,
            proj_bias_grad,
            fc2_bias_grad,
        ]
    )
    row_states = [skip_rows, qkv_rows, proj_rows[None], fc1_rows[None], fc2_rows[None]]
    col_states = [skip_cols, qkv_cols, proj_cols[None], fc1_cols[None], fc2_cols[None]]
    piece_width = D // dp_count
    dp_start = dp_index * piece_width
    zero_start = jnp.zeros((), jnp.int32)
    summed = lax.psum(
        (skip_grad, qkv_grad, proj_grad, fc1_grad, fc2_grad, vector_grad, hidden_grad), "dp"
    )

    def moments_mp(row_all, col_all, squares_all):
        return lax.psum((row_all, col_all, squares_all), "mp")

    def norm_mp(step_sq):
        return lax.psum(step_sq, "mp")

    grad_pieces = [summed[0], summed[1], summed[2][None], summed[3][None], summed[4][None]]
    weight_pieces = [skip_weight, qkv_weight, proj_weight[None], fc1_weight[None], fc2_weight[None]]
    starts = [
        (mp_index * width_local, zero_start),
        (zero_start, mp_index * width_local),
        (mp_index * width_local, zero_start),
        (zero_start, mp_index * hidden_local),
        (mp_index * hidden_local, zero_start),
    ]
    results = adafactor(
        grad_pieces,
        weight_pieces,
        starts,
        row_states,
        col_states,
        summed[5],
        vectors,
        vector_moments,
        summed[6],
        hidden_bias,
        hidden_moments,
        first_mask,
        moments_mp,
        norm_mp,
    )
    (
        new_weights,
        row_news,
        col_news,
        vector_state_new,
        vectors_new,
        hidden_state_new,
        hidden_new,
        update_rms,
    ) = results
    skip_new = new_weights[0]
    qkv_new = new_weights[1]
    proj_new = new_weights[2][0]
    fc1_new = new_weights[3][0]
    fc2_new = new_weights[4][0]
    skip_grad_out = lax.dynamic_slice_in_dim(summed[0], dp_start, piece_width, 2)
    qkv_grad_out = lax.dynamic_slice_in_dim(summed[1], dp_start, piece_width, 1)
    proj_grad_out = lax.dynamic_slice_in_dim(summed[2], dp_start, piece_width, 1)
    fc1_grad_out = lax.dynamic_slice_in_dim(summed[3], dp_start, piece_width, 0)
    fc2_grad_out = lax.dynamic_slice_in_dim(summed[4], dp_start, piece_width, 1)
    vector_grad_out = lax.dynamic_slice_in_dim(summed[5], dp_start, piece_width, 1)
    hidden_grad_out = summed[6]
    return (
        block_output,
        input_grad,
        skip_input_grad,
        skip_grad_out,
        qkv_grad_out,
        proj_grad_out,
        fc1_grad_out,
        fc2_grad_out,
        vector_grad_out,
        hidden_grad_out,
        row_news[0],
        col_news[0],
        row_news[1],
        col_news[1],
        row_news[2][0],
        col_news[2][0],
        row_news[3][0],
        col_news[3][0],
        row_news[4][0],
        col_news[4][0],
        vector_state_new,
        hidden_state_new,
        skip_new,
        qkv_new,
        proj_new,
        fc1_new,
        fc2_new,
        vectors_new,
        hidden_new,
        skip_new.astype(jnp.bfloat16),
        qkv_new.astype(jnp.bfloat16),
        proj_new.astype(jnp.bfloat16),
        fc1_new.astype(jnp.bfloat16),
        fc2_new.astype(jnp.bfloat16),
        update_rms,
    )


def body(*operands):
    images = operands[2].shape[0]
    if images % lax.axis_size("mp") == 0 and lax.axis_size("dp") == 8:
        return body_data(*operands)
    return body_tensor(*operands)


small_cost = pl.CostEstimate(flops=0, bytes_accessed=1024, transcendentals=0)


def to_core(array):
    return lax.ppermute(array, "dp", [(i, i ^ 1) for i in range(8)])


def to_x(array):
    return lax.ppermute(array, "dp", [(i, i ^ 2) for i in range(8)])


def to_y(array):
    return lax.ppermute(array, "dp", [(i, i ^ 4) for i in range(8)])


def turn_mp(array, shift):
    count = lax.axis_size("mp")
    return lax.ppermute(array, "mp", [(i, (i + shift) % count) for i in range(count)])


def pick(array, index, axis):
    return lax.dynamic_index_in_dim(array, index, axis, keepdims=False)


def assemble(steps, targets, core, rows, blocks, split):
    arrays = []
    for step in steps:
        for array, _ in step:
            if not any(array is other for other in arrays):
                arrays.append(array)
    place = [
        [(next(n for n, other in enumerate(arrays) if other is array), k) for array, k in step]
        for step in steps
    ]
    table = jnp.stack([jnp.asarray(v, jnp.int32) for v in [*targets, core]])
    depth = 4
    outs = 2 if split < blocks else 1

    def kernel(table_ref, *refs):
        sources = refs[: len(arrays)]
        wholes = refs[len(arrays) : len(arrays) + outs]
        wide, narrow, in_sem, out_sem = refs[len(arrays) + outs :]
        half = rows // 2
        first = pl.multiple_of(table_ref[len(steps)] * half, half)
        second = pl.multiple_of(half - first, half)

        def fetch(step):
            slot = step % depth
            if len(place[step]) == 1:
                ((n, k),) = place[step]
                return [pltpu.make_async_copy(sources[n].at[k], wide.at[slot], in_sem.at[slot, 0])]
            copies = []
            for part, ((n, k), start) in enumerate(zip(place[step], (first, second))):
                spot = wide.at[slot, pl.ds(start, half)]
                copies.append(pltpu.make_async_copy(sources[n].at[k], spot, in_sem.at[slot, part]))
            return copies

        def leave(step, whole, spot):
            slot = step % depth
            return pltpu.make_async_copy(narrow.at[slot], whole.at[spot], out_sem.at[slot])

        for step in range(len(steps) + depth - 1):
            if step < len(steps):
                for copy in fetch(step):
                    copy.start()
            step = step - (depth - 1)
            if step < 0:
                continue
            slot = step % depth
            for copy in fetch(step):
                copy.wait()
            if step >= depth:
                leave(step - depth, wholes[0], 0).wait()
            narrow[slot] = wide[slot].astype(jnp.bfloat16)
            spot = table_ref[step]
            if outs == 1:
                leave(step, wholes[0], spot).start()
            else:

                @pl.when(spot < split)
                def _():
                    leave(step, wholes[0], spot).start()

                @pl.when(spot >= split)
                def _():
                    leave(step, wholes[1], spot - split).start()

        for step in range(max(0, len(steps) - depth), len(steps)):
            leave(step, wholes[0], 0).wait()

    shapes = [jax.ShapeDtypeStruct((split, rows, D), jnp.bfloat16)]
    if outs == 2:
        shapes.append(jax.ShapeDtypeStruct((blocks - split, rows, D), jnp.bfloat16))
    anywhere = pl.BlockSpec(memory_space=pl.ANY)
    return pl.pallas_call(
        kernel,
        in_specs=[pl.BlockSpec(memory_space=pltpu.SMEM)] + [anywhere] * len(arrays),
        out_specs=[anywhere] * outs,
        out_shape=shapes,
        scratch_shapes=[
            pltpu.VMEM((depth, rows, D), jnp.float32),
            pltpu.VMEM((depth, rows, D), jnp.bfloat16),
            pltpu.SemaphoreType.DMA((depth, 2)),
            pltpu.SemaphoreType.DMA((depth,)),
        ],
        compiler_params=pltpu.CompilerParams(vmem_limit_bytes=32 * 1024 * 1024),
        cost_estimate=small_cost,
    )(table, *arrays)


class Order:
    def __init__(self):
        self.token = None

    def after(self, *arrays):
        if self.token is not None:
            arrays = lax.optimization_barrier((*arrays, self.token))[:-1]
        return arrays if len(arrays) > 1 else arrays[0]

    def mark(self, *arrays):
        arrays = self.after(*arrays)
        self.token = arrays[0] if isinstance(arrays, tuple) else arrays
        return arrays


def swap_plane(order, for_x, for_y):
    for_x, for_y = order.after(for_x, for_y)
    return to_x(for_x), to_y(for_y)


def in_turn(arrays):
    count = len(arrays)
    twice = jnp.stack(list(arrays[::-1]) * 2)
    return lax.dynamic_slice_in_dim(twice, count - 1 - lax.axis_index("mp"), count, 0)


def gather_deep(array):
    return in_turn([array] + [turn_mp(array, shift) for shift in range(1, lax.axis_size("mp"))])


def sum_flat(array):
    for swap in (to_core, to_x, to_y):
        array = array + swap(array)
    return array


def bring(order, shard, quarter, core):
    count = lax.axis_size("mp")
    part = pick(pick(shard.reshape(4, 2, -1, D), quarter, 0), core, 0)
    return lax.all_gather(order.after(part), "mp")


def others(whole):
    count = lax.axis_size("mp")
    twice = jnp.concatenate([whole, whole], 0)
    return lax.dynamic_slice_in_dim(twice, lax.axis_index("mp") + 1, count - 1, 0)


def assemble_weight(shard, parts, swapped, core, split):
    count = lax.axis_size("mp")
    rows = shard.shape[0] // 8

    def spot(shard_index, quarter):
        shard_index = lax.rem(lax.axis_index("mp") + shard_index, count)
        return quarter * count + shard_index

    if swapped is None:
        mine = pick(shard.reshape(4, 2, rows, D), core, 1)
    else:
        mine = shard.reshape(4, 2 * rows, D)
    steps = [((mine, n),) for n in range(4)]
    targets = [spot(0, n) for n in range(4)]
    for n, (array, quarter, first) in enumerate(parts):
        for k in range(array.shape[0]):
            steps.append(((array, k),) if swapped is None else ((array, k), (swapped[n], k)))
            targets.append(spot(first + k, quarter))
    rows = mine.shape[1]
    whole = assemble(steps, targets, core, rows, count * 4, split or count * 4)
    return [array.reshape(-1, D) for array in whole]


def cut_corner(grad, quarter):
    corner = pick(grad, quarter ^ 3, 0)
    half = corner.shape[0] // 2
    return corner[:half], corner[half:]


def cut_sides(grad, quarter, add_y, add_x):
    half = add_y.shape[0]
    for_y = pick(grad, quarter ^ 2, 0)
    for_x = pick(grad, quarter ^ 1, 0)
    for_y = jnp.concatenate([for_y[:half] + add_y, for_y[half:]], 0)
    for_x = jnp.concatenate([for_x[:half], for_x[half:] + add_x], 0)
    return for_x, for_y


def sum_deep(order, grad, quarter, from_x, from_y):
    own = order.mark(pick(grad, quarter, 0) + from_x + from_y)
    return lax.psum_scatter(own, "mp", scatter_dimension=0, tiled=False)


def place_rows(pieces, rows, near_state=None):
    arrays = []
    for array, *_ in pieces:
        if not any(array is other for other in arrays):
            arrays.append(array)
    steps = [
        (next(n for n, other in enumerate(arrays) if other is array), first, amount)
        for array, first, amount, _ in pieces
    ]
    table = jnp.stack([jnp.asarray(spot, jnp.int32) for *_, spot in pieces])

    def kernel(table_ref, *refs):
        sources = refs[: len(arrays)]
        sems = refs[-1]
        if near_state is None:
            out_ref = refs[len(arrays)]
        else:
            state_ref, out_ref, moment_ref = refs[len(arrays) : -1]
        copies = []
        for step, (n, first, amount) in enumerate(steps):
            spot = pl.multiple_of(table_ref[step], 8)
            source = sources[n].at[pl.ds(first, amount)]
            copies.append(
                pltpu.make_async_copy(source, out_ref.at[pl.ds(spot, amount)], sems.at[step])
            )
        for copy in copies:
            copy.start()
        for copy in copies:
            copy.wait()
        if near_state is None:
            return
        leading, length = near_state.shape
        chunk = length if length < 384 else 384
        for lead in range(leading):
            total = jnp.zeros((1, D), jnp.float32)
            for first in range(0, length, chunk):
                grad = out_ref[lead * length + first : lead * length + first + chunk]
                squares = grad * grad + moment_eps
                total = total + jnp.sum(squares, 0, keepdims=True)
                near = 0.5 * state_ref[lead, :1, first : first + chunk]
                near = near + 0.5 * (as_row(lanes_of(squares)) / D)
                moment_ref[lead, 1:2, first : first + chunk] = near
            moment_ref[lead, :1] = total
            if length < D:
                moment_ref[lead, 1:2, length:] = jnp.zeros((1, D - length), jnp.float32)

    vmem = pl.BlockSpec(memory_space=pltpu.VMEM)
    in_specs = [pl.BlockSpec(memory_space=pltpu.SMEM)]
    in_specs = in_specs + [pl.BlockSpec(memory_space=pl.ANY)] * len(arrays)
    out_specs, shapes = [vmem], [jax.ShapeDtypeStruct((rows, D), jnp.float32)]
    operands = [table, *arrays]
    if near_state is not None:
        leading, length = near_state.shape
        in_specs.append(vmem)
        operands.append(near_state.reshape(leading, 1, length))
        out_specs.append(vmem)
        shapes.append(jax.ShapeDtypeStruct((leading, 2, D), jnp.float32))
    result = pl.pallas_call(
        kernel,
        in_specs=in_specs,
        out_specs=out_specs,
        out_shape=shapes,
        scratch_shapes=[pltpu.SemaphoreType.DMA((len(steps),))],
        compiler_params=pltpu.CompilerParams(vmem_limit_bytes=40 * 1024 * 1024),
        cost_estimate=small_cost,
    )(*operands)
    return result[0] if near_state is None else result


def add_half(grads, given, core):
    rows = grads[0].shape[2]
    amounts = [array.shape[0] for array in grads]
    firsts = [sum(amounts[:n]) for n in range(len(amounts))]

    def kernel(core_ref, *refs):
        for n, (first, amount) in enumerate(zip(firsts, amounts)):

            @pl.when((pl.program_id(0) >= first) & (pl.program_id(0) < first + amount))
            def _():
                refs[-1][...] = refs[n][0] + refs[len(grads) + n][...]

    def at(first, amount):
        return lambda step: jnp.clip(step - first, 0, amount - 1)

    spots = [at(*pair) for pair in zip(firsts, amounts)]
    own_specs = [
        pl.BlockSpec((1, 1, rows, D), lambda step, core_ref, at=at: (at(step), core_ref[0], 0, 0))
        for at in spots
    ]
    given_specs = [
        pl.BlockSpec((1, rows, D), lambda step, core_ref, at=at: (at(step), 0, 0)) for at in spots
    ]
    total = sum(amounts)
    return pl.pallas_call(
        kernel,
        grid_spec=pltpu.PrefetchScalarGridSpec(
            num_scalar_prefetch=1,
            grid=(total,),
            in_specs=own_specs + given_specs,
            out_specs=pl.BlockSpec((1, rows, D), lambda step, core_ref: (step, 0, 0)),
        ),
        out_shape=jax.ShapeDtypeStruct((total, rows, D), jnp.float32),
        compiler_params=pltpu.CompilerParams(vmem_limit_bytes=40 * 1024 * 1024),
        cost_estimate=small_cost,
    )(core[None], *grads, *given)


def order_tokens(arrays, mp_index):
    count = len(arrays)
    tokens, width = arrays[0].shape[0], arrays[0].shape[1] // 2

    def kernel(place_ref, *refs):
        left_ref, right_ref, held, sems = refs[count:]

        def copy(n, index):
            return pltpu.make_async_copy(refs[n], held.at[index], sems.at[index])

        for index in range(count):
            for n in range(count):

                @pl.when(lax.rem(place_ref[0] + count - index, count) == n)
                def _():
                    copy(n, index).start()

        for index in range(count):
            copy(0, index).wait()
            rows = slice(index * tokens, (index + 1) * tokens)
            left_ref[rows] = held[index, :, :width]
            right_ref[rows] = held[index, :, width:]

    vmem = pl.BlockSpec(memory_space=pltpu.VMEM)
    shape = jax.ShapeDtypeStruct((count * tokens, width), jnp.float32)
    return pl.pallas_call(
        kernel,
        in_specs=[pl.BlockSpec(memory_space=pltpu.SMEM)]
        + [pl.BlockSpec(memory_space=pl.ANY)] * count,
        out_specs=[vmem, vmem],
        out_shape=[shape, shape],
        scratch_shapes=[
            pltpu.VMEM((count, tokens, 2 * width), jnp.float32),
            pltpu.SemaphoreType.DMA((count,)),
        ],
        compiler_params=pltpu.CompilerParams(vmem_limit_bytes=40 * 1024 * 1024),
        cost_estimate=small_cost,
    )(mp_index[None], *arrays)


def lanes_of(array):
    total = array[:, :128]
    for tile in range(1, array.shape[1] // 128):
        total = total + array[:, tile * 128 : (tile + 1) * 128]
    return total


def as_row(column):
    return jnp.sum(column.T, 0, keepdims=True)


def as_column(row):
    return jnp.broadcast_to(row, (128, row.shape[1])).T


def scale_kernel(count, by_rows, place_ref, grad_ref, state_ref, before_ref, *refs):
    sources = refs[:count]
    far_ref, scale_ref, near_ref, step_ref = refs[count:]
    rows = grad_ref.shape[1]
    total = jnp.zeros((1, D), jnp.float32)
    near_sum = jnp.zeros((1, 1), jnp.float32)
    for index in range(count):
        part = jnp.zeros((2, D), jnp.float32)
        for shift in range(count):
            part = jnp.where(place_ref[0] == (index + shift) % count, sources[shift][0], part)
        total = total + part[:1]
        near_sum = near_sum + jnp.sum(part[1:], 1, keepdims=True)
    far = 0.5 * state_ref[0] + 0.5 * (total / (count * rows))
    far_ref[0] = far
    lead = pl.program_id(0)
    near_mean = near_sum / (count * rows)
    far_mean = jnp.sum(far, 1, keepdims=True) / D
    if all(by_rows):
        mean = near_mean
    elif not any(by_rows):
        mean = far_mean
    else:
        split = by_rows.index(True)
        mean = jnp.where(lead >= split, near_mean, far_mean)
    far_scale = lax.rsqrt(far)
    near_scale = as_column(lax.rsqrt(sources[0][0][1:2, :rows] / mean))
    scale_ref[0] = far_scale
    near_ref[0] = near_scale
    step = grad_ref[0] * far_scale
    step = lanes_of(step * step) * near_scale * near_scale

    @pl.when(lead == 0)
    def _():
        step_ref[...] = before_ref[...]

    step_ref[...] += jnp.sum(step.reshape(rows // 8, 8, 128), 0)


def scales(grad, far_state, before, sources, first, mp_index, by_rows):
    leading, rows, _ = grad.shape
    count = len(sources)
    small = pl.BlockSpec((1, 2, D), lambda i: (i + first, 0, 0))
    line = pl.BlockSpec((1, 1, D), lambda i: (i, 0, 0))
    return pl.pallas_call(
        functools.partial(scale_kernel, count, by_rows),
        grid=(leading,),
        in_specs=[
            pl.BlockSpec(memory_space=pltpu.SMEM),
            pl.BlockSpec((1, rows, D), lambda i: (i, 0, 0)),
            line,
            pl.BlockSpec((8, 128), lambda i: (0, 0)),
        ]
        + [small] * count,
        out_specs=[
            line,
            line,
            pl.BlockSpec((1, rows, 128), lambda i: (i, 0, 0)),
            pl.BlockSpec((8, 128), lambda i: (0, 0)),
        ],
        out_shape=[
            jax.ShapeDtypeStruct((leading, 1, D), jnp.float32),
            jax.ShapeDtypeStruct((leading, 1, D), jnp.float32),
            jax.ShapeDtypeStruct((leading, rows, 128), jnp.float32),
            jax.ShapeDtypeStruct((8, 128), jnp.float32),
        ],
        compiler_params=pltpu.CompilerParams(vmem_limit_bytes=40 * 1024 * 1024),
        cost_estimate=small_cost,
    )(mp_index[None], grad, far_state.reshape(leading, 1, D), before, *sources)


param_count = 6.0 * D * D + 2.0 * D * FF + 7.0 * D + FF


def renew_kernel(turned, count, rate_ref, weight_ref, grad_ref, far_ref, near_ref, *refs):
    new_ref, low_ref = refs[count:]
    total = refs[0][...]
    for ref in refs[1:count]:
        total = total + ref[...]
    total = jnp.sum(jnp.sum(total, 0, keepdims=True), 1, keepdims=True) + rate_ref[1]
    divisor = jnp.maximum(1.0, jnp.sqrt(total / param_count) / clip_level)
    step = grad_ref[0] * far_ref[0] * (near_ref[0][:, :1] * (rate_ref[0] / divisor))
    new = weight_ref[0] - (step.T if turned else step)
    new_ref[0] = new
    low_ref[0] = new.astype(jnp.bfloat16)


def renew(weight, grad, far_scale, near_scale, rate, steps, turned, first=0):
    leading, rows = weight.shape[0], grad.shape[1]
    if turned:
        width = 384
        grid = (leading, D // width)
        weight_spec = pl.BlockSpec((1, width, rows), lambda i, j: (i, j, 0))
        grad_spec = pl.BlockSpec((1, rows, width), lambda i, j: (i + first, 0, j))
        far_spec = pl.BlockSpec((1, 1, width), lambda i, j: (i + first, 0, j))
        near_spec = pl.BlockSpec((1, rows, 128), lambda i, j: (i + first, 0, 0))
    else:
        height = min(rows, 288)
        grid = (leading, rows // height)
        weight_spec = pl.BlockSpec((1, height, D), lambda i, j: (i, j, 0))
        grad_spec = pl.BlockSpec((1, height, D), lambda i, j: (i + first, j, 0))
        far_spec = pl.BlockSpec((1, 1, D), lambda i, j: (i + first, 0, 0))
        near_spec = pl.BlockSpec((1, height, 128), lambda i, j: (i + first, j, 0))
    return pl.pallas_call(
        functools.partial(renew_kernel, turned, len(steps)),
        grid=grid,
        in_specs=[pl.BlockSpec(memory_space=pltpu.SMEM), weight_spec, grad_spec, far_spec, near_spec]
        + [pl.BlockSpec((8, 128), lambda i, j: (0, 0))] * len(steps),
        out_specs=[weight_spec, weight_spec],
        out_shape=[
            jax.ShapeDtypeStruct(weight.shape, jnp.float32),
            jax.ShapeDtypeStruct(weight.shape, jnp.bfloat16),
        ],
        compiler_params=pltpu.CompilerParams(vmem_limit_bytes=40 * 1024 * 1024),
        cost_estimate=small_cost,
    )(rate, weight, grad, far_scale, near_scale, *steps)


def head_windows():
    spans = []
    for head in range(D // HEAD_DIM):
        first = head * HEAD_DIM
        start = first // 128 * 128
        stop = -(-(first + HEAD_DIM) // 128) * 128
        spans.append((first, start, stop - start))
    return spans


def head_mask(first, start, width):
    lanes = start + lax.broadcasted_iota(jnp.int32, (SEQ, width), 1)
    return (lanes >= first) & (lanes < first + HEAD_DIM)


def dot_nt(left_side, right_side):
    return lax.dot_general(
        left_side, right_side, (((1,), (1,)), ((), ())), preferred_element_type=jnp.float32
    )


def attend_kernel(qkv_ref, out_ref, total):
    total[...] = jnp.zeros_like(total)
    for first, start, width in head_windows():
        keep = head_mask(first, start, width)
        query = qkv_ref[0, :, start : start + width]
        key = jnp.where(keep, qkv_ref[0, :, D + start : D + start + width], 0)
        value = jnp.where(keep, qkv_ref[0, :, 2 * D + start : 2 * D + start + width], 0)
        scores = dot_nt(query, key) * HEAD_DIM ** (-0.5)
        expo = jnp.exp(scores - jnp.max(scores, 1, keepdims=True))
        probs = (expo / jnp.sum(expo, 1, keepdims=True)).astype(jnp.bfloat16)
        total[:, start : start + width] += matmul(probs, value)
    out_ref[0] = total[...].astype(jnp.bfloat16)


def attend(qkv):
    images = qkv.shape[0]
    return pl.pallas_call(
        attend_kernel,
        grid=(images,),
        in_specs=[pl.BlockSpec((1, SEQ, 3 * D), lambda i: (i, 0, 0))],
        out_specs=pl.BlockSpec((1, SEQ, D), lambda i: (i, 0, 0)),
        out_shape=jax.ShapeDtypeStruct((images, SEQ, D), jnp.bfloat16),
        scratch_shapes=[pltpu.VMEM((SEQ, D), jnp.float32)],
        compiler_params=pltpu.CompilerParams(vmem_limit_bytes=40 * 1024 * 1024),
        cost_estimate=small_cost,
    )(qkv)


def attend_back_kernel(qkv_ref, grad_ref, out_ref, query_sum, key_sum, value_sum):
    scale = HEAD_DIM ** (-0.5)
    for ref in (query_sum, key_sum, value_sum):
        ref[...] = jnp.zeros_like(ref)
    for first, start, width in head_windows():
        span = slice(start, start + width)
        keep = head_mask(first, start, width)
        query = jnp.where(keep, qkv_ref[0, :, span], 0)
        key = jnp.where(keep, qkv_ref[0, :, D + start : D + start + width], 0)
        value = jnp.where(keep, qkv_ref[0, :, 2 * D + start : 2 * D + start + width], 0)
        above = jnp.where(keep, grad_ref[0, :, span], 0)
        scores = dot_nt(key, query) * scale
        expo = jnp.exp(scores - jnp.max(scores, 0, keepdims=True))
        probs = expo / jnp.sum(expo, 0, keepdims=True)
        prob_grad = dot_nt(value, above)
        inner = jnp.sum(probs * prob_grad, 0, keepdims=True)
        score_grad = (probs * (prob_grad - inner)).astype(jnp.bfloat16)
        value_sum[:, span] += matmul(probs.astype(jnp.bfloat16), above)
        key_sum[:, span] += matmul(score_grad, query) * scale
        query_sum[:, span] += (
            lax.dot_general(
                score_grad, key, (((0,), (0,)), ((), ())), preferred_element_type=jnp.float32
            )
            * scale
        )
    out_ref[0, :, :D] = query_sum[...].astype(jnp.bfloat16)
    out_ref[0, :, D : 2 * D] = key_sum[...].astype(jnp.bfloat16)
    out_ref[0, :, 2 * D :] = value_sum[...].astype(jnp.bfloat16)


def attend_back(qkv, grad):
    images = qkv.shape[0]
    return pl.pallas_call(
        attend_back_kernel,
        grid=(images,),
        in_specs=[
            pl.BlockSpec((1, SEQ, 3 * D), lambda i: (i, 0, 0)),
            pl.BlockSpec((1, SEQ, D), lambda i: (i, 0, 0)),
        ],
        out_specs=pl.BlockSpec((1, SEQ, 3 * D), lambda i: (i, 0, 0)),
        out_shape=jax.ShapeDtypeStruct((images, SEQ, 3 * D), jnp.bfloat16),
        scratch_shapes=[pltpu.VMEM((SEQ, D), jnp.float32)] * 3,
        compiler_params=pltpu.CompilerParams(vmem_limit_bytes=40 * 1024 * 1024),
        cost_estimate=small_cost,
    )(qkv, grad)


def body_data(
    block_input,
    skip_input,
    timesteps,
    class_labels,
    loss_weights,
    grad_output,
    skip_weight,
    qkv_weight,
    proj_weight,
    fc1_weight,
    fc2_weight,
    vectors,
    hidden_bias,
    skip_rows,
    skip_cols,
    qkv_rows,
    qkv_cols,
    proj_rows,
    proj_cols,
    fc1_rows,
    fc1_cols,
    fc2_rows,
    fc2_cols,
    vector_moments,
    hidden_moments,
):
    image_count = timesteps.shape[0]
    mp_count = lax.axis_size("mp")
    dp_count = lax.axis_size("dp")
    mp_index = lax.axis_index("mp")
    dp_index = lax.axis_index("dp")
    core = lax.rem(dp_index, 2)
    quarter = lax.div(dp_index, 2)
    images = image_count // mp_count
    tokens = images * SEQ
    width_local = qkv_weight.shape[2]
    hidden_local = fc1_weight.shape[1]
    hidden_slice = hidden_local // dp_count
    order = Order()

    skip_shard = skip_weight.reshape(-1, D)
    skip_whole = bring(order, skip_shard, quarter, core)
    hidden_all = gather_deep(hidden_bias)
    hidden_state = gather_deep(hidden_moments).reshape(-1)

    angles = (timesteps.astype(jnp.float32) + 0.5) * (0.5 * math.pi / total_steps)
    alpha_sq = jnp.square(jnp.cos(angles))
    sigma_sq = jnp.square(jnp.sin(angles))
    snr_weight = 5.0 * sigma_sq / jnp.maximum(alpha_sq, 5.0 * sigma_sq)
    base_weight = loss_weights * snr_weight
    one_hot = (class_labels[:, None] == jnp.arange(CLASSES, dtype=jnp.int32)[None, :]).astype(
        jnp.float32
    )
    batch = jnp.concatenate([jnp.sum(one_hot, 0), jnp.sum(base_weight)[None]])

    attn_shard = jnp.concatenate(
        [qkv_weight.transpose(0, 2, 1).reshape(3 * width_local, D), proj_weight], 0
    )
    attn_shard = order.mark(attn_shard)
    attn_whole = bring(order, attn_shard, quarter, core)
    batch = order.mark(batch + to_core(batch))
    batch_x = to_x(batch)
    fc1_shard = order.mark(fc1_weight.T)
    fc2_shard = fc2_weight
    batch = order.mark(batch + batch_x)
    batch_y = to_y(batch)
    start = mp_index * tokens
    block_local = lax.dynamic_slice_in_dim(block_input, start, tokens, 0)
    skip_local = lax.dynamic_slice_in_dim(skip_input, start, tokens, 0)
    both_inputs = jnp.concatenate(
        [
            array.reshape(tokens, mp_count, 2, -1).transpose(0, 2, 1, 3).reshape(tokens, D)
            for array in (block_local, skip_local)
        ],
        1,
    )
    both_inputs = order.mark(both_inputs)
    batch = order.mark(batch + batch_y)

    skip_own = others(order.mark(skip_whole))
    skip_x, skip_y = swap_plane(order, skip_own, skip_own)
    skip_swapped = [to_core(skip_own)]
    fc1_whole = bring(order, fc1_shard, quarter, core)
    hidden_own = pick(hidden_all.reshape(mp_count, 4, 2, hidden_slice), core, 2)
    hidden_own = hidden_own.transpose(1, 0, 2).reshape(-1)
    own_count = jnp.dot(one_hot, batch[:CLASSES], precision=lax.Precision.HIGHEST)
    item_weight = base_weight * lax.rsqrt(own_count)
    hidden_own, item_weight = order.mark(hidden_own, item_weight)
    batch_scale = image_count * dp_count / batch[CLASSES]
    grad_local = lax.dynamic_slice_in_dim(grad_output, start, tokens, 0)
    item_local = lax.dynamic_slice_in_dim(item_weight, mp_index * images, images, 0)
    upstream = (
        grad_local.astype(jnp.float32).reshape(images, SEQ, D) * item_local[:, None, None]
    ).reshape(-1, D)
    upstream = order.mark(upstream)

    skip_x, skip_y = order.mark(skip_x, skip_y)
    skip_one, skip_two = swap_plane(order, skip_y[:2], skip_x[2:])
    skip_swapped = skip_swapped + [to_core(skip_x), to_core(skip_y)]
    skip_one, skip_two = order.mark(skip_one, skip_two)
    skip_swapped = skip_swapped + [to_core(skip_one), to_core(skip_two)]
    attn_own = others(order.mark(attn_whole))
    attn_x, attn_y = swap_plane(order, attn_own, attn_own)
    fc2_whole = bring(order, fc2_shard, quarter, core)
    fc2_across = bring(order, fc2_shard, quarter ^ 3, core)
    skip_swapped = order.mark(*skip_swapped)
    attn_swapped = [to_core(order.after(attn_own))]
    skip_parts = [
        (skip_own, quarter, 1),
        (skip_x, quarter ^ 1, 1),
        (skip_y, quarter ^ 2, 1),
        (skip_one, quarter ^ 3, 1),
        (skip_two, quarter ^ 3, 3),
    ]
    (skip_low,) = assemble_weight(skip_shard, skip_parts, skip_swapped, core, 0)
    joined = matmul(both_inputs, skip_low) + vectors[4]
    normed, normal_one, inverse_one = norm_forward(joined, vectors[0], vectors[1])
    normed_low = normed.astype(jnp.bfloat16)
    joined, normed_low, normal_one = order.mark(joined, normed_low, normal_one)
    upstream_other = to_core(order.after(upstream))

    attn_x, attn_y = order.mark(attn_x, attn_y)
    attn_one, attn_two = swap_plane(order, attn_y[:1], attn_x[1:])
    attn_swapped = attn_swapped + [to_core(attn_x), to_core(attn_y)]
    upstream_other = order.mark(upstream_other) * batch_scale
    upstream = upstream * batch_scale
    upstream_low = jnp.concatenate([upstream, upstream_other], 0).astype(jnp.bfloat16)
    upstream_low = order.mark(upstream_low)
    weight_sq = jnp.stack(
        [
            jnp.sum(array * array)
            for array in (skip_weight, qkv_weight, proj_weight, fc1_weight, fc2_weight, hidden_bias)
        ]
    )
    weight_sq = order.mark(weight_sq)
    fc1_own = others(order.mark(fc1_whole))
    fc1_x, fc1_y = swap_plane(order, fc1_own, fc1_own)
    attn_one, attn_two = order.mark(attn_one, attn_two)
    attn_swapped = attn_swapped + [to_core(attn_one), to_core(attn_two)]
    attn_parts = [
        (attn_own, quarter, 1),
        (attn_x, quarter ^ 1, 1),
        (attn_y, quarter ^ 2, 1),
        (attn_one, quarter ^ 3, 1),
        (attn_two, quarter ^ 3, 2),
    ]
    attn_swapped = order.mark(*attn_swapped)
    qkv_low, proj_low = assemble_weight(
        attn_shard, attn_parts, attn_swapped, core, 3 * mp_count
    )
    qkv_all = jnp.einsum(
        "itd,ed->ite",
        normed_low.reshape(images, SEQ, D),
        qkv_low,
        preferred_element_type=jnp.float32,
    ).astype(jnp.bfloat16)
    qkv_all = order.mark(qkv_all)
    attended = attend(qkv_all).reshape(tokens, D)
    residual = joined + matmul(attended, proj_low) + vectors[5]
    residual = order.mark(residual)
    fc1_x, fc1_y = order.mark(fc1_x, fc1_y)
    fc1_cut = order.mark(fc1_y[:2], fc1_x[2:])
    fc1_one, fc1_two = swap_plane(order, *fc1_cut)
    fc2_own = others(order.mark(fc2_whole))
    fc2_x, fc2_y = swap_plane(order, fc2_own, fc2_own)
    normed_two, normal_two, inverse_two = norm_forward(
        order.after(residual), vectors[2], vectors[3]
    )
    normed_two, normal_two = order.mark(normed_two, normal_two)
    normed_two_other = to_core(normal_two)
    fc1_one, fc1_two = order.mark(fc1_one, fc1_two)
    fc1_parts = [
        (fc1_own, quarter, 1),
        (fc1_x, quarter ^ 1, 1),
        (fc1_y, quarter ^ 2, 1),
        (fc1_one, quarter ^ 3, 1),
        (fc1_two, quarter ^ 3, 3),
    ]
    (fc1_low,) = assemble_weight(fc1_shard, fc1_parts, None, core, 0)
    fc1_low = order.mark(fc1_low)
    normed_two_other = order.mark(normed_two_other) * vectors[2] + vectors[3]
    normed_two_low = jnp.concatenate([normed_two, normed_two_other], 0).astype(jnp.bfloat16)
    normed_two_low = order.mark(normed_two_low)
    pre_act = (
        jnp.einsum("td,fd->tf", normed_two_low, fc1_low, preferred_element_type=jnp.float32)
        + hidden_own
    )
    activated, gelu_pull = jax.vjp(gelu_exact, pre_act)
    activated_low = activated.astype(jnp.bfloat16)
    fc2_grad = jnp.einsum(
        "tf,td->fd", activated_low, upstream_low, preferred_element_type=jnp.float32
    ).reshape(4, mp_count, hidden_slice, D)
    fc2_grad = order.mark(fc2_grad)
    fc2_add = swap_plane(order, *order.mark(*cut_corner(fc2_grad, quarter)))

    fc2_x, fc2_y = order.mark(fc2_x, fc2_y)
    fc2_corner = others(order.mark(fc2_across))
    fc2_parts = [
        (fc2_own, quarter, 1),
        (fc2_x, quarter ^ 1, 1),
        (fc2_y, quarter ^ 2, 1),
        (fc2_corner, quarter ^ 3, 1),
    ]
    (fc2_low,) = assemble_weight(fc2_shard, fc2_parts, None, core, 0)
    fc2_low = order.mark(fc2_low)
    forward_part = order.mark(matmul(activated_low, fc2_low))
    forward_other = to_core(forward_part[tokens:])
    act_grad = jnp.einsum(
        "td,fd->tf", order.after(upstream_low), fc2_low, preferred_element_type=jnp.float32
    )
    pre_grad = gelu_pull(act_grad)[0]
    hidden_grad = jnp.sum(pre_grad, 0)
    pre_low, hidden_grad = order.mark(pre_grad.astype(jnp.bfloat16), hidden_grad)
    block_own = residual + forward_part[:tokens] + order.mark(forward_other)
    block_own = order.mark(block_own.reshape(images, SEQ, D))
    block_all = lax.all_gather(block_own, "mp")
    fc2_add = order.mark(*fc2_add)
    fc2_sides = swap_plane(order, *order.mark(*cut_sides(fc2_grad, quarter, *fc2_add)))
    back_part = order.mark(matmul(order.after(pre_low), fc1_low))
    back_other = to_core(back_part[tokens:])
    fc1_grad = jnp.einsum(
        "tf,td->fd",
        order.after(pre_low),
        normed_two_low,
        preferred_element_type=jnp.float32,
    ).reshape(4, mp_count, hidden_slice, D)
    fc1_grad = order.mark(fc1_grad)
    fc1_add = swap_plane(order, *order.mark(*cut_corner(fc1_grad, quarter)))
    norm_two_in = back_part[:tokens] + order.mark(back_other)
    back_two, gain_two_grad, bias_two_grad = norm_backward(
        norm_two_in, normal_two, inverse_two, vectors[2]
    )
    residual_grad = upstream + back_two
    residual_low = residual_grad.astype(jnp.bfloat16)
    residual_grad, residual_low = order.mark(residual_grad, residual_low)
    attended_grad = jnp.einsum(
        "td,ed->te", residual_low, proj_low, preferred_element_type=jnp.float32
    ).astype(jnp.bfloat16)
    qkv_grad_low = attend_back(
        qkv_all, order.mark(attended_grad.reshape(images, SEQ, D))
    ).reshape(tokens, 3 * D)
    qkv_grad_low = order.mark(qkv_grad_low)
    fc2_sides = order.mark(*fc2_sides)
    fc2_piece = sum_deep(order, fc2_grad, quarter, *fc2_sides)
    qkv_grad = jnp.einsum(
        "te,td->ed", order.after(qkv_grad_low), normed_low, preferred_element_type=jnp.float32
    ).reshape(3 * mp_count, 2, hidden_slice, D)
    proj_grad = jnp.einsum(
        "te,td->ed", attended, order.after(residual_low), preferred_element_type=jnp.float32
    ).reshape(mp_count, 2, hidden_slice, D)
    attn_given = order.mark(pick(qkv_grad, 1 - core, 1), pick(proj_grad, 1 - core, 1))
    fc1_add = order.mark(*fc1_add)
    fc1_sides = swap_plane(order, *order.mark(*cut_sides(fc1_grad, quarter, *fc1_add)))
    attn_given = [to_core(array) for array in order.after(*attn_given)]
    norm_one_in = matmul(order.after(qkv_grad_low), qkv_low)
    back_one, gain_one_grad, bias_one_grad = norm_backward(
        norm_one_in, normal_one, inverse_one, vectors[0]
    )
    joined_grad = residual_grad + back_one
    joined_low = joined_grad.astype(jnp.bfloat16)
    joined_grad, joined_low = order.mark(joined_grad, joined_low)
    skip_grad = jnp.einsum(
        "tc,td->cd", both_inputs, joined_low, preferred_element_type=jnp.float32
    ).reshape(4 * mp_count, 2, -1, D)
    skip_given = order.mark(pick(skip_grad, 1 - core, 1))
    skip_given = to_core(skip_given)
    block_all = order.mark(block_all)
    attn_given = order.mark(*attn_given)
    attn_grad = add_half([qkv_grad, proj_grad], attn_given, core)
    attn_grad = order.mark(attn_grad.reshape(4, mp_count, hidden_slice, D))
    attn_add = swap_plane(order, *order.mark(*cut_corner(attn_grad, quarter)))
    fc1_sides = order.mark(*fc1_sides)
    fc1_piece = sum_deep(order, fc1_grad, quarter, *fc1_sides)
    skip_shards = skip_low.reshape(4, mp_count, -1, D)

    def input_product(shift):
        shard_low = pick(skip_shards, lax.rem(mp_index + shift, mp_count), 1).reshape(-1, D)
        return order.mark(
            jnp.einsum("td,cd->tc", joined_low, shard_low, preferred_element_type=jnp.float32)
        )

    stay, turn_one, turn_two, turn_three = [input_product(shift) for shift in range(4)]
    attn_add = order.mark(*attn_add)
    attn_sides = swap_plane(order, *order.mark(*cut_sides(attn_grad, quarter, *attn_add)))
    skip_given = order.mark(skip_given)
    skip_grad = add_half([skip_grad], [skip_given], core)
    skip_grad = order.mark(skip_grad.reshape(4, mp_count, -1, D))
    skip_add = swap_plane(order, *order.mark(*cut_corner(skip_grad, quarter)))
    fc2_piece = order.mark(fc2_piece)
    vector_grad = jnp.stack(
        [
            gain_one_grad,
            bias_one_grad,
            gain_two_grad,
            bias_two_grad,
            jnp.sum(joined_grad, 0),
            jnp.sum(residual_grad, 0),
            jnp.sum(upstream, 0),
        ]
    )
    hidden_grad = hidden_grad.reshape(4, mp_count, 1, hidden_slice).transpose(1, 0, 2, 3)
    hidden_grad = jnp.where(jnp.arange(2)[None, None, :, None] == core, hidden_grad, 0.0)
    small = order.mark(jnp.concatenate([vector_grad.reshape(-1), hidden_grad.reshape(-1)]))
    small_core = to_core(small)
    attn_sides = order.mark(*attn_sides)
    attn_piece = sum_deep(order, attn_grad, quarter, *attn_sides)
    fc1_piece = order.mark(fc1_piece)
    skip_add = order.mark(*skip_add)
    skip_sides = swap_plane(order, *order.mark(*cut_sides(skip_grad, quarter, *skip_add)))
    small = order.mark(small + order.mark(small_core))
    small_x = to_x(small)
    skip_sides = order.mark(*skip_sides)
    small = order.mark(small + order.mark(small_x))
    small_y = to_y(small)
    skip_piece = sum_deep(order, skip_grad, quarter, *skip_sides)

    def spread(piece):
        return swap_plane(order, piece, piece)

    def half_of(rows):
        return (rows // 2 + 7) // 8 * 8

    def spread_far(near):
        half = half_of(near[0].shape[0])
        return swap_plane(order, near[1][:half], near[0][half:])

    def hold(piece, near, far):
        rows, half = piece.shape[0], far[0].shape[0]
        return place_rows(
            [
                (piece, 0, rows, quarter * rows),
                (near[0], 0, rows, (quarter ^ 1) * rows),
                (near[1], 0, rows, (quarter ^ 2) * rows),
                (far[0], 0, half, (quarter ^ 3) * rows),
                (far[1], 0, rows - half, (quarter ^ 3) * rows + half),
            ],
            4 * rows,
        )

    def interleave(held, other, near_state):
        rows = held.shape[0] // 4
        pieces = []
        for n in range(4):
            pieces.append((held, n * rows, rows, (2 * n + core) * rows))
            pieces.append((other, n * rows, rows, (2 * n + 1 - core) * rows))
        whole, sent = place_rows(pieces, 8 * rows, near_state)
        return whole.reshape(near_state.shape + (D,)), sent

    def own_state(state):
        width = state.shape[-1] // mp_count
        return lax.dynamic_slice_in_dim(state, mp_index * width, width, state.ndim - 1)

    def everywhere(array):
        return [array] + [turn_mp(array, shift) for shift in range(1, mp_count)]

    fc2_near, fc1_near = spread(fc2_piece), spread(fc1_piece)
    block_output = (block_all + vectors[6]).astype(jnp.bfloat16).reshape(-1, D)
    block_output = order.mark(block_output)
    fc2_near = order.mark(*fc2_near)
    fc2_far = spread_far(fc2_near)
    fc1_near = order.mark(*fc1_near)
    fc1_far = spread_far(fc1_near)
    turn_two = turn_mp(order.after(turn_two), 2)
    fc2_far = order.mark(*fc2_far)
    attn_piece = order.mark(attn_piece)
    attn_near = spread(attn_piece)
    fc2_held = order.mark(hold(fc2_piece, fc2_near, fc2_far))
    fc2_other = to_core(fc2_held)
    fc1_far = order.mark(*fc1_far)
    skip_piece = order.mark(skip_piece)
    skip_near = spread(skip_piece)
    turn_two = order.mark(turn_two)
    turn_one = turn_mp(order.after(turn_one), 1)
    fc1_held = order.mark(hold(fc1_piece, fc1_near, fc1_far))
    attn_near = order.mark(*attn_near)
    attn_far = spread_far(attn_near)
    fc1_other = to_core(order.after(fc1_held))
    skip_near = order.mark(*skip_near)
    skip_far = spread_far(skip_near)
    small = order.mark(small + order.mark(small_y))
    small = jnp.concatenate(
        [small, weight_sq, jnp.zeros((D - 6,), jnp.float32)], 0
    ).reshape(6, 2, D)
    fc2_sum, fc2_moments = order.mark(
        *interleave(fc2_held, order.mark(fc2_other), own_state(fc2_rows)[None])
    )
    attn_far = order.mark(*attn_far)
    attn_held = order.mark(hold(attn_piece, attn_near, attn_far))
    attn_other = to_core(attn_held)
    turn_one = order.mark(turn_one)
    turn_three = turn_mp(order.after(turn_three), 3)
    skip_far = order.mark(*skip_far)
    skip_held = order.mark(hold(skip_piece, skip_near, skip_far))
    skip_other = to_core(skip_held)
    fc1_sum, fc1_moments = order.mark(
        *interleave(fc1_held, order.mark(fc1_other), own_state(fc1_cols)[None])
    )
    hidden_sent = jnp.concatenate([fc2_moments, fc1_moments, small], 0)
    turn_three = order.mark(turn_three)
    hidden_sent = everywhere(order.mark(hidden_sent))
    attn_state = jnp.concatenate([own_state(qkv_cols), own_state(proj_rows)[None]], 0)
    attn_sum, attn_moments = order.mark(
        *interleave(attn_held, order.mark(attn_other), attn_state)
    )
    skip_sum, skip_moments = order.mark(
        *interleave(skip_held, order.mark(skip_other), own_state(skip_rows))
    )
    hidden_sent = order.mark(*hidden_sent)
    token_sent = everywhere(order.mark(jnp.concatenate([attn_moments, skip_moments], 0)))
    input_grad, skip_input_grad = order.mark(
        *order_tokens([stay, turn_one, turn_two, turn_three], mp_index)
    )
    step = jnp.zeros((8, 128), jnp.float32)
    fc2_far_new, *fc2_scales, step = order.mark(
        *scales(fc2_sum, fc2_cols[None], step, hidden_sent, 0, mp_index, (True,))
    )
    fc1_far_new, *fc1_scales, step = order.mark(
        *scales(fc1_sum, fc1_rows[None], step, hidden_sent, 1, mp_index, (False,))
    )
    token_sent = order.mark(*token_sent)
    attn_state = jnp.concatenate([qkv_rows, proj_cols[None]], 0)
    attn_far_new, *attn_scales, step = order.mark(
        *scales(attn_sum, attn_state, step, token_sent, 0, mp_index, (False, False, False, True))
    )
    skip_far_new, *skip_scales, step = order.mark(
        *scales(skip_sum, skip_cols, step, token_sent, 4, mp_index, (True, True))
    )
    steps = everywhere(step)
    small = jnp.sum(in_turn([array[2:] for array in hidden_sent]), 0).reshape(-1)
    vector_sum = small[: 7 * D].reshape(7, D)
    hidden_whole = small[7 * D : 7 * D + mp_count * hidden_local]
    weight_sq = small[11 * D : 11 * D + 6]
    vector_new = 0.5 * vector_moments + 0.5 * (vector_sum * vector_sum + moment_eps)
    vector_update = vector_sum * lax.rsqrt(vector_new)
    hidden_new = 0.5 * hidden_state + 0.5 * (hidden_whole * hidden_whole + moment_eps)
    hidden_update = hidden_whole * lax.rsqrt(hidden_new)
    vector_step = jnp.sum(vector_update * vector_update) + jnp.sum(hidden_update * hidden_update)

    def own_hidden(array):
        return lax.dynamic_slice_in_dim(array, mp_index * hidden_local, hidden_local, 0)

    hidden_sum, hidden_new = own_hidden(hidden_whole), own_hidden(hidden_new)
    hidden_update = own_hidden(hidden_update)
    tensor_sizes = (2.0 * D * D, 3.0 * D * D, 1.0 * D * D, 1.0 * D * FF, 1.0 * FF * D, 1.0 * FF)
    weight_rms = jnp.sqrt(weight_sq / jnp.array(tensor_sizes, jnp.float32))
    rates = step_rate * jnp.maximum(0.001, weight_rms)
    pairs = jnp.stack([rates, jnp.broadcast_to(vector_step, (6,))], 1)
    pairs = order.mark(pairs)
    steps = order.mark(*steps)

    qkv_turned = qkv_weight.transpose(0, 2, 1)
    skip_new, skip_new_low = renew(skip_weight, skip_sum, *skip_scales, pairs[0], steps, False)
    qkv_new, qkv_new_low = renew(qkv_turned, attn_sum, *attn_scales, pairs[1], steps, False)
    qkv_new, qkv_new_low = qkv_new.transpose(0, 2, 1), qkv_new_low.transpose(0, 2, 1)
    proj_new, proj_new_low = renew(
        proj_weight[None], attn_sum, *attn_scales, pairs[2], steps, False, first=3
    )
    fc1_new, fc1_new_low = renew(fc1_weight[None], fc1_sum, *fc1_scales, pairs[3], steps, True)
    fc2_new, fc2_new_low = renew(fc2_weight[None], fc2_sum, *fc2_scales, pairs[4], steps, False)
    step_total = jnp.sum(jnp.sum(in_turn(steps), 0)) + vector_step
    update_rms = jnp.sqrt(step_total / param_count)
    divisor = jnp.maximum(1.0, update_rms / clip_level)
    vector_rms = jnp.sqrt(jnp.mean(vectors * vectors, 1, keepdims=True))
    vectors_new = vectors - step_rate * jnp.maximum(0.001, vector_rms) * vector_update / divisor
    hidden_bias_new = hidden_bias - rates[5] / divisor * hidden_update
    piece_width = D // dp_count
    dp_start = dp_index * piece_width

    def own_piece(array, axis):
        return lax.dynamic_slice_in_dim(array, dp_start, piece_width, axis)

    def near_whole(sent, first, amount, width):
        near = in_turn([array[first : first + amount, 1, :width] for array in sent])
        return near.transpose(1, 0, 2).reshape(near.shape[1], -1)

    skip_near_new = near_whole(token_sent, 4, 2, width_local)
    attn_near_new = near_whole(token_sent, 0, 4, width_local)
    fc1_near_new = near_whole(hidden_sent, 1, 1, hidden_local)
    fc2_near_new = near_whole(hidden_sent, 0, 1, hidden_local)
    return (
        block_output,
        input_grad,
        skip_input_grad,
        own_piece(skip_sum, 2),
        own_piece(attn_sum[:3], 2).transpose(0, 2, 1),
        own_piece(attn_sum[3], 1),
        own_piece(fc1_sum[0], 1).T,
        own_piece(fc2_sum[0], 1),
        own_piece(vector_sum, 1),
        hidden_sum,
        skip_near_new,
        skip_far_new[:, 0],
        attn_far_new[:3, 0],
        attn_near_new[:3],
        attn_near_new[3],
        attn_far_new[3, 0],
        fc1_far_new[0, 0],
        fc1_near_new[0],
        fc2_near_new[0],
        fc2_far_new[0, 0],
        vector_new,
        hidden_new,
        skip_new,
        qkv_new,
        proj_new[0],
        fc1_new[0],
        fc2_new[0],
        vectors_new,
        hidden_bias_new,
        skip_new_low,
        qkv_new_low,
        proj_new_low[0],
        fc1_new_low[0],
        fc2_new_low[0],
        update_rms,
    )


def solution(mesh):
    placed = (
        P("dp", None),
        P("dp", None),
        P("dp"),
        P("dp"),
        P("dp"),
        P("dp", None),
        P(None, "mp", None),
        P(None, None, "mp"),
        P("mp", None),
        P(None, "mp"),
        P("mp", None),
        P(),
        P("mp"),
        P(),
        P(),
        P(),
        P(),
        P(),
        P(),
        P(),
        P(),
        P(),
        P(),
        P(),
        P("mp"),
    )
    return jax.shard_map(
        body,
        mesh=mesh,
        in_specs=placed,
        out_specs=(
            P("dp", None),
            P("dp", "mp"),
            P("dp", "mp"),
            P(None, "mp", "dp"),
            P(None, "dp", "mp"),
            P("mp", "dp"),
            P("dp", "mp"),
            P("mp", "dp"),
            P(None, "dp"),
            P("mp"),
            P(),
            P(),
            P(),
            P(),
            P(),
            P(),
            P(),
            P(),
            P(),
            P(),
            P(),
            P("mp"),
            P(None, "mp", None),
            P(None, None, "mp"),
            P("mp", None),
            P(None, "mp"),
            P("mp", None),
            P(),
            P("mp"),
            P(None, "mp", None),
            P(None, None, "mp"),
            P("mp", None),
            P(None, "mp"),
            P("mp", None),
            P(),
        ),
        check_vma=False,
    )
```

```python
import functools
import math

import jax
import jax.numpy as jnp
from jax import lax
from jax.experimental import pallas as pl
from jax.experimental.pallas import tpu as pltpu
from jax.sharding import PartitionSpec as P

D = 1152
HEAD_DIM = 72
FF = 4608
CLASSES = 1000
SEQ = 258


ln_eps = 1e-05
moment_eps = 1e-30
clip_level = 0.25
step_rate = 2.0
total_steps = 1000.0


def gelu_exact(inputs):
    return 0.5 * inputs * (1.0 + lax.erf(inputs * (1.0 / math.sqrt(2.0))))


def matmul(left_side, right_side):
    return jnp.dot(left_side, right_side, preferred_element_type=jnp.float32)


def norm_forward(inputs, norm_gain, norm_bias):
    centre = jnp.mean(inputs, -1, keepdims=True)
    centred = inputs - centre
    inverse = lax.rsqrt(jnp.mean(centred * centred, -1, keepdims=True) + ln_eps)
    normal = centred * inverse
    return (normal * norm_gain + norm_bias, normal, inverse)


def norm_backward(incoming, normal, inverse, norm_gain):
    scaled = incoming * norm_gain
    inner_mean = jnp.mean(scaled, -1, keepdims=True)
    proj_mean = jnp.mean(scaled * normal, -1, keepdims=True)
    return (
        inverse * (scaled - inner_mean - normal * proj_mean),
        jnp.sum(incoming * normal, 0),
        jnp.sum(incoming, 0),
    )


def adafactor(
    grad_pieces,
    weight_pieces,
    starts,
    row_states,
    col_states,
    vector_piece,
    vector_weight,
    vector_state,
    hidden_piece,
    hidden_weight,
    hidden_state,
    first_mask,
    reduce_moments,
    reduce_norm,
):
    full_shapes = ((D, D), (D, D), (D, D), (D, FF), (FF, D))
    tensor_sizes = (2.0 * D * D, 3.0 * D * D, 1.0 * D * D, 1.0 * D * FF, 1.0 * FF * D)
    zero_start = jnp.zeros((), jnp.int32)
    row_parts = []
    col_parts = []
    weight_sq = []
    for position in range(5):
        grad_piece = grad_pieces[position]
        leading = grad_piece.shape[0]
        squares = grad_piece * grad_piece + moment_eps
        row_zero = jnp.zeros((leading, full_shapes[position][0]), jnp.float32)
        col_zero = jnp.zeros((leading, full_shapes[position][1]), jnp.float32)
        row_parts.append(
            lax.dynamic_update_slice(
                row_zero, jnp.sum(squares, 2), (zero_start, starts[position][0])
            ).reshape(-1)
        )
        col_parts.append(
            lax.dynamic_update_slice(
                col_zero, jnp.sum(squares, 1), (zero_start, starts[position][1])
            ).reshape(-1)
        )
        weight_sq.append(jnp.sum(weight_pieces[position] * weight_pieces[position])[None])
    weight_sq.append(jnp.sum(vector_weight * vector_weight, 1) * first_mask)
    weight_sq.append(jnp.sum(hidden_weight * hidden_weight)[None])
    row_total, col_total, weight_total = reduce_moments(
        jnp.concatenate(row_parts), jnp.concatenate(col_parts), jnp.concatenate(weight_sq)
    )
    row_news = []
    col_news = []
    updates = []
    step_sq = jnp.zeros((), jnp.float32)
    row_offset = 0
    col_offset = 0
    for position in range(5):
        grad_piece = grad_pieces[position]
        leading = grad_piece.shape[0]
        rows_full, cols_full = full_shapes[position]
        row_sum = row_total[row_offset : row_offset + leading * rows_full].reshape(
            leading, rows_full
        )
        col_sum = col_total[col_offset : col_offset + leading * cols_full].reshape(
            leading, cols_full
        )
        row_offset = row_offset + leading * rows_full
        col_offset = col_offset + leading * cols_full
        row_new = 0.5 * row_states[position] + 0.5 * (row_sum / cols_full)
        col_new = 0.5 * col_states[position] + 0.5 * (col_sum / rows_full)
        row_piece = lax.dynamic_slice(
            row_new, (zero_start, starts[position][0]), (leading, grad_piece.shape[1])
        )
        col_piece = lax.dynamic_slice(
            col_new, (zero_start, starts[position][1]), (leading, grad_piece.shape[2])
        )
        row_mean = jnp.mean(row_new, 1)
        update = grad_piece * lax.rsqrt(
            row_piece[:, :, None] * col_piece[:, None, :] / row_mean[:, None, None]
        )
        step_sq = step_sq + jnp.sum(update * update)
        row_news.append(row_new)
        col_news.append(col_new)
        updates.append(update)
    vector_new = 0.5 * vector_state + 0.5 * (vector_piece * vector_piece + moment_eps)
    vector_update = vector_piece * lax.rsqrt(vector_new)
    hidden_new = 0.5 * hidden_state + 0.5 * (hidden_piece * hidden_piece + moment_eps)
    hidden_update = hidden_piece * lax.rsqrt(hidden_new)
    step_sq = (
        step_sq
        + jnp.sum(vector_update * vector_update) * first_mask
        + jnp.sum(hidden_update * hidden_update)
    )
    step_total = reduce_norm(step_sq)
    param_count = 6.0 * D * D + 2.0 * D * FF + 7.0 * D + FF
    update_rms = jnp.sqrt(step_total / param_count)
    divisor = jnp.maximum(1.0, update_rms / clip_level)
    new_weights = []
    for position in range(5):
        weight_rms = jnp.sqrt(weight_total[position] / tensor_sizes[position])
        new_weights.append(
            weight_pieces[position]
            - step_rate * jnp.maximum(0.001, weight_rms) * updates[position] / divisor
        )
    vector_rms = jnp.sqrt(weight_total[5:12] / D)[:, None]
    vector_weight_new = (
        vector_weight - step_rate * jnp.maximum(0.001, vector_rms) * vector_update / divisor
    )
    hidden_rms = jnp.sqrt(weight_total[12] / FF)
    hidden_weight_new = (
        hidden_weight - step_rate * jnp.maximum(0.001, hidden_rms) * hidden_update / divisor
    )
    return (
        new_weights,
        row_news,
        col_news,
        vector_new,
        vector_weight_new,
        hidden_new,
        hidden_weight_new,
        update_rms,
    )


def body_tensor(
    block_input,
    skip_input,
    timesteps,
    class_labels,
    loss_weights,
    grad_output,
    skip_weight,
    qkv_weight,
    proj_weight,
    fc1_weight,
    fc2_weight,
    vectors,
    hidden_bias,
    skip_rows,
    skip_cols,
    qkv_rows,
    qkv_cols,
    proj_rows,
    proj_cols,
    fc1_rows,
    fc1_cols,
    fc2_rows,
    fc2_cols,
    vector_moments,
    hidden_moments,
):
    image_count = timesteps.shape[0]
    width_local = qkv_weight.shape[2]
    heads_local = width_local // HEAD_DIM
    hidden_local = fc1_weight.shape[1]
    mp_index = lax.axis_index("mp")
    dp_index = lax.axis_index("dp")
    dp_count = lax.axis_size("dp")
    first_mask = (mp_index == 0).astype(jnp.float32)
    feature_start = mp_index * skip_weight.shape[1]
    block_local = lax.dynamic_slice_in_dim(block_input, feature_start, skip_weight.shape[1], 1)
    skip_local = lax.dynamic_slice_in_dim(skip_input, feature_start, skip_weight.shape[1], 1)
    angles = (timesteps.astype(jnp.float32) + 0.5) * (0.5 * math.pi / total_steps)
    alpha_sq = jnp.square(jnp.cos(angles))
    sigma_sq = jnp.square(jnp.sin(angles))
    snr_weight = 5.0 * sigma_sq / jnp.maximum(alpha_sq, 5.0 * sigma_sq)
    base_weight = loss_weights * snr_weight
    one_hot = (class_labels[:, None] == jnp.arange(CLASSES, dtype=jnp.int32)[None, :]).astype(
        jnp.float32
    )
    class_counts, weight_total = lax.psum((jnp.sum(one_hot, 0), jnp.sum(base_weight)), "dp")
    own_count = jnp.dot(one_hot, class_counts, precision=lax.Precision.HIGHEST)
    item_weight = base_weight * (image_count * dp_count / weight_total) * lax.rsqrt(own_count)
    upstream = (
        grad_output.astype(jnp.float32).reshape(image_count, SEQ, D) * item_weight[:, None, None]
    ).reshape(-1, D)
    skip_low = skip_weight.astype(jnp.bfloat16)
    qkv_low = qkv_weight.astype(jnp.bfloat16)
    proj_low = proj_weight.astype(jnp.bfloat16)
    fc1_low = fc1_weight.astype(jnp.bfloat16)
    fc2_low = fc2_weight.astype(jnp.bfloat16)
    joined = (
        lax.psum(matmul(block_local, skip_low[0]) + matmul(skip_local, skip_low[1]), "mp")
        + vectors[4]
    )
    normed, normal_one, inverse_one = norm_forward(joined, vectors[0], vectors[1])
    normed_low = normed.astype(jnp.bfloat16)
    qkv_all = jnp.einsum(
        "td,sde->ste", normed_low, qkv_low, preferred_element_type=jnp.float32
    ).astype(jnp.bfloat16)
    heads_view = qkv_all.reshape(3, image_count, SEQ, heads_local, HEAD_DIM)
    query_low = heads_view[0]
    key_low = heads_view[1]
    value_low = heads_view[2]
    score_scale = HEAD_DIM ** (-0.5)

    def score_block():
        return (
            jnp.einsum("iqhe,ikhe->ihqk", query_low, key_low, preferred_element_type=jnp.float32)
            * score_scale
        )

    scores = score_block()
    score_top = jnp.max(scores, -1, keepdims=True)
    expo_scores = jnp.exp(scores - score_top)
    expo_total = jnp.sum(expo_scores, -1, keepdims=True)
    weights_low = (expo_scores / expo_total).astype(jnp.bfloat16)
    log_total = score_top + jnp.log(expo_total)
    attended = (
        jnp.einsum("ihqk,ikhe->iqhe", weights_low, value_low, preferred_element_type=jnp.float32)
        .astype(jnp.bfloat16)
        .reshape(-1, width_local)
    )
    residual = joined + lax.psum(matmul(attended, proj_low), "mp") + vectors[5]
    normed_two, normal_two, inverse_two = norm_forward(residual, vectors[2], vectors[3])
    normed_two_low = normed_two.astype(jnp.bfloat16)
    pre_act = matmul(normed_two_low, fc1_low) + hidden_bias
    activated, gelu_pull = jax.vjp(gelu_exact, pre_act)
    activated_low = activated.astype(jnp.bfloat16)
    block_output = (residual + lax.psum(matmul(activated_low, fc2_low), "mp") + vectors[6]).astype(
        jnp.bfloat16
    )
    upstream_low = upstream.astype(jnp.bfloat16)
    fc2_grad = jnp.einsum(
        "tf,td->fd", activated_low, upstream_low, preferred_element_type=jnp.float32
    )
    fc2_bias_grad = jnp.sum(upstream, 0)
    act_grad = jnp.einsum("td,fd->tf", upstream_low, fc2_low, preferred_element_type=jnp.float32)
    pre_grad = gelu_pull(act_grad)[0]
    pre_low = pre_grad.astype(jnp.bfloat16)
    fc1_grad = jnp.einsum("td,tf->df", normed_two_low, pre_low, preferred_element_type=jnp.float32)
    hidden_grad = jnp.sum(pre_grad, 0)
    norm_two_in = lax.psum(
        jnp.einsum("tf,df->td", pre_low, fc1_low, preferred_element_type=jnp.float32), "mp"
    )
    back_two, gain_two_grad, bias_two_grad = norm_backward(
        norm_two_in, normal_two, inverse_two, vectors[2]
    )
    residual_grad = upstream + back_two
    proj_bias_grad = jnp.sum(residual_grad, 0)
    residual_low = residual_grad.astype(jnp.bfloat16)
    proj_grad = jnp.einsum("te,td->ed", attended, residual_low, preferred_element_type=jnp.float32)
    attended_grad = jnp.einsum(
        "td,ed->te", residual_low, proj_low, preferred_element_type=jnp.float32
    ).astype(jnp.bfloat16)
    attended_grad = attended_grad.reshape(image_count, SEQ, heads_local, HEAD_DIM)
    scores = score_block()
    probs_exact = jnp.exp(scores - log_total)
    prob_grad = jnp.einsum(
        "iqhe,ikhe->ihqk", attended_grad, value_low, preferred_element_type=jnp.float32
    )
    score_grad = (
        probs_exact * (prob_grad - jnp.sum(probs_exact * prob_grad, -1, keepdims=True))
    ).astype(jnp.bfloat16)
    query_grad = (
        jnp.einsum("ihqk,ikhe->iqhe", score_grad, key_low, preferred_element_type=jnp.float32)
        * score_scale
    )
    key_grad = (
        jnp.einsum("ihqk,iqhe->ikhe", score_grad, query_low, preferred_element_type=jnp.float32)
        * score_scale
    )
    value_grad = jnp.einsum(
        "ihqk,iqhe->ikhe", weights_low, attended_grad, preferred_element_type=jnp.float32
    )
    qkv_grad_low = (
        jnp.stack([query_grad, key_grad, value_grad])
        .astype(jnp.bfloat16)
        .reshape(3, -1, width_local)
    )
    qkv_grad = jnp.einsum(
        "td,ste->sde", normed_low, qkv_grad_low, preferred_element_type=jnp.float32
    )
    norm_one_in = lax.psum(
        jnp.einsum("ste,sde->td", qkv_grad_low, qkv_low, preferred_element_type=jnp.float32), "mp"
    )
    back_one, gain_one_grad, bias_one_grad = norm_backward(
        norm_one_in, normal_one, inverse_one, vectors[0]
    )
    joined_grad = residual_grad + back_one
    skip_bias_grad = jnp.sum(joined_grad, 0)
    joined_low = joined_grad.astype(jnp.bfloat16)
    skip_grad = jnp.stack(
        [
            jnp.einsum("tc,td->cd", block_local, joined_low, preferred_element_type=jnp.float32),
            jnp.einsum("tc,td->cd", skip_local, joined_low, preferred_element_type=jnp.float32),
        ]
    )
    input_grad = jnp.einsum(
        "td,cd->tc", joined_low, skip_low[0], preferred_element_type=jnp.float32
    )
    skip_input_grad = jnp.einsum(
        "td,cd->tc", joined_low, skip_low[1], preferred_element_type=jnp.float32
    )
    vector_grad = jnp.stack(
        [
            gain_one_grad,
            bias_one_grad,
            gain_two_grad,
            bias_two_grad,
            skip_bias_grad,
            proj_bias_grad,
            fc2_bias_grad,
        ]
    )
    row_states = [skip_rows, qkv_rows, proj_rows[None], fc1_rows[None], fc2_rows[None]]
    col_states = [skip_cols, qkv_cols, proj_cols[None], fc1_cols[None], fc2_cols[None]]
    piece_width = D // dp_count
    dp_start = dp_index * piece_width
    zero_start = jnp.zeros((), jnp.int32)
    summed = lax.psum(
        (skip_grad, qkv_grad, proj_grad, fc1_grad, fc2_grad, vector_grad, hidden_grad), "dp"
    )

    def moments_mp(row_all, col_all, squares_all):
        return lax.psum((row_all, col_all, squares_all), "mp")

    def norm_mp(step_sq):
        return lax.psum(step_sq, "mp")

    grad_pieces = [summed[0], summed[1], summed[2][None], summed[3][None], summed[4][None]]
    weight_pieces = [skip_weight, qkv_weight, proj_weight[None], fc1_weight[None], fc2_weight[None]]
    starts = [
        (mp_index * width_local, zero_start),
        (zero_start, mp_index * width_local),
        (mp_index * width_local, zero_start),
        (zero_start, mp_index * hidden_local),
        (mp_index * hidden_local, zero_start),
    ]
    results = adafactor(
        grad_pieces,
        weight_pieces,
        starts,
        row_states,
        col_states,
        summed[5],
        vectors,
        vector_moments,
        summed[6],
        hidden_bias,
        hidden_moments,
        first_mask,
        moments_mp,
        norm_mp,
    )
    (
        new_weights,
        row_news,
        col_news,
        vector_state_new,
        vectors_new,
        hidden_state_new,
        hidden_new,
        update_rms,
    ) = results
    skip_new = new_weights[0]
    qkv_new = new_weights[1]
    proj_new = new_weights[2][0]
    fc1_new = new_weights[3][0]
    fc2_new = new_weights[4][0]
    skip_grad_out = lax.dynamic_slice_in_dim(summed[0], dp_start, piece_width, 2)
    qkv_grad_out = lax.dynamic_slice_in_dim(summed[1], dp_start, piece_width, 1)
    proj_grad_out = lax.dynamic_slice_in_dim(summed[2], dp_start, piece_width, 1)
    fc1_grad_out = lax.dynamic_slice_in_dim(summed[3], dp_start, piece_width, 0)
    fc2_grad_out = lax.dynamic_slice_in_dim(summed[4], dp_start, piece_width, 1)
    vector_grad_out = lax.dynamic_slice_in_dim(summed[5], dp_start, piece_width, 1)
    hidden_grad_out = summed[6]
    return (
        block_output,
        input_grad,
        skip_input_grad,
        skip_grad_out,
        qkv_grad_out,
        proj_grad_out,
        fc1_grad_out,
        fc2_grad_out,
        vector_grad_out,
        hidden_grad_out,
        row_news[0],
        col_news[0],
        row_news[1],
        col_news[1],
        row_news[2][0],
        col_news[2][0],
        row_news[3][0],
        col_news[3][0],
        row_news[4][0],
        col_news[4][0],
        vector_state_new,
        hidden_state_new,
        skip_new,
        qkv_new,
        proj_new,
        fc1_new,
        fc2_new,
        vectors_new,
        hidden_new,
        skip_new.astype(jnp.bfloat16),
        qkv_new.astype(jnp.bfloat16),
        proj_new.astype(jnp.bfloat16),
        fc1_new.astype(jnp.bfloat16),
        fc2_new.astype(jnp.bfloat16),
        update_rms,
    )


def body(*operands):
    images = operands[2].shape[0]
    if images % lax.axis_size("mp") == 0 and lax.axis_size("dp") == 8:
        return body_data(*operands)
    return body_tensor(*operands)


small_cost = pl.CostEstimate(flops=0, bytes_accessed=1024, transcendentals=0)


def to_core(array):
    return lax.ppermute(array, "dp", [(i, i ^ 1) for i in range(8)])


def to_x(array):
    return lax.ppermute(array, "dp", [(i, i ^ 2) for i in range(8)])


def to_y(array):
    return lax.ppermute(array, "dp", [(i, i ^ 4) for i in range(8)])


def turn_mp(array, shift):
    count = lax.axis_size("mp")
    return lax.ppermute(array, "mp", [(i, (i + shift) % count) for i in range(count)])


def pick(array, index, axis):
    return lax.dynamic_index_in_dim(array, index, axis, keepdims=False)


def assemble(steps, targets, core, rows, blocks, split):
    arrays = []
    for step in steps:
        for array, _ in step:
            if not any(array is other for other in arrays):
                arrays.append(array)
    place = [
        [(next(n for n, other in enumerate(arrays) if other is array), k) for array, k in step]
        for step in steps
    ]
    table = jnp.stack([jnp.asarray(v, jnp.int32) for v in [*targets, core]])
    depth = 4
    outs = 2 if split < blocks else 1

    def kernel(table_ref, *refs):
        sources = refs[: len(arrays)]
        wholes = refs[len(arrays) : len(arrays) + outs]
        wide, narrow, in_sem, out_sem = refs[len(arrays) + outs :]
        half = rows // 2
        first = pl.multiple_of(table_ref[len(steps)] * half, half)
        second = pl.multiple_of(half - first, half)

        def fetch(step):
            slot = step % depth
            if len(place[step]) == 1:
                ((n, k),) = place[step]
                return [pltpu.make_async_copy(sources[n].at[k], wide.at[slot], in_sem.at[slot, 0])]
            copies = []
            for part, ((n, k), start) in enumerate(zip(place[step], (first, second))):
                spot = wide.at[slot, pl.ds(start, half)]
                copies.append(pltpu.make_async_copy(sources[n].at[k], spot, in_sem.at[slot, part]))
            return copies

        def leave(step, whole, spot):
            slot = step % depth
            return pltpu.make_async_copy(narrow.at[slot], whole.at[spot], out_sem.at[slot])

        for step in range(len(steps) + depth - 1):
            if step < len(steps):
                for copy in fetch(step):
                    copy.start()
            step = step - (depth - 1)
            if step < 0:
                continue
            slot = step % depth
            for copy in fetch(step):
                copy.wait()
            if step >= depth:
                leave(step - depth, wholes[0], 0).wait()
            narrow[slot] = wide[slot].astype(jnp.bfloat16)
            spot = table_ref[step]
            if outs == 1:
                leave(step, wholes[0], spot).start()
            else:

                @pl.when(spot < split)
                def _():
                    leave(step, wholes[0], spot).start()

                @pl.when(spot >= split)
                def _():
                    leave(step, wholes[1], spot - split).start()

        for step in range(max(0, len(steps) - depth), len(steps)):
            leave(step, wholes[0], 0).wait()

    shapes = [jax.ShapeDtypeStruct((split, rows, D), jnp.bfloat16)]
    if outs == 2:
        shapes.append(jax.ShapeDtypeStruct((blocks - split, rows, D), jnp.bfloat16))
    anywhere = pl.BlockSpec(memory_space=pl.ANY)
    return pl.pallas_call(
        kernel,
        in_specs=[pl.BlockSpec(memory_space=pltpu.SMEM)] + [anywhere] * len(arrays),
        out_specs=[anywhere] * outs,
        out_shape=shapes,
        scratch_shapes=[
            pltpu.VMEM((depth, rows, D), jnp.float32),
            pltpu.VMEM((depth, rows, D), jnp.bfloat16),
            pltpu.SemaphoreType.DMA((depth, 2)),
            pltpu.SemaphoreType.DMA((depth,)),
        ],
        compiler_params=pltpu.CompilerParams(vmem_limit_bytes=32 * 1024 * 1024),
        cost_estimate=small_cost,
    )(table, *arrays)


class Order:
    def __init__(self):
        self.token = None

    def after(self, *arrays):
        if self.token is not None:
            arrays = lax.optimization_barrier((*arrays, self.token))[:-1]
        return arrays if len(arrays) > 1 else arrays[0]

    def mark(self, *arrays):
        arrays = self.after(*arrays)
        self.token = arrays[0] if isinstance(arrays, tuple) else arrays
        return arrays


def swap_plane(order, for_x, for_y):
    for_x, for_y = order.after(for_x, for_y)
    return to_x(for_x), to_y(for_y)


def in_turn(arrays):
    count = len(arrays)
    twice = jnp.stack(list(arrays[::-1]) * 2)
    return lax.dynamic_slice_in_dim(twice, count - 1 - lax.axis_index("mp"), count, 0)


def gather_deep(array):
    return in_turn([array] + [turn_mp(array, shift) for shift in range(1, lax.axis_size("mp"))])


def sum_flat(array):
    for swap in (to_core, to_x, to_y):
        array = array + swap(array)
    return array


def bring(order, shard, quarter, core):
    count = lax.axis_size("mp")
    part = pick(pick(shard.reshape(4, 2, -1, D), quarter, 0), core, 0)
    return lax.all_gather(order.after(part), "mp")


def others(whole):
    count = lax.axis_size("mp")
    twice = jnp.concatenate([whole, whole], 0)
    return lax.dynamic_slice_in_dim(twice, lax.axis_index("mp") + 1, count - 1, 0)


def assemble_weight(shard, parts, swapped, core, split):
    count = lax.axis_size("mp")
    rows = shard.shape[0] // 8

    def spot(shard_index, quarter):
        shard_index = lax.rem(lax.axis_index("mp") + shard_index, count)
        return quarter * count + shard_index

    if swapped is None:
        mine = pick(shard.reshape(4, 2, rows, D), core, 1)
    else:
        mine = shard.reshape(4, 2 * rows, D)
    steps = [((mine, n),) for n in range(4)]
    targets = [spot(0, n) for n in range(4)]
    for n, (array, quarter, first) in enumerate(parts):
        for k in range(array.shape[0]):
            steps.append(((array, k),) if swapped is None else ((array, k), (swapped[n], k)))
            targets.append(spot(first + k, quarter))
    rows = mine.shape[1]
    whole = assemble(steps, targets, core, rows, count * 4, split or count * 4)
    return [array.reshape(-1, D) for array in whole]


def cut_corner(grad, quarter):
    corner = pick(grad, quarter ^ 3, 0)
    half = corner.shape[0] // 2
    return corner[:half], corner[half:]


def cut_sides(grad, quarter, add_y, add_x):
    half = add_y.shape[0]
    for_y = pick(grad, quarter ^ 2, 0)
    for_x = pick(grad, quarter ^ 1, 0)
    for_y = jnp.concatenate([for_y[:half] + add_y, for_y[half:]], 0)
    for_x = jnp.concatenate([for_x[:half], for_x[half:] + add_x], 0)
    return for_x, for_y


def sum_deep(order, grad, quarter, from_x, from_y):
    own = order.mark(pick(grad, quarter, 0) + from_x + from_y)
    return lax.psum_scatter(own, "mp", scatter_dimension=0, tiled=False)


def place_rows(pieces, rows, near_state=None):
    arrays = []
    for array, *_ in pieces:
        if not any(array is other for other in arrays):
            arrays.append(array)
    steps = [
        (next(n for n, other in enumerate(arrays) if other is array), first, amount)
        for array, first, amount, _ in pieces
    ]
    table = jnp.stack([jnp.asarray(spot, jnp.int32) for *_, spot in pieces])

    def kernel(table_ref, *refs):
        sources = refs[: len(arrays)]
        sems = refs[-1]
        if near_state is None:
            out_ref = refs[len(arrays)]
        else:
            state_ref, out_ref, moment_ref = refs[len(arrays) : -1]
        copies = []
        for step, (n, first, amount) in enumerate(steps):
            spot = pl.multiple_of(table_ref[step], 8)
            source = sources[n].at[pl.ds(first, amount)]
            copies.append(
                pltpu.make_async_copy(source, out_ref.at[pl.ds(spot, amount)], sems.at[step])
            )
        for copy in copies:
            copy.start()
        for copy in copies:
            copy.wait()
        if near_state is None:
            return
        leading, length = near_state.shape
        chunk = length if length < 384 else 384
        for lead in range(leading):
            total = jnp.zeros((1, D), jnp.float32)
            for first in range(0, length, chunk):
                grad = out_ref[lead * length + first : lead * length + first + chunk]
                squares = grad * grad + moment_eps
                total = total + jnp.sum(squares, 0, keepdims=True)
                near = 0.5 * state_ref[lead, :1, first : first + chunk]
                near = near + 0.5 * (as_row(lanes_of(squares)) / D)
                moment_ref[lead, 1:2, first : first + chunk] = near
            moment_ref[lead, :1] = total
            if length < D:
                moment_ref[lead, 1:2, length:] = jnp.zeros((1, D - length), jnp.float32)

    vmem = pl.BlockSpec(memory_space=pltpu.VMEM)
    in_specs = [pl.BlockSpec(memory_space=pltpu.SMEM)]
    in_specs = in_specs + [pl.BlockSpec(memory_space=pl.ANY)] * len(arrays)
    out_specs, shapes = [vmem], [jax.ShapeDtypeStruct((rows, D), jnp.float32)]
    operands = [table, *arrays]
    if near_state is not None:
        leading, length = near_state.shape
        in_specs.append(vmem)
        operands.append(near_state.reshape(leading, 1, length))
        out_specs.append(vmem)
        shapes.append(jax.ShapeDtypeStruct((leading, 2, D), jnp.float32))
    result = pl.pallas_call(
        kernel,
        in_specs=in_specs,
        out_specs=out_specs,
        out_shape=shapes,
        scratch_shapes=[pltpu.SemaphoreType.DMA((len(steps),))],
        compiler_params=pltpu.CompilerParams(vmem_limit_bytes=40 * 1024 * 1024),
        cost_estimate=small_cost,
    )(*operands)
    return result[0] if near_state is None else result


def add_half(grads, given, core):
    rows = grads[0].shape[2]
    amounts = [array.shape[0] for array in grads]
    firsts = [sum(amounts[:n]) for n in range(len(amounts))]

    def kernel(core_ref, *refs):
        for n, (first, amount) in enumerate(zip(firsts, amounts)):

            @pl.when((pl.program_id(0) >= first) & (pl.program_id(0) < first + amount))
            def _():
                refs[-1][...] = refs[n][0] + refs[len(grads) + n][...]

    def at(first, amount):
        return lambda step: jnp.clip(step - first, 0, amount - 1)

    spots = [at(*pair) for pair in zip(firsts, amounts)]
    own_specs = [
        pl.BlockSpec((1, 1, rows, D), lambda step, core_ref, at=at: (at(step), core_ref[0], 0, 0))
        for at in spots
    ]
    given_specs = [
        pl.BlockSpec((1, rows, D), lambda step, core_ref, at=at: (at(step), 0, 0)) for at in spots
    ]
    total = sum(amounts)
    return pl.pallas_call(
        kernel,
        grid_spec=pltpu.PrefetchScalarGridSpec(
            num_scalar_prefetch=1,
            grid=(total,),
            in_specs=own_specs + given_specs,
            out_specs=pl.BlockSpec((1, rows, D), lambda step, core_ref: (step, 0, 0)),
        ),
        out_shape=jax.ShapeDtypeStruct((total, rows, D), jnp.float32),
        compiler_params=pltpu.CompilerParams(vmem_limit_bytes=40 * 1024 * 1024),
        cost_estimate=small_cost,
    )(core[None], *grads, *given)


def order_tokens(arrays, mp_index):
    count = len(arrays)
    tokens, width = arrays[0].shape[0], arrays[0].shape[1] // 2

    def kernel(place_ref, *refs):
        left_ref, right_ref, held, sems = refs[count:]

        def copy(n, index):
            return pltpu.make_async_copy(refs[n], held.at[index], sems.at[index])

        for index in range(count):
            for n in range(count):

                @pl.when(lax.rem(place_ref[0] + count - index, count) == n)
                def _():
                    copy(n, index).start()

        for index in range(count):
            copy(0, index).wait()
            rows = slice(index * tokens, (index + 1) * tokens)
            left_ref[rows] = held[index, :, :width]
            right_ref[rows] = held[index, :, width:]

    vmem = pl.BlockSpec(memory_space=pltpu.VMEM)
    shape = jax.ShapeDtypeStruct((count * tokens, width), jnp.float32)
    return pl.pallas_call(
        kernel,
        in_specs=[pl.BlockSpec(memory_space=pltpu.SMEM)]
        + [pl.BlockSpec(memory_space=pl.ANY)] * count,
        out_specs=[vmem, vmem],
        out_shape=[shape, shape],
        scratch_shapes=[
            pltpu.VMEM((count, tokens, 2 * width), jnp.float32),
            pltpu.SemaphoreType.DMA((count,)),
        ],
        compiler_params=pltpu.CompilerParams(vmem_limit_bytes=40 * 1024 * 1024),
        cost_estimate=small_cost,
    )(mp_index[None], *arrays)


def lanes_of(array):
    total = array[:, :128]
    for tile in range(1, array.shape[1] // 128):
        total = total + array[:, tile * 128 : (tile + 1) * 128]
    return total


def as_row(column):
    return jnp.sum(column.T, 0, keepdims=True)


def as_column(row):
    return jnp.broadcast_to(row, (128, row.shape[1])).T


def scale_kernel(count, by_rows, place_ref, grad_ref, state_ref, before_ref, *refs):
    sources = refs[:count]
    far_ref, scale_ref, near_ref, step_ref = refs[count:]
    rows = grad_ref.shape[1]
    total = jnp.zeros((1, D), jnp.float32)
    near_sum = jnp.zeros((1, 1), jnp.float32)
    for index in range(count):
        part = jnp.zeros((2, D), jnp.float32)
        for shift in range(count):
            part = jnp.where(place_ref[0] == (index + shift) % count, sources[shift][0], part)
        total = total + part[:1]
        near_sum = near_sum + jnp.sum(part[1:], 1, keepdims=True)
    far = 0.5 * state_ref[0] + 0.5 * (total / (count * rows))
    far_ref[0] = far
    lead = pl.program_id(0)
    near_mean = near_sum / (count * rows)
    far_mean = jnp.sum(far, 1, keepdims=True) / D
    if all(by_rows):
        mean = near_mean
    elif not any(by_rows):
        mean = far_mean
    else:
        split = by_rows.index(True)
        mean = jnp.where(lead >= split, near_mean, far_mean)
    far_scale = lax.rsqrt(far)
    near_scale = as_column(lax.rsqrt(sources[0][0][1:2, :rows] / mean))
    scale_ref[0] = far_scale
    near_ref[0] = near_scale
    step = grad_ref[0] * far_scale
    step = lanes_of(step * step) * near_scale * near_scale

    @pl.when(lead == 0)
    def _():
        step_ref[...] = before_ref[...]

    step_ref[...] += jnp.sum(step.reshape(rows // 8, 8, 128), 0)


def scales(grad, far_state, before, sources, first, mp_index, by_rows):
    leading, rows, _ = grad.shape
    count = len(sources)
    small = pl.BlockSpec((1, 2, D), lambda i: (i + first, 0, 0))
    line = pl.BlockSpec((1, 1, D), lambda i: (i, 0, 0))
    return pl.pallas_call(
        functools.partial(scale_kernel, count, by_rows),
        grid=(leading,),
        in_specs=[
            pl.BlockSpec(memory_space=pltpu.SMEM),
            pl.BlockSpec((1, rows, D), lambda i: (i, 0, 0)),
            line,
            pl.BlockSpec((8, 128), lambda i: (0, 0)),
        ]
        + [small] * count,
        out_specs=[
            line,
            line,
            pl.BlockSpec((1, rows, 128), lambda i: (i, 0, 0)),
            pl.BlockSpec((8, 128), lambda i: (0, 0)),
        ],
        out_shape=[
            jax.ShapeDtypeStruct((leading, 1, D), jnp.float32),
            jax.ShapeDtypeStruct((leading, 1, D), jnp.float32),
            jax.ShapeDtypeStruct((leading, rows, 128), jnp.float32),
            jax.ShapeDtypeStruct((8, 128), jnp.float32),
        ],
        compiler_params=pltpu.CompilerParams(vmem_limit_bytes=40 * 1024 * 1024),
        cost_estimate=small_cost,
    )(mp_index[None], grad, far_state.reshape(leading, 1, D), before, *sources)


param_count = 6.0 * D * D + 2.0 * D * FF + 7.0 * D + FF


def renew_kernel(turned, count, rate_ref, weight_ref, grad_ref, far_ref, near_ref, *refs):
    new_ref, low_ref = refs[count:]
    total = refs[0][...]
    for ref in refs[1:count]:
        total = total + ref[...]
    total = jnp.sum(jnp.sum(total, 0, keepdims=True), 1, keepdims=True) + rate_ref[1]
    divisor = jnp.maximum(1.0, jnp.sqrt(total / param_count) / clip_level)
    step = grad_ref[0] * far_ref[0] * (near_ref[0][:, :1] * (rate_ref[0] / divisor))
    new = weight_ref[0] - (step.T if turned else step)
    new_ref[0] = new
    low_ref[0] = new.astype(jnp.bfloat16)


def renew(weight, grad, far_scale, near_scale, rate, steps, turned, first=0):
    leading, rows = weight.shape[0], grad.shape[1]
    if turned:
        width = 384
        grid = (leading, D // width)
        weight_spec = pl.BlockSpec((1, width, rows), lambda i, j: (i, j, 0))
        grad_spec = pl.BlockSpec((1, rows, width), lambda i, j: (i + first, 0, j))
        far_spec = pl.BlockSpec((1, 1, width), lambda i, j: (i + first, 0, j))
        near_spec = pl.BlockSpec((1, rows, 128), lambda i, j: (i + first, 0, 0))
    else:
        height = min(rows, 288)
        grid = (leading, rows // height)
        weight_spec = pl.BlockSpec((1, height, D), lambda i, j: (i, j, 0))
        grad_spec = pl.BlockSpec((1, height, D), lambda i, j: (i + first, j, 0))
        far_spec = pl.BlockSpec((1, 1, D), lambda i, j: (i + first, 0, 0))
        near_spec = pl.BlockSpec((1, height, 128), lambda i, j: (i + first, j, 0))
    return pl.pallas_call(
        functools.partial(renew_kernel, turned, len(steps)),
        grid=grid,
        in_specs=[pl.BlockSpec(memory_space=pltpu.SMEM), weight_spec, grad_spec, far_spec, near_spec]
        + [pl.BlockSpec((8, 128), lambda i, j: (0, 0))] * len(steps),
        out_specs=[weight_spec, weight_spec],
        out_shape=[
            jax.ShapeDtypeStruct(weight.shape, jnp.float32),
            jax.ShapeDtypeStruct(weight.shape, jnp.bfloat16),
        ],
        compiler_params=pltpu.CompilerParams(vmem_limit_bytes=40 * 1024 * 1024),
        cost_estimate=small_cost,
    )(rate, weight, grad, far_scale, near_scale, *steps)


def head_windows():
    spans = []
    for head in range(D // HEAD_DIM):
        first = head * HEAD_DIM
        start = first // 128 * 128
        stop = -(-(first + HEAD_DIM) // 128) * 128
        spans.append((first, start, stop - start))
    return spans


def head_mask(first, start, width):
    lanes = start + lax.broadcasted_iota(jnp.int32, (SEQ, width), 1)
    return (lanes >= first) & (lanes < first + HEAD_DIM)


def dot_nt(left_side, right_side):
    return lax.dot_general(
        left_side, right_side, (((1,), (1,)), ((), ())), preferred_element_type=jnp.float32
    )


def attend_kernel(qkv_ref, out_ref, total):
    total[...] = jnp.zeros_like(total)
    for first, start, width in head_windows():
        keep = head_mask(first, start, width)
        query = qkv_ref[0, :, start : start + width]
        key = jnp.where(keep, qkv_ref[0, :, D + start : D + start + width], 0)
        value = jnp.where(keep, qkv_ref[0, :, 2 * D + start : 2 * D + start + width], 0)
        scores = dot_nt(query, key) * HEAD_DIM ** (-0.5)
        expo = jnp.exp(scores - jnp.max(scores, 1, keepdims=True))
        probs = (expo / jnp.sum(expo, 1, keepdims=True)).astype(jnp.bfloat16)
        total[:, start : start + width] += matmul(probs, value)
    out_ref[0] = total[...].astype(jnp.bfloat16)


def attend(qkv):
    images = qkv.shape[0]
    return pl.pallas_call(
        attend_kernel,
        grid=(images,),
        in_specs=[pl.BlockSpec((1, SEQ, 3 * D), lambda i: (i, 0, 0))],
        out_specs=pl.BlockSpec((1, SEQ, D), lambda i: (i, 0, 0)),
        out_shape=jax.ShapeDtypeStruct((images, SEQ, D), jnp.bfloat16),
        scratch_shapes=[pltpu.VMEM((SEQ, D), jnp.float32)],
        compiler_params=pltpu.CompilerParams(vmem_limit_bytes=40 * 1024 * 1024),
        cost_estimate=small_cost,
    )(qkv)


def attend_back_kernel(qkv_ref, grad_ref, out_ref, query_sum, key_sum, value_sum):
    scale = HEAD_DIM ** (-0.5)
    for ref in (query_sum, key_sum, value_sum):
        ref[...] = jnp.zeros_like(ref)
    for first, start, width in head_windows():
        span = slice(start, start + width)
        keep = head_mask(first, start, width)
        query = jnp.where(keep, qkv_ref[0, :, span], 0)
        key = jnp.where(keep, qkv_ref[0, :, D + start : D + start + width], 0)
        value = jnp.where(keep, qkv_ref[0, :, 2 * D + start : 2 * D + start + width], 0)
        above = jnp.where(keep, grad_ref[0, :, span], 0)
        scores = dot_nt(key, query) * scale
        expo = jnp.exp(scores - jnp.max(scores, 0, keepdims=True))
        probs = expo / jnp.sum(expo, 0, keepdims=True)
        prob_grad = dot_nt(value, above)
        inner = jnp.sum(probs * prob_grad, 0, keepdims=True)
        score_grad = (probs * (prob_grad - inner)).astype(jnp.bfloat16)
        value_sum[:, span] += matmul(probs.astype(jnp.bfloat16), above)
        key_sum[:, span] += matmul(score_grad, query) * scale
        query_sum[:, span] += (
            lax.dot_general(
                score_grad, key, (((0,), (0,)), ((), ())), preferred_element_type=jnp.float32
            )
            * scale
        )
    out_ref[0, :, :D] = query_sum[...].astype(jnp.bfloat16)
    out_ref[0, :, D : 2 * D] = key_sum[...].astype(jnp.bfloat16)
    out_ref[0, :, 2 * D :] = value_sum[...].astype(jnp.bfloat16)


def attend_back(qkv, grad):
    images = qkv.shape[0]
    return pl.pallas_call(
        attend_back_kernel,
        grid=(images,),
        in_specs=[
            pl.BlockSpec((1, SEQ, 3 * D), lambda i: (i, 0, 0)),
            pl.BlockSpec((1, SEQ, D), lambda i: (i, 0, 0)),
        ],
        out_specs=pl.BlockSpec((1, SEQ, 3 * D), lambda i: (i, 0, 0)),
        out_shape=jax.ShapeDtypeStruct((images, SEQ, 3 * D), jnp.bfloat16),
        scratch_shapes=[pltpu.VMEM((SEQ, D), jnp.float32)] * 3,
        compiler_params=pltpu.CompilerParams(vmem_limit_bytes=40 * 1024 * 1024),
        cost_estimate=small_cost,
    )(qkv, grad)


def body_data(
    block_input,
    skip_input,
    timesteps,
    class_labels,
    loss_weights,
    grad_output,
    skip_weight,
    qkv_weight,
    proj_weight,
    fc1_weight,
    fc2_weight,
    vectors,
    hidden_bias,
    skip_rows,
    skip_cols,
    qkv_rows,
    qkv_cols,
    proj_rows,
    proj_cols,
    fc1_rows,
    fc1_cols,
    fc2_rows,
    fc2_cols,
    vector_moments,
    hidden_moments,
):
    image_count = timesteps.shape[0]
    mp_count = lax.axis_size("mp")
    dp_count = lax.axis_size("dp")
    mp_index = lax.axis_index("mp")
    dp_index = lax.axis_index("dp")
    core = lax.rem(dp_index, 2)
    quarter = lax.div(dp_index, 2)
    images = image_count // mp_count
    tokens = images * SEQ
    width_local = qkv_weight.shape[2]
    hidden_local = fc1_weight.shape[1]
    hidden_slice = hidden_local // dp_count
    order = Order()

    skip_shard = skip_weight.reshape(-1, D)
    skip_whole = bring(order, skip_shard, quarter, core)
    hidden_all = gather_deep(hidden_bias)
    hidden_state = gather_deep(hidden_moments).reshape(-1)

    angles = (timesteps.astype(jnp.float32) + 0.5) * (0.5 * math.pi / total_steps)
    alpha_sq = jnp.square(jnp.cos(angles))
    sigma_sq = jnp.square(jnp.sin(angles))
    snr_weight = 5.0 * sigma_sq / jnp.maximum(alpha_sq, 5.0 * sigma_sq)
    base_weight = loss_weights * snr_weight
    one_hot = (class_labels[:, None] == jnp.arange(CLASSES, dtype=jnp.int32)[None, :]).astype(
        jnp.float32
    )
    batch = jnp.concatenate([jnp.sum(one_hot, 0), jnp.sum(base_weight)[None]])

    attn_shard = jnp.concatenate(
        [qkv_weight.transpose(0, 2, 1).reshape(3 * width_local, D), proj_weight], 0
    )
    attn_shard = order.mark(attn_shard)
    attn_whole = bring(order, attn_shard, quarter, core)
    batch = order.mark(batch + to_core(batch))
    batch_x = to_x(batch)
    fc1_shard = order.mark(fc1_weight.T)
    fc2_shard = fc2_weight
    batch = order.mark(batch + batch_x)
    batch_y = to_y(batch)
    start = mp_index * tokens
    block_local = lax.dynamic_slice_in_dim(block_input, start, tokens, 0)
    skip_local = lax.dynamic_slice_in_dim(skip_input, start, tokens, 0)
    both_inputs = jnp.concatenate(
        [
            array.reshape(tokens, mp_count, 2, -1).transpose(0, 2, 1, 3).reshape(tokens, D)
            for array in (block_local, skip_local)
        ],
        1,
    )
    both_inputs = order.mark(both_inputs)
    batch = order.mark(batch + batch_y)

    skip_own = others(order.mark(skip_whole))
    skip_x, skip_y = swap_plane(order, skip_own, skip_own)
    skip_swapped = [to_core(skip_own)]
    fc1_whole = bring(order, fc1_shard, quarter, core)
    hidden_own = pick(hidden_all.reshape(mp_count, 4, 2, hidden_slice), core, 2)
    hidden_own = hidden_own.transpose(1, 0, 2).reshape(-1)
    own_count = jnp.dot(one_hot, batch[:CLASSES], precision=lax.Precision.HIGHEST)
    item_weight = base_weight * lax.rsqrt(own_count)
    hidden_own, item_weight = order.mark(hidden_own, item_weight)
    batch_scale = image_count * dp_count / batch[CLASSES]
    grad_local = lax.dynamic_slice_in_dim(grad_output, start, tokens, 0)
    item_local = lax.dynamic_slice_in_dim(item_weight, mp_index * images, images, 0)
    upstream = (
        grad_local.astype(jnp.float32).reshape(images, SEQ, D) * item_local[:, None, None]
    ).reshape(-1, D)
    upstream = order.mark(upstream)

    skip_x, skip_y = order.mark(skip_x, skip_y)
    skip_one, skip_two = swap_plane(order, skip_y[:2], skip_x[2:])
    skip_swapped = skip_swapped + [to_core(skip_x), to_core(skip_y)]
    skip_one, skip_two = order.mark(skip_one, skip_two)
    skip_swapped = skip_swapped + [to_core(skip_one), to_core(skip_two)]
    attn_own = others(order.mark(attn_whole))
    attn_x, attn_y = swap_plane(order, attn_own, attn_own)
    fc2_whole = bring(order, fc2_shard, quarter, core)
    fc2_across = bring(order, fc2_shard, quarter ^ 3, core)
    skip_swapped = order.mark(*skip_swapped)
    attn_swapped = [to_core(order.after(attn_own))]
    skip_parts = [
        (skip_own, quarter, 1),
        (skip_x, quarter ^ 1, 1),
        (skip_y, quarter ^ 2, 1),
        (skip_one, quarter ^ 3, 1),
        (skip_two, quarter ^ 3, 3),
    ]
    (skip_low,) = assemble_weight(skip_shard, skip_parts, skip_swapped, core, 0)
    joined = matmul(both_inputs, skip_low) + vectors[4]
    normed, normal_one, inverse_one = norm_forward(joined, vectors[0], vectors[1])
    normed_low = normed.astype(jnp.bfloat16)
    joined, normed_low, normal_one = order.mark(joined, normed_low, normal_one)
    upstream_other = to_core(order.after(upstream))

    attn_x, attn_y = order.mark(attn_x, attn_y)
    attn_one, attn_two = swap_plane(order, attn_y[:1], attn_x[1:])
    attn_swapped = attn_swapped + [to_core(attn_x), to_core(attn_y)]
    upstream_other = order.mark(upstream_other) * batch_scale
    upstream = upstream * batch_scale
    upstream_low = jnp.concatenate([upstream, upstream_other], 0).astype(jnp.bfloat16)
    upstream_low = order.mark(upstream_low)
    weight_sq = jnp.stack(
        [
            jnp.sum(array * array)
            for array in (skip_weight, qkv_weight, proj_weight, fc1_weight, fc2_weight, hidden_bias)
        ]
    )
    weight_sq = order.mark(weight_sq)
    fc1_own = others(order.mark(fc1_whole))
    fc1_x, fc1_y = swap_plane(order, fc1_own, fc1_own)
    attn_one, attn_two = order.mark(attn_one, attn_two)
    attn_swapped = attn_swapped + [to_core(attn_one), to_core(attn_two)]
    attn_parts = [
        (attn_own, quarter, 1),
        (attn_x, quarter ^ 1, 1),
        (attn_y, quarter ^ 2, 1),
        (attn_one, quarter ^ 3, 1),
        (attn_two, quarter ^ 3, 2),
    ]
    attn_swapped = order.mark(*attn_swapped)
    qkv_low, proj_low = assemble_weight(
        attn_shard, attn_parts, attn_swapped, core, 3 * mp_count
    )
    qkv_all = jnp.einsum(
        "itd,ed->ite",
        normed_low.reshape(images, SEQ, D),
        qkv_low,
        preferred_element_type=jnp.float32,
    ).astype(jnp.bfloat16)
    qkv_all = order.mark(qkv_all)
    attended = attend(qkv_all).reshape(tokens, D)
    residual = joined + matmul(attended, proj_low) + vectors[5]
    residual = order.mark(residual)
    fc1_x, fc1_y = order.mark(fc1_x, fc1_y)
    fc1_cut = order.mark(fc1_y[:2], fc1_x[2:])
    fc1_one, fc1_two = swap_plane(order, *fc1_cut)
    fc2_own = others(order.mark(fc2_whole))
    fc2_x, fc2_y = swap_plane(order, fc2_own, fc2_own)
    normed_two, normal_two, inverse_two = norm_forward(
        order.after(residual), vectors[2], vectors[3]
    )
    normed_two, normal_two = order.mark(normed_two, normal_two)
    normed_two_other = to_core(normal_two)
    fc1_one, fc1_two = order.mark(fc1_one, fc1_two)
    fc1_parts = [
        (fc1_own, quarter, 1),
        (fc1_x, quarter ^ 1, 1),
        (fc1_y, quarter ^ 2, 1),
        (fc1_one, quarter ^ 3, 1),
        (fc1_two, quarter ^ 3, 3),
    ]
    (fc1_low,) = assemble_weight(fc1_shard, fc1_parts, None, core, 0)
    fc1_low = order.mark(fc1_low)
    normed_two_other = order.mark(normed_two_other) * vectors[2] + vectors[3]
    normed_two_low = jnp.concatenate([normed_two, normed_two_other], 0).astype(jnp.bfloat16)
    normed_two_low = order.mark(normed_two_low)
    pre_act = (
        jnp.einsum("td,fd->tf", normed_two_low, fc1_low, preferred_element_type=jnp.float32)
        + hidden_own
    )
    activated, gelu_pull = jax.vjp(gelu_exact, pre_act)
    activated_low = activated.astype(jnp.bfloat16)
    fc2_grad = jnp.einsum(
        "tf,td->fd", activated_low, upstream_low, preferred_element_type=jnp.float32
    ).reshape(4, mp_count, hidden_slice, D)
    fc2_grad = order.mark(fc2_grad)
    fc2_add = swap_plane(order, *order.mark(*cut_corner(fc2_grad, quarter)))

    fc2_x, fc2_y = order.mark(fc2_x, fc2_y)
    fc2_corner = others(order.mark(fc2_across))
    fc2_parts = [
        (fc2_own, quarter, 1),
        (fc2_x, quarter ^ 1, 1),
        (fc2_y, quarter ^ 2, 1),
        (fc2_corner, quarter ^ 3, 1),
    ]
    (fc2_low,) = assemble_weight(fc2_shard, fc2_parts, None, core, 0)
    fc2_low = order.mark(fc2_low)
    forward_part = order.mark(matmul(activated_low, fc2_low))
    forward_other = to_core(forward_part[tokens:])
    act_grad = jnp.einsum(
        "td,fd->tf", order.after(upstream_low), fc2_low, preferred_element_type=jnp.float32
    )
    pre_grad = gelu_pull(act_grad)[0]
    hidden_grad = jnp.sum(pre_grad, 0)
    pre_low, hidden_grad = order.mark(pre_grad.astype(jnp.bfloat16), hidden_grad)
    block_own = residual + forward_part[:tokens] + order.mark(forward_other)
    block_own = order.mark(block_own.reshape(images, SEQ, D))
    block_all = lax.all_gather(block_own, "mp")
    fc2_add = order.mark(*fc2_add)
    fc2_sides = swap_plane(order, *order.mark(*cut_sides(fc2_grad, quarter, *fc2_add)))
    back_part = order.mark(matmul(order.after(pre_low), fc1_low))
    back_other = to_core(back_part[tokens:])
    fc1_grad = jnp.einsum(
        "tf,td->fd",
        order.after(pre_low),
        normed_two_low,
        preferred_element_type=jnp.float32,
    ).reshape(4, mp_count, hidden_slice, D)
    fc1_grad = order.mark(fc1_grad)
    fc1_add = swap_plane(order, *order.mark(*cut_corner(fc1_grad, quarter)))
    norm_two_in = back_part[:tokens] + order.mark(back_other)
    back_two, gain_two_grad, bias_two_grad = norm_backward(
        norm_two_in, normal_two, inverse_two, vectors[2]
    )
    residual_grad = upstream + back_two
    residual_low = residual_grad.astype(jnp.bfloat16)
    residual_grad, residual_low = order.mark(residual_grad, residual_low)
    attended_grad = jnp.einsum(
        "td,ed->te", residual_low, proj_low, preferred_element_type=jnp.float32
    ).astype(jnp.bfloat16)
    qkv_grad_low = attend_back(
        qkv_all, order.mark(attended_grad.reshape(images, SEQ, D))
    ).reshape(tokens, 3 * D)
    qkv_grad_low = order.mark(qkv_grad_low)
    fc2_sides = order.mark(*fc2_sides)
    fc2_piece = sum_deep(order, fc2_grad, quarter, *fc2_sides)
    qkv_grad = jnp.einsum(
        "te,td->ed", order.after(qkv_grad_low), normed_low, preferred_element_type=jnp.float32
    ).reshape(3 * mp_count, 2, hidden_slice, D)
    proj_grad = jnp.einsum(
        "te,td->ed", attended, order.after(residual_low), preferred_element_type=jnp.float32
    ).reshape(mp_count, 2, hidden_slice, D)
    attn_given = order.mark(pick(qkv_grad, 1 - core, 1), pick(proj_grad, 1 - core, 1))
    fc1_add = order.mark(*fc1_add)
    fc1_sides = swap_plane(order, *order.mark(*cut_sides(fc1_grad, quarter, *fc1_add)))
    attn_given = [to_core(array) for array in order.after(*attn_given)]
    norm_one_in = matmul(order.after(qkv_grad_low), qkv_low)
    back_one, gain_one_grad, bias_one_grad = norm_backward(
        norm_one_in, normal_one, inverse_one, vectors[0]
    )
    joined_grad = residual_grad + back_one
    joined_low = joined_grad.astype(jnp.bfloat16)
    joined_grad, joined_low = order.mark(joined_grad, joined_low)
    skip_grad = jnp.einsum(
        "tc,td->cd", both_inputs, joined_low, preferred_element_type=jnp.float32
    ).reshape(4 * mp_count, 2, -1, D)
    skip_given = order.mark(pick(skip_grad, 1 - core, 1))
    skip_given = to_core(skip_given)
    block_all = order.mark(block_all)
    attn_given = order.mark(*attn_given)
    attn_grad = add_half([qkv_grad, proj_grad], attn_given, core)
    attn_grad = order.mark(attn_grad.reshape(4, mp_count, hidden_slice, D))
    attn_add = swap_plane(order, *order.mark(*cut_corner(attn_grad, quarter)))
    fc1_sides = order.mark(*fc1_sides)
    fc1_piece = sum_deep(order, fc1_grad, quarter, *fc1_sides)
    skip_shards = skip_low.reshape(4, mp_count, -1, D)

    def input_product(shift):
        shard_low = pick(skip_shards, lax.rem(mp_index + shift, mp_count), 1).reshape(-1, D)
        return order.mark(
            jnp.einsum("td,cd->tc", joined_low, shard_low, preferred_element_type=jnp.float32)
        )

    stay, turn_one, turn_two, turn_three = [input_product(shift) for shift in range(4)]
    turn_one = turn_mp(order.after(turn_one), 1)
    attn_add = order.mark(*attn_add)
    attn_sides = swap_plane(order, *order.mark(*cut_sides(attn_grad, quarter, *attn_add)))
    skip_given = order.mark(skip_given)
    skip_grad = add_half([skip_grad], [skip_given], core)
    skip_grad = order.mark(skip_grad.reshape(4, mp_count, -1, D))
    skip_add = swap_plane(order, *order.mark(*cut_corner(skip_grad, quarter)))
    fc2_piece = order.mark(fc2_piece)
    vector_grad = jnp.stack(
        [
            gain_one_grad,
            bias_one_grad,
            gain_two_grad,
            bias_two_grad,
            jnp.sum(joined_grad, 0),
            jnp.sum(residual_grad, 0),
            jnp.sum(upstream, 0),
        ]
    )
    hidden_grad = hidden_grad.reshape(4, mp_count, 1, hidden_slice).transpose(1, 0, 2, 3)
    hidden_grad = jnp.where(jnp.arange(2)[None, None, :, None] == core, hidden_grad, 0.0)
    small = order.mark(jnp.concatenate([vector_grad.reshape(-1), hidden_grad.reshape(-1)]))
    small_core = to_core(small)
    attn_sides = order.mark(*attn_sides)
    attn_piece = sum_deep(order, attn_grad, quarter, *attn_sides)
    turn_one = order.mark(turn_one)
    fc1_piece = order.mark(fc1_piece)
    skip_add = order.mark(*skip_add)
    skip_sides = swap_plane(order, *order.mark(*cut_sides(skip_grad, quarter, *skip_add)))
    small = order.mark(small + order.mark(small_core))
    small_x = to_x(small)
    skip_sides = order.mark(*skip_sides)
    small = order.mark(small + order.mark(small_x))
    small_y = to_y(small)
    skip_piece = sum_deep(order, skip_grad, quarter, *skip_sides)

    def spread(piece):
        return swap_plane(order, piece, piece)

    def half_of(rows):
        return (rows // 2 + 7) // 8 * 8

    def spread_far(near):
        half = half_of(near[0].shape[0])
        return swap_plane(order, near[1][:half], near[0][half:])

    def hold(piece, near, far):
        rows, half = piece.shape[0], far[0].shape[0]
        return place_rows(
            [
                (piece, 0, rows, quarter * rows),
                (near[0], 0, rows, (quarter ^ 1) * rows),
                (near[1], 0, rows, (quarter ^ 2) * rows),
                (far[0], 0, half, (quarter ^ 3) * rows),
                (far[1], 0, rows - half, (quarter ^ 3) * rows + half),
            ],
            4 * rows,
        )

    def interleave(held, other, near_state):
        rows = held.shape[0] // 4
        pieces = []
        for n in range(4):
            pieces.append((held, n * rows, rows, (2 * n + core) * rows))
            pieces.append((other, n * rows, rows, (2 * n + 1 - core) * rows))
        whole, sent = place_rows(pieces, 8 * rows, near_state)
        return whole.reshape(near_state.shape + (D,)), sent

    def own_state(state):
        width = state.shape[-1] // mp_count
        return lax.dynamic_slice_in_dim(state, mp_index * width, width, state.ndim - 1)

    def everywhere(array):
        return [array] + [turn_mp(array, shift) for shift in range(1, mp_count)]

    fc2_near, fc1_near = spread(fc2_piece), spread(fc1_piece)
    block_output = (block_all + vectors[6]).astype(jnp.bfloat16).reshape(-1, D)
    block_output = order.mark(block_output)
    fc2_near = order.mark(*fc2_near)
    fc2_far = spread_far(fc2_near)
    fc1_near = order.mark(*fc1_near)
    fc1_far = spread_far(fc1_near)
    turn_two = turn_mp(order.after(turn_two), 2)
    fc2_far = order.mark(*fc2_far)
    attn_piece = order.mark(attn_piece)
    attn_near = spread(attn_piece)
    fc2_held = order.mark(hold(fc2_piece, fc2_near, fc2_far))
    fc2_other = to_core(fc2_held)
    fc1_far = order.mark(*fc1_far)
    fc1_held = order.mark(hold(fc1_piece, fc1_near, fc1_far))
    skip_piece = order.mark(skip_piece)
    skip_near = spread(skip_piece)
    attn_near = order.mark(*attn_near)
    attn_far = spread_far(attn_near)
    fc2_sum, fc2_moments = order.mark(
        *interleave(fc2_held, order.mark(fc2_other), own_state(fc2_rows)[None])
    )
    skip_near = order.mark(*skip_near)
    skip_far = spread_far(skip_near)
    attn_far = order.mark(*attn_far)
    attn_held = order.mark(hold(attn_piece, attn_near, attn_far))
    attn_other = to_core(attn_held)
    turn_two = order.mark(turn_two)
    turn_three = turn_mp(order.after(turn_three), 3)
    fc1_other = to_core(order.after(fc1_held))
    skip_far = order.mark(*skip_far)
    skip_held = order.mark(hold(skip_piece, skip_near, skip_far))
    skip_other = to_core(skip_held)
    small = order.mark(small + order.mark(small_y))
    small = jnp.concatenate(
        [small, weight_sq, jnp.zeros((D - 6,), jnp.float32)], 0
    ).reshape(6, 2, D)
    fc1_sum, fc1_moments = order.mark(
        *interleave(fc1_held, order.mark(fc1_other), own_state(fc1_cols)[None])
    )
    hidden_sent = jnp.concatenate([fc2_moments, fc1_moments, small], 0)
    turn_three = order.mark(turn_three)
    hidden_sent = everywhere(order.mark(hidden_sent))
    attn_state = jnp.concatenate([own_state(qkv_cols), own_state(proj_rows)[None]], 0)
    attn_sum, attn_moments = order.mark(
        *interleave(attn_held, order.mark(attn_other), attn_state)
    )
    skip_sum, skip_moments = order.mark(
        *interleave(skip_held, order.mark(skip_other), own_state(skip_rows))
    )
    hidden_sent = order.mark(*hidden_sent)
    token_sent = everywhere(order.mark(jnp.concatenate([attn_moments, skip_moments], 0)))
    input_grad, skip_input_grad = order.mark(
        *order_tokens([stay, turn_one, turn_two, turn_three], mp_index)
    )
    step = jnp.zeros((8, 128), jnp.float32)
    fc2_far_new, *fc2_scales, step = order.mark(
        *scales(fc2_sum, fc2_cols[None], step, hidden_sent, 0, mp_index, (True,))
    )
    fc1_far_new, *fc1_scales, step = order.mark(
        *scales(fc1_sum, fc1_rows[None], step, hidden_sent, 1, mp_index, (False,))
    )
    token_sent = order.mark(*token_sent)
    attn_state = jnp.concatenate([qkv_rows, proj_cols[None]], 0)
    attn_far_new, *attn_scales, step = order.mark(
        *scales(attn_sum, attn_state, step, token_sent, 0, mp_index, (False, False, False, True))
    )
    skip_far_new, *skip_scales, step = order.mark(
        *scales(skip_sum, skip_cols, step, token_sent, 4, mp_index, (True, True))
    )
    steps = everywhere(step)
    small = jnp.sum(in_turn([array[2:] for array in hidden_sent]), 0).reshape(-1)
    vector_sum = small[: 7 * D].reshape(7, D)
    hidden_whole = small[7 * D : 7 * D + mp_count * hidden_local]
    weight_sq = small[11 * D : 11 * D + 6]
    vector_new = 0.5 * vector_moments + 0.5 * (vector_sum * vector_sum + moment_eps)
    vector_update = vector_sum * lax.rsqrt(vector_new)
    hidden_new = 0.5 * hidden_state + 0.5 * (hidden_whole * hidden_whole + moment_eps)
    hidden_update = hidden_whole * lax.rsqrt(hidden_new)
    vector_step = jnp.sum(vector_update * vector_update) + jnp.sum(hidden_update * hidden_update)

    def own_hidden(array):
        return lax.dynamic_slice_in_dim(array, mp_index * hidden_local, hidden_local, 0)

    hidden_sum, hidden_new = own_hidden(hidden_whole), own_hidden(hidden_new)
    hidden_update = own_hidden(hidden_update)
    tensor_sizes = (2.0 * D * D, 3.0 * D * D, 1.0 * D * D, 1.0 * D * FF, 1.0 * FF * D, 1.0 * FF)
    weight_rms = jnp.sqrt(weight_sq / jnp.array(tensor_sizes, jnp.float32))
    rates = step_rate * jnp.maximum(0.001, weight_rms)
    pairs = jnp.stack([rates, jnp.broadcast_to(vector_step, (6,))], 1)
    pairs = order.mark(pairs)
    steps = order.mark(*steps)

    qkv_turned = qkv_weight.transpose(0, 2, 1)
    skip_new, skip_new_low = renew(skip_weight, skip_sum, *skip_scales, pairs[0], steps, False)
    qkv_new, qkv_new_low = renew(qkv_turned, attn_sum, *attn_scales, pairs[1], steps, False)
    qkv_new, qkv_new_low = qkv_new.transpose(0, 2, 1), qkv_new_low.transpose(0, 2, 1)
    proj_new, proj_new_low = renew(
        proj_weight[None], attn_sum, *attn_scales, pairs[2], steps, False, first=3
    )
    fc1_new, fc1_new_low = renew(fc1_weight[None], fc1_sum, *fc1_scales, pairs[3], steps, True)
    fc2_new, fc2_new_low = renew(fc2_weight[None], fc2_sum, *fc2_scales, pairs[4], steps, False)
    step_total = jnp.sum(jnp.sum(in_turn(steps), 0)) + vector_step
    update_rms = jnp.sqrt(step_total / param_count)
    divisor = jnp.maximum(1.0, update_rms / clip_level)
    vector_rms = jnp.sqrt(jnp.mean(vectors * vectors, 1, keepdims=True))
    vectors_new = vectors - step_rate * jnp.maximum(0.001, vector_rms) * vector_update / divisor
    hidden_bias_new = hidden_bias - rates[5] / divisor * hidden_update
    piece_width = D // dp_count
    dp_start = dp_index * piece_width

    def own_piece(array, axis):
        return lax.dynamic_slice_in_dim(array, dp_start, piece_width, axis)

    def near_whole(sent, first, amount, width):
        near = in_turn([array[first : first + amount, 1, :width] for array in sent])
        return near.transpose(1, 0, 2).reshape(near.shape[1], -1)

    skip_near_new = near_whole(token_sent, 4, 2, width_local)
    attn_near_new = near_whole(token_sent, 0, 4, width_local)
    fc1_near_new = near_whole(hidden_sent, 1, 1, hidden_local)
    fc2_near_new = near_whole(hidden_sent, 0, 1, hidden_local)
    return (
        block_output,
        input_grad,
        skip_input_grad,
        own_piece(skip_sum, 2),
        own_piece(attn_sum[:3], 2).transpose(0, 2, 1),
        own_piece(attn_sum[3], 1),
        own_piece(fc1_sum[0], 1).T,
        own_piece(fc2_sum[0], 1),
        own_piece(vector_sum, 1),
        hidden_sum,
        skip_near_new,
        skip_far_new[:, 0],
        attn_far_new[:3, 0],
        attn_near_new[:3],
        attn_near_new[3],
        attn_far_new[3, 0],
        fc1_far_new[0, 0],
        fc1_near_new[0],
        fc2_near_new[0],
        fc2_far_new[0, 0],
        vector_new,
        hidden_new,
        skip_new,
        qkv_new,
        proj_new[0],
        fc1_new[0],
        fc2_new[0],
        vectors_new,
        hidden_bias_new,
        skip_new_low,
        qkv_new_low,
        proj_new_low[0],
        fc1_new_low[0],
        fc2_new_low[0],
        update_rms,
    )


def solution(mesh):
    placed = (
        P("dp", None),
        P("dp", None),
        P("dp"),
        P("dp"),
        P("dp"),
        P("dp", None),
        P(None, "mp", None),
        P(None, None, "mp"),
        P("mp", None),
        P(None, "mp"),
        P("mp", None),
        P(),
        P("mp"),
        P(),
        P(),
        P(),
        P(),
        P(),
        P(),
        P(),
        P(),
        P(),
        P(),
        P(),
        P("mp"),
    )
    return jax.shard_map(
        body,
        mesh=mesh,
        in_specs=placed,
        out_specs=(
            P("dp", None),
            P("dp", "mp"),
            P("dp", "mp"),
            P(None, "mp", "dp"),
            P(None, "dp", "mp"),
            P("mp", "dp"),
            P("dp", "mp"),
            P("mp", "dp"),
            P(None, "dp"),
            P("mp"),
            P(),
            P(),
            P(),
            P(),
            P(),
            P(),
            P(),
            P(),
            P(),
            P(),
            P(),
            P("mp"),
            P(None, "mp", None),
            P(None, None, "mp"),
            P("mp", None),
            P(None, "mp"),
            P("mp", None),
            P(),
            P("mp"),
            P(None, "mp", None),
            P(None, None, "mp"),
            P("mp", None),
            P(None, "mp"),
            P("mp", None),
            P(),
        ),
        check_vma=False,
    )
```

```python
import functools
import math

import jax
import jax.numpy as jnp
from jax import lax
from jax.experimental import pallas as pl
from jax.experimental.pallas import tpu as pltpu
from jax.sharding import PartitionSpec as P

D = 1152
HEAD_DIM = 72
FF = 4608
CLASSES = 1000
SEQ = 258


ln_eps = 1e-05
moment_eps = 1e-30
clip_level = 0.25
step_rate = 2.0
total_steps = 1000.0


def gelu_exact(inputs):
    return 0.5 * inputs * (1.0 + lax.erf(inputs * (1.0 / math.sqrt(2.0))))


def matmul(left_side, right_side):
    return jnp.dot(left_side, right_side, preferred_element_type=jnp.float32)


def norm_forward(inputs, norm_gain, norm_bias):
    centre = jnp.mean(inputs, -1, keepdims=True)
    centred = inputs - centre
    inverse = lax.rsqrt(jnp.mean(centred * centred, -1, keepdims=True) + ln_eps)
    normal = centred * inverse
    return (normal * norm_gain + norm_bias, normal, inverse)


def norm_backward(incoming, normal, inverse, norm_gain):
    scaled = incoming * norm_gain
    inner_mean = jnp.mean(scaled, -1, keepdims=True)
    proj_mean = jnp.mean(scaled * normal, -1, keepdims=True)
    return (
        inverse * (scaled - inner_mean - normal * proj_mean),
        jnp.sum(incoming * normal, 0),
        jnp.sum(incoming, 0),
    )


def adafactor(
    grad_pieces,
    weight_pieces,
    starts,
    row_states,
    col_states,
    vector_piece,
    vector_weight,
    vector_state,
    hidden_piece,
    hidden_weight,
    hidden_state,
    first_mask,
    reduce_moments,
    reduce_norm,
):
    full_shapes = ((D, D), (D, D), (D, D), (D, FF), (FF, D))
    tensor_sizes = (2.0 * D * D, 3.0 * D * D, 1.0 * D * D, 1.0 * D * FF, 1.0 * FF * D)
    zero_start = jnp.zeros((), jnp.int32)
    row_parts = []
    col_parts = []
    weight_sq = []
    for position in range(5):
        grad_piece = grad_pieces[position]
        leading = grad_piece.shape[0]
        squares = grad_piece * grad_piece + moment_eps
        row_zero = jnp.zeros((leading, full_shapes[position][0]), jnp.float32)
        col_zero = jnp.zeros((leading, full_shapes[position][1]), jnp.float32)
        row_parts.append(
            lax.dynamic_update_slice(
                row_zero, jnp.sum(squares, 2), (zero_start, starts[position][0])
            ).reshape(-1)
        )
        col_parts.append(
            lax.dynamic_update_slice(
                col_zero, jnp.sum(squares, 1), (zero_start, starts[position][1])
            ).reshape(-1)
        )
        weight_sq.append(jnp.sum(weight_pieces[position] * weight_pieces[position])[None])
    weight_sq.append(jnp.sum(vector_weight * vector_weight, 1) * first_mask)
    weight_sq.append(jnp.sum(hidden_weight * hidden_weight)[None])
    row_total, col_total, weight_total = reduce_moments(
        jnp.concatenate(row_parts), jnp.concatenate(col_parts), jnp.concatenate(weight_sq)
    )
    row_news = []
    col_news = []
    updates = []
    step_sq = jnp.zeros((), jnp.float32)
    row_offset = 0
    col_offset = 0
    for position in range(5):
        grad_piece = grad_pieces[position]
        leading = grad_piece.shape[0]
        rows_full, cols_full = full_shapes[position]
        row_sum = row_total[row_offset : row_offset + leading * rows_full].reshape(
            leading, rows_full
        )
        col_sum = col_total[col_offset : col_offset + leading * cols_full].reshape(
            leading, cols_full
        )
        row_offset = row_offset + leading * rows_full
        col_offset = col_offset + leading * cols_full
        row_new = 0.5 * row_states[position] + 0.5 * (row_sum / cols_full)
        col_new = 0.5 * col_states[position] + 0.5 * (col_sum / rows_full)
        row_piece = lax.dynamic_slice(
            row_new, (zero_start, starts[position][0]), (leading, grad_piece.shape[1])
        )
        col_piece = lax.dynamic_slice(
            col_new, (zero_start, starts[position][1]), (leading, grad_piece.shape[2])
        )
        row_mean = jnp.mean(row_new, 1)
        update = grad_piece * lax.rsqrt(
            row_piece[:, :, None] * col_piece[:, None, :] / row_mean[:, None, None]
        )
        step_sq = step_sq + jnp.sum(update * update)
        row_news.append(row_new)
        col_news.append(col_new)
        updates.append(update)
    vector_new = 0.5 * vector_state + 0.5 * (vector_piece * vector_piece + moment_eps)
    vector_update = vector_piece * lax.rsqrt(vector_new)
    hidden_new = 0.5 * hidden_state + 0.5 * (hidden_piece * hidden_piece + moment_eps)
    hidden_update = hidden_piece * lax.rsqrt(hidden_new)
    step_sq = (
        step_sq
        + jnp.sum(vector_update * vector_update) * first_mask
        + jnp.sum(hidden_update * hidden_update)
    )
    step_total = reduce_norm(step_sq)
    param_count = 6.0 * D * D + 2.0 * D * FF + 7.0 * D + FF
    update_rms = jnp.sqrt(step_total / param_count)
    divisor = jnp.maximum(1.0, update_rms / clip_level)
    new_weights = []
    for position in range(5):
        weight_rms = jnp.sqrt(weight_total[position] / tensor_sizes[position])
        new_weights.append(
            weight_pieces[position]
            - step_rate * jnp.maximum(0.001, weight_rms) * updates[position] / divisor
        )
    vector_rms = jnp.sqrt(weight_total[5:12] / D)[:, None]
    vector_weight_new = (
        vector_weight - step_rate * jnp.maximum(0.001, vector_rms) * vector_update / divisor
    )
    hidden_rms = jnp.sqrt(weight_total[12] / FF)
    hidden_weight_new = (
        hidden_weight - step_rate * jnp.maximum(0.001, hidden_rms) * hidden_update / divisor
    )
    return (
        new_weights,
        row_news,
        col_news,
        vector_new,
        vector_weight_new,
        hidden_new,
        hidden_weight_new,
        update_rms,
    )


def body_tensor(
    block_input,
    skip_input,
    timesteps,
    class_labels,
    loss_weights,
    grad_output,
    skip_weight,
    qkv_weight,
    proj_weight,
    fc1_weight,
    fc2_weight,
    vectors,
    hidden_bias,
    skip_rows,
    skip_cols,
    qkv_rows,
    qkv_cols,
    proj_rows,
    proj_cols,
    fc1_rows,
    fc1_cols,
    fc2_rows,
    fc2_cols,
    vector_moments,
    hidden_moments,
):
    image_count = timesteps.shape[0]
    width_local = qkv_weight.shape[2]
    heads_local = width_local // HEAD_DIM
    hidden_local = fc1_weight.shape[1]
    mp_index = lax.axis_index("mp")
    dp_index = lax.axis_index("dp")
    dp_count = lax.axis_size("dp")
    first_mask = (mp_index == 0).astype(jnp.float32)
    feature_start = mp_index * skip_weight.shape[1]
    block_local = lax.dynamic_slice_in_dim(block_input, feature_start, skip_weight.shape[1], 1)
    skip_local = lax.dynamic_slice_in_dim(skip_input, feature_start, skip_weight.shape[1], 1)
    angles = (timesteps.astype(jnp.float32) + 0.5) * (0.5 * math.pi / total_steps)
    alpha_sq = jnp.square(jnp.cos(angles))
    sigma_sq = jnp.square(jnp.sin(angles))
    snr_weight = 5.0 * sigma_sq / jnp.maximum(alpha_sq, 5.0 * sigma_sq)
    base_weight = loss_weights * snr_weight
    one_hot = (class_labels[:, None] == jnp.arange(CLASSES, dtype=jnp.int32)[None, :]).astype(
        jnp.float32
    )
    class_counts, weight_total = lax.psum((jnp.sum(one_hot, 0), jnp.sum(base_weight)), "dp")
    own_count = jnp.dot(one_hot, class_counts, precision=lax.Precision.HIGHEST)
    item_weight = base_weight * (image_count * dp_count / weight_total) * lax.rsqrt(own_count)
    upstream = (
        grad_output.astype(jnp.float32).reshape(image_count, SEQ, D) * item_weight[:, None, None]
    ).reshape(-1, D)
    skip_low = skip_weight.astype(jnp.bfloat16)
    qkv_low = qkv_weight.astype(jnp.bfloat16)
    proj_low = proj_weight.astype(jnp.bfloat16)
    fc1_low = fc1_weight.astype(jnp.bfloat16)
    fc2_low = fc2_weight.astype(jnp.bfloat16)
    joined = (
        lax.psum(matmul(block_local, skip_low[0]) + matmul(skip_local, skip_low[1]), "mp")
        + vectors[4]
    )
    normed, normal_one, inverse_one = norm_forward(joined, vectors[0], vectors[1])
    normed_low = normed.astype(jnp.bfloat16)
    qkv_all = jnp.einsum(
        "td,sde->ste", normed_low, qkv_low, preferred_element_type=jnp.float32
    ).astype(jnp.bfloat16)
    heads_view = qkv_all.reshape(3, image_count, SEQ, heads_local, HEAD_DIM)
    query_low = heads_view[0]
    key_low = heads_view[1]
    value_low = heads_view[2]
    score_scale = HEAD_DIM ** (-0.5)

    def score_block():
        return (
            jnp.einsum("iqhe,ikhe->ihqk", query_low, key_low, preferred_element_type=jnp.float32)
            * score_scale
        )

    scores = score_block()
    score_top = jnp.max(scores, -1, keepdims=True)
    expo_scores = jnp.exp(scores - score_top)
    expo_total = jnp.sum(expo_scores, -1, keepdims=True)
    weights_low = (expo_scores / expo_total).astype(jnp.bfloat16)
    log_total = score_top + jnp.log(expo_total)
    attended = (
        jnp.einsum("ihqk,ikhe->iqhe", weights_low, value_low, preferred_element_type=jnp.float32)
        .astype(jnp.bfloat16)
        .reshape(-1, width_local)
    )
    residual = joined + lax.psum(matmul(attended, proj_low), "mp") + vectors[5]
    normed_two, normal_two, inverse_two = norm_forward(residual, vectors[2], vectors[3])
    normed_two_low = normed_two.astype(jnp.bfloat16)
    pre_act = matmul(normed_two_low, fc1_low) + hidden_bias
    activated, gelu_pull = jax.vjp(gelu_exact, pre_act)
    activated_low = activated.astype(jnp.bfloat16)
    block_output = (residual + lax.psum(matmul(activated_low, fc2_low), "mp") + vectors[6]).astype(
        jnp.bfloat16
    )
    upstream_low = upstream.astype(jnp.bfloat16)
    fc2_grad = jnp.einsum(
        "tf,td->fd", activated_low, upstream_low, preferred_element_type=jnp.float32
    )
    fc2_bias_grad = jnp.sum(upstream, 0)
    act_grad = jnp.einsum("td,fd->tf", upstream_low, fc2_low, preferred_element_type=jnp.float32)
    pre_grad = gelu_pull(act_grad)[0]
    pre_low = pre_grad.astype(jnp.bfloat16)
    fc1_grad = jnp.einsum("td,tf->df", normed_two_low, pre_low, preferred_element_type=jnp.float32)
    hidden_grad = jnp.sum(pre_grad, 0)
    norm_two_in = lax.psum(
        jnp.einsum("tf,df->td", pre_low, fc1_low, preferred_element_type=jnp.float32), "mp"
    )
    back_two, gain_two_grad, bias_two_grad = norm_backward(
        norm_two_in, normal_two, inverse_two, vectors[2]
    )
    residual_grad = upstream + back_two
    proj_bias_grad = jnp.sum(residual_grad, 0)
    residual_low = residual_grad.astype(jnp.bfloat16)
    proj_grad = jnp.einsum("te,td->ed", attended, residual_low, preferred_element_type=jnp.float32)
    attended_grad = jnp.einsum(
        "td,ed->te", residual_low, proj_low, preferred_element_type=jnp.float32
    ).astype(jnp.bfloat16)
    attended_grad = attended_grad.reshape(image_count, SEQ, heads_local, HEAD_DIM)
    scores = score_block()
    probs_exact = jnp.exp(scores - log_total)
    prob_grad = jnp.einsum(
        "iqhe,ikhe->ihqk", attended_grad, value_low, preferred_element_type=jnp.float32
    )
    score_grad = (
        probs_exact * (prob_grad - jnp.sum(probs_exact * prob_grad, -1, keepdims=True))
    ).astype(jnp.bfloat16)
    query_grad = (
        jnp.einsum("ihqk,ikhe->iqhe", score_grad, key_low, preferred_element_type=jnp.float32)
        * score_scale
    )
    key_grad = (
        jnp.einsum("ihqk,iqhe->ikhe", score_grad, query_low, preferred_element_type=jnp.float32)
        * score_scale
    )
    value_grad = jnp.einsum(
        "ihqk,iqhe->ikhe", weights_low, attended_grad, preferred_element_type=jnp.float32
    )
    qkv_grad_low = (
        jnp.stack([query_grad, key_grad, value_grad])
        .astype(jnp.bfloat16)
        .reshape(3, -1, width_local)
    )
    qkv_grad = jnp.einsum(
        "td,ste->sde", normed_low, qkv_grad_low, preferred_element_type=jnp.float32
    )
    norm_one_in = lax.psum(
        jnp.einsum("ste,sde->td", qkv_grad_low, qkv_low, preferred_element_type=jnp.float32), "mp"
    )
    back_one, gain_one_grad, bias_one_grad = norm_backward(
        norm_one_in, normal_one, inverse_one, vectors[0]
    )
    joined_grad = residual_grad + back_one
    skip_bias_grad = jnp.sum(joined_grad, 0)
    joined_low = joined_grad.astype(jnp.bfloat16)
    skip_grad = jnp.stack(
        [
            jnp.einsum("tc,td->cd", block_local, joined_low, preferred_element_type=jnp.float32),
            jnp.einsum("tc,td->cd", skip_local, joined_low, preferred_element_type=jnp.float32),
        ]
    )
    input_grad = jnp.einsum(
        "td,cd->tc", joined_low, skip_low[0], preferred_element_type=jnp.float32
    )
    skip_input_grad = jnp.einsum(
        "td,cd->tc", joined_low, skip_low[1], preferred_element_type=jnp.float32
    )
    vector_grad = jnp.stack(
        [
            gain_one_grad,
            bias_one_grad,
            gain_two_grad,
            bias_two_grad,
            skip_bias_grad,
            proj_bias_grad,
            fc2_bias_grad,
        ]
    )
    row_states = [skip_rows, qkv_rows, proj_rows[None], fc1_rows[None], fc2_rows[None]]
    col_states = [skip_cols, qkv_cols, proj_cols[None], fc1_cols[None], fc2_cols[None]]
    piece_width = D // dp_count
    dp_start = dp_index * piece_width
    zero_start = jnp.zeros((), jnp.int32)
    summed = lax.psum(
        (skip_grad, qkv_grad, proj_grad, fc1_grad, fc2_grad, vector_grad, hidden_grad), "dp"
    )

    def moments_mp(row_all, col_all, squares_all):
        return lax.psum((row_all, col_all, squares_all), "mp")

    def norm_mp(step_sq):
        return lax.psum(step_sq, "mp")

    grad_pieces = [summed[0], summed[1], summed[2][None], summed[3][None], summed[4][None]]
    weight_pieces = [skip_weight, qkv_weight, proj_weight[None], fc1_weight[None], fc2_weight[None]]
    starts = [
        (mp_index * width_local, zero_start),
        (zero_start, mp_index * width_local),
        (mp_index * width_local, zero_start),
        (zero_start, mp_index * hidden_local),
        (mp_index * hidden_local, zero_start),
    ]
    results = adafactor(
        grad_pieces,
        weight_pieces,
        starts,
        row_states,
        col_states,
        summed[5],
        vectors,
        vector_moments,
        summed[6],
        hidden_bias,
        hidden_moments,
        first_mask,
        moments_mp,
        norm_mp,
    )
    (
        new_weights,
        row_news,
        col_news,
        vector_state_new,
        vectors_new,
        hidden_state_new,
        hidden_new,
        update_rms,
    ) = results
    skip_new = new_weights[0]
    qkv_new = new_weights[1]
    proj_new = new_weights[2][0]
    fc1_new = new_weights[3][0]
    fc2_new = new_weights[4][0]
    skip_grad_out = lax.dynamic_slice_in_dim(summed[0], dp_start, piece_width, 2)
    qkv_grad_out = lax.dynamic_slice_in_dim(summed[1], dp_start, piece_width, 1)
    proj_grad_out = lax.dynamic_slice_in_dim(summed[2], dp_start, piece_width, 1)
    fc1_grad_out = lax.dynamic_slice_in_dim(summed[3], dp_start, piece_width, 0)
    fc2_grad_out = lax.dynamic_slice_in_dim(summed[4], dp_start, piece_width, 1)
    vector_grad_out = lax.dynamic_slice_in_dim(summed[5], dp_start, piece_width, 1)
    hidden_grad_out = summed[6]
    return (
        block_output,
        input_grad,
        skip_input_grad,
        skip_grad_out,
        qkv_grad_out,
        proj_grad_out,
        fc1_grad_out,
        fc2_grad_out,
        vector_grad_out,
        hidden_grad_out,
        row_news[0],
        col_news[0],
        row_news[1],
        col_news[1],
        row_news[2][0],
        col_news[2][0],
        row_news[3][0],
        col_news[3][0],
        row_news[4][0],
        col_news[4][0],
        vector_state_new,
        hidden_state_new,
        skip_new,
        qkv_new,
        proj_new,
        fc1_new,
        fc2_new,
        vectors_new,
        hidden_new,
        skip_new.astype(jnp.bfloat16),
        qkv_new.astype(jnp.bfloat16),
        proj_new.astype(jnp.bfloat16),
        fc1_new.astype(jnp.bfloat16),
        fc2_new.astype(jnp.bfloat16),
        update_rms,
    )


def body(*operands):
    images = operands[2].shape[0]
    if images % lax.axis_size("mp") == 0 and lax.axis_size("dp") == 8:
        return body_data(*operands)
    return body_tensor(*operands)


small_cost = pl.CostEstimate(flops=0, bytes_accessed=1024, transcendentals=0)


def to_core(array):
    return lax.ppermute(array, "dp", [(i, i ^ 1) for i in range(8)])


def to_x(array):
    return lax.ppermute(array, "dp", [(i, i ^ 2) for i in range(8)])


def to_y(array):
    return lax.ppermute(array, "dp", [(i, i ^ 4) for i in range(8)])


def turn_mp(array, shift):
    count = lax.axis_size("mp")
    return lax.ppermute(array, "mp", [(i, (i + shift) % count) for i in range(count)])


def pick(array, index, axis):
    return lax.dynamic_index_in_dim(array, index, axis, keepdims=False)


def assemble(steps, targets, core, rows, blocks, split):
    arrays = []
    for step in steps:
        for array, _ in step:
            if not any(array is other for other in arrays):
                arrays.append(array)
    place = [
        [(next(n for n, other in enumerate(arrays) if other is array), k) for array, k in step]
        for step in steps
    ]
    table = jnp.stack([jnp.asarray(v, jnp.int32) for v in [*targets, core]])
    depth = 4
    outs = 2 if split < blocks else 1

    def kernel(table_ref, *refs):
        sources = refs[: len(arrays)]
        wholes = refs[len(arrays) : len(arrays) + outs]
        wide, narrow, in_sem, out_sem = refs[len(arrays) + outs :]
        half = rows // 2
        first = pl.multiple_of(table_ref[len(steps)] * half, half)
        second = pl.multiple_of(half - first, half)

        def fetch(step):
            slot = step % depth
            if len(place[step]) == 1:
                ((n, k),) = place[step]
                return [pltpu.make_async_copy(sources[n].at[k], wide.at[slot], in_sem.at[slot, 0])]
            copies = []
            for part, ((n, k), start) in enumerate(zip(place[step], (first, second))):
                spot = wide.at[slot, pl.ds(start, half)]
                copies.append(pltpu.make_async_copy(sources[n].at[k], spot, in_sem.at[slot, part]))
            return copies

        def leave(step, whole, spot):
            slot = step % depth
            return pltpu.make_async_copy(narrow.at[slot], whole.at[spot], out_sem.at[slot])

        for step in range(len(steps) + depth - 1):
            if step < len(steps):
                for copy in fetch(step):
                    copy.start()
            step = step - (depth - 1)
            if step < 0:
                continue
            slot = step % depth
            for copy in fetch(step):
                copy.wait()
            if step >= depth:
                leave(step - depth, wholes[0], 0).wait()
            narrow[slot] = wide[slot].astype(jnp.bfloat16)
            spot = table_ref[step]
            if outs == 1:
                leave(step, wholes[0], spot).start()
            else:

                @pl.when(spot < split)
                def _():
                    leave(step, wholes[0], spot).start()

                @pl.when(spot >= split)
                def _():
                    leave(step, wholes[1], spot - split).start()

        for step in range(max(0, len(steps) - depth), len(steps)):
            leave(step, wholes[0], 0).wait()

    shapes = [jax.ShapeDtypeStruct((split, rows, D), jnp.bfloat16)]
    if outs == 2:
        shapes.append(jax.ShapeDtypeStruct((blocks - split, rows, D), jnp.bfloat16))
    anywhere = pl.BlockSpec(memory_space=pl.ANY)
    return pl.pallas_call(
        kernel,
        in_specs=[pl.BlockSpec(memory_space=pltpu.SMEM)] + [anywhere] * len(arrays),
        out_specs=[anywhere] * outs,
        out_shape=shapes,
        scratch_shapes=[
            pltpu.VMEM((depth, rows, D), jnp.float32),
            pltpu.VMEM((depth, rows, D), jnp.bfloat16),
            pltpu.SemaphoreType.DMA((depth, 2)),
            pltpu.SemaphoreType.DMA((depth,)),
        ],
        compiler_params=pltpu.CompilerParams(vmem_limit_bytes=32 * 1024 * 1024),
        cost_estimate=small_cost,
    )(table, *arrays)


class Order:
    def __init__(self):
        self.token = None

    def after(self, *arrays):
        if self.token is not None:
            arrays = lax.optimization_barrier((*arrays, self.token))[:-1]
        return arrays if len(arrays) > 1 else arrays[0]

    def mark(self, *arrays):
        arrays = self.after(*arrays)
        self.token = arrays[0] if isinstance(arrays, tuple) else arrays
        return arrays


def swap_plane(order, for_x, for_y):
    for_x, for_y = order.after(for_x, for_y)
    return to_x(for_x), to_y(for_y)


def in_turn(arrays):
    count = len(arrays)
    twice = jnp.stack(list(arrays[::-1]) * 2)
    return lax.dynamic_slice_in_dim(twice, count - 1 - lax.axis_index("mp"), count, 0)


def gather_deep(array):
    return in_turn([array] + [turn_mp(array, shift) for shift in range(1, lax.axis_size("mp"))])


def sum_flat(array):
    for swap in (to_core, to_x, to_y):
        array = array + swap(array)
    return array


def bring(order, shard, quarter, core):
    count = lax.axis_size("mp")
    part = pick(pick(shard.reshape(4, 2, -1, D), quarter, 0), core, 0)
    return lax.all_gather(order.after(part), "mp")


def others(whole):
    count = lax.axis_size("mp")
    twice = jnp.concatenate([whole, whole], 0)
    return lax.dynamic_slice_in_dim(twice, lax.axis_index("mp") + 1, count - 1, 0)


def assemble_weight(shard, parts, swapped, core, split):
    count = lax.axis_size("mp")
    rows = shard.shape[0] // 8

    def spot(shard_index, quarter):
        shard_index = lax.rem(lax.axis_index("mp") + shard_index, count)
        return quarter * count + shard_index

    if swapped is None:
        mine = pick(shard.reshape(4, 2, rows, D), core, 1)
    else:
        mine = shard.reshape(4, 2 * rows, D)
    steps = [((mine, n),) for n in range(4)]
    targets = [spot(0, n) for n in range(4)]
    for n, (array, quarter, first) in enumerate(parts):
        for k in range(array.shape[0]):
            steps.append(((array, k),) if swapped is None else ((array, k), (swapped[n], k)))
            targets.append(spot(first + k, quarter))
    rows = mine.shape[1]
    whole = assemble(steps, targets, core, rows, count * 4, split or count * 4)
    return [array.reshape(-1, D) for array in whole]


def cut_corner(grad, quarter):
    corner = pick(grad, quarter ^ 3, 0)
    half = corner.shape[0] // 2
    return corner[:half], corner[half:]


def cut_sides(grad, quarter, add_y, add_x):
    half = add_y.shape[0]
    for_y = pick(grad, quarter ^ 2, 0)
    for_x = pick(grad, quarter ^ 1, 0)
    for_y = jnp.concatenate([for_y[:half] + add_y, for_y[half:]], 0)
    for_x = jnp.concatenate([for_x[:half], for_x[half:] + add_x], 0)
    return for_x, for_y


def sum_deep(order, grad, quarter, from_x, from_y):
    own = order.mark(pick(grad, quarter, 0) + from_x + from_y)
    return lax.psum_scatter(own, "mp", scatter_dimension=0, tiled=False)


def place_rows(pieces, rows, near_state=None):
    arrays = []
    for array, *_ in pieces:
        if not any(array is other for other in arrays):
            arrays.append(array)
    steps = [
        (next(n for n, other in enumerate(arrays) if other is array), first, amount)
        for array, first, amount, _ in pieces
    ]
    table = jnp.stack([jnp.asarray(spot, jnp.int32) for *_, spot in pieces])

    def kernel(table_ref, *refs):
        sources = refs[: len(arrays)]
        sems = refs[-1]
        if near_state is None:
            out_ref = refs[len(arrays)]
        else:
            state_ref, out_ref, moment_ref = refs[len(arrays) : -1]
        copies = []
        for step, (n, first, amount) in enumerate(steps):
            spot = pl.multiple_of(table_ref[step], 8)
            source = sources[n].at[pl.ds(first, amount)]
            copies.append(
                pltpu.make_async_copy(source, out_ref.at[pl.ds(spot, amount)], sems.at[step])
            )
        for copy in copies:
            copy.start()
        for copy in copies:
            copy.wait()
        if near_state is None:
            return
        leading, length = near_state.shape
        chunk = length if length < 384 else 384
        for lead in range(leading):
            total = jnp.zeros((1, D), jnp.float32)
            for first in range(0, length, chunk):
                grad = out_ref[lead * length + first : lead * length + first + chunk]
                squares = grad * grad + moment_eps
                total = total + jnp.sum(squares, 0, keepdims=True)
                near = 0.5 * state_ref[lead, :1, first : first + chunk]
                near = near + 0.5 * (as_row(lanes_of(squares)) / D)
                moment_ref[lead, 1:2, first : first + chunk] = near
            moment_ref[lead, :1] = total
            if length < D:
                moment_ref[lead, 1:2, length:] = jnp.zeros((1, D - length), jnp.float32)

    vmem = pl.BlockSpec(memory_space=pltpu.VMEM)
    in_specs = [pl.BlockSpec(memory_space=pltpu.SMEM)]
    in_specs = in_specs + [pl.BlockSpec(memory_space=pl.ANY)] * len(arrays)
    out_specs, shapes = [vmem], [jax.ShapeDtypeStruct((rows, D), jnp.float32)]
    operands = [table, *arrays]
    if near_state is not None:
        leading, length = near_state.shape
        in_specs.append(vmem)
        operands.append(near_state.reshape(leading, 1, length))
        out_specs.append(vmem)
        shapes.append(jax.ShapeDtypeStruct((leading, 2, D), jnp.float32))
    result = pl.pallas_call(
        kernel,
        in_specs=in_specs,
        out_specs=out_specs,
        out_shape=shapes,
        scratch_shapes=[pltpu.SemaphoreType.DMA((len(steps),))],
        compiler_params=pltpu.CompilerParams(vmem_limit_bytes=40 * 1024 * 1024),
        cost_estimate=small_cost,
    )(*operands)
    return result[0] if near_state is None else result


def add_half(grads, given, core):
    rows = grads[0].shape[2]
    amounts = [array.shape[0] for array in grads]
    firsts = [sum(amounts[:n]) for n in range(len(amounts))]

    def kernel(core_ref, *refs):
        for n, (first, amount) in enumerate(zip(firsts, amounts)):

            @pl.when((pl.program_id(0) >= first) & (pl.program_id(0) < first + amount))
            def _():
                refs[-1][...] = refs[n][0] + refs[len(grads) + n][...]

    def at(first, amount):
        return lambda step: jnp.clip(step - first, 0, amount - 1)

    spots = [at(*pair) for pair in zip(firsts, amounts)]
    own_specs = [
        pl.BlockSpec((1, 1, rows, D), lambda step, core_ref, at=at: (at(step), core_ref[0], 0, 0))
        for at in spots
    ]
    given_specs = [
        pl.BlockSpec((1, rows, D), lambda step, core_ref, at=at: (at(step), 0, 0)) for at in spots
    ]
    total = sum(amounts)
    return pl.pallas_call(
        kernel,
        grid_spec=pltpu.PrefetchScalarGridSpec(
            num_scalar_prefetch=1,
            grid=(total,),
            in_specs=own_specs + given_specs,
            out_specs=pl.BlockSpec((1, rows, D), lambda step, core_ref: (step, 0, 0)),
        ),
        out_shape=jax.ShapeDtypeStruct((total, rows, D), jnp.float32),
        compiler_params=pltpu.CompilerParams(vmem_limit_bytes=40 * 1024 * 1024),
        cost_estimate=small_cost,
    )(core[None], *grads, *given)


def order_tokens(arrays, mp_index):
    count = len(arrays)
    tokens, width = arrays[0].shape[0], arrays[0].shape[1] // 2

    def kernel(place_ref, *refs):
        left_ref, right_ref, held, sems = refs[count:]

        def copy(n, index):
            return pltpu.make_async_copy(refs[n], held.at[index], sems.at[index])

        for index in range(count):
            for n in range(count):

                @pl.when(lax.rem(place_ref[0] + count - index, count) == n)
                def _():
                    copy(n, index).start()

        for index in range(count):
            copy(0, index).wait()
            rows = slice(index * tokens, (index + 1) * tokens)
            left_ref[rows] = held[index, :, :width]
            right_ref[rows] = held[index, :, width:]

    vmem = pl.BlockSpec(memory_space=pltpu.VMEM)
    shape = jax.ShapeDtypeStruct((count * tokens, width), jnp.float32)
    return pl.pallas_call(
        kernel,
        in_specs=[pl.BlockSpec(memory_space=pltpu.SMEM)]
        + [pl.BlockSpec(memory_space=pl.ANY)] * count,
        out_specs=[vmem, vmem],
        out_shape=[shape, shape],
        scratch_shapes=[
            pltpu.VMEM((count, tokens, 2 * width), jnp.float32),
            pltpu.SemaphoreType.DMA((count,)),
        ],
        compiler_params=pltpu.CompilerParams(vmem_limit_bytes=40 * 1024 * 1024),
        cost_estimate=small_cost,
    )(mp_index[None], *arrays)


def lanes_of(array):
    total = array[:, :128]
    for tile in range(1, array.shape[1] // 128):
        total = total + array[:, tile * 128 : (tile + 1) * 128]
    return total


def as_row(column):
    return jnp.sum(column.T, 0, keepdims=True)


def as_column(row):
    return jnp.broadcast_to(row, (128, row.shape[1])).T


def scale_kernel(count, by_rows, place_ref, grad_ref, state_ref, before_ref, *refs):
    sources = refs[:count]
    far_ref, scale_ref, near_ref, step_ref = refs[count:]
    rows = grad_ref.shape[1]
    total = jnp.zeros((1, D), jnp.float32)
    near_sum = jnp.zeros((1, 1), jnp.float32)
    for index in range(count):
        part = jnp.zeros((2, D), jnp.float32)
        for shift in range(count):
            part = jnp.where(place_ref[0] == (index + shift) % count, sources[shift][0], part)
        total = total + part[:1]
        near_sum = near_sum + jnp.sum(part[1:], 1, keepdims=True)
    far = 0.5 * state_ref[0] + 0.5 * (total / (count * rows))
    far_ref[0] = far
    lead = pl.program_id(0)
    near_mean = near_sum / (count * rows)
    far_mean = jnp.sum(far, 1, keepdims=True) / D
    if all(by_rows):
        mean = near_mean
    elif not any(by_rows):
        mean = far_mean
    else:
        split = by_rows.index(True)
        mean = jnp.where(lead >= split, near_mean, far_mean)
    far_scale = lax.rsqrt(far)
    near_scale = as_column(lax.rsqrt(sources[0][0][1:2, :rows] / mean))
    scale_ref[0] = far_scale
    near_ref[0] = near_scale
    step = grad_ref[0] * far_scale
    step = lanes_of(step * step) * near_scale * near_scale

    @pl.when(lead == 0)
    def _():
        step_ref[...] = before_ref[...]

    step_ref[...] += jnp.sum(step.reshape(rows // 8, 8, 128), 0)


def scales(grad, far_state, before, sources, first, mp_index, by_rows):
    leading, rows, _ = grad.shape
    count = len(sources)
    small = pl.BlockSpec((1, 2, D), lambda i: (i + first, 0, 0))
    line = pl.BlockSpec((1, 1, D), lambda i: (i, 0, 0))
    return pl.pallas_call(
        functools.partial(scale_kernel, count, by_rows),
        grid=(leading,),
        in_specs=[
            pl.BlockSpec(memory_space=pltpu.SMEM),
            pl.BlockSpec((1, rows, D), lambda i: (i, 0, 0)),
            line,
            pl.BlockSpec((8, 128), lambda i: (0, 0)),
        ]
        + [small] * count,
        out_specs=[
            line,
            line,
            pl.BlockSpec((1, rows, 128), lambda i: (i, 0, 0)),
            pl.BlockSpec((8, 128), lambda i: (0, 0)),
        ],
        out_shape=[
            jax.ShapeDtypeStruct((leading, 1, D), jnp.float32),
            jax.ShapeDtypeStruct((leading, 1, D), jnp.float32),
            jax.ShapeDtypeStruct((leading, rows, 128), jnp.float32),
            jax.ShapeDtypeStruct((8, 128), jnp.float32),
        ],
        compiler_params=pltpu.CompilerParams(vmem_limit_bytes=40 * 1024 * 1024),
        cost_estimate=small_cost,
    )(mp_index[None], grad, far_state.reshape(leading, 1, D), before, *sources)


param_count = 6.0 * D * D + 2.0 * D * FF + 7.0 * D + FF


def renew_kernel(turned, count, rate_ref, weight_ref, grad_ref, far_ref, near_ref, *refs):
    new_ref, low_ref = refs[count:]
    total = refs[0][...]
    for ref in refs[1:count]:
        total = total + ref[...]
    total = jnp.sum(jnp.sum(total, 0, keepdims=True), 1, keepdims=True) + rate_ref[1]
    divisor = jnp.maximum(1.0, jnp.sqrt(total / param_count) / clip_level)
    step = grad_ref[0] * far_ref[0] * (near_ref[0][:, :1] * (rate_ref[0] / divisor))
    new = weight_ref[0] - (step.T if turned else step)
    new_ref[0] = new
    low_ref[0] = new.astype(jnp.bfloat16)


def renew(weight, grad, far_scale, near_scale, rate, steps, turned, first=0):
    leading, rows = weight.shape[0], grad.shape[1]
    if turned:
        width = 384
        grid = (leading, D // width)
        weight_spec = pl.BlockSpec((1, width, rows), lambda i, j: (i, j, 0))
        grad_spec = pl.BlockSpec((1, rows, width), lambda i, j: (i + first, 0, j))
        far_spec = pl.BlockSpec((1, 1, width), lambda i, j: (i + first, 0, j))
        near_spec = pl.BlockSpec((1, rows, 128), lambda i, j: (i + first, 0, 0))
    else:
        height = min(rows, 288)
        grid = (leading, rows // height)
        weight_spec = pl.BlockSpec((1, height, D), lambda i, j: (i, j, 0))
        grad_spec = pl.BlockSpec((1, height, D), lambda i, j: (i + first, j, 0))
        far_spec = pl.BlockSpec((1, 1, D), lambda i, j: (i + first, 0, 0))
        near_spec = pl.BlockSpec((1, height, 128), lambda i, j: (i + first, j, 0))
    return pl.pallas_call(
        functools.partial(renew_kernel, turned, len(steps)),
        grid=grid,
        in_specs=[pl.BlockSpec(memory_space=pltpu.SMEM), weight_spec, grad_spec, far_spec, near_spec]
        + [pl.BlockSpec((8, 128), lambda i, j: (0, 0))] * len(steps),
        out_specs=[weight_spec, weight_spec],
        out_shape=[
            jax.ShapeDtypeStruct(weight.shape, jnp.float32),
            jax.ShapeDtypeStruct(weight.shape, jnp.bfloat16),
        ],
        compiler_params=pltpu.CompilerParams(vmem_limit_bytes=40 * 1024 * 1024),
        cost_estimate=small_cost,
    )(rate, weight, grad, far_scale, near_scale, *steps)


def head_windows():
    spans = []
    for head in range(D // HEAD_DIM):
        first = head * HEAD_DIM
        start = first // 128 * 128
        stop = -(-(first + HEAD_DIM) // 128) * 128
        spans.append((first, start, stop - start))
    return spans


def head_mask(first, start, width):
    lanes = start + lax.broadcasted_iota(jnp.int32, (SEQ, width), 1)
    return (lanes >= first) & (lanes < first + HEAD_DIM)


def dot_nt(left_side, right_side):
    return lax.dot_general(
        left_side, right_side, (((1,), (1,)), ((), ())), preferred_element_type=jnp.float32
    )


def attend_kernel(qkv_ref, out_ref, total):
    total[...] = jnp.zeros_like(total)
    for first, start, width in head_windows():
        keep = head_mask(first, start, width)
        query = qkv_ref[0, :, start : start + width]
        key = jnp.where(keep, qkv_ref[0, :, D + start : D + start + width], 0)
        value = jnp.where(keep, qkv_ref[0, :, 2 * D + start : 2 * D + start + width], 0)
        scores = dot_nt(query, key) * HEAD_DIM ** (-0.5)
        expo = jnp.exp(scores - jnp.max(scores, 1, keepdims=True))
        probs = (expo / jnp.sum(expo, 1, keepdims=True)).astype(jnp.bfloat16)
        total[:, start : start + width] += matmul(probs, value)
    out_ref[0] = total[...].astype(jnp.bfloat16)


def attend(qkv):
    images = qkv.shape[0]
    return pl.pallas_call(
        attend_kernel,
        grid=(images,),
        in_specs=[pl.BlockSpec((1, SEQ, 3 * D), lambda i: (i, 0, 0))],
        out_specs=pl.BlockSpec((1, SEQ, D), lambda i: (i, 0, 0)),
        out_shape=jax.ShapeDtypeStruct((images, SEQ, D), jnp.bfloat16),
        scratch_shapes=[pltpu.VMEM((SEQ, D), jnp.float32)],
        compiler_params=pltpu.CompilerParams(vmem_limit_bytes=40 * 1024 * 1024),
        cost_estimate=small_cost,
    )(qkv)


def attend_back_kernel(qkv_ref, grad_ref, out_ref, query_sum, key_sum, value_sum):
    scale = HEAD_DIM ** (-0.5)
    for ref in (query_sum, key_sum, value_sum):
        ref[...] = jnp.zeros_like(ref)
    for first, start, width in head_windows():
        span = slice(start, start + width)
        keep = head_mask(first, start, width)
        query = jnp.where(keep, qkv_ref[0, :, span], 0)
        key = jnp.where(keep, qkv_ref[0, :, D + start : D + start + width], 0)
        value = jnp.where(keep, qkv_ref[0, :, 2 * D + start : 2 * D + start + width], 0)
        above = jnp.where(keep, grad_ref[0, :, span], 0)
        scores = dot_nt(key, query) * scale
        expo = jnp.exp(scores - jnp.max(scores, 0, keepdims=True))
        probs = expo / jnp.sum(expo, 0, keepdims=True)
        prob_grad = dot_nt(value, above)
        inner = jnp.sum(probs * prob_grad, 0, keepdims=True)
        score_grad = (probs * (prob_grad - inner)).astype(jnp.bfloat16)
        value_sum[:, span] += matmul(probs.astype(jnp.bfloat16), above)
        key_sum[:, span] += matmul(score_grad, query) * scale
        query_sum[:, span] += (
            lax.dot_general(
                score_grad, key, (((0,), (0,)), ((), ())), preferred_element_type=jnp.float32
            )
            * scale
        )
    out_ref[0, :, :D] = query_sum[...].astype(jnp.bfloat16)
    out_ref[0, :, D : 2 * D] = key_sum[...].astype(jnp.bfloat16)
    out_ref[0, :, 2 * D :] = value_sum[...].astype(jnp.bfloat16)


def attend_back(qkv, grad):
    images = qkv.shape[0]
    return pl.pallas_call(
        attend_back_kernel,
        grid=(images,),
        in_specs=[
            pl.BlockSpec((1, SEQ, 3 * D), lambda i: (i, 0, 0)),
            pl.BlockSpec((1, SEQ, D), lambda i: (i, 0, 0)),
        ],
        out_specs=pl.BlockSpec((1, SEQ, 3 * D), lambda i: (i, 0, 0)),
        out_shape=jax.ShapeDtypeStruct((images, SEQ, 3 * D), jnp.bfloat16),
        scratch_shapes=[pltpu.VMEM((SEQ, D), jnp.float32)] * 3,
        compiler_params=pltpu.CompilerParams(vmem_limit_bytes=40 * 1024 * 1024),
        cost_estimate=small_cost,
    )(qkv, grad)


def body_data(
    block_input,
    skip_input,
    timesteps,
    class_labels,
    loss_weights,
    grad_output,
    skip_weight,
    qkv_weight,
    proj_weight,
    fc1_weight,
    fc2_weight,
    vectors,
    hidden_bias,
    skip_rows,
    skip_cols,
    qkv_rows,
    qkv_cols,
    proj_rows,
    proj_cols,
    fc1_rows,
    fc1_cols,
    fc2_rows,
    fc2_cols,
    vector_moments,
    hidden_moments,
):
    image_count = timesteps.shape[0]
    mp_count = lax.axis_size("mp")
    dp_count = lax.axis_size("dp")
    mp_index = lax.axis_index("mp")
    dp_index = lax.axis_index("dp")
    core = lax.rem(dp_index, 2)
    quarter = lax.div(dp_index, 2)
    images = image_count // mp_count
    tokens = images * SEQ
    width_local = qkv_weight.shape[2]
    hidden_local = fc1_weight.shape[1]
    hidden_slice = hidden_local // dp_count
    order = Order()

    skip_shard = skip_weight.reshape(-1, D)
    skip_whole = bring(order, skip_shard, quarter, core)
    hidden_all = gather_deep(hidden_bias)
    hidden_state = gather_deep(hidden_moments).reshape(-1)

    angles = (timesteps.astype(jnp.float32) + 0.5) * (0.5 * math.pi / total_steps)
    alpha_sq = jnp.square(jnp.cos(angles))
    sigma_sq = jnp.square(jnp.sin(angles))
    snr_weight = 5.0 * sigma_sq / jnp.maximum(alpha_sq, 5.0 * sigma_sq)
    base_weight = loss_weights * snr_weight
    one_hot = (class_labels[:, None] == jnp.arange(CLASSES, dtype=jnp.int32)[None, :]).astype(
        jnp.float32
    )
    batch = jnp.concatenate([jnp.sum(one_hot, 0), jnp.sum(base_weight)[None]])

    attn_shard = jnp.concatenate(
        [qkv_weight.transpose(0, 2, 1).reshape(3 * width_local, D), proj_weight], 0
    )
    attn_shard = order.mark(attn_shard)
    attn_whole = bring(order, attn_shard, quarter, core)
    batch = order.mark(batch + to_core(batch))
    batch_x = to_x(batch)
    fc1_shard = order.mark(fc1_weight.T)
    fc2_shard = fc2_weight
    batch = order.mark(batch + batch_x)
    batch_y = to_y(batch)
    start = mp_index * tokens
    block_local = lax.dynamic_slice_in_dim(block_input, start, tokens, 0)
    skip_local = lax.dynamic_slice_in_dim(skip_input, start, tokens, 0)
    both_inputs = jnp.concatenate(
        [
            array.reshape(tokens, mp_count, 2, -1).transpose(0, 2, 1, 3).reshape(tokens, D)
            for array in (block_local, skip_local)
        ],
        1,
    )
    both_inputs = order.mark(both_inputs)
    batch = order.mark(batch + batch_y)

    skip_own = others(order.mark(skip_whole))
    skip_x, skip_y = swap_plane(order, skip_own, skip_own)
    skip_swapped = [to_core(skip_own)]
    fc1_whole = bring(order, fc1_shard, quarter, core)
    hidden_own = pick(hidden_all.reshape(mp_count, 4, 2, hidden_slice), core, 2)
    hidden_own = hidden_own.transpose(1, 0, 2).reshape(-1)
    own_count = jnp.dot(one_hot, batch[:CLASSES], precision=lax.Precision.HIGHEST)
    item_weight = base_weight * lax.rsqrt(own_count)
    hidden_own, item_weight = order.mark(hidden_own, item_weight)
    batch_scale = image_count * dp_count / batch[CLASSES]
    grad_local = lax.dynamic_slice_in_dim(grad_output, start, tokens, 0)
    item_local = lax.dynamic_slice_in_dim(item_weight, mp_index * images, images, 0)
    upstream = (
        grad_local.astype(jnp.float32).reshape(images, SEQ, D) * item_local[:, None, None]
    ).reshape(-1, D)
    upstream = order.mark(upstream)

    skip_x, skip_y = order.mark(skip_x, skip_y)
    skip_one, skip_two = swap_plane(order, skip_y[:2], skip_x[2:])
    skip_swapped = skip_swapped + [to_core(skip_x), to_core(skip_y)]
    skip_one, skip_two = order.mark(skip_one, skip_two)
    skip_swapped = skip_swapped + [to_core(skip_one), to_core(skip_two)]
    attn_own = others(order.mark(attn_whole))
    attn_x, attn_y = swap_plane(order, attn_own, attn_own)
    fc2_whole = bring(order, fc2_shard, quarter, core)
    fc2_across = bring(order, fc2_shard, quarter ^ 3, core)
    skip_swapped = order.mark(*skip_swapped)
    attn_swapped = [to_core(order.after(attn_own))]
    skip_parts = [
        (skip_own, quarter, 1),
        (skip_x, quarter ^ 1, 1),
        (skip_y, quarter ^ 2, 1),
        (skip_one, quarter ^ 3, 1),
        (skip_two, quarter ^ 3, 3),
    ]
    (skip_low,) = assemble_weight(skip_shard, skip_parts, skip_swapped, core, 0)
    joined = matmul(both_inputs, skip_low) + vectors[4]
    normed, normal_one, inverse_one = norm_forward(joined, vectors[0], vectors[1])
    normed_low = normed.astype(jnp.bfloat16)
    joined, normed_low, normal_one = order.mark(joined, normed_low, normal_one)
    upstream_other = to_core(order.after(upstream))

    attn_x, attn_y = order.mark(attn_x, attn_y)
    attn_one, attn_two = swap_plane(order, attn_y[:1], attn_x[1:])
    attn_swapped = attn_swapped + [to_core(attn_x), to_core(attn_y)]
    upstream_other = order.mark(upstream_other) * batch_scale
    upstream = upstream * batch_scale
    upstream_low = jnp.concatenate([upstream, upstream_other], 0).astype(jnp.bfloat16)
    upstream_low = order.mark(upstream_low)
    weight_sq = jnp.stack(
        [
            jnp.sum(array * array)
            for array in (skip_weight, qkv_weight, proj_weight, fc1_weight, fc2_weight, hidden_bias)
        ]
    )
    weight_sq = order.mark(weight_sq)
    fc1_own = others(order.mark(fc1_whole))
    fc1_x, fc1_y = swap_plane(order, fc1_own, fc1_own)
    attn_one, attn_two = order.mark(attn_one, attn_two)
    attn_swapped = attn_swapped + [to_core(attn_one), to_core(attn_two)]
    attn_parts = [
        (attn_own, quarter, 1),
        (attn_x, quarter ^ 1, 1),
        (attn_y, quarter ^ 2, 1),
        (attn_one, quarter ^ 3, 1),
        (attn_two, quarter ^ 3, 2),
    ]
    attn_swapped = order.mark(*attn_swapped)
    qkv_low, proj_low = assemble_weight(
        attn_shard, attn_parts, attn_swapped, core, 3 * mp_count
    )
    qkv_all = jnp.einsum(
        "itd,ed->ite",
        normed_low.reshape(images, SEQ, D),
        qkv_low,
        preferred_element_type=jnp.float32,
    ).astype(jnp.bfloat16)
    qkv_all = order.mark(qkv_all)
    attended = attend(qkv_all).reshape(tokens, D)
    residual = joined + matmul(attended, proj_low) + vectors[5]
    residual = order.mark(residual)
    fc1_x, fc1_y = order.mark(fc1_x, fc1_y)
    fc1_cut = order.mark(fc1_y[:2], fc1_x[2:])
    fc1_one, fc1_two = swap_plane(order, *fc1_cut)
    fc2_own = others(order.mark(fc2_whole))
    fc2_x, fc2_y = swap_plane(order, fc2_own, fc2_own)
    normed_two, normal_two, inverse_two = norm_forward(
        order.after(residual), vectors[2], vectors[3]
    )
    normed_two, normal_two = order.mark(normed_two, normal_two)
    normed_two_other = to_core(normal_two)
    fc1_one, fc1_two = order.mark(fc1_one, fc1_two)
    fc1_parts = [
        (fc1_own, quarter, 1),
        (fc1_x, quarter ^ 1, 1),
        (fc1_y, quarter ^ 2, 1),
        (fc1_one, quarter ^ 3, 1),
        (fc1_two, quarter ^ 3, 3),
    ]
    (fc1_low,) = assemble_weight(fc1_shard, fc1_parts, None, core, 0)
    fc1_low = order.mark(fc1_low)
    normed_two_other = order.mark(normed_two_other) * vectors[2] + vectors[3]
    normed_two_low = jnp.concatenate([normed_two, normed_two_other], 0).astype(jnp.bfloat16)
    normed_two_low = order.mark(normed_two_low)
    pre_act = (
        jnp.einsum("td,fd->tf", normed_two_low, fc1_low, preferred_element_type=jnp.float32)
        + hidden_own
    )
    activated, gelu_pull = jax.vjp(gelu_exact, pre_act)
    activated_low = activated.astype(jnp.bfloat16)
    fc2_grad = jnp.einsum(
        "tf,td->fd", activated_low, upstream_low, preferred_element_type=jnp.float32
    ).reshape(4, mp_count, hidden_slice, D)
    fc2_grad = order.mark(fc2_grad)
    fc2_add = swap_plane(order, *order.mark(*cut_corner(fc2_grad, quarter)))

    fc2_x, fc2_y = order.mark(fc2_x, fc2_y)
    fc2_corner = others(order.mark(fc2_across))
    fc2_parts = [
        (fc2_own, quarter, 1),
        (fc2_x, quarter ^ 1, 1),
        (fc2_y, quarter ^ 2, 1),
        (fc2_corner, quarter ^ 3, 1),
    ]
    (fc2_low,) = assemble_weight(fc2_shard, fc2_parts, None, core, 0)
    fc2_low = order.mark(fc2_low)
    forward_part = order.mark(matmul(activated_low, fc2_low))
    forward_other = to_core(forward_part[tokens:])
    act_grad = jnp.einsum(
        "td,fd->tf", order.after(upstream_low), fc2_low, preferred_element_type=jnp.float32
    )
    pre_grad = gelu_pull(act_grad)[0]
    hidden_grad = jnp.sum(pre_grad, 0)
    pre_low, hidden_grad = order.mark(pre_grad.astype(jnp.bfloat16), hidden_grad)
    block_own = residual + forward_part[:tokens] + order.mark(forward_other)
    block_own = order.mark(block_own.reshape(images, SEQ, D))
    block_all = lax.all_gather(block_own, "mp")
    fc2_add = order.mark(*fc2_add)
    fc2_sides = swap_plane(order, *order.mark(*cut_sides(fc2_grad, quarter, *fc2_add)))
    back_part = order.mark(matmul(order.after(pre_low), fc1_low))
    back_other = to_core(back_part[tokens:])
    fc1_grad = jnp.einsum(
        "tf,td->fd",
        order.after(pre_low),
        normed_two_low,
        preferred_element_type=jnp.float32,
    ).reshape(4, mp_count, hidden_slice, D)
    fc1_grad = order.mark(fc1_grad)
    fc1_add = swap_plane(order, *order.mark(*cut_corner(fc1_grad, quarter)))
    norm_two_in = back_part[:tokens] + order.mark(back_other)
    back_two, gain_two_grad, bias_two_grad = norm_backward(
        norm_two_in, normal_two, inverse_two, vectors[2]
    )
    residual_grad = upstream + back_two
    residual_low = residual_grad.astype(jnp.bfloat16)
    residual_grad, residual_low = order.mark(residual_grad, residual_low)
    attended_grad = jnp.einsum(
        "td,ed->te", residual_low, proj_low, preferred_element_type=jnp.float32
    ).astype(jnp.bfloat16)
    qkv_grad_low = attend_back(
        qkv_all, order.mark(attended_grad.reshape(images, SEQ, D))
    ).reshape(tokens, 3 * D)
    qkv_grad_low = order.mark(qkv_grad_low)
    fc2_sides = order.mark(*fc2_sides)
    fc2_piece = sum_deep(order, fc2_grad, quarter, *fc2_sides)
    qkv_grad = jnp.einsum(
        "te,td->ed", order.after(qkv_grad_low), normed_low, preferred_element_type=jnp.float32
    ).reshape(3 * mp_count, 2, hidden_slice, D)
    proj_grad = jnp.einsum(
        "te,td->ed", attended, order.after(residual_low), preferred_element_type=jnp.float32
    ).reshape(mp_count, 2, hidden_slice, D)
    attn_given = order.mark(pick(qkv_grad, 1 - core, 1), pick(proj_grad, 1 - core, 1))
    fc1_add = order.mark(*fc1_add)
    fc1_sides = swap_plane(order, *order.mark(*cut_sides(fc1_grad, quarter, *fc1_add)))
    attn_given = [to_core(array) for array in order.after(*attn_given)]
    norm_one_in = matmul(order.after(qkv_grad_low), qkv_low)
    back_one, gain_one_grad, bias_one_grad = norm_backward(
        norm_one_in, normal_one, inverse_one, vectors[0]
    )
    joined_grad = residual_grad + back_one
    joined_low = joined_grad.astype(jnp.bfloat16)
    joined_grad, joined_low = order.mark(joined_grad, joined_low)
    skip_grad = jnp.einsum(
        "tc,td->cd", both_inputs, joined_low, preferred_element_type=jnp.float32
    ).reshape(4 * mp_count, 2, -1, D)
    skip_given = order.mark(pick(skip_grad, 1 - core, 1))
    skip_given = to_core(skip_given)
    block_all = order.mark(block_all)
    attn_given = order.mark(*attn_given)
    attn_grad = add_half([qkv_grad, proj_grad], attn_given, core)
    attn_grad = order.mark(attn_grad.reshape(4, mp_count, hidden_slice, D))
    attn_add = swap_plane(order, *order.mark(*cut_corner(attn_grad, quarter)))
    fc1_sides = order.mark(*fc1_sides)
    fc1_piece = sum_deep(order, fc1_grad, quarter, *fc1_sides)
    skip_shards = skip_low.reshape(4, mp_count, -1, D)

    def input_product(shift):
        shard_low = pick(skip_shards, lax.rem(mp_index + shift, mp_count), 1).reshape(-1, D)
        return order.mark(
            jnp.einsum("td,cd->tc", joined_low, shard_low, preferred_element_type=jnp.float32)
        )

    stay, turn_one, turn_two, turn_three = [input_product(shift) for shift in range(4)]
    turn_one = turn_mp(order.after(turn_one), 1)
    attn_add = order.mark(*attn_add)
    attn_sides = swap_plane(order, *order.mark(*cut_sides(attn_grad, quarter, *attn_add)))
    skip_given = order.mark(skip_given)
    skip_grad = add_half([skip_grad], [skip_given], core)
    skip_grad = order.mark(skip_grad.reshape(4, mp_count, -1, D))
    skip_add = swap_plane(order, *order.mark(*cut_corner(skip_grad, quarter)))
    fc2_piece = order.mark(fc2_piece)
    vector_grad = jnp.stack(
        [
            gain_one_grad,
            bias_one_grad,
            gain_two_grad,
            bias_two_grad,
            jnp.sum(joined_grad, 0),
            jnp.sum(residual_grad, 0),
            jnp.sum(upstream, 0),
        ]
    )
    hidden_grad = hidden_grad.reshape(4, mp_count, 1, hidden_slice).transpose(1, 0, 2, 3)
    hidden_grad = jnp.where(jnp.arange(2)[None, None, :, None] == core, hidden_grad, 0.0)
    small = order.mark(jnp.concatenate([vector_grad.reshape(-1), hidden_grad.reshape(-1)]))
    small_core = to_core(small)
    attn_sides = order.mark(*attn_sides)
    attn_piece = sum_deep(order, attn_grad, quarter, *attn_sides)
    turn_one = order.mark(turn_one)
    fc1_piece = order.mark(fc1_piece)
    skip_add = order.mark(*skip_add)
    skip_sides = swap_plane(order, *order.mark(*cut_sides(skip_grad, quarter, *skip_add)))
    small = order.mark(small + order.mark(small_core))
    small_x = to_x(small)
    skip_sides = order.mark(*skip_sides)
    small = order.mark(small + order.mark(small_x))
    small_y = to_y(small)
    skip_piece = sum_deep(order, skip_grad, quarter, *skip_sides)

    def spread(piece):
        return swap_plane(order, piece, piece)

    def half_of(rows):
        return (rows // 2 + 7) // 8 * 8

    def spread_far(near):
        half = half_of(near[0].shape[0])
        return swap_plane(order, near[1][:half], near[0][half:])

    def hold(piece, near, far):
        rows, half = piece.shape[0], far[0].shape[0]
        return place_rows(
            [
                (piece, 0, rows, quarter * rows),
                (near[0], 0, rows, (quarter ^ 1) * rows),
                (near[1], 0, rows, (quarter ^ 2) * rows),
                (far[0], 0, half, (quarter ^ 3) * rows),
                (far[1], 0, rows - half, (quarter ^ 3) * rows + half),
            ],
            4 * rows,
        )

    def interleave(held, other, near_state):
        rows = held.shape[0] // 4
        pieces = []
        for n in range(4):
            pieces.append((held, n * rows, rows, (2 * n + core) * rows))
            pieces.append((other, n * rows, rows, (2 * n + 1 - core) * rows))
        whole, sent = place_rows(pieces, 8 * rows, near_state)
        return whole.reshape(near_state.shape + (D,)), sent

    def own_state(state):
        width = state.shape[-1] // mp_count
        return lax.dynamic_slice_in_dim(state, mp_index * width, width, state.ndim - 1)

    def everywhere(array):
        return [array] + [turn_mp(array, shift) for shift in range(1, mp_count)]

    fc2_near, fc1_near = spread(fc2_piece), spread(fc1_piece)
    block_output = (block_all + vectors[6]).astype(jnp.bfloat16).reshape(-1, D)
    block_output = order.mark(block_output)
    fc2_near = order.mark(*fc2_near)
    fc2_far = spread_far(fc2_near)
    fc1_near = order.mark(*fc1_near)
    fc1_far = spread_far(fc1_near)
    turn_two = turn_mp(order.after(turn_two), 2)
    fc2_far = order.mark(*fc2_far)
    attn_piece = order.mark(attn_piece)
    attn_near = spread(attn_piece)
    fc2_held = order.mark(hold(fc2_piece, fc2_near, fc2_far))
    fc2_other = to_core(fc2_held)
    fc1_far = order.mark(*fc1_far)
    skip_piece = order.mark(skip_piece)
    skip_near = spread(skip_piece)
    fc1_held = order.mark(hold(fc1_piece, fc1_near, fc1_far))
    attn_near = order.mark(*attn_near)
    attn_far = spread_far(attn_near)
    fc2_sum, fc2_moments = order.mark(
        *interleave(fc2_held, order.mark(fc2_other), own_state(fc2_rows)[None])
    )
    skip_near = order.mark(*skip_near)
    skip_far = spread_far(skip_near)
    attn_far = order.mark(*attn_far)
    attn_held = order.mark(hold(attn_piece, attn_near, attn_far))
    attn_other = to_core(attn_held)
    turn_two = order.mark(turn_two)
    turn_three = turn_mp(order.after(turn_three), 3)
    fc1_other = to_core(order.after(fc1_held))
    skip_far = order.mark(*skip_far)
    skip_held = order.mark(hold(skip_piece, skip_near, skip_far))
    skip_other = to_core(skip_held)
    small = order.mark(small + order.mark(small_y))
    small = jnp.concatenate(
        [small, weight_sq, jnp.zeros((D - 6,), jnp.float32)], 0
    ).reshape(6, 2, D)
    fc1_sum, fc1_moments = order.mark(
        *interleave(fc1_held, order.mark(fc1_other), own_state(fc1_cols)[None])
    )
    hidden_sent = jnp.concatenate([fc2_moments, fc1_moments, small], 0)
    turn_three = order.mark(turn_three)
    hidden_sent = everywhere(order.mark(hidden_sent))
    attn_state = jnp.concatenate([own_state(qkv_cols), own_state(proj_rows)[None]], 0)
    attn_sum, attn_moments = order.mark(
        *interleave(attn_held, order.mark(attn_other), attn_state)
    )
    skip_sum, skip_moments = order.mark(
        *interleave(skip_held, order.mark(skip_other), own_state(skip_rows))
    )
    hidden_sent = order.mark(*hidden_sent)
    token_sent = everywhere(order.mark(jnp.concatenate([attn_moments, skip_moments], 0)))
    input_grad, skip_input_grad = order.mark(
        *order_tokens([stay, turn_one, turn_two, turn_three], mp_index)
    )
    step = jnp.zeros((8, 128), jnp.float32)
    fc2_far_new, *fc2_scales, step = order.mark(
        *scales(fc2_sum, fc2_cols[None], step, hidden_sent, 0, mp_index, (True,))
    )
    fc1_far_new, *fc1_scales, step = order.mark(
        *scales(fc1_sum, fc1_rows[None], step, hidden_sent, 1, mp_index, (False,))
    )
    token_sent = order.mark(*token_sent)
    attn_state = jnp.concatenate([qkv_rows, proj_cols[None]], 0)
    attn_far_new, *attn_scales, step = order.mark(
        *scales(attn_sum, attn_state, step, token_sent, 0, mp_index, (False, False, False, True))
    )
    skip_far_new, *skip_scales, step = order.mark(
        *scales(skip_sum, skip_cols, step, token_sent, 4, mp_index, (True, True))
    )
    steps = everywhere(step)
    small = jnp.sum(in_turn([array[2:] for array in hidden_sent]), 0).reshape(-1)
    vector_sum = small[: 7 * D].reshape(7, D)
    hidden_whole = small[7 * D : 7 * D + mp_count * hidden_local]
    weight_sq = small[11 * D : 11 * D + 6]
    vector_new = 0.5 * vector_moments + 0.5 * (vector_sum * vector_sum + moment_eps)
    vector_update = vector_sum * lax.rsqrt(vector_new)
    hidden_new = 0.5 * hidden_state + 0.5 * (hidden_whole * hidden_whole + moment_eps)
    hidden_update = hidden_whole * lax.rsqrt(hidden_new)
    vector_step = jnp.sum(vector_update * vector_update) + jnp.sum(hidden_update * hidden_update)

    def own_hidden(array):
        return lax.dynamic_slice_in_dim(array, mp_index * hidden_local, hidden_local, 0)

    hidden_sum, hidden_new = own_hidden(hidden_whole), own_hidden(hidden_new)
    hidden_update = own_hidden(hidden_update)
    tensor_sizes = (2.0 * D * D, 3.0 * D * D, 1.0 * D * D, 1.0 * D * FF, 1.0 * FF * D, 1.0 * FF)
    weight_rms = jnp.sqrt(weight_sq / jnp.array(tensor_sizes, jnp.float32))
    rates = step_rate * jnp.maximum(0.001, weight_rms)
    pairs = jnp.stack([rates, jnp.broadcast_to(vector_step, (6,))], 1)
    pairs = order.mark(pairs)
    steps = order.mark(*steps)

    qkv_turned = qkv_weight.transpose(0, 2, 1)
    skip_new, skip_new_low = renew(skip_weight, skip_sum, *skip_scales, pairs[0], steps, False)
    qkv_new, qkv_new_low = renew(qkv_turned, attn_sum, *attn_scales, pairs[1], steps, False)
    qkv_new, qkv_new_low = qkv_new.transpose(0, 2, 1), qkv_new_low.transpose(0, 2, 1)
    proj_new, proj_new_low = renew(
        proj_weight[None], attn_sum, *attn_scales, pairs[2], steps, False, first=3
    )
    fc1_new, fc1_new_low = renew(fc1_weight[None], fc1_sum, *fc1_scales, pairs[3], steps, True)
    fc2_new, fc2_new_low = renew(fc2_weight[None], fc2_sum, *fc2_scales, pairs[4], steps, False)
    step_total = jnp.sum(jnp.sum(in_turn(steps), 0)) + vector_step
    update_rms = jnp.sqrt(step_total / param_count)
    divisor = jnp.maximum(1.0, update_rms / clip_level)
    vector_rms = jnp.sqrt(jnp.mean(vectors * vectors, 1, keepdims=True))
    vectors_new = vectors - step_rate * jnp.maximum(0.001, vector_rms) * vector_update / divisor
    hidden_bias_new = hidden_bias - rates[5] / divisor * hidden_update
    piece_width = D // dp_count
    dp_start = dp_index * piece_width

    def own_piece(array, axis):
        return lax.dynamic_slice_in_dim(array, dp_start, piece_width, axis)

    def near_whole(sent, first, amount, width):
        near = in_turn([array[first : first + amount, 1, :width] for array in sent])
        return near.transpose(1, 0, 2).reshape(near.shape[1], -1)

    skip_near_new = near_whole(token_sent, 4, 2, width_local)
    attn_near_new = near_whole(token_sent, 0, 4, width_local)
    fc1_near_new = near_whole(hidden_sent, 1, 1, hidden_local)
    fc2_near_new = near_whole(hidden_sent, 0, 1, hidden_local)
    return (
        block_output,
        input_grad,
        skip_input_grad,
        own_piece(skip_sum, 2),
        own_piece(attn_sum[:3], 2).transpose(0, 2, 1),
        own_piece(attn_sum[3], 1),
        own_piece(fc1_sum[0], 1).T,
        own_piece(fc2_sum[0], 1),
        own_piece(vector_sum, 1),
        hidden_sum,
        skip_near_new,
        skip_far_new[:, 0],
        attn_far_new[:3, 0],
        attn_near_new[:3],
        attn_near_new[3],
        attn_far_new[3, 0],
        fc1_far_new[0, 0],
        fc1_near_new[0],
        fc2_near_new[0],
        fc2_far_new[0, 0],
        vector_new,
        hidden_new,
        skip_new,
        qkv_new,
        proj_new[0],
        fc1_new[0],
        fc2_new[0],
        vectors_new,
        hidden_bias_new,
        skip_new_low,
        qkv_new_low,
        proj_new_low[0],
        fc1_new_low[0],
        fc2_new_low[0],
        update_rms,
    )


def solution(mesh):
    placed = (
        P("dp", None),
        P("dp", None),
        P("dp"),
        P("dp"),
        P("dp"),
        P("dp", None),
        P(None, "mp", None),
        P(None, None, "mp"),
        P("mp", None),
        P(None, "mp"),
        P("mp", None),
        P(),
        P("mp"),
        P(),
        P(),
        P(),
        P(),
        P(),
        P(),
        P(),
        P(),
        P(),
        P(),
        P(),
        P("mp"),
    )
    return jax.shard_map(
        body,
        mesh=mesh,
        in_specs=placed,
        out_specs=(
            P("dp", None),
            P("dp", "mp"),
            P("dp", "mp"),
            P(None, "mp", "dp"),
            P(None, "dp", "mp"),
            P("mp", "dp"),
            P("dp", "mp"),
            P("mp", "dp"),
            P(None, "dp"),
            P("mp"),
            P(),
            P(),
            P(),
            P(),
            P(),
            P(),
            P(),
            P(),
            P(),
            P(),
            P(),
            P("mp"),
            P(None, "mp", None),
            P(None, None, "mp"),
            P("mp", None),
            P(None, "mp"),
            P("mp", None),
            P(),
            P("mp"),
            P(None, "mp", None),
            P(None, None, "mp"),
            P("mp", None),
            P(None, "mp"),
            P("mp", None),
            P(),
        ),
        check_vma=False,
    )
```
